32 devices in a mesh: row: 4 (over y, core), col: 8 (over z, x).
Axes of the slice: x: 2, y: 2, z: 4, core: 2. Of those that a mesh axis runs over, the one named last changes fastest.
Arguments:
- operator_blocks: float32 [256, 64, 512], P(('row', 'col')), may hold values from -0.75 to 0.75
- operator_count: int32 [256], P(('row', 'col')), may hold values from 1 to 8
- operator_slot: int32 [256, 8], P(('row', 'col')), may hold values from 0 to 31
- fetch_lists: int32 [4, 8, 8, 4], P('row', 'col'), may hold values from 0 to 255, as said below
- prolong_blocks: float32 [256, 64, 128], P(('row', 'col')), may hold values from -0.75 to 0.75
- prolong_cols: int32 [256, 2], P(('row', 'col')), may hold values from 0 to 7
- restrict_blocks: float32 [256, 64, 128], P(('row', 'col')), may hold values from -0.09375 to 0.09375
- restrict_rows: int32 [256, 2], P(('row', 'col')), may hold values from 0 to 1
Outputs:
- coarse_operator: float32 [512, 512], P('row', 'col')
The draws below stay inside these ranges and needn't reach their ends.
Inputs may be any that keep to these rules, and one draw needn't show every extreme that they name: fetch_lists[r, c, p, s] names a fine block held by the device with column index p and row index r2 = (r + c + p * 4 + s + h) mod 4, for one whole number h of the draw; that device holds fine blocks (r2 * 8 + p) * 8 to (r2 * 8 + p + 1) * 8 - 1.
All inputs are finite; a program needn't handle non-finite values.
Results may differ from the reference program's by a relative error of at most 0.0003.
Values sent between devices are 32-bit elements; how exact they have to be, the bound alone decides.
No kernel may reach another device: no remote copies, remote signals or barrier semaphores. Data moves between devices by JAX's collectives and lax.ppermute only.
A program may use at most 64 MiB of HBM per device.

```python
import jax
import jax.numpy as jnp
from jax import lax

BS = 64
KA = 8
KP = 2
KR = 2
SLOT = 4
NCR = 2
FBD = 8
NF = 256
NC = 8
N_ROW = 4
N_COL = 8


def draw_fetch_lists(key, part):
    first, second = jax.random.split(jax.random.fold_in(key, 11))
    turn = jax.random.randint(first, (), 0, N_ROW)
    row_idx = jnp.arange(N_ROW, dtype=jnp.int32)[:, None, None, None]
    col_idx = jnp.arange(N_COL, dtype=jnp.int32)[None, :, None, None]
    peer_idx = jnp.arange(N_COL, dtype=jnp.int32)[None, None, :, None]
    slot_idx = jnp.arange(SLOT, dtype=jnp.int32)[None, None, None, :]
    owner_row = (row_idx + col_idx + peer_idx * SLOT + slot_idx + turn) % N_ROW
    inside = jax.random.randint(second, (N_ROW, N_COL, N_COL, SLOT), 0, FBD)
    holder = owner_row * N_COL + peer_idx
    inside = jnp.where(holder == 0, 0, inside)
    inside = jnp.where(holder == N_ROW * N_COL - 1, FBD - 1, inside)
    return (holder * FBD + inside).astype(jnp.int32)


def with_ends(values, stream_key, smallest, largest):
    shape = values.shape
    place = [jax.random.randint(jax.random.fold_in(stream_key, axis), (), 0, shape[axis]) for axis in range(len(shape))]
    values = values.at[tuple(place)].set(smallest)
    longest = shape.index(max(shape))
    place[longest] = (place[longest] + 1) % shape[longest]
    return values.at[tuple(place)].set(largest)


def steps_of(rng, dims, shards, smallest, largest):
    gain, own = 1.0, jax.random.fold_in(rng, 6)
    for position, parts in shards:
        heights = jnp.exp(jax.random.uniform(jax.random.fold_in(own, position), (parts,), jnp.float32, smallest / len(shards), largest / len(shards)))
        gain = gain * jnp.repeat(heights, dims[position] // parts).reshape([-1 if axis == position else 1 for axis in range(len(dims))])
    return gain


def centred(key, extent, scale, reach, cuts=(), kind=jnp.bfloat16):
    array = jax.random.normal(key, extent, jnp.float32) * scale
    if len(cuts) > 0:
        array = steps_of(key, extent, cuts, -0.22, 0.18) * array
    return jnp.clip(array, min=-reach, max=reach).astype(kind)


def setup_inputs(seed: int = 0) -> dict:
    streams_of = jax.random.split(jax.random.key(seed), 9)
    operator_blocks = centred(streams_of[0], (NF, BS, KA * BS), BS ** -0.5, 0.75, ((0, 32),), jnp.float32)
    operator_count = with_ends(jax.random.randint(streams_of[1], (NF,), 1, KA + 1), jax.random.fold_in(streams_of[1], 1), 1, KA).astype(jnp.int32)
    operator_slot = with_ends(jax.random.randint(streams_of[2], (NF, KA), 0, N_COL * SLOT), jax.random.fold_in(streams_of[2], 1), 0, (N_COL * SLOT) - 1).astype(jnp.int32)
    fetch_lists = draw_fetch_lists(jax.random.fold_in(streams_of[8], 71), 0)
    prolong_blocks = centred(streams_of[4], (NF, BS, KP * BS), BS ** -0.5, 0.75, ((0, 32),), jnp.float32)
    prolong_cols = with_ends(jax.random.randint(streams_of[5], (NF, KP), 0, NC), jax.random.fold_in(streams_of[5], 1), 0, NC - 1).astype(jnp.int32)
    restrict_blocks = centred(streams_of[6], (NF, BS, KR * BS), (BS * FBD * N_COL * KA * KP // NC // 2) ** -0.5, 0.09375, ((0, 32),), jnp.float32)
    restrict_rows = with_ends(jax.random.randint(streams_of[7], (NF, KR), 0, NCR), jax.random.fold_in(streams_of[7], 1), 0, NCR - 1).astype(jnp.int32)
    return dict(operator_blocks=operator_blocks, operator_count=operator_count, operator_slot=operator_slot, fetch_lists=fetch_lists, prolong_blocks=prolong_blocks, prolong_cols=prolong_cols, restrict_blocks=restrict_blocks, restrict_rows=restrict_rows)


def contract(form, left, right):
    return jnp.einsum(form, left, right, precision=lax.Precision.HIGHEST)


def reference(operator_blocks, operator_count, operator_slot, fetch_lists, prolong_blocks, prolong_cols, restrict_blocks, restrict_rows):
    slab_blocks = FBD * N_COL
    wanted_all = fetch_lists.reshape(N_ROW * N_COL, N_COL * SLOT)

    def mesh_slab(group):
        start = (group * slab_blocks).astype(jnp.int32)
        blocks = lax.dynamic_slice_in_dim(operator_blocks, start, slab_blocks, 0).reshape(slab_blocks, BS, KA, BS)
        counts = lax.dynamic_slice_in_dim(operator_count, start, slab_blocks, 0)
        slots = lax.dynamic_slice_in_dim(operator_slot, start, slab_blocks, 0)
        restrict_part = lax.dynamic_slice_in_dim(restrict_blocks, start, slab_blocks, 0).reshape(slab_blocks, BS, KR, BS)
        restrict_idx = lax.dynamic_slice_in_dim(restrict_rows, start, slab_blocks, 0)
        device = group * N_COL + jnp.arange(slab_blocks, dtype=jnp.int32) // FBD
        fine_index = wanted_all[device[:, None], slots]
        picked = prolong_blocks[fine_index]
        picked_columns = prolong_cols[fine_index]
        live_mask = (jnp.arange(KA, dtype=jnp.int32)[None, :] < counts[:, None]).astype(jnp.float32)
        products = contract("iakb,ikbn->ikan", blocks, picked)
        prolong_hot = (picked_columns[..., None] == jnp.arange(NC, dtype=jnp.int32)).astype(jnp.float32) * live_mask[:, :, None, None]
        product_dense = contract("ikamc,ikmJ->iaJc", products.reshape(slab_blocks, KA, BS, KP, BS), prolong_hot)
        restrict_hot = (restrict_idx[..., None] == jnp.arange(NCR, dtype=jnp.int32)).astype(jnp.float32)
        restrict_dense = contract("iaqb,iqQ->iaQb", restrict_part, restrict_hot)
        return contract("iaQb,iaJc->QbJc", restrict_dense, product_dense).reshape(NCR * BS, NC * BS)

    stacked = lax.map(mesh_slab, jnp.arange(N_ROW, dtype=jnp.int32))
    return stacked.reshape(NC * BS, NC * BS)
```

```python
import functools

import jax
import jax.numpy as jnp
from jax import lax
from jax.experimental import pallas as pl
from jax.experimental.pallas import tpu as pltpu
from jax.sharding import PartitionSpec as P

NCR = 2
LANES = 128
AXES = ("row", "col")
VMEM_LIMIT = 48 * 1024 * 1024


def split3(x, order):
    high = x.astype(jnp.bfloat16)
    low = (x - high.astype(jnp.float32)).astype(jnp.bfloat16)
    parts = {"left": (high, low, high), "right": (high, high, low)}[order]
    return jnp.concatenate(parts, axis=0)


def transposed_dot(left, right):
    return lax.dot_general(left, right, (((0,), (0,)), ((), ())), preferred_element_type=jnp.float32)


def restrict_kernel(count_ref, slot_ref, rows_ref, operator_ref, restrict_ref, out_ref, sums_ref):
    fine_rows, block_size, _ = operator_ref.shape
    entries = slot_ref.shape[1]
    sums_ref[...] = jnp.zeros_like(sums_ref)
    lane = lax.broadcasted_iota(jnp.int32, (block_size, NCR * block_size), 1)
    second = (lane >= block_size).astype(jnp.int32)

    for i in range(fine_rows):
        value = restrict_ref[i]
        swapped = pltpu.roll(value, block_size, 1)
        own_row = jnp.where(second == 0, rows_ref[i, 0], rows_ref[i, 1])
        other_row = jnp.where(second == 0, rows_ref[i, 1], rows_ref[i, 0])
        dense = jnp.where(own_row == second, value, 0.0) + jnp.where(other_row == second, swapped, 0.0)
        product = transposed_dot(split3(operator_ref[i], "left"), split3(dense, "right"))
        for k in range(entries):
            part = product[k * block_size : (k + 1) * block_size]
            slot = slot_ref[i, k]
            sums_ref[slot] += jnp.where(k < count_ref[i], part, 0.0)

    def finish(slot, carry):
        out_ref[slot] = split3(sums_ref[slot], "right")
        return carry

    lax.fori_loop(0, out_ref.shape[0], finish, 0, unroll=8)


def restrict_operator(operator_count, operator_slot, restrict_rows, operator_blocks, restrict_blocks, slots):
    fine_rows, block_size, width = operator_blocks.shape
    wide = NCR * block_size
    return pl.pallas_call(
        restrict_kernel,
        out_shape=jax.ShapeDtypeStruct((slots, 3 * block_size, wide), jnp.bfloat16),
        in_specs=[pl.BlockSpec(memory_space=pltpu.SMEM)] * 3 + [pl.BlockSpec(memory_space=pltpu.VMEM)] * 2,
        out_specs=pl.BlockSpec(memory_space=pltpu.VMEM),
        scratch_shapes=[pltpu.VMEM((slots, block_size, wide), jnp.float32)],
        compiler_params=pltpu.CompilerParams(vmem_limit_bytes=VMEM_LIMIT),
        cost_estimate=pl.CostEstimate(
            flops=6 * fine_rows * block_size * width * wide, bytes_accessed=4 << 20, transcendentals=0
        ),
        name="restrict_operator",
    )(operator_count, operator_slot, restrict_rows, operator_blocks, restrict_blocks)


def combine_kernel(sizes, fetch_ref, table_ref, restricted_ref, blocks_ref, out_ref):
    slots = restricted_ref.shape[0]
    block_size = out_ref.shape[1]
    slot_count = fetch_ref.shape[1]
    fine_rows, columns, prolong_entries = sizes
    out_ref[...] = jnp.zeros_like(out_ref)

    def step(slot, carry):
        peer = lax.div(slot, slot_count)
        wanted = fetch_ref[peer, lax.rem(slot, slot_count)]
        inside = lax.rem(wanted, fine_rows)
        group = lax.div(wanted, fine_rows * columns)
        place = group * columns + peer
        product = transposed_dot(split3(blocks_ref[place], "left"), restricted_ref[slot])
        for m in range(prolong_entries):
            column = table_ref[place, 1 + prolong_entries * inside + m]
            out_ref[column] += product[m * block_size : (m + 1) * block_size]
        return carry

    lax.fori_loop(0, slots, step, 0, unroll=8)


def combine(sizes, fetch, table, restricted, blocks, coarse_all):
    block_size = blocks.shape[1]
    wide = restricted.shape[2]
    return pl.pallas_call(
        functools.partial(combine_kernel, sizes),
        out_shape=jax.ShapeDtypeStruct((coarse_all, block_size, wide), jnp.float32),
        in_specs=[pl.BlockSpec(memory_space=pltpu.SMEM)] * 2 + [pl.BlockSpec(memory_space=pltpu.VMEM)] * 2,
        out_specs=pl.BlockSpec(memory_space=pltpu.VMEM),
        compiler_params=pltpu.CompilerParams(vmem_limit_bytes=VMEM_LIMIT),
        cost_estimate=pl.CostEstimate(flops=1 << 28, bytes_accessed=4 << 20, transcendentals=0),
        name="combine",
    )(fetch, table, restricted, blocks)


def pick_kernel(table_ref, blocks_ref, out_ref):
    def step(place, carry):
        out_ref[place] = blocks_ref[table_ref[place, 0]]
        return carry

    lax.fori_loop(0, out_ref.shape[0], step, 0, unroll=8)


def pick(table, blocks):
    return pl.pallas_call(
        pick_kernel,
        out_shape=jax.ShapeDtypeStruct((table.shape[0],) + blocks.shape[1:], blocks.dtype),
        in_specs=[pl.BlockSpec(memory_space=pltpu.SMEM), pl.BlockSpec(memory_space=pltpu.VMEM)],
        out_specs=pl.BlockSpec(memory_space=pltpu.VMEM),
        compiler_params=pltpu.CompilerParams(vmem_limit_bytes=VMEM_LIMIT),
        cost_estimate=pl.CostEstimate(flops=0, bytes_accessed=2 << 20, transcendentals=0),
        name="pick",
    )(table, blocks)


def add_kernel(parts_ref, out_ref):
    total = parts_ref[0]
    for i in range(1, parts_ref.shape[0]):
        total = total + parts_ref[i]
    out_ref[...] = total.T


def add_up(parts):
    return pl.pallas_call(
        add_kernel,
        out_shape=jax.ShapeDtypeStruct((parts.shape[2], parts.shape[1]), parts.dtype),
        in_specs=[pl.BlockSpec(memory_space=pltpu.VMEM)],
        out_specs=pl.BlockSpec(memory_space=pltpu.VMEM),
        compiler_params=pltpu.CompilerParams(vmem_limit_bytes=VMEM_LIMIT),
        name="add_up",
    )(parts)


def local(
    operator_blocks,
    operator_count,
    operator_slot,
    fetch_lists,
    prolong_blocks,
    prolong_cols,
    restrict_blocks,
    restrict_rows,
):
    fine_rows = operator_blocks.shape[0]
    prolong_entries = prolong_cols.shape[1]
    rows, columns = lax.axis_size("row"), lax.axis_size("col")
    devices = rows * columns
    slot_count = fetch_lists.shape[3]
    fetch = fetch_lists.reshape(columns, slot_count)

    owner_row = fetch // (fine_rows * columns)
    inside = fetch % fine_rows
    mine = owner_row[None] == jnp.arange(rows, dtype=jnp.int32)[:, None, None]
    request = jnp.sum(jnp.where(mine, inside[None], 0), axis=2).reshape(devices, 1)
    own_columns = jnp.broadcast_to(prolong_cols.reshape(1, -1), (devices, prolong_cols.size))
    message = jnp.concatenate([request, own_columns], axis=1)
    message = jnp.pad(message, ((0, 0), (0, LANES - message.shape[1])))
    table = lax.all_to_all(message[:, None, :], AXES, split_axis=0, concat_axis=0, tiled=True)[:, 0, :]

    restricted = restrict_operator(
        operator_count, operator_slot, restrict_rows, operator_blocks, restrict_blocks, columns * slot_count
    )
    picked = pick(table, prolong_blocks)
    blocks = lax.all_to_all(picked, AXES, split_axis=0, concat_axis=0, tiled=True)
    partial_sums = combine((fine_rows, columns, prolong_entries), fetch, table, restricted, blocks, NCR * rows)
    parts = lax.all_to_all(partial_sums, "col", split_axis=0, concat_axis=0, tiled=True)
    return add_up(parts)


def solution(mesh):
    return jax.shard_map(
        local,
        mesh=mesh,
        in_specs=(
            P(("row", "col"), None, None),
            P(("row", "col")),
            P(("row", "col"), None),
            P("row", "col", None, None),
            P(("row", "col"), None, None),
            P(("row", "col"), None),
            P(("row", "col"), None, None),
            P(("row", "col"), None),
        ),
        out_specs=P("row", "col"),
        check_vma=False,
    )
```

```python
import functools

import jax
import jax.numpy as jnp
from jax import lax
from jax.experimental import pallas as pl
from jax.experimental.pallas import tpu as pltpu
from jax.sharding import Mesh
from jax.sharding import PartitionSpec as P

NCR = 2
LANES = 128
VMEM_LIMIT = 48 * 1024 * 1024


def split3(x, order):
    high = x.astype(jnp.bfloat16)
    low = (x - high.astype(jnp.float32)).astype(jnp.bfloat16)
    parts = {"left": (high, low, high), "right": (high, high, low)}[order]
    return jnp.concatenate(parts, axis=0)


def transposed_dot(left, right):
    return lax.dot_general(left, right, (((0,), (0,)), ((), ())), preferred_element_type=jnp.float32)


def restrict_kernel(count_ref, slot_ref, rows_ref, operator_ref, restrict_ref, out_ref, sums_ref):
    fine_rows, block_size, _ = operator_ref.shape
    entries = slot_ref.shape[1]
    sums_ref[...] = jnp.zeros_like(sums_ref)
    lane = lax.broadcasted_iota(jnp.int32, (block_size, NCR * block_size), 1)
    second = (lane >= block_size).astype(jnp.int32)

    for i in range(fine_rows):
        value = restrict_ref[i]
        swapped = pltpu.roll(value, block_size, 1)
        own_row = jnp.where(second == 0, rows_ref[0, i], rows_ref[1, i])
        other_row = jnp.where(second == 0, rows_ref[1, i], rows_ref[0, i])
        dense = jnp.where(own_row == second, value, 0.0) + jnp.where(other_row == second, swapped, 0.0)
        product = transposed_dot(split3(operator_ref[i], "left"), split3(dense, "right"))
        for k in range(entries):
            part = product[k * block_size : (k + 1) * block_size]
            slot = slot_ref[i, k]
            sums_ref[slot] += jnp.where(k < count_ref[i], part, 0.0)

    def finish(slot, carry):
        out_ref[slot] = split3(sums_ref[slot], "right")
        return carry

    lax.fori_loop(0, out_ref.shape[0], finish, 0, unroll=8)


def restrict_operator(operator_count, operator_slot, restrict_rows, operator_blocks, restrict_blocks, slots):
    fine_rows, block_size, width = operator_blocks.shape
    wide = NCR * block_size
    return pl.pallas_call(
        restrict_kernel,
        out_shape=jax.ShapeDtypeStruct((slots, 3 * block_size, wide), jnp.bfloat16),
        in_specs=[pl.BlockSpec(memory_space=pltpu.SMEM)] * 3 + [pl.BlockSpec(memory_space=pltpu.VMEM)] * 2,
        out_specs=pl.BlockSpec(memory_space=pltpu.VMEM),
        scratch_shapes=[pltpu.VMEM((slots, block_size, wide), jnp.float32)],
        compiler_params=pltpu.CompilerParams(vmem_limit_bytes=VMEM_LIMIT),
        cost_estimate=pl.CostEstimate(
            flops=6 * fine_rows * block_size * width * wide, bytes_accessed=4 << 20, transcendentals=0
        ),
        name="restrict_operator",
    )(operator_count, operator_slot, restrict_rows, operator_blocks, restrict_blocks)


def lookup_kernel(half_ref, fetch_ref, table_ref, out_ref, *, fine_rows, rows, columns, entries):
    slot_count = fetch_ref.shape[0]
    half = columns // 2
    own_half = half_ref[0]

    for peer in range(columns):
        for s in range(slot_count):
            slot = peer * slot_count + s
            wanted = fetch_ref[s, peer]
            group = lax.div(wanted, fine_rows * columns)
            inside = lax.rem(wanted, fine_rows)
            far = jnp.where(own_half == peer // half, 0, 1)
            out_ref[0, slot] = 2 * (group * half + peer % half) + far
            holder = (group * 2 + peer // half) * half + peer % half
            for m in range(entries):
                out_ref[1 + m, slot] = table_ref[holder, 2 + entries * inside + m]


def lookup(fetch, table, **sizes):
    slots = fetch.size
    return pl.pallas_call(
        functools.partial(lookup_kernel, **sizes),
        out_shape=jax.ShapeDtypeStruct((1 + sizes["entries"], slots), jnp.int32),
        in_specs=[pl.BlockSpec(memory_space=pltpu.SMEM)] * 3,
        out_specs=pl.BlockSpec(memory_space=pltpu.SMEM),
        cost_estimate=pl.CostEstimate(flops=1 << 20, bytes_accessed=1 << 20, transcendentals=0),
        name="lookup",
    )(lax.axis_index("half").reshape(1), fetch, table)


def combine_kernel(where_ref, restricted_ref, blocks_ref, out_ref):
    slots = restricted_ref.shape[0]
    block_size = out_ref.shape[1]
    out_ref[...] = jnp.zeros_like(out_ref)

    def step(slot, carry):
        block = blocks_ref[where_ref[0, slot]]
        product = transposed_dot(split3(block, "left"), restricted_ref[slot])
        for m in range(where_ref.shape[0] - 1):
            out_ref[where_ref[1 + m, slot]] += product[m * block_size : (m + 1) * block_size]
        return carry

    lax.fori_loop(0, slots, step, 0, unroll=8)


def combine(where, restricted, blocks, coarse_all):
    block_size = blocks.shape[1]
    wide = restricted.shape[2]
    return pl.pallas_call(
        combine_kernel,
        out_shape=jax.ShapeDtypeStruct((coarse_all, block_size, wide), jnp.float32),
        in_specs=[pl.BlockSpec(memory_space=pltpu.SMEM)] + [pl.BlockSpec(memory_space=pltpu.VMEM)] * 2,
        out_specs=pl.BlockSpec(memory_space=pltpu.VMEM),
        compiler_params=pltpu.CompilerParams(vmem_limit_bytes=VMEM_LIMIT),
        cost_estimate=pl.CostEstimate(flops=1 << 28, bytes_accessed=4 << 20, transcendentals=0),
        name="combine",
    )(where, restricted, blocks)


def pick_kernel(request_ref, near_ref, far_ref, out_ref):
    def step(place, carry):
        out_ref[2 * place] = near_ref[request_ref[0, place]]
        out_ref[2 * place + 1] = far_ref[request_ref[1, place]]
        return carry

    lax.fori_loop(0, request_ref.shape[1], step, 0, unroll=8)


def pick(request, near, far):
    return pl.pallas_call(
        pick_kernel,
        out_shape=jax.ShapeDtypeStruct((2 * request.shape[1],) + near.shape[1:], near.dtype),
        in_specs=[pl.BlockSpec(memory_space=pltpu.SMEM)] + [pl.BlockSpec(memory_space=pltpu.VMEM)] * 2,
        out_specs=pl.BlockSpec(memory_space=pltpu.VMEM),
        compiler_params=pltpu.CompilerParams(vmem_limit_bytes=VMEM_LIMIT),
        cost_estimate=pl.CostEstimate(flops=0, bytes_accessed=2 << 20, transcendentals=0),
        name="pick",
    )(request, near, far)


def add_kernel(parts_ref, out_ref):
    total = parts_ref[0]
    for i in range(1, parts_ref.shape[0]):
        total = total + parts_ref[i]
    out_ref[...] = total


def add_up(parts):
    return pl.pallas_call(
        add_kernel,
        out_shape=jax.ShapeDtypeStruct(parts.shape[1:], parts.dtype),
        in_specs=[pl.BlockSpec(memory_space=pltpu.VMEM)],
        out_specs=pl.BlockSpec(memory_space=pltpu.VMEM),
        compiler_params=pltpu.CompilerParams(vmem_limit_bytes=VMEM_LIMIT),
        name="add_up",
    )(parts)


def requests(fetch, prolong_cols, fine_rows, rows, columns):
    half = columns // 2
    own_half = lax.axis_index("half")
    owner_row = fetch // (fine_rows * columns)
    inside = fetch % fine_rows
    mine = owner_row[None] == jnp.arange(rows, dtype=jnp.int32)[:, None, None]
    wanted = jnp.sum(jnp.where(mine, inside[None], 0), axis=1)
    first, second = wanted[:, :half], wanted[:, half:]
    near = jnp.where(own_half == 0, first, second)
    far = jnp.where(own_half == 0, second, first)
    pair = jnp.stack([near, far], axis=-1)[:, None]
    pair = jnp.broadcast_to(pair, (rows, 2, half, 2)).reshape(rows * columns, 2)
    own_columns = jnp.broadcast_to(prolong_cols.reshape(1, -1), (rows * columns, prolong_cols.size))
    message = jnp.concatenate([pair, own_columns], axis=1)
    return jnp.pad(message, ((0, 0), (0, LANES - message.shape[1])))


def local(
    operator_blocks,
    operator_count,
    operator_slot,
    fetch_lists,
    prolong_blocks,
    prolong_cols,
    restrict_blocks,
    restrict_rows,
):
    fine_rows = operator_blocks.shape[0]
    entries = prolong_cols.shape[1]
    rows, half = lax.axis_size("row"), lax.axis_size("near")
    columns = 2 * half
    fetch = fetch_lists.reshape(columns, fetch_lists.shape[3]).T

    far_blocks = lax.ppermute(prolong_blocks, "half", [(0, 1), (1, 0)])
    message = requests(fetch, prolong_cols, fine_rows, rows, columns)
    table = lax.all_to_all(message[:, None, :], ("row", "half", "near"), split_axis=0, concat_axis=0, tiled=True)[:, 0]
    here = lax.dynamic_index_in_dim(table.reshape(rows, 2, half, LANES), lax.axis_index("half"), 1, False)
    request = here[..., :2].reshape(rows * half, 2).T

    restricted = restrict_operator(
        operator_count, operator_slot, restrict_rows.T, operator_blocks, restrict_blocks, fetch.size
    )
    picked = pick(request, prolong_blocks, far_blocks)
    pairs = picked.reshape((rows * half, 2) + picked.shape[1:])
    blocks = lax.all_to_all(pairs, ("row", "near"), split_axis=0, concat_axis=0, tiled=True)
    where = lookup(fetch, table, fine_rows=fine_rows, rows=rows, columns=columns, entries=entries)
    partial_sums = combine(where, restricted, blocks.reshape(picked.shape), NCR * rows)
    parts = lax.all_to_all(partial_sums, ("half", "near"), split_axis=0, concat_axis=0, tiled=True)
    return add_up(parts).T


def solution(mesh):
    rows, columns = mesh.shape["row"], mesh.shape["col"]
    split = Mesh(mesh.devices.reshape(rows, 2, columns // 2), ("row", "half", "near"))
    flat = ("row", "half", "near")
    return jax.shard_map(
        local,
        mesh=split,
        in_specs=(
            P(flat, None, None),
            P(flat),
            P(flat, None),
            P("row", ("half", "near"), None, None),
            P(flat, None, None),
            P(flat, None),
            P(flat, None, None),
            P(flat, None),
        ),
        out_specs=P("row", ("half", "near")),
        check_vma=False,
    )
```

```python
import functools

import jax
import jax.numpy as jnp
from jax import lax
from jax.experimental import pallas as pl
from jax.experimental.pallas import tpu as pltpu
from jax.sharding import Mesh
from jax.sharding import PartitionSpec as P

NCR = 2
LANES = 128
VMEM_LIMIT = 48 * 1024 * 1024


def split3(x, order):
    high = x.astype(jnp.bfloat16)
    low = (x - high.astype(jnp.float32)).astype(jnp.bfloat16)
    parts = {"left": (high, low, high), "right": (high, high, low)}[order]
    return jnp.concatenate(parts, axis=0)


def transposed_dot(left, right):
    return lax.dot_general(left, right, (((0,), (0,)), ((), ())), preferred_element_type=jnp.float32)


def restrict_kernel(count_ref, slot_ref, rows_ref, operator_ref, restrict_ref, out_ref, sums_ref):
    fine_rows, block_size, _ = operator_ref.shape
    entries = slot_ref.shape[1]
    sums_ref[...] = jnp.zeros_like(sums_ref)
    lane = lax.broadcasted_iota(jnp.int32, (block_size, NCR * block_size), 1)
    second = (lane >= block_size).astype(jnp.int32)

    for i in range(fine_rows):
        value = restrict_ref[i]
        swapped = pltpu.roll(value, block_size, 1)
        own_row = jnp.where(second == 0, rows_ref[0, i], rows_ref[1, i])
        other_row = jnp.where(second == 0, rows_ref[1, i], rows_ref[0, i])
        dense = jnp.where(own_row == second, value, 0.0) + jnp.where(other_row == second, swapped, 0.0)
        product = transposed_dot(split3(operator_ref[i], "left"), split3(dense, "right"))
        for k in range(entries):
            part = product[k * block_size : (k + 1) * block_size]
            slot = slot_ref[i, k]
            sums_ref[slot] += jnp.where(k < count_ref[i], part, 0.0)

    def finish(slot, carry):
        out_ref[slot] = split3(sums_ref[slot], "right")
        return carry

    lax.fori_loop(0, out_ref.shape[0], finish, 0, unroll=8)


def restrict_operator(operator_count, operator_slot, restrict_rows, operator_blocks, restrict_blocks, slots):
    fine_rows, block_size, width = operator_blocks.shape
    wide = NCR * block_size
    return pl.pallas_call(
        restrict_kernel,
        out_shape=jax.ShapeDtypeStruct((slots, 3 * block_size, wide), jnp.bfloat16),
        in_specs=[pl.BlockSpec(memory_space=pltpu.SMEM)] * 3 + [pl.BlockSpec(memory_space=pltpu.VMEM)] * 2,
        out_specs=pl.BlockSpec(memory_space=pltpu.VMEM),
        scratch_shapes=[pltpu.VMEM((slots, block_size, wide), jnp.float32)],
        compiler_params=pltpu.CompilerParams(vmem_limit_bytes=VMEM_LIMIT),
        cost_estimate=pl.CostEstimate(
            flops=6 * fine_rows * block_size * width * wide, bytes_accessed=4 << 20, transcendentals=0
        ),
        name="restrict_operator",
    )(operator_count, operator_slot, restrict_rows, operator_blocks, restrict_blocks)


def message_kernel(half_ref, fetch_ref, columns_ref, out_ref, *, fine_rows):
    slot_count, columns = fetch_ref.shape
    entries = columns_ref.shape[0]
    half = columns // 2
    own_half = half_ref[0]
    row = lax.broadcasted_iota(jnp.int32, out_ref.shape, 0)
    lane = lax.broadcasted_iota(jnp.int32, out_ref.shape, 1)
    value = jnp.zeros(out_ref.shape, jnp.int32)
    for i in range(fine_rows):
        for m in range(entries):
            value = jnp.where(lane == 2 + entries * i + m, columns_ref[m, i], value)
    for peer in range(columns):
        far = jnp.where(own_half == peer // half, 0, 1)
        for s in range(slot_count):
            wanted = fetch_ref[s, peer]
            place = lax.div(wanted, fine_rows * columns) * half + peer % half
            value = jnp.where((row == place) & (lane == far), lax.rem(wanted, fine_rows), value)
    out_ref[...] = value


def build_message(own_half, fetch, columns, rows, fine_rows):
    return pl.pallas_call(
        functools.partial(message_kernel, fine_rows=fine_rows),
        out_shape=jax.ShapeDtypeStruct((rows, LANES), jnp.int32),
        in_specs=[pl.BlockSpec(memory_space=pltpu.SMEM)] * 3,
        out_specs=pl.BlockSpec(memory_space=pltpu.VMEM),
        cost_estimate=pl.CostEstimate(flops=0, bytes_accessed=1 << 14, transcendentals=0),
        name="build_message",
    )(own_half, fetch, columns)


def pick_kernel(table_ref, blocks_ref, out_ref, sems, *, far):
    places = out_ref.shape[0]

    def copy(place):
        return pltpu.make_async_copy(blocks_ref.at[table_ref[place, far]], out_ref.at[place], sems.at[place])

    def start(place, carry):
        copy(place).start()
        return carry

    def wait(place, carry):
        copy(place).wait()
        return carry

    lax.fori_loop(0, places, start, 0, unroll=16)
    lax.fori_loop(0, places, wait, 0, unroll=16)


def pick(table, blocks, far):
    places = table.shape[0]
    return pl.pallas_call(
        functools.partial(pick_kernel, far=far),
        out_shape=jax.ShapeDtypeStruct((places,) + blocks.shape[1:], blocks.dtype),
        in_specs=[pl.BlockSpec(memory_space=pltpu.SMEM), pl.BlockSpec(memory_space=pltpu.HBM)],
        out_specs=pl.BlockSpec(memory_space=pltpu.HBM),
        scratch_shapes=[pltpu.SemaphoreType.DMA((places,))],
        cost_estimate=pl.CostEstimate(flops=0, bytes_accessed=1 << 20, transcendentals=0),
        name="pick_far" if far else "pick_near",
    )(table, blocks)


def combine_kernel(half_ref, fetch_ref, table_ref, restricted_ref, blocks_ref, *rest, fine_rows, entries):
    out_ref = rest[-1]
    far = len(rest) - 1
    slot_count, columns = fetch_ref.shape
    half = columns // 2
    block_size = out_ref.shape[1]
    first_peer = half * (half_ref[0] if far == 0 else 1 - half_ref[0])
    first_slot = far * half * slot_count
    out_ref[...] = rest[0][...] if far else jnp.zeros_like(out_ref)

    def step(j, carry):
        near_peer = lax.div(j, slot_count)
        wanted = fetch_ref[lax.rem(j, slot_count), first_peer + near_peer]
        place = lax.div(wanted, fine_rows * columns) * half + near_peer
        inside = lax.rem(wanted, fine_rows)
        product = transposed_dot(split3(blocks_ref[place], "left"), restricted_ref[first_slot + j])
        for m in range(entries):
            column = table_ref[place, 2 + entries * inside + m]
            out_ref[column] += product[m * block_size : (m + 1) * block_size]
        return carry

    lax.fori_loop(0, half * slot_count, step, 0, unroll=16)


def combine(own_half, fetch, table, restricted, blocks, so_far, coarse_all, fine_rows, entries):
    block_size = blocks.shape[1]
    wide = restricted.shape[2]
    return pl.pallas_call(
        functools.partial(combine_kernel, fine_rows=fine_rows, entries=entries),
        out_shape=jax.ShapeDtypeStruct((coarse_all, block_size, wide), jnp.float32),
        in_specs=[pl.BlockSpec(memory_space=pltpu.SMEM)] * 3
        + [pl.BlockSpec(memory_space=pltpu.VMEM)] * (2 + len(so_far)),
        out_specs=pl.BlockSpec(memory_space=pltpu.VMEM),
        compiler_params=pltpu.CompilerParams(vmem_limit_bytes=VMEM_LIMIT),
        cost_estimate=pl.CostEstimate(flops=1 << 27, bytes_accessed=2 << 20, transcendentals=0),
        name="combine_far" if so_far else "combine_near",
    )(own_half, fetch, table, restricted, blocks, *so_far)


def add_kernel(parts_ref, out_ref):
    total = parts_ref[0]
    for i in range(1, parts_ref.shape[0]):
        total = total + parts_ref[i]
    out_ref[...] = total


def add_up(parts):
    return pl.pallas_call(
        add_kernel,
        out_shape=jax.ShapeDtypeStruct(parts.shape[1:], parts.dtype),
        in_specs=[pl.BlockSpec(memory_space=pltpu.VMEM)],
        out_specs=pl.BlockSpec(memory_space=pltpu.VMEM),
        compiler_params=pltpu.CompilerParams(vmem_limit_bytes=VMEM_LIMIT),
        name="add_up",
    )(parts)


def local(
    operator_blocks,
    operator_count,
    operator_slot,
    fetch_lists,
    prolong_blocks,
    prolong_cols,
    restrict_blocks,
    restrict_rows,
):
    fine_rows = operator_blocks.shape[0]
    entries = prolong_cols.shape[1]
    rows, half = lax.axis_size("row"), lax.axis_size("near")
    fetch = fetch_lists.reshape(2 * half, fetch_lists.shape[3]).T
    own_half = lax.axis_index("half").reshape(1)
    swap = [(0, 1), (1, 0)]

    far_blocks = lax.ppermute(prolong_blocks, "half", swap)
    message = build_message(own_half, fetch, prolong_cols.T, rows * half, fine_rows)
    table = lax.all_to_all(message[:, None], ("row", "near"), split_axis=0, concat_axis=0, tiled=True)[:, 0]
    far_table = lax.ppermute(table, "half", swap)
    near = lax.all_to_all(pick(table, prolong_blocks, 0), ("row", "near"), split_axis=0, concat_axis=0, tiled=True)
    far = lax.all_to_all(pick(table, far_blocks, 1), ("row", "near"), split_axis=0, concat_axis=0, tiled=True)

    slot = (operator_slot + own_half * (fetch.size // 2)) % fetch.size
    restricted = restrict_operator(
        operator_count, slot, restrict_rows.T, operator_blocks, restrict_blocks, fetch.size
    )
    sizes = (NCR * rows, fine_rows, entries)
    sums = combine(own_half, fetch, table, restricted, near, (), *sizes)
    sums = combine(own_half, fetch, far_table, restricted, far, (sums,), *sizes)
    parts = lax.all_to_all(sums, ("half", "near"), split_axis=0, concat_axis=0, tiled=True)
    return add_up(parts).T


def solution(mesh):
    rows, columns = mesh.shape["row"], mesh.shape["col"]
    split = Mesh(mesh.devices.reshape(rows, 2, columns // 2), ("row", "half", "near"))
    flat = ("row", "half", "near")
    return jax.shard_map(
        local,
        mesh=split,
        in_specs=(
            P(flat, None, None),
            P(flat),
            P(flat, None),
            P("row", ("half", "near"), None, None),
            P(flat, None, None),
            P(flat, None),
            P(flat, None, None),
            P(flat, None),
        ),
        out_specs=P("row", ("half", "near")),
        check_vma=False,
    )
```

```python
import functools

import jax
import jax.numpy as jnp
from jax import lax
from jax.experimental import pallas as pl
from jax.experimental.pallas import tpu as pltpu
from jax.sharding import Mesh
from jax.sharding import PartitionSpec as P

NCR = 2
LANES = 128
EXTRA = 8
VMEM_LIMIT = 48 * 1024 * 1024


def split3(x, order):
    high = x.astype(jnp.bfloat16)
    low = (x - high.astype(jnp.float32)).astype(jnp.bfloat16)
    parts = {"left": (high, low, high), "right": (high, high, low)}[order]
    return jnp.concatenate(parts, axis=0)


def transposed_dot(left, right):
    return lax.dot_general(left, right, (((0,), (0,)), ((), ())), preferred_element_type=jnp.float32)


def extend_kernel(columns_ref, blocks_ref, out_ref):
    fine_rows, block_size, width = blocks_ref.shape
    entries = columns_ref.shape[0]
    used = fine_rows * block_size
    out_ref[:used] = blocks_ref[...].reshape(used, width)
    lane = lax.broadcasted_iota(jnp.int32, (EXTRA, width), 1)
    value = jnp.zeros((EXTRA, width), jnp.int32)
    for i in range(fine_rows):
        for m in range(entries):
            value = jnp.where(lane == entries * i + m, columns_ref[m, i], value)
    out_ref[used:] = value.astype(jnp.float32)


def extend(columns, blocks):
    fine_rows, block_size, width = blocks.shape
    return pl.pallas_call(
        extend_kernel,
        out_shape=jax.ShapeDtypeStruct((fine_rows * block_size + EXTRA, width), blocks.dtype),
        in_specs=[pl.BlockSpec(memory_space=pltpu.SMEM), pl.BlockSpec(memory_space=pltpu.VMEM)],
        out_specs=pl.BlockSpec(memory_space=pltpu.VMEM),
        cost_estimate=pl.CostEstimate(flops=0, bytes_accessed=1 << 19, transcendentals=0),
        name="extend",
    )(columns, blocks)


def restrict_kernel(count_ref, slot_ref, rows_ref, fetch_ref, operator_ref, restrict_ref, out_ref):
    fine_rows, block_size, _ = operator_ref.shape
    entries = slot_ref.shape[1]
    slot_count, columns = fetch_ref.shape
    half = columns // 2
    used = 2 * slot_count * block_size
    wide = NCR * block_size
    lane = lax.broadcasted_iota(jnp.int32, (block_size, wide), 1)
    second = (lane >= block_size).astype(jnp.int32)
    short_lane = lax.broadcasted_iota(jnp.int32, (EXTRA, wide), 1)

    for near in range(half):
        out_ref[near, :used] = jnp.zeros((used, wide), jnp.float32)
        value = jnp.zeros((EXTRA, wide), jnp.int32)
        for side in range(2):
            for s in range(slot_count):
                wanted = fetch_ref[s, side * half + near]
                value = jnp.where(short_lane == side * slot_count + s, wanted, value)
        out_ref[near, used:] = value.astype(jnp.float32)

    for i in range(fine_rows):
        value = restrict_ref[i]
        swapped = pltpu.roll(value, block_size, 1)
        own_row = jnp.where(second == 0, rows_ref[0, i], rows_ref[1, i])
        other_row = jnp.where(second == 0, rows_ref[1, i], rows_ref[0, i])
        dense = jnp.where(own_row == second, value, 0.0) + jnp.where(other_row == second, swapped, 0.0)
        product = transposed_dot(split3(operator_ref[i], "left"), split3(dense, "right"))
        for k in range(entries):
            part = jnp.where(k < count_ref[i], product[k * block_size : (k + 1) * block_size], 0.0)
            peer = lax.div(slot_ref[i, k], slot_count)
            place = lax.div(peer, half) * slot_count + lax.rem(slot_ref[i, k], slot_count)
            start = pl.multiple_of(place * block_size, block_size)
            out_ref[lax.rem(peer, half), pl.ds(start, block_size)] += part


def restrict_operator(operator_count, operator_slot, restrict_rows, fetch, operator_blocks, restrict_blocks):
    fine_rows, block_size, width = operator_blocks.shape
    slot_count, columns = fetch.shape
    wide = NCR * block_size
    rows = 2 * slot_count * block_size + EXTRA
    return pl.pallas_call(
        restrict_kernel,
        out_shape=jax.ShapeDtypeStruct((columns // 2, rows, wide), jnp.float32),
        in_specs=[pl.BlockSpec(memory_space=pltpu.SMEM)] * 4 + [pl.BlockSpec(memory_space=pltpu.VMEM)] * 2,
        out_specs=pl.BlockSpec(memory_space=pltpu.VMEM),
        compiler_params=pltpu.CompilerParams(vmem_limit_bytes=VMEM_LIMIT),
        cost_estimate=pl.CostEstimate(
            flops=6 * fine_rows * block_size * width * wide, bytes_accessed=4 << 20, transcendentals=0
        ),
        name="restrict_operator",
    )(operator_count, operator_slot, restrict_rows, fetch, operator_blocks, restrict_blocks)


def combine_kernel(own_ref, restricted_ref, *rest, slot_count, fine_rows, entries):
    pieces, (out_ref, held_ref, table_ref, index_ref, sem) = rest[:-5], rest[-5:]
    half = restricted_ref.shape[0]
    block_size = out_ref.shape[1]
    rows = len(pieces) // 2
    columns = 2 * half
    used = 2 * slot_count * block_size
    held = fine_rows * block_size

    table_ref[...] = jnp.zeros_like(table_ref)
    for near in range(half):
        table_ref[near : near + 1] = restricted_ref[near, used : used + 1].astype(jnp.int32)
    for i, piece in enumerate(pieces):
        table_ref[half + i : half + i + 1] = piece[held : held + 1].astype(jnp.int32)
    copy = pltpu.make_async_copy(table_ref, index_ref, sem)
    copy.start()
    for i, piece in enumerate(pieces):
        held_ref[i] = piece[:held]
    out_ref[...] = jnp.zeros_like(out_ref)
    copy.wait()

    def step(i, carry):
        near = lax.div(i, 2 * slot_count)
        place = lax.rem(i, 2 * slot_count)
        wanted = index_ref[near, place]
        far = lax.div(place, slot_count) ^ own_ref[1]
        inside = lax.rem(wanted, fine_rows)
        piece = far * rows + (lax.div(wanted, fine_rows * columns) ^ own_ref[0])
        block = held_ref[piece, pl.ds(pl.multiple_of(inside * block_size, block_size), block_size)]
        restricted = restricted_ref[near, pl.ds(pl.multiple_of(place * block_size, block_size), block_size)]
        product = transposed_dot(split3(block, "left"), split3(restricted, "right"))
        for m in range(entries):
            column = index_ref[half + piece, entries * inside + m]
            out_ref[column] += product[m * block_size : (m + 1) * block_size]
        return carry

    lax.fori_loop(0, half * 2 * slot_count, step, 0, unroll=16)


def combine(own, restricted, pieces, coarse_all, block_size, slot_count, fine_rows, entries):
    half, _, wide = restricted.shape
    table_rows = -(-(half + len(pieces)) // 8) * 8
    return pl.pallas_call(
        functools.partial(combine_kernel, slot_count=slot_count, fine_rows=fine_rows, entries=entries),
        out_shape=jax.ShapeDtypeStruct((coarse_all, block_size, wide), jnp.float32),
        in_specs=[pl.BlockSpec(memory_space=pltpu.SMEM)]
        + [pl.BlockSpec(memory_space=pltpu.VMEM)] * (1 + len(pieces)),
        out_specs=pl.BlockSpec(memory_space=pltpu.VMEM),
        scratch_shapes=[
            pltpu.VMEM((len(pieces), fine_rows * block_size, entries * block_size), jnp.float32),
            pltpu.VMEM((table_rows, LANES), jnp.int32),
            pltpu.SMEM((table_rows, LANES), jnp.int32),
            pltpu.SemaphoreType.DMA,
        ],
        compiler_params=pltpu.CompilerParams(vmem_limit_bytes=VMEM_LIMIT),
        cost_estimate=pl.CostEstimate(flops=1 << 28, bytes_accessed=4 << 20, transcendentals=0),
        name="combine",
    )(own, restricted, *pieces)


def add_kernel(parts_ref, out_ref):
    total = parts_ref[0]
    for i in range(1, parts_ref.shape[0]):
        total = total + parts_ref[i]
    out_ref[...] = total


def add_up(parts):
    return pl.pallas_call(
        add_kernel,
        out_shape=jax.ShapeDtypeStruct(parts.shape[1:], parts.dtype),
        in_specs=[pl.BlockSpec(memory_space=pltpu.VMEM)],
        out_specs=pl.BlockSpec(memory_space=pltpu.VMEM),
        compiler_params=pltpu.CompilerParams(vmem_limit_bytes=VMEM_LIMIT),
        name="add_up",
    )(parts)


def spread_over_rows(blocks, rows):
    pieces = {0: blocks}
    bit = rows // 2
    while bit:
        for mask in list(pieces):
            pieces[mask ^ bit] = lax.ppermute(pieces[mask], "row", [(r, r ^ bit) for r in range(rows)])
        bit //= 2
    return [pieces[mask] for mask in range(rows)]


def local(
    operator_blocks,
    operator_count,
    operator_slot,
    fetch_lists,
    prolong_blocks,
    prolong_cols,
    restrict_blocks,
    restrict_rows,
):
    fine_rows, block_size, _ = operator_blocks.shape
    entries = prolong_cols.shape[1]
    rows, half = lax.axis_size("row"), lax.axis_size("near")
    slot_count = fetch_lists.shape[3]
    fetch = fetch_lists.reshape(2 * half, slot_count).T
    own = jnp.stack([lax.axis_index("row"), lax.axis_index("half")])

    near_blocks = extend(prolong_cols.T, prolong_blocks)
    far_blocks = lax.ppermute(near_blocks, "half", [(0, 1), (1, 0)])
    restricted = restrict_operator(
        operator_count, operator_slot, restrict_rows.T, fetch, operator_blocks, restrict_blocks
    )
    restricted = lax.all_to_all(restricted, "near", split_axis=0, concat_axis=0, tiled=True)
    pieces = spread_over_rows(near_blocks, rows) + spread_over_rows(far_blocks, rows)
    sums = combine(own, restricted, pieces, NCR * rows, block_size, slot_count, fine_rows, entries)
    parts = lax.all_to_all(sums, ("half", "near"), split_axis=0, concat_axis=0, tiled=True)
    return add_up(parts).T


def solution(mesh):
    rows, columns = mesh.shape["row"], mesh.shape["col"]
    split = Mesh(mesh.devices.reshape(rows, 2, columns // 2), ("row", "half", "near"))
    flat = ("row", "half", "near")
    return jax.shard_map(
        local,
        mesh=split,
        in_specs=(
            P(flat, None, None),
            P(flat),
            P(flat, None),
            P("row", ("half", "near"), None, None),
            P(flat, None, None),
            P(flat, None),
            P(flat, None, None),
            P(flat, None),
        ),
        out_specs=P("row", ("half", "near")),
        check_vma=False,
    )
```

```python
import functools

import jax
import jax.numpy as jnp
from jax import lax
from jax.experimental import pallas as pl
from jax.experimental.pallas import tpu as pltpu
from jax.sharding import Mesh
from jax.sharding import PartitionSpec as P

NCR = 2
LANES = 128
EXTRA = 8
VMEM_LIMIT = 48 * 1024 * 1024


def split3(x, order):
    high = x.astype(jnp.bfloat16)
    low = (x - high.astype(jnp.float32)).astype(jnp.bfloat16)
    parts = {"left": (high, low, high), "right": (high, high, low)}[order]
    return jnp.concatenate(parts, axis=0)


def transposed_dot(left, right):
    return lax.dot_general(left, right, (((0,), (0,)), ((), ())), preferred_element_type=jnp.float32)


def restrict_kernel(
    count_any, slot_any, rows_any, fetch_any, restrict_any, operator_any, out_ref,
    count_ref, slot_ref, rows_ref, fetch_ref, restrict_ref, operator_ref, sems, operator_sems,
):
    fine_rows, block_size, _ = operator_ref.shape
    entries = slot_ref.shape[1]
    slot_count, columns = fetch_ref.shape
    half = columns // 2
    used = 2 * slot_count * block_size
    wide = NCR * block_size

    pairs = [
        (count_any, count_ref), (slot_any, slot_ref), (rows_any, rows_ref),
        (fetch_any, fetch_ref), (restrict_any, restrict_ref),
    ]
    copies = [pltpu.make_async_copy(a, b, sems.at[i]) for i, (a, b) in enumerate(pairs)]
    operators = [
        pltpu.make_async_copy(operator_any.at[i], operator_ref.at[i], operator_sems.at[i]) for i in range(fine_rows)
    ]
    for copy in copies + operators:
        copy.start()

    lane = lax.broadcasted_iota(jnp.int32, (block_size, wide), 1)
    second = (lane >= block_size).astype(jnp.int32)
    short_lane = lax.broadcasted_iota(jnp.int32, (EXTRA, wide), 1)
    for near in range(half):
        out_ref[near, :used] = jnp.zeros((used, wide), jnp.float32)
    for copy in copies:
        copy.wait()

    for near in range(half):
        value = jnp.zeros((EXTRA, wide), jnp.int32)
        for side in range(2):
            for s in range(slot_count):
                wanted = fetch_ref[s, side * half + near]
                value = jnp.where(short_lane == side * slot_count + s, wanted, value)
        out_ref[near, used:] = value.astype(jnp.float32)

    for i in range(fine_rows):
        value = restrict_ref[i]
        swapped = pltpu.roll(value, block_size, 1)
        own_row = jnp.where(second == 0, rows_ref[0, i], rows_ref[1, i])
        other_row = jnp.where(second == 0, rows_ref[1, i], rows_ref[0, i])
        dense = jnp.where(own_row == second, value, 0.0) + jnp.where(other_row == second, swapped, 0.0)
        operators[i].wait()
        product = transposed_dot(split3(operator_ref[i], "left"), split3(dense, "right"))
        for k in range(entries):
            part = jnp.where(k < count_ref[i], product[k * block_size : (k + 1) * block_size], 0.0)
            peer = lax.div(slot_ref[i, k], slot_count)
            place = lax.div(peer, half) * slot_count + lax.rem(slot_ref[i, k], slot_count)
            start = pl.multiple_of(place * block_size, block_size)
            out_ref[lax.rem(peer, half), pl.ds(start, block_size)] += part


def restrict_operator(operator_count, operator_slot, restrict_rows, fetch, operator_blocks, restrict_blocks):
    fine_rows, block_size, width = operator_blocks.shape
    slot_count, columns = fetch.shape
    wide = NCR * block_size
    rows = 2 * slot_count * block_size + EXTRA
    small = (operator_count, operator_slot, restrict_rows, fetch)
    return pl.pallas_call(
        restrict_kernel,
        out_shape=jax.ShapeDtypeStruct((columns // 2, rows, wide), jnp.float32),
        in_specs=[pl.BlockSpec(memory_space=pltpu.HBM)] * 6,
        out_specs=pl.BlockSpec(memory_space=pltpu.VMEM),
        scratch_shapes=[pltpu.SMEM(x.shape, x.dtype) for x in small]
        + [pltpu.VMEM(x.shape, x.dtype) for x in (restrict_blocks, operator_blocks)]
        + [pltpu.SemaphoreType.DMA((5,)), pltpu.SemaphoreType.DMA((fine_rows,))],
        compiler_params=pltpu.CompilerParams(vmem_limit_bytes=VMEM_LIMIT),
        cost_estimate=pl.CostEstimate(
            flops=6 * fine_rows * block_size * width * wide, bytes_accessed=4 << 20, transcendentals=0
        ),
        name="restrict_operator",
    )(*small, restrict_blocks, operator_blocks)


def combine_kernel(own_ref, columns_ref, restricted_ref, *rest, far, slot_count, fine_rows, entries):
    out_ref, held_ref, table_ref, index_ref, sem, held_sem = rest[-6:]
    pieces, so_far = (rest[:-7], rest[-7]) if far else (rest[:-6], None)
    half = restricted_ref.shape[0]
    block_size = out_ref.shape[1]
    columns = 2 * half
    used = 2 * slot_count * block_size
    side = 1 - own_ref[1] if far else own_ref[1]

    if not far:
        own_copy = pltpu.make_async_copy(pieces[0], held_ref.at[0], held_sem)
        own_copy.start()
    table_ref[...] = jnp.zeros_like(table_ref)
    for near in range(half):
        table_ref[near : near + 1] = restricted_ref[near, used : used + 1].astype(jnp.int32)
    copy = pltpu.make_async_copy(table_ref, index_ref, sem)
    copy.start()
    for i, piece in enumerate(pieces):
        if far or i:
            held_ref[i] = piece[...]
    out_ref[...] = so_far[...] if far else jnp.zeros_like(out_ref)
    copy.wait()
    if not far:
        own_copy.wait()

    def step(i, carry):
        near = lax.div(i, slot_count)
        place = side * slot_count + lax.rem(i, slot_count)
        wanted = index_ref[near, place]
        inside = lax.rem(wanted, fine_rows)
        piece = lax.div(wanted, fine_rows * columns) ^ own_ref[0]
        restricted = restricted_ref[near, pl.ds(pl.multiple_of(place * block_size, block_size), block_size)]
        product = transposed_dot(split3(held_ref[piece, inside], "left"), split3(restricted, "right"))
        for m in range(entries):
            column = columns_ref[entries * piece + m, inside]
            out_ref[column] += product[m * block_size : (m + 1) * block_size]
        return carry

    lax.fori_loop(0, half * slot_count, step, 0, unroll=16)


def combine(own, columns, restricted, pieces, so_far, coarse_all, slot_count):
    half, _, wide = restricted.shape
    fine_rows, block_size, width = pieces[0].shape
    table_rows = -(-half // 8) * 8
    far = len(so_far)
    first = pl.BlockSpec(memory_space=pltpu.VMEM if far else pltpu.HBM)
    return pl.pallas_call(
        functools.partial(
            combine_kernel, far=far, slot_count=slot_count, fine_rows=fine_rows, entries=width // block_size
        ),
        out_shape=jax.ShapeDtypeStruct((coarse_all, block_size, wide), jnp.float32),
        in_specs=[pl.BlockSpec(memory_space=pltpu.SMEM)] * 2
        + [pl.BlockSpec(memory_space=pltpu.VMEM), first]
        + [pl.BlockSpec(memory_space=pltpu.VMEM)] * (len(pieces) - 1 + far),
        out_specs=pl.BlockSpec(memory_space=pltpu.VMEM),
        scratch_shapes=[
            pltpu.VMEM((len(pieces), fine_rows, block_size, width), jnp.float32),
            pltpu.VMEM((table_rows, LANES), jnp.int32),
            pltpu.SMEM((table_rows, LANES), jnp.int32),
            pltpu.SemaphoreType.DMA,
            pltpu.SemaphoreType.DMA,
        ],
        compiler_params=pltpu.CompilerParams(vmem_limit_bytes=VMEM_LIMIT),
        cost_estimate=pl.CostEstimate(flops=1 << 27, bytes_accessed=2 << 20, transcendentals=0),
        name="combine_far" if far else "combine_near",
    )(own, columns, restricted, *pieces, *so_far)


def add_kernel(parts_ref, out_ref):
    total = parts_ref[0]
    for i in range(1, parts_ref.shape[0]):
        total = total + parts_ref[i]
    out_ref[...] = total


def add_up(parts):
    return pl.pallas_call(
        add_kernel,
        out_shape=jax.ShapeDtypeStruct(parts.shape[1:], parts.dtype),
        in_specs=[pl.BlockSpec(memory_space=pltpu.VMEM)],
        out_specs=pl.BlockSpec(memory_space=pltpu.VMEM),
        compiler_params=pltpu.CompilerParams(vmem_limit_bytes=VMEM_LIMIT),
        name="add_up",
    )(parts)


def row_swap(x, bit):
    return lax.ppermute(x, "row", [(r, r ^ bit) for r in range(lax.axis_size("row"))])


def half_swap(x):
    return lax.ppermute(x, "half", [(0, 1), (1, 0)])


def spread_over_rows(blocks, rows):
    pieces = {0: blocks}
    bit = rows // 2
    while bit:
        for mask in list(pieces):
            pieces[mask ^ bit] = row_swap(pieces[mask], bit)
        bit //= 2
    return [pieces[mask] for mask in range(rows)]


def columns_of_rows(columns, rows):
    bit = 1
    while bit < rows:
        columns = jnp.concatenate([columns, row_swap(columns, bit)], axis=0)
        bit *= 2
    return columns


def local(
    operator_blocks,
    operator_count,
    operator_slot,
    fetch_lists,
    prolong_blocks,
    prolong_cols,
    restrict_blocks,
    restrict_rows,
):
    rows, half = lax.axis_size("row"), lax.axis_size("near")
    slot_count = fetch_lists.shape[3]
    fetch = fetch_lists.reshape(2 * half, slot_count).T
    own = jnp.stack([lax.axis_index("row"), lax.axis_index("half")])

    far_blocks = half_swap(prolong_blocks)
    restricted = restrict_operator(
        operator_count, operator_slot, restrict_rows.T, fetch, operator_blocks, restrict_blocks
    )
    restricted = lax.all_to_all(restricted, "near", split_axis=0, concat_axis=0, tiled=True)
    near_columns = columns_of_rows(prolong_cols.T, rows)
    far_columns = half_swap(near_columns)
    near_pieces = spread_over_rows(prolong_blocks, rows)
    far_pieces = spread_over_rows(far_blocks, rows)
    sums = combine(own, near_columns, restricted, near_pieces, (), NCR * rows, slot_count)
    sums = combine(own, far_columns, restricted, far_pieces, (sums,), NCR * rows, slot_count)
    parts = lax.all_to_all(sums, ("half", "near"), split_axis=0, concat_axis=0, tiled=True)
    return add_up(parts).T


def solution(mesh):
    rows, columns = mesh.shape["row"], mesh.shape["col"]
    split = Mesh(mesh.devices.reshape(rows, 2, columns // 2), ("row", "half", "near"))
    flat = ("row", "half", "near")
    return jax.shard_map(
        local,
        mesh=split,
        in_specs=(
            P(flat, None, None),
            P(flat),
            P(flat, None),
            P("row", ("half", "near"), None, None),
            P(flat, None, None),
            P(flat, None),
            P(flat, None, None),
            P(flat, None),
        ),
        out_specs=P("row", ("half", "near")),
        check_vma=False,
    )
```

```python
import functools

import jax
import jax.numpy as jnp
from jax import lax
from jax.experimental import pallas as pl
from jax.experimental.pallas import tpu as pltpu
from jax.sharding import Mesh
from jax.sharding import PartitionSpec as P

NCR = 2
LANES = 128
EXTRA = 8
HOLD_FLOPS = 4 << 30
HOLD_BYTES = 12 << 20
VMEM_LIMIT = 48 * 1024 * 1024


def split3(x, order):
    high = x.astype(jnp.bfloat16)
    low = (x - high.astype(jnp.float32)).astype(jnp.bfloat16)
    parts = {"left": (high, low, high), "right": (high, high, low)}[order]
    return jnp.concatenate(parts, axis=0)


def transposed_dot(left, right):
    return lax.dot_general(left, right, (((0,), (0,)), ((), ())), preferred_element_type=jnp.float32)


def hold_kernel(columns_ref, mark_ref, blocks_ref, out_ref):
    out_ref[...] = blocks_ref[...]


def hold_until(columns, mark, blocks):
    return pl.pallas_call(
        hold_kernel,
        out_shape=jax.ShapeDtypeStruct(blocks.shape, blocks.dtype),
        in_specs=[pl.BlockSpec(memory_space=pltpu.VMEM)] * 3,
        out_specs=pl.BlockSpec(memory_space=pltpu.VMEM),
        compiler_params=pltpu.CompilerParams(vmem_limit_bytes=VMEM_LIMIT),
        cost_estimate=pl.CostEstimate(flops=HOLD_FLOPS, bytes_accessed=HOLD_BYTES, transcendentals=0),
        name="hold_until",
    )(columns, mark, blocks)


def restrict_kernel(
    count_any, slot_any, rows_any, fetch_any, restrict_any, operator_any, out_ref, mark_ref,
    count_ref, slot_ref, rows_ref, fetch_ref, restrict_ref, operator_ref, sems, operator_sems,
):
    fine_rows, block_size, _ = operator_ref.shape
    entries = slot_ref.shape[1]
    slot_count, columns = fetch_ref.shape
    half = columns // 2
    used = 2 * slot_count * block_size
    wide = NCR * block_size

    pairs = [
        (count_any, count_ref), (slot_any, slot_ref), (rows_any, rows_ref),
        (fetch_any, fetch_ref), (restrict_any, restrict_ref),
    ]
    copies = [pltpu.make_async_copy(a, b, sems.at[i]) for i, (a, b) in enumerate(pairs)]
    operators = [
        pltpu.make_async_copy(operator_any.at[i], operator_ref.at[i], operator_sems.at[i]) for i in range(fine_rows)
    ]
    for copy in copies + operators:
        copy.start()

    lane = lax.broadcasted_iota(jnp.int32, (block_size, wide), 1)
    second = (lane >= block_size).astype(jnp.int32)
    short_lane = lax.broadcasted_iota(jnp.int32, (EXTRA, wide), 1)
    for near in range(half):
        out_ref[near, :used] = jnp.zeros((used, wide), jnp.float32)
    for copy in copies:
        copy.wait()

    for near in range(half):
        value = jnp.zeros((EXTRA, wide), jnp.int32)
        for side in range(2):
            for s in range(slot_count):
                wanted = fetch_ref[s, side * half + near]
                value = jnp.where(short_lane == side * slot_count + s, wanted, value)
        out_ref[near, used:] = value.astype(jnp.float32)
    mark_ref[...] = out_ref[0, used:]

    for i in range(fine_rows):
        value = restrict_ref[i]
        swapped = pltpu.roll(value, block_size, 1)
        own_row = jnp.where(second == 0, rows_ref[0, i], rows_ref[1, i])
        other_row = jnp.where(second == 0, rows_ref[1, i], rows_ref[0, i])
        dense = jnp.where(own_row == second, value, 0.0) + jnp.where(other_row == second, swapped, 0.0)
        operators[i].wait()
        product = transposed_dot(split3(operator_ref[i], "left"), split3(dense, "right"))
        for k in range(entries):
            part = jnp.where(k < count_ref[i], product[k * block_size : (k + 1) * block_size], 0.0)
            peer = lax.div(slot_ref[i, k], slot_count)
            place = lax.div(peer, half) * slot_count + lax.rem(slot_ref[i, k], slot_count)
            start = pl.multiple_of(place * block_size, block_size)
            out_ref[lax.rem(peer, half), pl.ds(start, block_size)] += part


def restrict_operator(operator_count, operator_slot, restrict_rows, fetch, operator_blocks, restrict_blocks):
    fine_rows, block_size, width = operator_blocks.shape
    slot_count, columns = fetch.shape
    wide = NCR * block_size
    rows = 2 * slot_count * block_size + EXTRA
    small = (operator_count, operator_slot, restrict_rows, fetch)
    return pl.pallas_call(
        restrict_kernel,
        out_shape=(
            jax.ShapeDtypeStruct((columns // 2, rows, wide), jnp.float32),
            jax.ShapeDtypeStruct((EXTRA, wide), jnp.float32),
        ),
        in_specs=[pl.BlockSpec(memory_space=pltpu.HBM)] * 6,
        out_specs=[pl.BlockSpec(memory_space=pltpu.VMEM)] * 2,
        scratch_shapes=[pltpu.SMEM(x.shape, x.dtype) for x in small]
        + [pltpu.VMEM(x.shape, x.dtype) for x in (restrict_blocks, operator_blocks)]
        + [pltpu.SemaphoreType.DMA((5,)), pltpu.SemaphoreType.DMA((fine_rows,))],
        cost_estimate=pl.CostEstimate(
            flops=6 * fine_rows * block_size * width * wide, bytes_accessed=4 << 20, transcendentals=0
        ),
        name="restrict_operator",
    )(*small, restrict_blocks, operator_blocks)


def combine_kernel(own_ref, columns_ref, restricted_ref, *rest, far, slot_count, fine_rows, entries):
    out_ref, held_ref, table_ref, index_ref, sem, held_sem = rest[-6:]
    pieces, so_far = (rest[:-7], rest[-7]) if far else (rest[:-6], None)
    half = restricted_ref.shape[0]
    block_size = out_ref.shape[1]
    columns = 2 * half
    used = 2 * slot_count * block_size
    side = 1 - own_ref[1] if far else own_ref[1]

    if not far:
        own_copy = pltpu.make_async_copy(pieces[0], held_ref.at[0], held_sem)
        own_copy.start()
    table_ref[...] = jnp.zeros_like(table_ref)
    for near in range(half):
        table_ref[near : near + 1] = restricted_ref[near, used : used + 1].astype(jnp.int32)
    copy = pltpu.make_async_copy(table_ref, index_ref, sem)
    copy.start()
    for i, piece in enumerate(pieces):
        if far or i:
            held_ref[i] = piece[...]
    out_ref[...] = so_far[...] if far else jnp.zeros_like(out_ref)
    copy.wait()
    if not far:
        own_copy.wait()

    def step(i, carry):
        near = lax.div(i, slot_count)
        place = side * slot_count + lax.rem(i, slot_count)
        wanted = index_ref[near, place]
        inside = lax.rem(wanted, fine_rows)
        piece = lax.div(wanted, fine_rows * columns) ^ own_ref[0]
        restricted = restricted_ref[near, pl.ds(pl.multiple_of(place * block_size, block_size), block_size)]
        product = transposed_dot(split3(held_ref[piece, inside], "left"), split3(restricted, "right"))
        for m in range(entries):
            column = columns_ref[entries * piece + m, inside]
            out_ref[column] += product[m * block_size : (m + 1) * block_size]
        return carry

    lax.fori_loop(0, half * slot_count, step, 0, unroll=16)


def combine(own, columns, restricted, pieces, so_far, coarse_all, slot_count):
    half, _, wide = restricted.shape
    fine_rows, block_size, width = pieces[0].shape
    table_rows = -(-half // 8) * 8
    far = len(so_far)
    first = pl.BlockSpec(memory_space=pltpu.VMEM if far else pltpu.HBM)
    return pl.pallas_call(
        functools.partial(
            combine_kernel, far=far, slot_count=slot_count, fine_rows=fine_rows, entries=width // block_size
        ),
        out_shape=jax.ShapeDtypeStruct((coarse_all, block_size, wide), jnp.float32),
        in_specs=[pl.BlockSpec(memory_space=pltpu.SMEM)] * 2
        + [pl.BlockSpec(memory_space=pltpu.VMEM), first]
        + [pl.BlockSpec(memory_space=pltpu.VMEM)] * (len(pieces) - 1 + far),
        out_specs=pl.BlockSpec(memory_space=pltpu.VMEM),
        scratch_shapes=[
            pltpu.VMEM((len(pieces), fine_rows, block_size, width), jnp.float32),
            pltpu.VMEM((table_rows, LANES), jnp.int32),
            pltpu.SMEM((table_rows, LANES), jnp.int32),
            pltpu.SemaphoreType.DMA,
            pltpu.SemaphoreType.DMA,
        ],
        compiler_params=pltpu.CompilerParams(vmem_limit_bytes=VMEM_LIMIT),
        cost_estimate=pl.CostEstimate(flops=1 << 27, bytes_accessed=2 << 20, transcendentals=0),
        name="combine_far" if far else "combine_near",
    )(own, columns, restricted, *pieces, *so_far)


def add_kernel(parts_ref, out_ref):
    total = parts_ref[0]
    for i in range(1, parts_ref.shape[0]):
        total = total + parts_ref[i]
    out_ref[...] = total


def add_up(parts):
    return pl.pallas_call(
        add_kernel,
        out_shape=jax.ShapeDtypeStruct(parts.shape[1:], parts.dtype),
        in_specs=[pl.BlockSpec(memory_space=pltpu.VMEM)],
        out_specs=pl.BlockSpec(memory_space=pltpu.VMEM),
        compiler_params=pltpu.CompilerParams(vmem_limit_bytes=VMEM_LIMIT),
        name="add_up",
    )(parts)


def row_swap(x, bit):
    return lax.ppermute(x, "row", [(r, r ^ bit) for r in range(lax.axis_size("row"))])


def half_swap(x):
    return lax.ppermute(x, "half", [(0, 1), (1, 0)])


def spread_over_rows(blocks, rows):
    pieces = {0: blocks}
    bit = rows // 2
    while bit:
        for mask in list(pieces):
            pieces[mask ^ bit] = row_swap(pieces[mask], bit)
        bit //= 2
    return [pieces[mask] for mask in range(rows)]


def columns_of_rows(columns, rows):
    bit = 1
    while bit < rows:
        columns = jnp.concatenate([columns, row_swap(columns, bit)], axis=0)
        bit *= 2
    return columns


def local(
    operator_blocks,
    operator_count,
    operator_slot,
    fetch_lists,
    prolong_blocks,
    prolong_cols,
    restrict_blocks,
    restrict_rows,
):
    rows, half = lax.axis_size("row"), lax.axis_size("near")
    slot_count = fetch_lists.shape[3]
    fetch = fetch_lists.reshape(2 * half, slot_count).T
    own = jnp.stack([lax.axis_index("row"), lax.axis_index("half")])

    far_blocks = half_swap(prolong_blocks)
    restricted, mark = restrict_operator(
        operator_count, operator_slot, restrict_rows.T, fetch, operator_blocks, restrict_blocks
    )
    restricted = lax.all_to_all(restricted, "near", split_axis=0, concat_axis=0, tiled=True)
    near_columns = columns_of_rows(prolong_cols.T, rows)
    far_columns = half_swap(near_columns)
    far_blocks = hold_until(near_columns, mark, far_blocks)
    near_pieces = spread_over_rows(prolong_blocks, rows)
    far_pieces = spread_over_rows(far_blocks, rows)
    sums = combine(own, near_columns, restricted, near_pieces, (), NCR * rows, slot_count)
    sums = combine(own, far_columns, restricted, far_pieces, (sums,), NCR * rows, slot_count)
    parts = lax.all_to_all(sums, ("half", "near"), split_axis=0, concat_axis=0, tiled=True)
    return add_up(parts).T


def solution(mesh):
    rows, columns = mesh.shape["row"], mesh.shape["col"]
    split = Mesh(mesh.devices.reshape(rows, 2, columns // 2), ("row", "half", "near"))
    flat = ("row", "half", "near")
    return jax.shard_map(
        local,
        mesh=split,
        in_specs=(
            P(flat, None, None),
            P(flat),
            P(flat, None),
            P("row", ("half", "near"), None, None),
            P(flat, None, None),
            P(flat, None),
            P(flat, None, None),
            P(flat, None),
        ),
        out_specs=P("row", ("half", "near")),
        check_vma=False,
    )
```

```python
import functools

import jax
import jax.numpy as jnp
from jax import lax
from jax.experimental import pallas as pl
from jax.experimental.pallas import tpu as pltpu
from jax.sharding import Mesh
from jax.sharding import PartitionSpec as P

NCR = 2
LANES = 128
EXTRA = 8
HOLD_FLOPS = 16 << 30
HOLD_BYTES = 48 << 20
VMEM_LIMIT = 48 * 1024 * 1024


def split3(x, order):
    high = x.astype(jnp.bfloat16)
    low = (x - high.astype(jnp.float32)).astype(jnp.bfloat16)
    parts = {"left": (high, low, high), "right": (high, high, low)}[order]
    return jnp.concatenate(parts, axis=0)


def transposed_dot(left, right):
    return lax.dot_general(left, right, (((0,), (0,)), ((), ())), preferred_element_type=jnp.float32)


def hold_kernel(columns_ref, mark_ref, blocks_ref, out_ref):
    out_ref[...] = blocks_ref[...]


def hold_until(columns, mark, blocks):
    return pl.pallas_call(
        hold_kernel,
        out_shape=jax.ShapeDtypeStruct(blocks.shape, blocks.dtype),
        in_specs=[pl.BlockSpec(memory_space=pltpu.VMEM)] * 3,
        out_specs=pl.BlockSpec(memory_space=pltpu.VMEM),
        compiler_params=pltpu.CompilerParams(vmem_limit_bytes=VMEM_LIMIT),
        cost_estimate=pl.CostEstimate(flops=HOLD_FLOPS, bytes_accessed=HOLD_BYTES, transcendentals=0),
        name="hold_until",
    )(columns, mark, blocks)


def restrict_kernel(
    count_any, slot_any, rows_any, fetch_any, restrict_any, operator_any, out_ref, mark_ref,
    count_ref, slot_ref, rows_ref, fetch_ref, restrict_ref, operator_ref, sems, operator_sems,
):
    fine_rows, block_size, _ = operator_ref.shape
    entries = slot_ref.shape[1]
    slot_count, columns = fetch_ref.shape
    half = columns // 2
    used = 2 * slot_count * block_size
    wide = NCR * block_size

    pairs = [
        (count_any, count_ref), (slot_any, slot_ref), (rows_any, rows_ref),
        (fetch_any, fetch_ref), (restrict_any, restrict_ref),
    ]
    copies = [pltpu.make_async_copy(a, b, sems.at[i]) for i, (a, b) in enumerate(pairs)]
    operators = [
        pltpu.make_async_copy(operator_any.at[i], operator_ref.at[i], operator_sems.at[i]) for i in range(fine_rows)
    ]
    for copy in copies + operators:
        copy.start()

    lane = lax.broadcasted_iota(jnp.int32, (block_size, wide), 1)
    second = (lane >= block_size).astype(jnp.int32)
    short_lane = lax.broadcasted_iota(jnp.int32, (EXTRA, wide), 1)
    for near in range(half):
        out_ref[near, :used] = jnp.zeros((used, wide), jnp.float32)
    for copy in copies + operators:
        copy.wait()

    for near in range(half):
        value = jnp.zeros((EXTRA, wide), jnp.int32)
        for side in range(2):
            for s in range(slot_count):
                wanted = fetch_ref[s, side * half + near]
                value = jnp.where(short_lane == side * slot_count + s, wanted, value)
        out_ref[near, used:] = value.astype(jnp.float32)
    mark_ref[...] = out_ref[0, used:]

    for i in range(fine_rows):
        value = restrict_ref[i]
        swapped = pltpu.roll(value, block_size, 1)
        own_row = jnp.where(second == 0, rows_ref[0, i], rows_ref[1, i])
        other_row = jnp.where(second == 0, rows_ref[1, i], rows_ref[0, i])
        dense = jnp.where(own_row == second, value, 0.0) + jnp.where(other_row == second, swapped, 0.0)
        product = transposed_dot(split3(operator_ref[i], "left"), split3(dense, "right"))
        for k in range(entries):
            part = jnp.where(k < count_ref[i], product[k * block_size : (k + 1) * block_size], 0.0)
            peer = lax.div(slot_ref[i, k], slot_count)
            place = lax.div(peer, half) * slot_count + lax.rem(slot_ref[i, k], slot_count)
            start = pl.multiple_of(place * block_size, block_size)
            out_ref[lax.rem(peer, half), pl.ds(start, block_size)] += part


def restrict_operator(operator_count, operator_slot, restrict_rows, fetch, operator_blocks, restrict_blocks):
    fine_rows, block_size, width = operator_blocks.shape
    slot_count, columns = fetch.shape
    wide = NCR * block_size
    rows = 2 * slot_count * block_size + EXTRA
    small = (operator_count, operator_slot, restrict_rows, fetch)
    return pl.pallas_call(
        restrict_kernel,
        out_shape=(
            jax.ShapeDtypeStruct((columns // 2, rows, wide), jnp.float32),
            jax.ShapeDtypeStruct((EXTRA, wide), jnp.float32),
        ),
        in_specs=[pl.BlockSpec(memory_space=pltpu.HBM)] * 6,
        out_specs=[pl.BlockSpec(memory_space=pltpu.VMEM)] * 2,
        scratch_shapes=[pltpu.SMEM(x.shape, x.dtype) for x in small]
        + [pltpu.VMEM(x.shape, x.dtype) for x in (restrict_blocks, operator_blocks)]
        + [pltpu.SemaphoreType.DMA((5,)), pltpu.SemaphoreType.DMA((fine_rows,))],
        cost_estimate=pl.CostEstimate(
            flops=6 * fine_rows * block_size * width * wide, bytes_accessed=4 << 20, transcendentals=0
        ),
        name="restrict_operator",
    )(*small, restrict_blocks, operator_blocks)


def combine_kernel(own_ref, columns_ref, restricted_ref, *rest, far, slot_count, fine_rows, entries):
    out_ref, held_ref, table_ref, index_ref, sem, held_sem = rest[-6:]
    pieces, so_far = (rest[:-7], rest[-7]) if far else (rest[:-6], None)
    half = restricted_ref.shape[0]
    block_size = out_ref.shape[1]
    columns = 2 * half
    used = 2 * slot_count * block_size
    side = 1 - own_ref[1] if far else own_ref[1]

    if not far:
        own_copy = pltpu.make_async_copy(pieces[0], held_ref.at[0], held_sem)
        own_copy.start()
    table_ref[...] = jnp.zeros_like(table_ref)
    for near in range(half):
        table_ref[near : near + 1] = restricted_ref[near, used : used + 1].astype(jnp.int32)
    copy = pltpu.make_async_copy(table_ref, index_ref, sem)
    copy.start()
    for i, piece in enumerate(pieces):
        if far or i:
            held_ref[i] = piece[...]
    out_ref[...] = so_far[...] if far else jnp.zeros_like(out_ref)
    copy.wait()
    if not far:
        own_copy.wait()

    def step(i, carry):
        near = lax.div(i, slot_count)
        place = side * slot_count + lax.rem(i, slot_count)
        wanted = index_ref[near, place]
        inside = lax.rem(wanted, fine_rows)
        piece = lax.div(wanted, fine_rows * columns) ^ own_ref[0]
        restricted = restricted_ref[near, pl.ds(pl.multiple_of(place * block_size, block_size), block_size)]
        product = transposed_dot(split3(held_ref[piece, inside], "left"), split3(restricted, "right"))
        for m in range(entries):
            column = columns_ref[entries * piece + m, inside]
            out_ref[column] += product[m * block_size : (m + 1) * block_size]
        return carry

    lax.fori_loop(0, half * slot_count, step, 0, unroll=16)


def combine(own, columns, restricted, pieces, so_far, coarse_all, slot_count):
    half, _, wide = restricted.shape
    fine_rows, block_size, width = pieces[0].shape
    table_rows = -(-half // 8) * 8
    far = len(so_far)
    first = pl.BlockSpec(memory_space=pltpu.VMEM if far else pltpu.HBM)
    return pl.pallas_call(
        functools.partial(
            combine_kernel, far=far, slot_count=slot_count, fine_rows=fine_rows, entries=width // block_size
        ),
        out_shape=jax.ShapeDtypeStruct((coarse_all, block_size, wide), jnp.float32),
        in_specs=[pl.BlockSpec(memory_space=pltpu.SMEM)] * 2
        + [pl.BlockSpec(memory_space=pltpu.VMEM), first]
        + [pl.BlockSpec(memory_space=pltpu.VMEM)] * (len(pieces) - 1 + far),
        out_specs=pl.BlockSpec(memory_space=pltpu.VMEM),
        scratch_shapes=[
            pltpu.VMEM((len(pieces), fine_rows, block_size, width), jnp.float32),
            pltpu.VMEM((table_rows, LANES), jnp.int32),
            pltpu.SMEM((table_rows, LANES), jnp.int32),
            pltpu.SemaphoreType.DMA,
            pltpu.SemaphoreType.DMA,
        ],
        compiler_params=pltpu.CompilerParams(vmem_limit_bytes=VMEM_LIMIT),
        cost_estimate=pl.CostEstimate(flops=1 << 27, bytes_accessed=2 << 20, transcendentals=0),
        name="combine_far" if far else "combine_near",
    )(own, columns, restricted, *pieces, *so_far)


def add_kernel(parts_ref, out_ref):
    total = parts_ref[0]
    for i in range(1, parts_ref.shape[0]):
        total = total + parts_ref[i]
    out_ref[...] = total


def add_up(parts):
    return pl.pallas_call(
        add_kernel,
        out_shape=jax.ShapeDtypeStruct(parts.shape[1:], parts.dtype),
        in_specs=[pl.BlockSpec(memory_space=pltpu.VMEM)],
        out_specs=pl.BlockSpec(memory_space=pltpu.VMEM),
        compiler_params=pltpu.CompilerParams(vmem_limit_bytes=VMEM_LIMIT),
        name="add_up",
    )(parts)


def row_swap(x, bit):
    return lax.ppermute(x, "row", [(r, r ^ bit) for r in range(lax.axis_size("row"))])


def half_swap(x):
    return lax.ppermute(x, "half", [(0, 1), (1, 0)])


def spread_over_rows(blocks, rows):
    pieces = {0: blocks}
    bit = rows // 2
    while bit:
        for mask in list(pieces):
            pieces[mask ^ bit] = row_swap(pieces[mask], bit)
        bit //= 2
    return [pieces[mask] for mask in range(rows)]


def columns_of_rows(columns, rows):
    bit = 1
    while bit < rows:
        columns = jnp.concatenate([columns, row_swap(columns, bit)], axis=0)
        bit *= 2
    return columns


def local(
    operator_blocks,
    operator_count,
    operator_slot,
    fetch_lists,
    prolong_blocks,
    prolong_cols,
    restrict_blocks,
    restrict_rows,
):
    rows, half = lax.axis_size("row"), lax.axis_size("near")
    slot_count = fetch_lists.shape[3]
    fetch = fetch_lists.reshape(2 * half, slot_count).T
    own = jnp.stack([lax.axis_index("row"), lax.axis_index("half")])

    far_blocks = half_swap(prolong_blocks)
    restricted, mark = restrict_operator(
        operator_count, operator_slot, restrict_rows.T, fetch, operator_blocks, restrict_blocks
    )
    restricted = lax.all_to_all(restricted, "near", split_axis=0, concat_axis=0, tiled=True)
    near_columns = columns_of_rows(prolong_cols.T, rows)
    far_columns = half_swap(near_columns)
    far_blocks = hold_until(near_columns, mark, far_blocks)
    near_pieces = spread_over_rows(prolong_blocks, rows)
    far_pieces = spread_over_rows(far_blocks, rows)
    sums = combine(own, near_columns, restricted, near_pieces, (), NCR * rows, slot_count)
    sums = combine(own, far_columns, restricted, far_pieces, (sums,), NCR * rows, slot_count)
    parts = lax.all_to_all(sums, ("half", "near"), split_axis=0, concat_axis=0, tiled=True)
    return add_up(parts).T


def solution(mesh):
    rows, columns = mesh.shape["row"], mesh.shape["col"]
    split = Mesh(mesh.devices.reshape(rows, 2, columns // 2), ("row", "half", "near"))
    flat = ("row", "half", "near")
    return jax.shard_map(
        local,
        mesh=split,
        in_specs=(
            P(flat, None, None),
            P(flat),
            P(flat, None),
            P("row", ("half", "near"), None, None),
            P(flat, None, None),
            P(flat, None),
            P(flat, None, None),
            P(flat, None),
        ),
        out_specs=P("row", ("half", "near")),
        check_vma=False,
    )
```

```python
import functools

import jax
import jax.numpy as jnp
from jax import lax
from jax.experimental import pallas as pl
from jax.experimental.pallas import tpu as pltpu
from jax.sharding import Mesh
from jax.sharding import PartitionSpec as P

NCR = 2
LANES = 128
EXTRA = 8
HOLD_FLOPS = 16 << 30
VMEM_LIMIT = 48 * 1024 * 1024


def split3(x, order):
    high = x.astype(jnp.bfloat16)
    low = (x - high.astype(jnp.float32)).astype(jnp.bfloat16)
    parts = {"left": (high, low, high), "right": (high, high, low)}[order]
    return jnp.concatenate(parts, axis=0)


def transposed_dot(left, right):
    return lax.dot_general(left, right, (((0,), (0,)), ((), ())), preferred_element_type=jnp.float32)


def hold_kernel(mark_ref, blocks_ref, out_ref):
    out_ref[...] = blocks_ref[...]


def hold_until(mark, blocks, flops):
    return pl.pallas_call(
        hold_kernel,
        out_shape=jax.ShapeDtypeStruct(blocks.shape, blocks.dtype),
        in_specs=[pl.BlockSpec(memory_space=pltpu.VMEM)] * 2,
        out_specs=pl.BlockSpec(memory_space=pltpu.VMEM),
        compiler_params=pltpu.CompilerParams(vmem_limit_bytes=VMEM_LIMIT),
        cost_estimate=pl.CostEstimate(flops=flops, bytes_accessed=flops >> 8, transcendentals=0),
        name="hold_until",
    )(mark, blocks)


def restrict_kernel(
    count_any, slot_any, rows_any, fetch_any, restrict_any, operator_any, columns_ref, out_ref, mark_ref,
    count_ref, slot_ref, rows_ref, fetch_ref, restrict_ref, operator_ref, sems, operator_sems,
):
    fine_rows, block_size, _ = operator_ref.shape
    entries = slot_ref.shape[1]
    slot_count, columns = fetch_ref.shape
    half = columns // 2
    used = 2 * slot_count * block_size
    wide = NCR * block_size

    pairs = [
        (count_any, count_ref), (slot_any, slot_ref), (rows_any, rows_ref),
        (fetch_any, fetch_ref), (restrict_any, restrict_ref),
    ]
    copies = [pltpu.make_async_copy(a, b, sems.at[i]) for i, (a, b) in enumerate(pairs)]
    operators = [
        pltpu.make_async_copy(operator_any.at[i], operator_ref.at[i], operator_sems.at[i]) for i in range(fine_rows)
    ]
    for copy in copies + operators:
        copy.start()

    lane = lax.broadcasted_iota(jnp.int32, (block_size, wide), 1)
    second = (lane >= block_size).astype(jnp.int32)
    short_lane = lax.broadcasted_iota(jnp.int32, (EXTRA, wide), 1)
    for near in range(half):
        out_ref[near, :used] = jnp.zeros((used, wide), jnp.float32)
    for copy in copies + operators:
        copy.wait()

    for near in range(half):
        value = jnp.zeros((EXTRA, wide), jnp.int32)
        for side in range(2):
            for s in range(slot_count):
                wanted = fetch_ref[s, side * half + near]
                value = jnp.where(short_lane == side * slot_count + s, wanted, value)
        out_ref[near, used:] = value.astype(jnp.float32)
    mark_ref[...] = columns_ref[...]

    for i in range(fine_rows):
        value = restrict_ref[i]
        swapped = pltpu.roll(value, block_size, 1)
        own_row = jnp.where(second == 0, rows_ref[0, i], rows_ref[1, i])
        other_row = jnp.where(second == 0, rows_ref[1, i], rows_ref[0, i])
        dense = jnp.where(own_row == second, value, 0.0) + jnp.where(other_row == second, swapped, 0.0)
        product = transposed_dot(split3(operator_ref[i], "left"), split3(dense, "right"))
        for k in range(entries):
            part = jnp.where(k < count_ref[i], product[k * block_size : (k + 1) * block_size], 0.0)
            peer = lax.div(slot_ref[i, k], slot_count)
            place = lax.div(peer, half) * slot_count + lax.rem(slot_ref[i, k], slot_count)
            start = pl.multiple_of(place * block_size, block_size)
            out_ref[lax.rem(peer, half), pl.ds(start, block_size)] += part


def restrict_operator(
    operator_count, operator_slot, restrict_rows, fetch, operator_blocks, restrict_blocks, prolong_columns
):
    fine_rows, block_size, width = operator_blocks.shape
    slot_count, columns = fetch.shape
    wide = NCR * block_size
    rows = 2 * slot_count * block_size + EXTRA
    small = (operator_count, operator_slot, restrict_rows, fetch)
    return pl.pallas_call(
        restrict_kernel,
        out_shape=(
            jax.ShapeDtypeStruct((columns // 2, rows, wide), jnp.float32),
            jax.ShapeDtypeStruct(prolong_columns.shape, prolong_columns.dtype),
        ),
        in_specs=[pl.BlockSpec(memory_space=pltpu.HBM)] * 6 + [pl.BlockSpec(memory_space=pltpu.VMEM)],
        out_specs=[pl.BlockSpec(memory_space=pltpu.VMEM)] * 2,
        scratch_shapes=[pltpu.SMEM(x.shape, x.dtype) for x in small]
        + [pltpu.VMEM(x.shape, x.dtype) for x in (restrict_blocks, operator_blocks)]
        + [pltpu.SemaphoreType.DMA((5,)), pltpu.SemaphoreType.DMA((fine_rows,))],
        cost_estimate=pl.CostEstimate(
            flops=6 * fine_rows * block_size * width * wide, bytes_accessed=4 << 20, transcendentals=0
        ),
        name="restrict_operator",
    )(*small, restrict_blocks, operator_blocks, prolong_columns)


def combine_kernel(own_ref, columns_ref, restricted_ref, *rest, slot_count, fine_rows, entries):
    pieces, (out_ref, held_ref, table_ref, index_ref, sem) = rest[:-5], rest[-5:]
    half = restricted_ref.shape[0]
    rows = len(pieces) // 2
    block_size = out_ref.shape[1]
    columns = 2 * half
    used = 2 * slot_count * block_size

    for near in range(half):
        table_ref[near : near + 1] = restricted_ref[near, used : used + 1].astype(jnp.int32)
    copy = pltpu.make_async_copy(table_ref, index_ref, sem)
    copy.start()
    for i, piece in enumerate(pieces):
        held_ref[i] = piece[...]
    out_ref[...] = jnp.zeros_like(out_ref)
    copy.wait()

    def step(i, carry):
        near = lax.div(i, 2 * slot_count)
        place = lax.rem(i, 2 * slot_count)
        wanted = index_ref[near, place]
        inside = lax.rem(wanted, fine_rows)
        far = lax.div(place, slot_count) ^ own_ref[1]
        piece = far * rows + (lax.div(wanted, fine_rows * columns) ^ own_ref[0])
        restricted = restricted_ref[near, pl.ds(pl.multiple_of(place * block_size, block_size), block_size)]
        product = transposed_dot(split3(held_ref[piece, inside], "left"), split3(restricted, "right"))
        for m in range(entries):
            column = columns_ref[entries * piece + m, inside]
            out_ref[column] += product[m * block_size : (m + 1) * block_size]
        return carry

    lax.fori_loop(0, half * 2 * slot_count, step, 0, unroll=16)


def combine(own, columns, restricted, pieces, coarse_all, slot_count):
    half, _, wide = restricted.shape
    fine_rows, block_size, width = pieces[0].shape
    table_rows = -(-half // 8) * 8
    return pl.pallas_call(
        functools.partial(
            combine_kernel, slot_count=slot_count, fine_rows=fine_rows, entries=width // block_size
        ),
        out_shape=jax.ShapeDtypeStruct((coarse_all, block_size, wide), jnp.float32),
        in_specs=[pl.BlockSpec(memory_space=pltpu.SMEM)] * 2
        + [pl.BlockSpec(memory_space=pltpu.VMEM)] * (1 + len(pieces)),
        out_specs=pl.BlockSpec(memory_space=pltpu.VMEM),
        scratch_shapes=[
            pltpu.VMEM((len(pieces), fine_rows, block_size, width), jnp.float32),
            pltpu.VMEM((table_rows, LANES), jnp.int32),
            pltpu.SMEM((table_rows, LANES), jnp.int32),
            pltpu.SemaphoreType.DMA,
        ],
        compiler_params=pltpu.CompilerParams(vmem_limit_bytes=VMEM_LIMIT),
        cost_estimate=pl.CostEstimate(flops=1 << 28, bytes_accessed=4 << 20, transcendentals=0),
        name="combine",
    )(own, columns, restricted, *pieces)


def add_kernel(parts_ref, out_ref):
    total = parts_ref[0]
    for i in range(1, parts_ref.shape[0]):
        total = total + parts_ref[i]
    out_ref[...] = total


def add_up(parts):
    return pl.pallas_call(
        add_kernel,
        out_shape=jax.ShapeDtypeStruct(parts.shape[1:], parts.dtype),
        in_specs=[pl.BlockSpec(memory_space=pltpu.VMEM)],
        out_specs=pl.BlockSpec(memory_space=pltpu.VMEM),
        compiler_params=pltpu.CompilerParams(vmem_limit_bytes=VMEM_LIMIT),
        name="add_up",
    )(parts)


def row_swap(x, bit):
    return lax.ppermute(x, "row", [(r, r ^ bit) for r in range(lax.axis_size("row"))])


def half_swap(x):
    return lax.ppermute(x, "half", [(0, 1), (1, 0)])


def spread_over_rows(blocks, rows, mark=None):
    pieces = {0: blocks}
    bit = rows // 2
    while bit:
        for mask in list(pieces):
            pieces[mask ^ bit] = row_swap(pieces[mask], bit)
        if mark is not None and bit == rows // 2:
            pieces[bit] = hold_until(mark, pieces[bit], 1 << 20)
        bit //= 2
    return [pieces[mask] for mask in range(rows)]


def columns_of_rows(columns, rows):
    bit = 1
    while bit < rows:
        columns = jnp.concatenate([columns, row_swap(columns, bit)], axis=0)
        bit *= 2
    return columns


def local(
    operator_blocks,
    operator_count,
    operator_slot,
    fetch_lists,
    prolong_blocks,
    prolong_cols,
    restrict_blocks,
    restrict_rows,
):
    rows, half = lax.axis_size("row"), lax.axis_size("near")
    slot_count = fetch_lists.shape[3]
    fetch = fetch_lists.reshape(2 * half, slot_count).T
    own = jnp.stack([lax.axis_index("row"), lax.axis_index("half")])

    far_blocks = half_swap(prolong_blocks)
    restricted, own_columns = restrict_operator(
        operator_count,
        operator_slot,
        restrict_rows.T,
        fetch,
        operator_blocks,
        restrict_blocks,
        prolong_cols.T,
    )
    restricted_here = lax.all_to_all(restricted, "near", split_axis=0, concat_axis=0, tiled=True)
    near_columns = columns_of_rows(own_columns, rows)
    all_columns = jnp.concatenate([near_columns, half_swap(near_columns)], axis=0)
    far_blocks = hold_until(own_columns, far_blocks, HOLD_FLOPS)
    near_pieces = spread_over_rows(prolong_blocks, rows)
    far_pieces = spread_over_rows(far_blocks, rows, all_columns)
    sums = combine(own, all_columns, restricted_here, near_pieces + far_pieces, NCR * rows, slot_count)
    parts = lax.all_to_all(sums, ("half", "near"), split_axis=0, concat_axis=0, tiled=True)
    return add_up(parts).T


def solution(mesh):
    rows, columns = mesh.shape["row"], mesh.shape["col"]
    split = Mesh(mesh.devices.reshape(rows, 2, columns // 2), ("row", "half", "near"))
    flat = ("row", "half", "near")
    return jax.shard_map(
        local,
        mesh=split,
        in_specs=(
            P(flat, None, None),
            P(flat),
            P(flat, None),
            P("row", ("half", "near"), None, None),
            P(flat, None, None),
            P(flat, None),
            P(flat, None, None),
            P(flat, None),
        ),
        out_specs=P("row", ("half", "near")),
        check_vma=False,
    )
```

```python
import functools

import jax
import jax.numpy as jnp
from jax import lax
from jax.experimental import pallas as pl
from jax.experimental.pallas import tpu as pltpu
from jax.sharding import Mesh
from jax.sharding import PartitionSpec as P

NCR = 2
LANES = 128
EXTRA = 8
HOLD_FLOPS = 16 << 30
VMEM_LIMIT = 48 * 1024 * 1024


def split3(x, order):
    high = x.astype(jnp.bfloat16)
    low = (x - high.astype(jnp.float32)).astype(jnp.bfloat16)
    parts = {"left": (high, low, high), "right": (high, high, low)}[order]
    return jnp.concatenate(parts, axis=0)


def transposed_dot(left, right):
    return lax.dot_general(left, right, (((0,), (0,)), ((), ())), preferred_element_type=jnp.float32)


def extend_kernel(columns_ref, blocks_any, out_ref, sem):
    used = blocks_any.shape[0]
    entries, fine_rows = columns_ref.shape
    copy = pltpu.make_async_copy(blocks_any, out_ref.at[pl.ds(0, used)], sem)
    copy.start()
    out_ref[used:] = jnp.zeros((EXTRA, out_ref.shape[1]), jnp.float32)
    out_ref[used : used + entries, :fine_rows] = columns_ref[...].astype(jnp.float32)
    copy.wait()


def extend(columns, blocks):
    used, width = blocks.shape
    return pl.pallas_call(
        extend_kernel,
        out_shape=jax.ShapeDtypeStruct((used + EXTRA, width), blocks.dtype),
        in_specs=[pl.BlockSpec(memory_space=pltpu.VMEM), pl.BlockSpec(memory_space=pltpu.HBM)],
        out_specs=pl.BlockSpec(memory_space=pltpu.VMEM),
        scratch_shapes=[pltpu.SemaphoreType.DMA],
        cost_estimate=pl.CostEstimate(flops=0, bytes_accessed=1 << 19, transcendentals=0),
        name="extend",
    )(columns, blocks)


def hold_kernel(mark_ref, blocks_ref, out_ref):
    out_ref[...] = blocks_ref[...]


def hold_until(mark, blocks, flops):
    return pl.pallas_call(
        hold_kernel,
        out_shape=jax.ShapeDtypeStruct(blocks.shape, blocks.dtype),
        in_specs=[pl.BlockSpec(memory_space=pltpu.VMEM)] * 2,
        out_specs=pl.BlockSpec(memory_space=pltpu.VMEM),
        compiler_params=pltpu.CompilerParams(vmem_limit_bytes=VMEM_LIMIT),
        cost_estimate=pl.CostEstimate(flops=flops, bytes_accessed=flops >> 8, transcendentals=0),
        name="hold_until",
    )(mark, blocks)


def restrict_kernel(
    count_any, slot_any, rows_any, fetch_any, restrict_any, operator_any, out_ref, mark_ref,
    count_ref, slot_ref, rows_ref, fetch_ref, restrict_ref, operator_ref, sems, operator_sems,
):
    fine_rows, block_size, _ = operator_ref.shape
    entries = slot_ref.shape[1]
    slot_count, columns = fetch_ref.shape
    half = columns // 2
    used = 2 * slot_count * block_size
    wide = NCR * block_size

    pairs = [
        (count_any, count_ref), (slot_any, slot_ref), (rows_any, rows_ref),
        (fetch_any, fetch_ref), (restrict_any, restrict_ref),
    ]
    copies = [pltpu.make_async_copy(a, b, sems.at[i]) for i, (a, b) in enumerate(pairs)]
    operators = [
        pltpu.make_async_copy(operator_any.at[i], operator_ref.at[i], operator_sems.at[i]) for i in range(fine_rows)
    ]
    for copy in copies + operators:
        copy.start()

    lane = lax.broadcasted_iota(jnp.int32, (block_size, wide), 1)
    second = (lane >= block_size).astype(jnp.int32)
    short_lane = lax.broadcasted_iota(jnp.int32, (EXTRA, wide), 1)
    for near in range(half):
        out_ref[near, :used] = jnp.zeros((used, wide), jnp.float32)
    for copy in copies + operators:
        copy.wait()

    for near in range(half):
        value = jnp.zeros((EXTRA, wide), jnp.int32)
        for side in range(2):
            for s in range(slot_count):
                wanted = fetch_ref[s, side * half + near]
                value = jnp.where(short_lane == side * slot_count + s, wanted, value)
        out_ref[near, used:] = value.astype(jnp.float32)
    mark_ref[...] = out_ref[0, used:]

    for i in range(fine_rows):
        value = restrict_ref[i]
        swapped = pltpu.roll(value, block_size, 1)
        own_row = jnp.where(second == 0, rows_ref[0, i], rows_ref[1, i])
        other_row = jnp.where(second == 0, rows_ref[1, i], rows_ref[0, i])
        dense = jnp.where(own_row == second, value, 0.0) + jnp.where(other_row == second, swapped, 0.0)
        product = transposed_dot(split3(operator_ref[i], "left"), split3(dense, "right"))
        for k in range(entries):
            part = jnp.where(k < count_ref[i], product[k * block_size : (k + 1) * block_size], 0.0)
            peer = lax.div(slot_ref[i, k], slot_count)
            place = lax.div(peer, half) * slot_count + lax.rem(slot_ref[i, k], slot_count)
            start = pl.multiple_of(place * block_size, block_size)
            out_ref[lax.rem(peer, half), pl.ds(start, block_size)] += part


def restrict_operator(operator_count, operator_slot, restrict_rows, fetch, operator_blocks, restrict_blocks):
    fine_rows, block_size, width = operator_blocks.shape
    slot_count, columns = fetch.shape
    wide = NCR * block_size
    rows = 2 * slot_count * block_size + EXTRA
    small = (operator_count, operator_slot, restrict_rows, fetch)
    return pl.pallas_call(
        restrict_kernel,
        out_shape=(
            jax.ShapeDtypeStruct((columns // 2, rows, wide), jnp.float32),
            jax.ShapeDtypeStruct((EXTRA, wide), jnp.float32),
        ),
        in_specs=[pl.BlockSpec(memory_space=pltpu.HBM)] * 6,
        out_specs=[pl.BlockSpec(memory_space=pltpu.VMEM)] * 2,
        scratch_shapes=[pltpu.SMEM(x.shape, x.dtype) for x in small]
        + [pltpu.VMEM(x.shape, x.dtype) for x in (restrict_blocks, operator_blocks)]
        + [pltpu.SemaphoreType.DMA((5,)), pltpu.SemaphoreType.DMA((fine_rows,))],
        cost_estimate=pl.CostEstimate(
            flops=6 * fine_rows * block_size * width * wide, bytes_accessed=4 << 20, transcendentals=0
        ),
        name="restrict_operator",
    )(*small, restrict_blocks, operator_blocks)


def combine_kernel(own_ref, restricted_ref, *rest, slot_count, fine_rows, entries):
    pieces, (out_ref, held_ref, table_ref, index_ref, sem) = rest[:-5], rest[-5:]
    half = restricted_ref.shape[0]
    rows = len(pieces) // 2
    block_size = out_ref.shape[1]
    columns = 2 * half
    used = 2 * slot_count * block_size
    held = fine_rows * block_size

    for near in range(half):
        table_ref[near : near + 1] = restricted_ref[near, used : used + 1].astype(jnp.int32)
    for i, piece in enumerate(pieces):
        first = half + entries * i
        table_ref[first : first + entries] = piece[held : held + entries].astype(jnp.int32)
    copy = pltpu.make_async_copy(table_ref, index_ref, sem)
    copy.start()
    for i, piece in enumerate(pieces):
        held_ref[i] = piece[:held]
    out_ref[...] = jnp.zeros_like(out_ref)
    copy.wait()

    def step(i, carry):
        near = lax.div(i, 2 * slot_count)
        place = lax.rem(i, 2 * slot_count)
        wanted = index_ref[near, place]
        inside = lax.rem(wanted, fine_rows)
        far = lax.div(place, slot_count) ^ own_ref[1]
        piece = far * rows + (lax.div(wanted, fine_rows * columns) ^ own_ref[0])
        block = held_ref[piece, pl.ds(pl.multiple_of(inside * block_size, block_size), block_size)]
        restricted = restricted_ref[near, pl.ds(pl.multiple_of(place * block_size, block_size), block_size)]
        product = transposed_dot(split3(block, "left"), split3(restricted, "right"))
        for m in range(entries):
            column = own_ref[2 + index_ref[half + entries * piece + m, inside]]
            out_ref[column] += product[m * block_size : (m + 1) * block_size]
        return carry

    lax.fori_loop(0, half * 2 * slot_count, step, 0, unroll=16)


def combine(own, restricted, pieces, coarse_all, slot_count, fine_rows, block_size):
    half, _, wide = restricted.shape
    width = pieces[0].shape[1]
    entries = width // block_size
    table_rows = -(-(half + entries * len(pieces)) // 8) * 8
    return pl.pallas_call(
        functools.partial(combine_kernel, slot_count=slot_count, fine_rows=fine_rows, entries=entries),
        out_shape=jax.ShapeDtypeStruct((coarse_all, block_size, wide), jnp.float32),
        in_specs=[pl.BlockSpec(memory_space=pltpu.SMEM)]
        + [pl.BlockSpec(memory_space=pltpu.VMEM)] * (1 + len(pieces)),
        out_specs=pl.BlockSpec(memory_space=pltpu.VMEM),
        scratch_shapes=[
            pltpu.VMEM((len(pieces), fine_rows * block_size, width), jnp.float32),
            pltpu.VMEM((table_rows, LANES), jnp.int32),
            pltpu.SMEM((table_rows, LANES), jnp.int32),
            pltpu.SemaphoreType.DMA,
        ],
        compiler_params=pltpu.CompilerParams(vmem_limit_bytes=VMEM_LIMIT),
        cost_estimate=pl.CostEstimate(flops=1 << 28, bytes_accessed=4 << 20, transcendentals=0),
        name="combine",
    )(own, restricted, *pieces)


def row_swap(x, bit):
    return lax.ppermute(x, "row", [(r, r ^ bit) for r in range(lax.axis_size("row"))])


def half_swap(x):
    return lax.ppermute(x, "half", [(0, 1), (1, 0)])


def spread_over_rows(blocks, rows):
    pieces = {0: blocks}
    bit = rows // 2
    while bit:
        for mask in list(pieces):
            pieces[mask ^ bit] = row_swap(pieces[mask], bit)
        bit //= 2
    return [pieces[mask] for mask in range(rows)]


def place_of_columns(columns):
    ahead = jnp.arange(columns, dtype=jnp.int32) ^ (lax.axis_index("half") * (columns // 2) + lax.axis_index("near"))
    place = jnp.zeros_like(ahead)
    low, high = 1, columns // 2
    while high:
        place = place + jnp.where(ahead & low != 0, high, 0)
        low, high = low * 2, high // 2
    return place


def add_over_columns(sums, half):
    bit = 1
    while bit < half:
        kept, sent = jnp.split(sums, 2)
        sums = kept + lax.ppermute(sent, "near", [(n, n ^ bit) for n in range(half)])
        bit *= 2
    kept, sent = jnp.split(sums, 2)
    return kept[0] + half_swap(sent)[0]


def local(
    operator_blocks,
    operator_count,
    operator_slot,
    fetch_lists,
    prolong_blocks,
    prolong_cols,
    restrict_blocks,
    restrict_rows,
):
    rows, half = lax.axis_size("row"), lax.axis_size("near")
    slot_count = fetch_lists.shape[3]
    fine_rows, block_size, width = prolong_blocks.shape
    fetch = fetch_lists.reshape(2 * half, slot_count).T
    own = jnp.stack([lax.axis_index("row"), lax.axis_index("half")])
    own = jnp.concatenate([own, place_of_columns(2 * half)])

    near_blocks = extend(prolong_cols.T, prolong_blocks.reshape(fine_rows * block_size, width))
    far_blocks = half_swap(near_blocks)
    restricted, mark = restrict_operator(
        operator_count, operator_slot, restrict_rows.T, fetch, operator_blocks, restrict_blocks
    )
    restricted = lax.all_to_all(restricted, "near", split_axis=0, concat_axis=0, tiled=True)
    far_blocks = hold_until(mark, far_blocks, HOLD_FLOPS)
    pieces = spread_over_rows(near_blocks, rows) + spread_over_rows(far_blocks, rows)
    sums = combine(own, restricted, pieces, NCR * rows, slot_count, fine_rows, block_size)
    return add_over_columns(sums, half).T


def solution(mesh):
    rows, columns = mesh.shape["row"], mesh.shape["col"]
    split = Mesh(mesh.devices.reshape(rows, 2, columns // 2), ("row", "half", "near"))
    flat = ("row", "half", "near")
    return jax.shard_map(
        local,
        mesh=split,
        in_specs=(
            P(flat, None, None),
            P(flat),
            P(flat, None),
            P("row", ("half", "near"), None, None),
            P(flat, None, None),
            P(flat, None),
            P(flat, None, None),
            P(flat, None),
        ),
        out_specs=P("row", ("half", "near")),
        check_vma=False,
    )
```

```python
import functools

import jax
import jax.numpy as jnp
from jax import lax
from jax.experimental import pallas as pl
from jax.experimental.pallas import tpu as pltpu
from jax.sharding import Mesh
from jax.sharding import PartitionSpec as P

NCR = 2
LANES = 128
EXTRA = 8
HOLD_FLOPS = 16 << 30
VMEM_LIMIT = 48 * 1024 * 1024


def split3(x, order):
    high = x.astype(jnp.bfloat16)
    low = (x - high.astype(jnp.float32)).astype(jnp.bfloat16)
    parts = {"left": (high, low, high), "right": (high, high, low)}[order]
    return jnp.concatenate(parts, axis=0)


def transposed_dot(left, right):
    return lax.dot_general(left, right, (((0,), (0,)), ((), ())), preferred_element_type=jnp.float32)


def append_kernel(mark_ref, far_columns_ref, own_columns_ref, blocks_ref, out_ref):
    used = blocks_ref.shape[0]
    entries, fine_rows = own_columns_ref.shape
    out_ref[:used] = blocks_ref[...]
    out_ref[used:] = jnp.zeros((EXTRA, out_ref.shape[1]), jnp.float32)
    out_ref[used : used + entries, :fine_rows] = far_columns_ref[...].astype(jnp.float32)
    out_ref[used + entries : used + 2 * entries, :fine_rows] = own_columns_ref[...].astype(jnp.float32)


def append_columns(mark, far_columns, own_columns, blocks):
    used, width = blocks.shape
    return pl.pallas_call(
        append_kernel,
        out_shape=jax.ShapeDtypeStruct((used + EXTRA, width), blocks.dtype),
        in_specs=[pl.BlockSpec(memory_space=pltpu.VMEM)] * 4,
        out_specs=pl.BlockSpec(memory_space=pltpu.VMEM),
        compiler_params=pltpu.CompilerParams(vmem_limit_bytes=VMEM_LIMIT),
        cost_estimate=pl.CostEstimate(flops=HOLD_FLOPS, bytes_accessed=HOLD_FLOPS >> 8, transcendentals=0),
        name="append_columns",
    )(mark, far_columns, own_columns, blocks)


def restrict_kernel(
    count_any, slot_any, rows_any, fetch_any, restrict_any, operator_any, out_ref, mark_ref,
    count_ref, slot_ref, rows_ref, fetch_ref, restrict_ref, operator_ref, sems, operator_sems,
):
    fine_rows, block_size, _ = operator_ref.shape
    entries = slot_ref.shape[1]
    slot_count, columns = fetch_ref.shape
    half = columns // 2
    used = 2 * slot_count * block_size
    wide = NCR * block_size

    pairs = [
        (count_any, count_ref), (slot_any, slot_ref), (rows_any, rows_ref),
        (fetch_any, fetch_ref), (restrict_any, restrict_ref),
    ]
    copies = [pltpu.make_async_copy(a, b, sems.at[i]) for i, (a, b) in enumerate(pairs)]
    operators = [
        pltpu.make_async_copy(operator_any.at[i], operator_ref.at[i], operator_sems.at[i]) for i in range(fine_rows)
    ]
    for copy in copies + operators:
        copy.start()

    lane = lax.broadcasted_iota(jnp.int32, (block_size, wide), 1)
    second = (lane >= block_size).astype(jnp.int32)
    short_lane = lax.broadcasted_iota(jnp.int32, (EXTRA, wide), 1)
    for near in range(half):
        out_ref[near, :used] = jnp.zeros((used, wide), jnp.float32)
    for copy in copies + operators:
        copy.wait()

    for near in range(half):
        value = jnp.zeros((EXTRA, wide), jnp.int32)
        for side in range(2):
            for s in range(slot_count):
                wanted = fetch_ref[s, side * half + near]
                value = jnp.where(short_lane == side * slot_count + s, wanted, value)
        out_ref[near, used:] = value.astype(jnp.float32)
    mark_ref[...] = out_ref[0, used:]

    for i in range(fine_rows):
        value = restrict_ref[i]
        swapped = pltpu.roll(value, block_size, 1)
        own_row = jnp.where(second == 0, rows_ref[0, i], rows_ref[1, i])
        other_row = jnp.where(second == 0, rows_ref[1, i], rows_ref[0, i])
        dense = jnp.where(own_row == second, value, 0.0) + jnp.where(other_row == second, swapped, 0.0)
        product = transposed_dot(split3(operator_ref[i], "left"), split3(dense, "right"))
        for k in range(entries):
            part = jnp.where(k < count_ref[i], product[k * block_size : (k + 1) * block_size], 0.0)
            peer = lax.div(slot_ref[i, k], slot_count)
            place = lax.div(peer, half) * slot_count + lax.rem(slot_ref[i, k], slot_count)
            start = pl.multiple_of(place * block_size, block_size)
            out_ref[lax.rem(peer, half), pl.ds(start, block_size)] += part


def restrict_operator(operator_count, operator_slot, restrict_rows, fetch, operator_blocks, restrict_blocks):
    fine_rows, block_size, width = operator_blocks.shape
    slot_count, columns = fetch.shape
    wide = NCR * block_size
    rows = 2 * slot_count * block_size + EXTRA
    small = (operator_count, operator_slot, restrict_rows, fetch)
    return pl.pallas_call(
        restrict_kernel,
        out_shape=(
            jax.ShapeDtypeStruct((columns // 2, rows, wide), jnp.float32),
            jax.ShapeDtypeStruct((EXTRA, wide), jnp.float32),
        ),
        in_specs=[pl.BlockSpec(memory_space=pltpu.HBM)] * 6,
        out_specs=[pl.BlockSpec(memory_space=pltpu.VMEM)] * 2,
        scratch_shapes=[pltpu.SMEM(x.shape, x.dtype) for x in small]
        + [pltpu.VMEM(x.shape, x.dtype) for x in (restrict_blocks, operator_blocks)]
        + [pltpu.SemaphoreType.DMA((5,)), pltpu.SemaphoreType.DMA((fine_rows,))],
        cost_estimate=pl.CostEstimate(
            flops=6 * fine_rows * block_size * width * wide, bytes_accessed=4 << 20, transcendentals=0
        ),
        name="restrict_operator",
    )(*small, restrict_blocks, operator_blocks)


def combine_kernel(own_ref, restricted_ref, *rest, slot_count, fine_rows, entries):
    pieces, (out_ref, held_ref, table_ref, index_ref, sem) = rest[:-5], rest[-5:]
    half = restricted_ref.shape[0]
    rows = len(pieces) // 2
    block_size = out_ref.shape[1]
    columns = 2 * half
    used = 2 * slot_count * block_size
    held = fine_rows * block_size

    for near in range(half):
        table_ref[near : near + 1] = restricted_ref[near, used : used + 1].astype(jnp.int32)
    for i, piece in enumerate(pieces[rows:]):
        for far in range(2):
            first = half + entries * (far * rows + i)
            row = held + entries * (1 - far)
            table_ref[first : first + entries] = piece[row : row + entries].astype(jnp.int32)
    copy = pltpu.make_async_copy(table_ref, index_ref, sem)
    copy.start()
    for i, piece in enumerate(pieces):
        held_ref[i] = piece[...] if i < rows else piece[:held]
    out_ref[...] = jnp.zeros_like(out_ref)
    copy.wait()

    def step(i, carry):
        near = lax.div(i, 2 * slot_count)
        place = lax.rem(i, 2 * slot_count)
        wanted = index_ref[near, place]
        inside = lax.rem(wanted, fine_rows)
        far = lax.div(place, slot_count) ^ own_ref[1]
        piece = far * rows + (lax.div(wanted, fine_rows * columns) ^ own_ref[0])
        block = held_ref[piece, pl.ds(pl.multiple_of(inside * block_size, block_size), block_size)]
        restricted = restricted_ref[near, pl.ds(pl.multiple_of(place * block_size, block_size), block_size)]
        product = transposed_dot(split3(block, "left"), split3(restricted, "right"))
        for m in range(entries):
            column = index_ref[half + entries * piece + m, inside]
            out_ref[column] += product[m * block_size : (m + 1) * block_size]
        return carry

    lax.fori_loop(0, half * 2 * slot_count, step, 0, unroll=16)


def combine(own, restricted, pieces, coarse_all, slot_count, fine_rows, block_size):
    half, _, wide = restricted.shape
    width = pieces[0].shape[1]
    entries = width // block_size
    table_rows = -(-(half + entries * len(pieces)) // 8) * 8
    return pl.pallas_call(
        functools.partial(combine_kernel, slot_count=slot_count, fine_rows=fine_rows, entries=entries),
        out_shape=jax.ShapeDtypeStruct((coarse_all, block_size, wide), jnp.float32),
        in_specs=[pl.BlockSpec(memory_space=pltpu.SMEM)]
        + [pl.BlockSpec(memory_space=pltpu.VMEM)] * (1 + len(pieces)),
        out_specs=pl.BlockSpec(memory_space=pltpu.VMEM),
        scratch_shapes=[
            pltpu.VMEM((len(pieces), fine_rows * block_size, width), jnp.float32),
            pltpu.VMEM((table_rows, LANES), jnp.int32),
            pltpu.SMEM((table_rows, LANES), jnp.int32),
            pltpu.SemaphoreType.DMA,
        ],
        compiler_params=pltpu.CompilerParams(vmem_limit_bytes=VMEM_LIMIT),
        cost_estimate=pl.CostEstimate(flops=1 << 28, bytes_accessed=4 << 20, transcendentals=0),
        name="combine",
    )(own, restricted, *pieces)


def add_kernel(parts_ref, out_ref):
    total = parts_ref[0]
    for i in range(1, parts_ref.shape[0]):
        total = total + parts_ref[i]
    out_ref[...] = total


def add_up(parts):
    return pl.pallas_call(
        add_kernel,
        out_shape=jax.ShapeDtypeStruct(parts.shape[1:], parts.dtype),
        in_specs=[pl.BlockSpec(memory_space=pltpu.VMEM)],
        out_specs=pl.BlockSpec(memory_space=pltpu.VMEM),
        compiler_params=pltpu.CompilerParams(vmem_limit_bytes=VMEM_LIMIT),
        name="add_up",
    )(parts)


def row_swap(x, bit):
    return lax.ppermute(x, "row", [(r, r ^ bit) for r in range(lax.axis_size("row"))])


def half_swap(x):
    return lax.ppermute(x, "half", [(0, 1), (1, 0)])


def spread_over_rows(blocks, rows):
    pieces = {0: blocks}
    bit = rows // 2
    while bit:
        for mask in list(pieces):
            pieces[mask ^ bit] = row_swap(pieces[mask], bit)
        bit //= 2
    return [pieces[mask] for mask in range(rows)]


def local(
    operator_blocks,
    operator_count,
    operator_slot,
    fetch_lists,
    prolong_blocks,
    prolong_cols,
    restrict_blocks,
    restrict_rows,
):
    rows, half = lax.axis_size("row"), lax.axis_size("near")
    slot_count = fetch_lists.shape[3]
    fine_rows, block_size, width = prolong_blocks.shape
    fetch = fetch_lists.reshape(2 * half, slot_count).T
    own = jnp.stack([lax.axis_index("row"), lax.axis_index("half")])
    own_columns = prolong_cols.T

    near_blocks = prolong_blocks.reshape(fine_rows * block_size, width)
    far_blocks = half_swap(near_blocks)
    far_columns = half_swap(own_columns)
    restricted, mark = restrict_operator(
        operator_count, operator_slot, restrict_rows.T, fetch, operator_blocks, restrict_blocks
    )
    restricted = lax.all_to_all(restricted, "near", split_axis=0, concat_axis=0, tiled=True)
    far_blocks = append_columns(mark, far_columns, own_columns, far_blocks)
    pieces = spread_over_rows(near_blocks, rows) + spread_over_rows(far_blocks, rows)
    sums = combine(own, restricted, pieces, NCR * rows, slot_count, fine_rows, block_size)
    parts = lax.all_to_all(sums, ("half", "near"), split_axis=0, concat_axis=0, tiled=True)
    return add_up(parts).T


def solution(mesh):
    rows, columns = mesh.shape["row"], mesh.shape["col"]
    split = Mesh(mesh.devices.reshape(rows, 2, columns // 2), ("row", "half", "near"))
    flat = ("row", "half", "near")
    return jax.shard_map(
        local,
        mesh=split,
        in_specs=(
            P(flat, None, None),
            P(flat),
            P(flat, None),
            P("row", ("half", "near"), None, None),
            P(flat, None, None),
            P(flat, None),
            P(flat, None, None),
            P(flat, None),
        ),
        out_specs=P("row", ("half", "near")),
        check_vma=False,
    )
```

```python
import functools

import jax
import jax.numpy as jnp
from jax import lax
from jax.experimental import pallas as pl
from jax.experimental.pallas import tpu as pltpu
from jax.sharding import Mesh
from jax.sharding import PartitionSpec as P

NCR = 2
LANES = 128
EXTRA = 8
HOLD_FLOPS = 16 << 30
VMEM_LIMIT = 48 * 1024 * 1024


def split3(x, order):
    high = x.astype(jnp.bfloat16)
    low = (x - high.astype(jnp.float32)).astype(jnp.bfloat16)
    parts = {"left": (high, low, high), "right": (high, high, low)}[order]
    return jnp.concatenate(parts, axis=0)


def transposed_dot(left, right):
    return lax.dot_general(left, right, (((0,), (0,)), ((), ())), preferred_element_type=jnp.float32)


def hold_kernel(mark_ref, blocks_ref, out_ref):
    out_ref[...] = blocks_ref[...]


def hold_until(mark, blocks):
    return pl.pallas_call(
        hold_kernel,
        out_shape=jax.ShapeDtypeStruct(blocks.shape, blocks.dtype),
        in_specs=[pl.BlockSpec(memory_space=pltpu.VMEM)] * 2,
        out_specs=pl.BlockSpec(memory_space=pltpu.VMEM),
        compiler_params=pltpu.CompilerParams(vmem_limit_bytes=VMEM_LIMIT),
        cost_estimate=pl.CostEstimate(flops=HOLD_FLOPS, bytes_accessed=HOLD_FLOPS >> 8, transcendentals=0),
        name="hold_until",
    )(mark, blocks)


def append_kernel(far_columns_ref, own_columns_ref, next_ref, blocks_ref, out_ref):
    used = blocks_ref.shape[0]
    entries, fine_rows = own_columns_ref.shape
    out_ref[:used] = blocks_ref[...]
    out_ref[used:] = jnp.zeros((EXTRA, out_ref.shape[1]), jnp.float32)
    out_ref[used : used + entries, :fine_rows] = far_columns_ref[...].astype(jnp.float32)
    out_ref[used + entries : used + 2 * entries, :fine_rows] = own_columns_ref[...].astype(jnp.float32)


def append_columns(far_columns, own_columns, next_blocks, blocks):
    used, width = blocks.shape
    return pl.pallas_call(
        append_kernel,
        out_shape=jax.ShapeDtypeStruct((used + EXTRA, width), blocks.dtype),
        in_specs=[pl.BlockSpec(memory_space=pltpu.VMEM)] * 4,
        out_specs=pl.BlockSpec(memory_space=pltpu.VMEM),
        compiler_params=pltpu.CompilerParams(vmem_limit_bytes=VMEM_LIMIT),
        cost_estimate=pl.CostEstimate(flops=0, bytes_accessed=1 << 19, transcendentals=0),
        name="append_columns",
    )(far_columns, own_columns, next_blocks, blocks)


def restrict_kernel(
    count_any, slot_any, rows_any, fetch_any, restrict_any, operator_any, columns_any, out_ref, mark_ref,
    count_ref, slot_ref, rows_ref, fetch_ref, restrict_ref, operator_ref, sems, operator_sems,
):
    fine_rows, block_size, _ = operator_ref.shape
    entries = slot_ref.shape[1]
    slot_count, columns = fetch_ref.shape
    half = columns // 2
    used = 2 * slot_count * block_size
    wide = NCR * block_size

    pairs = [
        (count_any, count_ref), (slot_any, slot_ref), (rows_any, rows_ref),
        (fetch_any, fetch_ref), (restrict_any, restrict_ref), (columns_any, mark_ref),
    ]
    copies = [pltpu.make_async_copy(a, b, sems.at[i]) for i, (a, b) in enumerate(pairs)]
    operators = [
        pltpu.make_async_copy(operator_any.at[i], operator_ref.at[i], operator_sems.at[i]) for i in range(fine_rows)
    ]
    for copy in copies + operators:
        copy.start()

    lane = lax.broadcasted_iota(jnp.int32, (block_size, wide), 1)
    second = (lane >= block_size).astype(jnp.int32)
    short_lane = lax.broadcasted_iota(jnp.int32, (EXTRA, wide), 1)
    for near in range(half):
        out_ref[near, :used] = jnp.zeros((used, wide), jnp.float32)
    for copy in copies + operators:
        copy.wait()

    for near in range(half):
        value = jnp.zeros((EXTRA, wide), jnp.int32)
        for side in range(2):
            for s in range(slot_count):
                wanted = fetch_ref[s, side * half + near]
                value = jnp.where(short_lane == side * slot_count + s, wanted, value)
        out_ref[near, used:] = value.astype(jnp.float32)

    for i in range(fine_rows):
        value = restrict_ref[i]
        swapped = pltpu.roll(value, block_size, 1)
        own_row = jnp.where(second == 0, rows_ref[0, i], rows_ref[1, i])
        other_row = jnp.where(second == 0, rows_ref[1, i], rows_ref[0, i])
        dense = jnp.where(own_row == second, value, 0.0) + jnp.where(other_row == second, swapped, 0.0)
        product = transposed_dot(split3(operator_ref[i], "left"), split3(dense, "right"))
        for k in range(entries):
            part = jnp.where(k < count_ref[i], product[k * block_size : (k + 1) * block_size], 0.0)
            peer = lax.div(slot_ref[i, k], slot_count)
            place = lax.div(peer, half) * slot_count + lax.rem(slot_ref[i, k], slot_count)
            start = pl.multiple_of(place * block_size, block_size)
            out_ref[lax.rem(peer, half), pl.ds(start, block_size)] += part


def restrict_operator(
    operator_count, operator_slot, restrict_rows, fetch, operator_blocks, restrict_blocks, prolong_columns
):
    fine_rows, block_size, width = operator_blocks.shape
    slot_count, columns = fetch.shape
    wide = NCR * block_size
    rows = 2 * slot_count * block_size + EXTRA
    small = (operator_count, operator_slot, restrict_rows, fetch)
    return pl.pallas_call(
        restrict_kernel,
        out_shape=(
            jax.ShapeDtypeStruct((columns // 2, rows, wide), jnp.float32),
            jax.ShapeDtypeStruct(prolong_columns.shape, prolong_columns.dtype),
        ),
        in_specs=[pl.BlockSpec(memory_space=pltpu.HBM)] * 7,
        out_specs=[pl.BlockSpec(memory_space=pltpu.VMEM)] * 2,
        scratch_shapes=[pltpu.SMEM(x.shape, x.dtype) for x in small]
        + [pltpu.VMEM(x.shape, x.dtype) for x in (restrict_blocks, operator_blocks)]
        + [pltpu.SemaphoreType.DMA((6,)), pltpu.SemaphoreType.DMA((fine_rows,))],
        cost_estimate=pl.CostEstimate(
            flops=6 * fine_rows * block_size * width * wide, bytes_accessed=4 << 20, transcendentals=0
        ),
        name="restrict_operator",
    )(*small, restrict_blocks, operator_blocks, prolong_columns)


def combine_kernel(own_ref, restricted_ref, *rest, slot_count, fine_rows, entries):
    pieces, (out_ref, held_ref, table_ref, index_ref, sem) = rest[:-5], rest[-5:]
    half = restricted_ref.shape[0]
    rows = len(pieces) // 2
    block_size = out_ref.shape[1]
    columns = 2 * half
    used = 2 * slot_count * block_size
    held = fine_rows * block_size

    for near in range(half):
        table_ref[near : near + 1] = restricted_ref[near, used : used + 1].astype(jnp.int32)
    for i, piece in enumerate(pieces[rows:]):
        for far in range(2):
            first = half + entries * (far * rows + i)
            row = held + entries * (1 - far)
            table_ref[first : first + entries] = piece[row : row + entries].astype(jnp.int32)
    copy = pltpu.make_async_copy(table_ref, index_ref, sem)
    copy.start()
    for i, piece in enumerate(pieces):
        held_ref[i] = piece[...] if i < rows else piece[:held]
    out_ref[...] = jnp.zeros_like(out_ref)
    copy.wait()

    def step(i, carry):
        near = lax.div(i, 2 * slot_count)
        place = lax.rem(i, 2 * slot_count)
        wanted = index_ref[near, place]
        inside = lax.rem(wanted, fine_rows)
        far = lax.div(place, slot_count) ^ own_ref[1]
        piece = far * rows + (lax.div(wanted, fine_rows * columns) ^ own_ref[0])
        block = held_ref[piece, pl.ds(pl.multiple_of(inside * block_size, block_size), block_size)]
        restricted = restricted_ref[near, pl.ds(pl.multiple_of(place * block_size, block_size), block_size)]
        product = transposed_dot(split3(block, "left"), split3(restricted, "right"))
        for m in range(entries):
            column = index_ref[half + entries * piece + m, inside]
            out_ref[column] += product[m * block_size : (m + 1) * block_size]
        return carry

    lax.fori_loop(0, half * 2 * slot_count, step, 0, unroll=16)


def combine(own, restricted, pieces, coarse_all, slot_count, fine_rows, block_size):
    half, _, wide = restricted.shape
    width = pieces[0].shape[1]
    entries = width // block_size
    table_rows = -(-(half + entries * len(pieces)) // 8) * 8
    return pl.pallas_call(
        functools.partial(combine_kernel, slot_count=slot_count, fine_rows=fine_rows, entries=entries),
        out_shape=jax.ShapeDtypeStruct((coarse_all, block_size, wide), jnp.float32),
        in_specs=[pl.BlockSpec(memory_space=pltpu.SMEM)]
        + [pl.BlockSpec(memory_space=pltpu.VMEM)] * (1 + len(pieces)),
        out_specs=pl.BlockSpec(memory_space=pltpu.VMEM),
        scratch_shapes=[
            pltpu.VMEM((len(pieces), fine_rows * block_size, width), jnp.float32),
            pltpu.VMEM((table_rows, LANES), jnp.int32),
            pltpu.SMEM((table_rows, LANES), jnp.int32),
            pltpu.SemaphoreType.DMA,
        ],
        compiler_params=pltpu.CompilerParams(vmem_limit_bytes=VMEM_LIMIT),
        cost_estimate=pl.CostEstimate(flops=1 << 28, bytes_accessed=4 << 20, transcendentals=0),
        name="combine",
    )(own, restricted, *pieces)


def add_kernel(parts_ref, out_ref):
    total = parts_ref[0]
    for i in range(1, parts_ref.shape[0]):
        total = total + parts_ref[i]
    out_ref[...] = total


def add_up(parts):
    return pl.pallas_call(
        add_kernel,
        out_shape=jax.ShapeDtypeStruct(parts.shape[1:], parts.dtype),
        in_specs=[pl.BlockSpec(memory_space=pltpu.VMEM)],
        out_specs=pl.BlockSpec(memory_space=pltpu.VMEM),
        compiler_params=pltpu.CompilerParams(vmem_limit_bytes=VMEM_LIMIT),
        name="add_up",
    )(parts)


def row_swap(x, bit):
    return lax.ppermute(x, "row", [(r, r ^ bit) for r in range(lax.axis_size("row"))])


def half_swap(x):
    return lax.ppermute(x, "half", [(0, 1), (1, 0)])


def spread_over_rows(blocks, rows):
    pieces = {0: blocks}
    bit = rows // 2
    while bit:
        for mask in list(pieces):
            pieces[mask ^ bit] = row_swap(pieces[mask], bit)
        bit //= 2
    return [pieces[mask] for mask in range(rows)]


def local(
    operator_blocks,
    operator_count,
    operator_slot,
    fetch_lists,
    prolong_blocks,
    prolong_cols,
    restrict_blocks,
    restrict_rows,
):
    rows, half = lax.axis_size("row"), lax.axis_size("near")
    slot_count = fetch_lists.shape[3]
    fine_rows, block_size, width = prolong_blocks.shape
    fetch = fetch_lists.reshape(2 * half, slot_count).T
    own = jnp.stack([lax.axis_index("row"), lax.axis_index("half")])

    near_blocks = prolong_blocks.reshape(fine_rows * block_size, width)
    far_blocks = half_swap(near_blocks)
    restricted, own_columns = restrict_operator(
        operator_count, operator_slot, restrict_rows.T, fetch, operator_blocks, restrict_blocks, prolong_cols.T
    )
    restricted = lax.all_to_all(restricted, "near", split_axis=0, concat_axis=0, tiled=True)
    far_columns = half_swap(own_columns)
    near_pieces = spread_over_rows(near_blocks, rows)
    far_blocks = hold_until(own_columns, far_blocks)
    far_blocks = append_columns(far_columns, own_columns, near_pieces[rows // 2], far_blocks)
    pieces = near_pieces + spread_over_rows(far_blocks, rows)
    sums = combine(own, restricted, pieces, NCR * rows, slot_count, fine_rows, block_size)
    parts = lax.all_to_all(sums, ("half", "near"), split_axis=0, concat_axis=0, tiled=True)
    return add_up(parts).T


def solution(mesh):
    rows, columns = mesh.shape["row"], mesh.shape["col"]
    split = Mesh(mesh.devices.reshape(rows, 2, columns // 2), ("row", "half", "near"))
    flat = ("row", "half", "near")
    return jax.shard_map(
        local,
        mesh=split,
        in_specs=(
            P(flat, None, None),
            P(flat),
            P(flat, None),
            P("row", ("half", "near"), None, None),
            P(flat, None, None),
            P(flat, None),
            P(flat, None, None),
            P(flat, None),
        ),
        out_specs=P("row", ("half", "near")),
        check_vma=False,
    )
```

```python
import functools

import jax
import jax.numpy as jnp
from jax import lax
from jax.experimental import pallas as pl
from jax.experimental.pallas import tpu as pltpu
from jax.sharding import Mesh
from jax.sharding import PartitionSpec as P

NCR = 2
LANES = 128
EXTRA = 8
HOLD_FLOPS = 16 << 30
VMEM_LIMIT = 48 * 1024 * 1024


def split3(x, order):
    high = x.astype(jnp.bfloat16)
    low = (x - high.astype(jnp.float32)).astype(jnp.bfloat16)
    parts = {"left": (high, low, high), "right": (high, high, low)}[order]
    return jnp.concatenate(parts, axis=0)


def transposed_dot(left, right):
    return lax.dot_general(left, right, (((0,), (0,)), ((), ())), preferred_element_type=jnp.float32)


def hold_kernel(mark_ref, blocks_ref, out_ref):
    out_ref[...] = blocks_ref[...]


def hold_until(mark, blocks, flops):
    return pl.pallas_call(
        hold_kernel,
        out_shape=jax.ShapeDtypeStruct(blocks.shape, blocks.dtype),
        in_specs=[pl.BlockSpec(memory_space=pltpu.VMEM)] * 2,
        out_specs=pl.BlockSpec(memory_space=pltpu.VMEM),
        compiler_params=pltpu.CompilerParams(vmem_limit_bytes=VMEM_LIMIT),
        cost_estimate=pl.CostEstimate(flops=flops, bytes_accessed=flops >> 8, transcendentals=0),
        name="hold_until",
    )(mark, blocks)


def restrict_kernel(
    count_any, slot_any, rows_any, fetch_any, restrict_any, operator_any, out_ref, mark_ref,
    count_ref, slot_ref, rows_ref, fetch_ref, restrict_ref, operator_ref, sems, operator_sems,
):
    fine_rows, block_size, _ = operator_ref.shape
    entries = slot_ref.shape[1]
    slot_count, columns = fetch_ref.shape
    half = columns // 2
    used = 2 * slot_count * block_size
    wide = NCR * block_size

    pairs = [
        (count_any, count_ref), (slot_any, slot_ref), (rows_any, rows_ref),
        (fetch_any, fetch_ref), (restrict_any, restrict_ref),
    ]
    copies = [pltpu.make_async_copy(a, b, sems.at[i]) for i, (a, b) in enumerate(pairs)]
    operators = [
        pltpu.make_async_copy(operator_any.at[i], operator_ref.at[i], operator_sems.at[i]) for i in range(fine_rows)
    ]
    for copy in copies + operators:
        copy.start()

    lane = lax.broadcasted_iota(jnp.int32, (block_size, wide), 1)
    second = (lane >= block_size).astype(jnp.int32)
    short_lane = lax.broadcasted_iota(jnp.int32, (EXTRA, wide), 1)
    for near in range(half):
        out_ref[near, :used] = jnp.zeros((used, wide), jnp.float32)
    for copy in copies + operators:
        copy.wait()

    for near in range(half):
        value = jnp.zeros((EXTRA, wide), jnp.int32)
        for side in range(2):
            for s in range(slot_count):
                wanted = fetch_ref[s, side * half + near]
                value = jnp.where(short_lane == side * slot_count + s, wanted, value)
        out_ref[near, used:] = value.astype(jnp.float32)
    mark_ref[...] = out_ref[0, used:]

    for i in range(fine_rows):
        value = restrict_ref[i]
        swapped = pltpu.roll(value, block_size, 1)
        own_row = jnp.where(second == 0, rows_ref[0, i], rows_ref[1, i])
        other_row = jnp.where(second == 0, rows_ref[1, i], rows_ref[0, i])
        dense = jnp.where(own_row == second, value, 0.0) + jnp.where(other_row == second, swapped, 0.0)
        product = transposed_dot(split3(operator_ref[i], "left"), split3(dense, "right"))
        for k in range(entries):
            part = jnp.where(k < count_ref[i], product[k * block_size : (k + 1) * block_size], 0.0)
            peer = lax.div(slot_ref[i, k], slot_count)
            place = lax.div(peer, half) * slot_count + lax.rem(slot_ref[i, k], slot_count)
            start = pl.multiple_of(place * block_size, block_size)
            out_ref[lax.rem(peer, half), pl.ds(start, block_size)] += part


def restrict_operator(operator_count, operator_slot, restrict_rows, fetch, operator_blocks, restrict_blocks):
    fine_rows, block_size, width = operator_blocks.shape
    slot_count, columns = fetch.shape
    wide = NCR * block_size
    rows = 2 * slot_count * block_size + EXTRA
    small = (operator_count, operator_slot, restrict_rows, fetch)
    return pl.pallas_call(
        restrict_kernel,
        out_shape=(
            jax.ShapeDtypeStruct((columns // 2, rows, wide), jnp.float32),
            jax.ShapeDtypeStruct((EXTRA, wide), jnp.float32),
        ),
        in_specs=[pl.BlockSpec(memory_space=pltpu.HBM)] * 6,
        out_specs=[pl.BlockSpec(memory_space=pltpu.VMEM)] * 2,
        scratch_shapes=[pltpu.SMEM(x.shape, x.dtype) for x in small]
        + [pltpu.VMEM(x.shape, x.dtype) for x in (restrict_blocks, operator_blocks)]
        + [pltpu.SemaphoreType.DMA((5,)), pltpu.SemaphoreType.DMA((fine_rows,))],
        cost_estimate=pl.CostEstimate(
            flops=6 * fine_rows * block_size * width * wide, bytes_accessed=4 << 20, transcendentals=0
        ),
        name="restrict_operator",
    )(*small, restrict_blocks, operator_blocks)


def combine_kernel(own_ref, restricted_ref, *rest, slot_count, fine_rows, entries):
    pieces, (out_ref, held_ref, table_ref, index_ref, sem) = rest[:-5], rest[-5:]
    half = restricted_ref.shape[0]
    rows = len(pieces) // 2
    block_size = out_ref.shape[1]
    columns = 2 * half
    used = 2 * slot_count * block_size
    held = fine_rows * block_size

    for near in range(half):
        table_ref[near : near + 1] = restricted_ref[near, used : used + 1].astype(jnp.int32)
    for i, piece in enumerate(pieces):
        first = half + entries * i
        table_ref[first : first + entries] = piece[held : held + entries].astype(jnp.int32)
    copy = pltpu.make_async_copy(table_ref, index_ref, sem)
    copy.start()
    for i, piece in enumerate(pieces):
        held_ref[i] = piece[:held]
    out_ref[...] = jnp.zeros_like(out_ref)
    copy.wait()

    def step(i, carry):
        near = lax.div(i, 2 * slot_count)
        place = lax.rem(i, 2 * slot_count)
        wanted = index_ref[near, place]
        inside = lax.rem(wanted, fine_rows)
        far = lax.div(place, slot_count) ^ own_ref[1]
        piece = far * rows + (lax.div(wanted, fine_rows * columns) ^ own_ref[0])
        block = held_ref[piece, pl.ds(pl.multiple_of(inside * block_size, block_size), block_size)]
        restricted = restricted_ref[near, pl.ds(pl.multiple_of(place * block_size, block_size), block_size)]
        product = transposed_dot(split3(block, "left"), split3(restricted, "right"))
        for m in range(entries):
            column = own_ref[2 + index_ref[half + entries * piece + m, inside]]
            out_ref[column] += product[m * block_size : (m + 1) * block_size]
        return carry

    lax.fori_loop(0, half * 2 * slot_count, step, 0, unroll=16)


def combine(own, restricted, pieces, coarse_all, slot_count, fine_rows, block_size):
    half, _, wide = restricted.shape
    width = pieces[0].shape[1]
    entries = width // block_size
    table_rows = -(-(half + entries * len(pieces)) // 8) * 8
    return pl.pallas_call(
        functools.partial(combine_kernel, slot_count=slot_count, fine_rows=fine_rows, entries=entries),
        out_shape=jax.ShapeDtypeStruct((coarse_all, block_size, wide), jnp.float32),
        in_specs=[pl.BlockSpec(memory_space=pltpu.SMEM)]
        + [pl.BlockSpec(memory_space=pltpu.VMEM)] * (1 + len(pieces)),
        out_specs=pl.BlockSpec(memory_space=pltpu.VMEM),
        scratch_shapes=[
            pltpu.VMEM((len(pieces), fine_rows * block_size, width), jnp.float32),
            pltpu.VMEM((table_rows, LANES), jnp.int32),
            pltpu.SMEM((table_rows, LANES), jnp.int32),
            pltpu.SemaphoreType.DMA,
        ],
        compiler_params=pltpu.CompilerParams(vmem_limit_bytes=VMEM_LIMIT),
        cost_estimate=pl.CostEstimate(flops=1 << 28, bytes_accessed=4 << 20, transcendentals=0),
        name="combine",
    )(own, restricted, *pieces)


def row_swap(x, bit):
    return lax.ppermute(x, "row", [(r, r ^ bit) for r in range(lax.axis_size("row"))])


def half_swap(x):
    return lax.ppermute(x, "half", [(0, 1), (1, 0)])


def spread_over_rows(blocks, rows):
    pieces = {0: blocks}
    bit = rows // 2
    while bit:
        for mask in list(pieces):
            pieces[mask ^ bit] = row_swap(pieces[mask], bit)
        bit //= 2
    return [pieces[mask] for mask in range(rows)]


def place_of_columns(half):
    own = lax.axis_index("half") * half + lax.axis_index("near")
    ahead = jnp.arange(2 * half, dtype=jnp.int32) ^ own
    return ahead % half * 2 + ahead // half


def add_over_columns(sums, half):
    total = sums[:2]
    for near in range(1, half):
        total = total + lax.ppermute(sums[2 * near : 2 * near + 2], "near", [(n, n ^ near) for n in range(half)])
    return total[0] + half_swap(total[1])


def with_columns(columns, blocks):
    entries, fine_rows = columns.shape
    used, width = blocks.shape
    rows = jnp.pad(columns.astype(blocks.dtype), ((0, EXTRA - entries), (0, width - fine_rows)))
    return jnp.concatenate([blocks, rows], axis=0)


def local(
    operator_blocks,
    operator_count,
    operator_slot,
    fetch_lists,
    prolong_blocks,
    prolong_cols,
    restrict_blocks,
    restrict_rows,
):
    rows, half = lax.axis_size("row"), lax.axis_size("near")
    slot_count = fetch_lists.shape[3]
    fine_rows, block_size, width = prolong_blocks.shape
    fetch = fetch_lists.reshape(2 * half, slot_count).T
    own = jnp.stack([lax.axis_index("row"), lax.axis_index("half")])
    own = jnp.concatenate([own, place_of_columns(half)])

    near_blocks = with_columns(prolong_cols.T, prolong_blocks.reshape(fine_rows * block_size, width))
    far_blocks = half_swap(near_blocks)
    restricted, mark = restrict_operator(
        operator_count, operator_slot, restrict_rows.T, fetch, operator_blocks, restrict_blocks
    )
    restricted = lax.all_to_all(restricted, "near", split_axis=0, concat_axis=0, tiled=True)
    far_blocks = hold_until(mark, far_blocks, HOLD_FLOPS)
    pieces = spread_over_rows(near_blocks, rows) + spread_over_rows(far_blocks, rows)
    sums = combine(own, restricted, pieces, NCR * rows, slot_count, fine_rows, block_size)
    return add_over_columns(sums, half).T


def solution(mesh):
    rows, columns = mesh.shape["row"], mesh.shape["col"]
    split = Mesh(mesh.devices.reshape(rows, 2, columns // 2), ("row", "half", "near"))
    flat = ("row", "half", "near")
    return jax.shard_map(
        local,
        mesh=split,
        in_specs=(
            P(flat, None, None),
            P(flat),
            P(flat, None),
            P("row", ("half", "near"), None, None),
            P(flat, None, None),
            P(flat, None),
            P(flat, None, None),
            P(flat, None),
        ),
        out_specs=P("row", ("half", "near")),
        check_vma=False,
    )
```

```python
import functools

import jax
import jax.numpy as jnp
from jax import lax
from jax.experimental import pallas as pl
from jax.experimental.pallas import tpu as pltpu
from jax.sharding import Mesh
from jax.sharding import PartitionSpec as P

NCR = 2
LANES = 128
EXTRA = 8
HOLD_FLOPS = 16 << 30
VMEM_LIMIT = 48 * 1024 * 1024


def split3(x, order):
    high = x.astype(jnp.bfloat16)
    low = (x - high.astype(jnp.float32)).astype(jnp.bfloat16)
    parts = {"left": (high, low, high), "right": (high, high, low)}[order]
    return jnp.concatenate(parts, axis=0)


def transposed_dot(left, right):
    return lax.dot_general(left, right, (((0,), (0,)), ((), ())), preferred_element_type=jnp.float32)


def hold_kernel(mark_ref, blocks_ref, out_ref):
    out_ref[...] = blocks_ref[...]


def hold_until(mark, blocks, flops):
    return pl.pallas_call(
        hold_kernel,
        out_shape=jax.ShapeDtypeStruct(blocks.shape, blocks.dtype),
        in_specs=[pl.BlockSpec(memory_space=pltpu.VMEM)] * 2,
        out_specs=pl.BlockSpec(memory_space=pltpu.VMEM),
        compiler_params=pltpu.CompilerParams(vmem_limit_bytes=VMEM_LIMIT),
        cost_estimate=pl.CostEstimate(flops=flops, bytes_accessed=flops >> 8, transcendentals=0),
        name="hold_until",
    )(mark, blocks)


def restrict_kernel(
    count_any, slot_any, rows_any, fetch_any, restrict_ref, operator_ref, out_ref, mark_ref,
    count_ref, slot_ref, rows_ref, fetch_ref, sems,
):
    fine_rows, block_size, _ = operator_ref.shape
    entries = slot_ref.shape[1]
    slot_count, columns = fetch_ref.shape
    half = columns // 2
    used = 2 * slot_count * block_size
    wide = NCR * block_size

    pairs = [(count_any, count_ref), (slot_any, slot_ref), (rows_any, rows_ref), (fetch_any, fetch_ref)]
    copies = [pltpu.make_async_copy(a, b, sems.at[i]) for i, (a, b) in enumerate(pairs)]
    for copy in copies:
        copy.start()

    lane = lax.broadcasted_iota(jnp.int32, (block_size, wide), 1)
    second = (lane >= block_size).astype(jnp.int32)
    short_lane = lax.broadcasted_iota(jnp.int32, (EXTRA, wide), 1)
    for near in range(half):
        out_ref[near, :used] = jnp.zeros((used, wide), jnp.float32)
    for copy in copies:
        copy.wait()

    for near in range(half):
        value = jnp.zeros((EXTRA, wide), jnp.int32)
        for side in range(2):
            for s in range(slot_count):
                wanted = fetch_ref[s, side * half + near]
                value = jnp.where(short_lane == side * slot_count + s, wanted, value)
        out_ref[near, used:] = value.astype(jnp.float32)
    mark_ref[...] = out_ref[0, used:]

    for i in range(fine_rows):
        value = restrict_ref[i]
        swapped = pltpu.roll(value, block_size, 1)
        own_row = jnp.where(second == 0, rows_ref[0, i], rows_ref[1, i])
        other_row = jnp.where(second == 0, rows_ref[1, i], rows_ref[0, i])
        dense = jnp.where(own_row == second, value, 0.0) + jnp.where(other_row == second, swapped, 0.0)
        product = transposed_dot(split3(operator_ref[i], "left"), split3(dense, "right"))
        for k in range(entries):
            part = jnp.where(k < count_ref[i], product[k * block_size : (k + 1) * block_size], 0.0)
            peer = lax.div(slot_ref[i, k], slot_count)
            place = lax.div(peer, half) * slot_count + lax.rem(slot_ref[i, k], slot_count)
            start = pl.multiple_of(place * block_size, block_size)
            out_ref[lax.rem(peer, half), pl.ds(start, block_size)] += part


def restrict_operator(operator_count, operator_slot, restrict_rows, fetch, operator_blocks, restrict_blocks):
    fine_rows, block_size, width = operator_blocks.shape
    slot_count, columns = fetch.shape
    wide = NCR * block_size
    rows = 2 * slot_count * block_size + EXTRA
    small = (operator_count, operator_slot, restrict_rows, fetch)
    return pl.pallas_call(
        restrict_kernel,
        out_shape=(
            jax.ShapeDtypeStruct((columns // 2, rows, wide), jnp.float32),
            jax.ShapeDtypeStruct((EXTRA, wide), jnp.float32),
        ),
        in_specs=[pl.BlockSpec(memory_space=pltpu.HBM)] * 4 + [pl.BlockSpec(memory_space=pltpu.VMEM)] * 2,
        out_specs=[pl.BlockSpec(memory_space=pltpu.VMEM)] * 2,
        scratch_shapes=[pltpu.SMEM(x.shape, x.dtype) for x in small] + [pltpu.SemaphoreType.DMA((4,))],
        compiler_params=pltpu.CompilerParams(vmem_limit_bytes=VMEM_LIMIT),
        cost_estimate=pl.CostEstimate(
            flops=6 * fine_rows * block_size * width * wide, bytes_accessed=4 << 20, transcendentals=0
        ),
        name="restrict_operator",
    )(*small, restrict_blocks, operator_blocks)


def combine_kernel(own_ref, restricted_ref, *rest, slot_count, fine_rows, entries):
    pieces, (out_ref, held_ref, table_ref, index_ref, sem) = rest[:-5], rest[-5:]
    half = restricted_ref.shape[0]
    rows = len(pieces) // 2
    block_size = out_ref.shape[1]
    columns = 2 * half
    used = 2 * slot_count * block_size
    held = fine_rows * block_size

    for near in range(half):
        table_ref[near : near + 1] = restricted_ref[near, used : used + 1].astype(jnp.int32)
    for i, piece in enumerate(pieces):
        first = half + entries * i
        table_ref[first : first + entries] = piece[held : held + entries].astype(jnp.int32)
    copy = pltpu.make_async_copy(table_ref, index_ref, sem)
    copy.start()
    for i, piece in enumerate(pieces):
        held_ref[i] = piece[:held]
    out_ref[...] = jnp.zeros_like(out_ref)
    copy.wait()

    def step(i, carry):
        near = lax.div(i, 2 * slot_count)
        place = lax.rem(i, 2 * slot_count)
        wanted = index_ref[near, place]
        inside = lax.rem(wanted, fine_rows)
        far = lax.div(place, slot_count) ^ own_ref[1]
        piece = far * rows + (lax.div(wanted, fine_rows * columns) ^ own_ref[0])
        block = held_ref[piece, pl.ds(pl.multiple_of(inside * block_size, block_size), block_size)]
        restricted = restricted_ref[near, pl.ds(pl.multiple_of(place * block_size, block_size), block_size)]
        product = transposed_dot(split3(block, "left"), split3(restricted, "right"))
        for m in range(entries):
            column = own_ref[2 + index_ref[half + entries * piece + m, inside]]
            out_ref[column] += product[m * block_size : (m + 1) * block_size]
        return carry

    lax.fori_loop(0, half * 2 * slot_count, step, 0, unroll=16)


def combine(own, restricted, pieces, coarse_all, slot_count, fine_rows, block_size):
    half, _, wide = restricted.shape
    width = pieces[0].shape[1]
    entries = width // block_size
    table_rows = -(-(half + entries * len(pieces)) // 8) * 8
    return pl.pallas_call(
        functools.partial(combine_kernel, slot_count=slot_count, fine_rows=fine_rows, entries=entries),
        out_shape=jax.ShapeDtypeStruct((coarse_all, block_size, wide), jnp.float32),
        in_specs=[pl.BlockSpec(memory_space=pltpu.SMEM)]
        + [pl.BlockSpec(memory_space=pltpu.VMEM)] * (1 + len(pieces)),
        out_specs=pl.BlockSpec(memory_space=pltpu.VMEM),
        scratch_shapes=[
            pltpu.VMEM((len(pieces), fine_rows * block_size, width), jnp.float32),
            pltpu.VMEM((table_rows, LANES), jnp.int32),
            pltpu.SMEM((table_rows, LANES), jnp.int32),
            pltpu.SemaphoreType.DMA,
        ],
        compiler_params=pltpu.CompilerParams(vmem_limit_bytes=VMEM_LIMIT),
        cost_estimate=pl.CostEstimate(flops=1 << 28, bytes_accessed=4 << 20, transcendentals=0),
        name="combine",
    )(own, restricted, *pieces)


def row_swap(x, bit):
    return lax.ppermute(x, "row", [(r, r ^ bit) for r in range(lax.axis_size("row"))])


def half_swap(x):
    return lax.ppermute(x, "half", [(0, 1), (1, 0)])


def spread_over_rows(blocks, rows):
    pieces = {0: blocks}
    bit = rows // 2
    while bit:
        for mask in list(pieces):
            pieces[mask ^ bit] = row_swap(pieces[mask], bit)
        bit //= 2
    return [pieces[mask] for mask in range(rows)]


def place_of_columns(half):
    own = lax.axis_index("half") * half + lax.axis_index("near")
    ahead = jnp.arange(2 * half, dtype=jnp.int32) ^ own
    return ahead % half * 2 + ahead // half


def add_over_columns(sums, half):
    total = sums[:2]
    for near in range(1, half):
        total = total + lax.ppermute(sums[2 * near : 2 * near + 2], "near", [(n, n ^ near) for n in range(half)])
    return total[0] + half_swap(total[1])


def with_columns(columns, blocks):
    entries, fine_rows = columns.shape
    used, width = blocks.shape
    rows = jnp.pad(columns.astype(blocks.dtype), ((0, EXTRA - entries), (0, width - fine_rows)))
    return jnp.concatenate([blocks, rows], axis=0)


def local(
    operator_blocks,
    operator_count,
    operator_slot,
    fetch_lists,
    prolong_blocks,
    prolong_cols,
    restrict_blocks,
    restrict_rows,
):
    rows, half = lax.axis_size("row"), lax.axis_size("near")
    slot_count = fetch_lists.shape[3]
    fine_rows, block_size, width = prolong_blocks.shape
    fetch = fetch_lists.reshape(2 * half, slot_count).T
    own = jnp.stack([lax.axis_index("row"), lax.axis_index("half")])
    own = jnp.concatenate([own, place_of_columns(half)])

    near_blocks = with_columns(prolong_cols.T, prolong_blocks.reshape(fine_rows * block_size, width))
    far_blocks = half_swap(near_blocks)
    restricted, mark = restrict_operator(
        operator_count, operator_slot, restrict_rows.T, fetch, operator_blocks, restrict_blocks
    )
    restricted = lax.all_to_all(restricted, "near", split_axis=0, concat_axis=0, tiled=True)
    far_blocks = hold_until(mark, far_blocks, HOLD_FLOPS)
    pieces = spread_over_rows(near_blocks, rows) + spread_over_rows(far_blocks, rows)
    sums = combine(own, restricted, pieces, NCR * rows, slot_count, fine_rows, block_size)
    return add_over_columns(sums, half).T


def solution(mesh):
    rows, columns = mesh.shape["row"], mesh.shape["col"]
    split = Mesh(mesh.devices.reshape(rows, 2, columns // 2), ("row", "half", "near"))
    flat = ("row", "half", "near")
    return jax.shard_map(
        local,
        mesh=split,
        in_specs=(
            P(flat, None, None),
            P(flat),
            P(flat, None),
            P("row", ("half", "near"), None, None),
            P(flat, None, None),
            P(flat, None),
            P(flat, None, None),
            P(flat, None),
        ),
        out_specs=P("row", ("half", "near")),
        check_vma=False,
    )
```

```python
import functools

import jax
import jax.numpy as jnp
from jax import lax
from jax.experimental import pallas as pl
from jax.experimental.pallas import tpu as pltpu
from jax.sharding import Mesh
from jax.sharding import PartitionSpec as P

NCR = 2
LANES = 128
EXTRA = 8
HOLD_FLOPS = 16 << 30
VMEM_LIMIT = 48 * 1024 * 1024


def split3(x, order):
    high = x.astype(jnp.bfloat16)
    low = (x - high.astype(jnp.float32)).astype(jnp.bfloat16)
    parts = {"left": (high, low, high), "right": (high, high, low)}[order]
    return jnp.concatenate(parts, axis=0)


def transposed_dot(left, right):
    return lax.dot_general(left, right, (((0,), (0,)), ((), ())), preferred_element_type=jnp.float32)


def append_kernel(mark_ref, next_ref, far_columns_ref, own_columns_ref, blocks_ref, out_ref):
    used = blocks_ref.shape[0]
    entries, fine_rows = own_columns_ref.shape
    out_ref[:used] = blocks_ref[...]
    out_ref[used:] = jnp.zeros((EXTRA, out_ref.shape[1]), jnp.float32)
    out_ref[used : used + entries, :fine_rows] = far_columns_ref[...].astype(jnp.float32)
    out_ref[used + entries : used + 2 * entries, :fine_rows] = own_columns_ref[...].astype(jnp.float32)


def append_columns(mark, next_blocks, far_columns, own_columns, blocks):
    used, width = blocks.shape
    return pl.pallas_call(
        append_kernel,
        out_shape=jax.ShapeDtypeStruct((used + EXTRA, width), blocks.dtype),
        in_specs=[pl.BlockSpec(memory_space=pltpu.VMEM)] * 5,
        out_specs=pl.BlockSpec(memory_space=pltpu.VMEM),
        compiler_params=pltpu.CompilerParams(vmem_limit_bytes=VMEM_LIMIT),
        cost_estimate=pl.CostEstimate(flops=HOLD_FLOPS, bytes_accessed=HOLD_FLOPS >> 8, transcendentals=0),
        name="append_columns",
    )(mark, next_blocks, far_columns, own_columns, blocks)


def restrict_kernel(
    count_any, slot_any, rows_any, fetch_any, restrict_any, operator_any, out_ref, mark_ref,
    count_ref, slot_ref, rows_ref, fetch_ref, restrict_ref, operator_ref, sems, operator_sems,
):
    fine_rows, block_size, _ = operator_ref.shape
    entries = slot_ref.shape[1]
    slot_count, columns = fetch_ref.shape
    half = columns // 2
    used = 2 * slot_count * block_size
    wide = NCR * block_size

    pairs = [
        (count_any, count_ref), (slot_any, slot_ref), (rows_any, rows_ref),
        (fetch_any, fetch_ref), (restrict_any, restrict_ref),
    ]
    copies = [pltpu.make_async_copy(a, b, sems.at[i]) for i, (a, b) in enumerate(pairs)]
    operators = [
        pltpu.make_async_copy(operator_any.at[i], operator_ref.at[i], operator_sems.at[i]) for i in range(fine_rows)
    ]
    for copy in copies + operators:
        copy.start()

    lane = lax.broadcasted_iota(jnp.int32, (block_size, wide), 1)
    second = (lane >= block_size).astype(jnp.int32)
    short_lane = lax.broadcasted_iota(jnp.int32, (EXTRA, wide), 1)
    for near in range(half):
        out_ref[near, :used] = jnp.zeros((used, wide), jnp.float32)
    for copy in copies + operators:
        copy.wait()

    for near in range(half):
        value = jnp.zeros((EXTRA, wide), jnp.int32)
        for side in range(2):
            for s in range(slot_count):
                wanted = fetch_ref[s, side * half + near]
                value = jnp.where(short_lane == side * slot_count + s, wanted, value)
        out_ref[near, used:] = value.astype(jnp.float32)
    mark_ref[...] = out_ref[0, used:]

    for i in range(fine_rows):
        value = restrict_ref[i]
        swapped = pltpu.roll(value, block_size, 1)
        own_row = jnp.where(second == 0, rows_ref[0, i], rows_ref[1, i])
        other_row = jnp.where(second == 0, rows_ref[1, i], rows_ref[0, i])
        dense = jnp.where(own_row == second, value, 0.0) + jnp.where(other_row == second, swapped, 0.0)
        product = transposed_dot(split3(operator_ref[i], "left"), split3(dense, "right"))
        for k in range(entries):
            part = jnp.where(k < count_ref[i], product[k * block_size : (k + 1) * block_size], 0.0)
            peer = lax.div(slot_ref[i, k], slot_count)
            place = lax.div(peer, half) * slot_count + lax.rem(slot_ref[i, k], slot_count)
            start = pl.multiple_of(place * block_size, block_size)
            out_ref[lax.rem(peer, half), pl.ds(start, block_size)] += part


def restrict_operator(operator_count, operator_slot, restrict_rows, fetch, operator_blocks, restrict_blocks):
    fine_rows, block_size, width = operator_blocks.shape
    slot_count, columns = fetch.shape
    wide = NCR * block_size
    rows = 2 * slot_count * block_size + EXTRA
    small = (operator_count, operator_slot, restrict_rows, fetch)
    return pl.pallas_call(
        restrict_kernel,
        out_shape=(
            jax.ShapeDtypeStruct((columns // 2, rows, wide), jnp.float32),
            jax.ShapeDtypeStruct((EXTRA, wide), jnp.float32),
        ),
        in_specs=[pl.BlockSpec(memory_space=pltpu.HBM)] * 6,
        out_specs=[pl.BlockSpec(memory_space=pltpu.VMEM)] * 2,
        scratch_shapes=[pltpu.SMEM(x.shape, x.dtype) for x in small]
        + [pltpu.VMEM(x.shape, x.dtype) for x in (restrict_blocks, operator_blocks)]
        + [pltpu.SemaphoreType.DMA((5,)), pltpu.SemaphoreType.DMA((fine_rows,))],
        cost_estimate=pl.CostEstimate(
            flops=6 * fine_rows * block_size * width * wide, bytes_accessed=4 << 20, transcendentals=0
        ),
        name="restrict_operator",
    )(*small, restrict_blocks, operator_blocks)


def combine_kernel(own_ref, restricted_ref, *rest, slot_count, fine_rows, entries):
    pieces, (out_ref, held_ref, table_ref, index_ref, sem) = rest[:-9], rest[-9:-4]
    sums = rest[-4:]
    half = restricted_ref.shape[0]
    rows = len(pieces) // 2
    block_size = out_ref.shape[1]
    columns = 2 * half
    used = 2 * slot_count * block_size
    held = fine_rows * block_size

    for near in range(half):
        table_ref[near : near + 1] = restricted_ref[near, used : used + 1].astype(jnp.int32)
    for i, piece in enumerate(pieces[rows:]):
        for far in range(2):
            first = half + entries * (far * rows + i)
            row = held + entries * (1 - far)
            table_ref[first : first + entries] = piece[row : row + entries].astype(jnp.int32)
    copy = pltpu.make_async_copy(table_ref, index_ref, sem)
    copy.start()
    for i, piece in enumerate(pieces):
        held_ref[i] = piece[...] if i < rows else piece[:held]
    for total in sums:
        total[...] = jnp.zeros_like(total)
    copy.wait()

    def add_product(i, total):
        near = lax.div(i, 2 * slot_count)
        place = lax.rem(i, 2 * slot_count)
        wanted = index_ref[near, place]
        inside = lax.rem(wanted, fine_rows)
        far = lax.div(place, slot_count) ^ own_ref[1]
        piece = far * rows + (lax.div(wanted, fine_rows * columns) ^ own_ref[0])
        block = held_ref[piece, pl.ds(pl.multiple_of(inside * block_size, block_size), block_size)]
        restricted = restricted_ref[near, pl.ds(pl.multiple_of(place * block_size, block_size), block_size)]
        product = transposed_dot(split3(block, "left"), split3(restricted, "right"))
        for m in range(entries):
            column = own_ref[2 + index_ref[half + entries * piece + m, inside]]
            total[m % len(total)][column] += product[m * block_size : (m + 1) * block_size]

    def step(i, carry):
        add_product(2 * i, sums[:2])
        add_product(2 * i + 1, sums[2:])
        return carry

    lax.fori_loop(0, half * slot_count, step, 0, unroll=8)
    out_ref[...] = (sums[0][...] + sums[1][...]) + (sums[2][...] + sums[3][...])


def combine(own, restricted, pieces, coarse_all, slot_count, fine_rows, block_size):
    half, _, wide = restricted.shape
    width = pieces[0].shape[1]
    entries = width // block_size
    table_rows = -(-(half + entries * len(pieces)) // 8) * 8
    return pl.pallas_call(
        functools.partial(combine_kernel, slot_count=slot_count, fine_rows=fine_rows, entries=entries),
        out_shape=jax.ShapeDtypeStruct((coarse_all, block_size, wide), jnp.float32),
        in_specs=[pl.BlockSpec(memory_space=pltpu.SMEM)]
        + [pl.BlockSpec(memory_space=pltpu.VMEM)] * (1 + len(pieces)),
        out_specs=pl.BlockSpec(memory_space=pltpu.VMEM),
        scratch_shapes=[
            pltpu.VMEM((len(pieces), fine_rows * block_size, width), jnp.float32),
            pltpu.VMEM((table_rows, LANES), jnp.int32),
            pltpu.SMEM((table_rows, LANES), jnp.int32),
            pltpu.SemaphoreType.DMA,
        ]
        + [pltpu.VMEM((coarse_all, block_size, wide), jnp.float32)] * 4,
        compiler_params=pltpu.CompilerParams(vmem_limit_bytes=VMEM_LIMIT),
        cost_estimate=pl.CostEstimate(flops=1 << 28, bytes_accessed=4 << 20, transcendentals=0),
        name="combine",
    )(own, restricted, *pieces)


def row_swap(x, bit):
    return lax.ppermute(x, "row", [(r, r ^ bit) for r in range(lax.axis_size("row"))])


def half_swap(x):
    return lax.ppermute(x, "half", [(0, 1), (1, 0)])


def spread_over_rows(blocks, rows):
    pieces = {0: blocks}
    bit = rows // 2
    while bit:
        for mask in list(pieces):
            pieces[mask ^ bit] = row_swap(pieces[mask], bit)
        bit //= 2
    return [pieces[mask] for mask in range(rows)]


def place_of_columns(half):
    own = lax.axis_index("half") * half + lax.axis_index("near")
    ahead = jnp.arange(2 * half, dtype=jnp.int32) ^ own
    return ahead % half * 2 + ahead // half


def add_over_columns(sums, half):
    total = sums[:2]
    for near in range(1, half):
        total = total + lax.ppermute(sums[2 * near : 2 * near + 2], "near", [(n, n ^ near) for n in range(half)])
    return total[0] + half_swap(total[1])


def local(
    operator_blocks,
    operator_count,
    operator_slot,
    fetch_lists,
    prolong_blocks,
    prolong_cols,
    restrict_blocks,
    restrict_rows,
):
    rows, half = lax.axis_size("row"), lax.axis_size("near")
    slot_count = fetch_lists.shape[3]
    fine_rows, block_size, width = prolong_blocks.shape
    fetch = fetch_lists.reshape(2 * half, slot_count).T
    own = jnp.stack([lax.axis_index("row"), lax.axis_index("half")])
    own = jnp.concatenate([own, place_of_columns(half)])

    own_columns = prolong_cols.T
    near_blocks = prolong_blocks.reshape(fine_rows * block_size, width)
    far_blocks = half_swap(near_blocks)
    far_columns = half_swap(own_columns)
    restricted, mark = restrict_operator(
        operator_count, operator_slot, restrict_rows.T, fetch, operator_blocks, restrict_blocks
    )
    restricted = lax.all_to_all(restricted, "near", split_axis=0, concat_axis=0, tiled=True)
    near_pieces = spread_over_rows(near_blocks, rows)
    far_blocks = append_columns(mark, near_pieces[rows // 2], far_columns, own_columns, far_blocks)
    pieces = near_pieces + spread_over_rows(far_blocks, rows)
    sums = combine(own, restricted, pieces, NCR * rows, slot_count, fine_rows, block_size)
    return add_over_columns(sums, half).T


def solution(mesh):
    rows, columns = mesh.shape["row"], mesh.shape["col"]
    split = Mesh(mesh.devices.reshape(rows, 2, columns // 2), ("row", "half", "near"))
    flat = ("row", "half", "near")
    return jax.shard_map(
        local,
        mesh=split,
        in_specs=(
            P(flat, None, None),
            P(flat),
            P(flat, None),
            P("row", ("half", "near"), None, None),
            P(flat, None, None),
            P(flat, None),
            P(flat, None, None),
            P(flat, None),
        ),
        out_specs=P("row", ("half", "near")),
        check_vma=False,
    )
```

```python
import functools

import jax
import jax.numpy as jnp
from jax import lax
from jax.experimental import pallas as pl
from jax.experimental.pallas import tpu as pltpu
from jax.sharding import Mesh
from jax.sharding import PartitionSpec as P

NCR = 2
LANES = 128
EXTRA = 8
HOLD_FLOPS = 16 << 30
VMEM_LIMIT = 48 * 1024 * 1024


def halves(x):
    high = x.astype(jnp.bfloat16)
    return high, (x - high.astype(jnp.float32)).astype(jnp.bfloat16)


def transposed_product(left, right):
    tall = jnp.concatenate(halves(left), axis=0)
    wide = jnp.concatenate(halves(right), axis=1)
    wide = jnp.concatenate([wide, wide], axis=0)
    both = lax.dot_general(tall, wide, (((0,), (0,)), ((), ())), preferred_element_type=jnp.float32)
    width = right.shape[1]
    return both[:, :width] + both[:, width:]


def append_kernel(next_ref, far_columns_ref, own_columns_ref, blocks_ref, out_ref):
    used = blocks_ref.shape[0]
    entries, fine_rows = own_columns_ref.shape
    out_ref[:used] = blocks_ref[...]
    out_ref[used:] = jnp.zeros((EXTRA, out_ref.shape[1]), jnp.float32)
    out_ref[used : used + entries, :fine_rows] = far_columns_ref[...].astype(jnp.float32)
    out_ref[used + entries : used + 2 * entries, :fine_rows] = own_columns_ref[...].astype(jnp.float32)


def append_columns(next_blocks, far_columns, own_columns, blocks):
    used, width = blocks.shape
    return pl.pallas_call(
        append_kernel,
        out_shape=jax.ShapeDtypeStruct((used + EXTRA, width), blocks.dtype),
        in_specs=[pl.BlockSpec(memory_space=pltpu.VMEM)] * 4,
        out_specs=pl.BlockSpec(memory_space=pltpu.VMEM),
        compiler_params=pltpu.CompilerParams(vmem_limit_bytes=VMEM_LIMIT),
        cost_estimate=pl.CostEstimate(flops=HOLD_FLOPS, bytes_accessed=HOLD_FLOPS >> 8, transcendentals=0),
        name="append_columns",
    )(next_blocks, far_columns, own_columns, blocks)


def restrict_kernel(
    count_any, slot_any, rows_any, fetch_any, restrict_any, operator_any, columns_any, blocks_any,
    out_ref, own_columns_ref, own_blocks_ref,
    count_ref, slot_ref, rows_ref, fetch_ref, restrict_ref, operator_ref, sems, operator_sems,
):
    fine_rows, block_size, _ = operator_ref.shape
    entries = slot_ref.shape[1]
    slot_count, columns = fetch_ref.shape
    half = columns // 2
    used = 2 * slot_count * block_size
    wide = NCR * block_size

    pairs = [
        (count_any, count_ref), (slot_any, slot_ref), (rows_any, rows_ref),
        (fetch_any, fetch_ref), (restrict_any, restrict_ref),
        (columns_any, own_columns_ref), (blocks_any, own_blocks_ref),
    ]
    copies = [pltpu.make_async_copy(a, b, sems.at[i]) for i, (a, b) in enumerate(pairs)]
    operators = [
        pltpu.make_async_copy(operator_any.at[i], operator_ref.at[i], operator_sems.at[i]) for i in range(fine_rows)
    ]
    for copy in copies + operators:
        copy.start()

    lane = lax.broadcasted_iota(jnp.int32, (block_size, wide), 1)
    second = (lane >= block_size).astype(jnp.int32)
    short_lane = lax.broadcasted_iota(jnp.int32, (EXTRA, wide), 1)
    for near in range(half):
        out_ref[near, :used] = jnp.zeros((used, wide), jnp.float32)
    for copy in copies + operators:
        copy.wait()

    for near in range(half):
        value = jnp.zeros((EXTRA, wide), jnp.int32)
        for side in range(2):
            for s in range(slot_count):
                wanted = fetch_ref[s, side * half + near]
                value = jnp.where(short_lane == side * slot_count + s, wanted, value)
        out_ref[near, used:] = value.astype(jnp.float32)

    for i in range(fine_rows):
        value = restrict_ref[i]
        swapped = pltpu.roll(value, block_size, 1)
        own_row = jnp.where(second == 0, rows_ref[0, i], rows_ref[1, i])
        other_row = jnp.where(second == 0, rows_ref[1, i], rows_ref[0, i])
        dense = jnp.where(own_row == second, value, 0.0) + jnp.where(other_row == second, swapped, 0.0)
        product = transposed_product(operator_ref[i], dense)
        for k in range(entries):
            part = jnp.where(k < count_ref[i], product[k * block_size : (k + 1) * block_size], 0.0)
            peer = lax.div(slot_ref[i, k], slot_count)
            place = lax.div(peer, half) * slot_count + lax.rem(slot_ref[i, k], slot_count)
            start = pl.multiple_of(place * block_size, block_size)
            out_ref[lax.rem(peer, half), pl.ds(start, block_size)] += part


def restrict_operator(
    operator_count, operator_slot, restrict_rows, fetch, operator_blocks, restrict_blocks, own_columns, own_blocks
):
    fine_rows, block_size, width = operator_blocks.shape
    slot_count, columns = fetch.shape
    wide = NCR * block_size
    rows = 2 * slot_count * block_size + EXTRA
    small = (operator_count, operator_slot, restrict_rows, fetch)
    return pl.pallas_call(
        restrict_kernel,
        out_shape=(
            jax.ShapeDtypeStruct((columns // 2, rows, wide), jnp.float32),
            jax.ShapeDtypeStruct(own_columns.shape, own_columns.dtype),
            jax.ShapeDtypeStruct(own_blocks.shape, own_blocks.dtype),
        ),
        in_specs=[pl.BlockSpec(memory_space=pltpu.HBM)] * 8,
        out_specs=[pl.BlockSpec(memory_space=pltpu.VMEM)] * 3,
        scratch_shapes=[pltpu.SMEM(x.shape, x.dtype) for x in small]
        + [pltpu.VMEM(x.shape, x.dtype) for x in (restrict_blocks, operator_blocks)]
        + [pltpu.SemaphoreType.DMA((7,)), pltpu.SemaphoreType.DMA((fine_rows,))],
        cost_estimate=pl.CostEstimate(
            flops=6 * fine_rows * block_size * width * wide, bytes_accessed=4 << 20, transcendentals=0
        ),
        name="restrict_operator",
    )(*small, restrict_blocks, operator_blocks, own_columns, own_blocks)


def combine_kernel(own_ref, restricted_ref, *rest, slot_count, fine_rows, entries):
    pieces, (out_ref, held_ref, table_ref, index_ref, sem) = rest[:-9], rest[-9:-4]
    sums = rest[-4:]
    half = restricted_ref.shape[0]
    rows = len(pieces) // 2
    block_size = out_ref.shape[1]
    columns = 2 * half
    used = 2 * slot_count * block_size
    held = fine_rows * block_size

    for near in range(half):
        table_ref[near : near + 1] = restricted_ref[near, used : used + 1].astype(jnp.int32)
    for i, piece in enumerate(pieces[rows:]):
        for far in range(2):
            first = half + entries * (far * rows + i)
            row = held + entries * (1 - far)
            table_ref[first : first + entries] = piece[row : row + entries].astype(jnp.int32)
    copy = pltpu.make_async_copy(table_ref, index_ref, sem)
    copy.start()
    for i, piece in enumerate(pieces):
        held_ref[i] = piece[...] if i < rows else piece[:held]
    for total in sums:
        total[...] = jnp.zeros_like(total)
    copy.wait()

    def add_product(i, total):
        near = lax.div(i, 2 * slot_count)
        place = lax.rem(i, 2 * slot_count)
        wanted = index_ref[near, place]
        inside = lax.rem(wanted, fine_rows)
        far = lax.div(place, slot_count) ^ own_ref[1]
        piece = far * rows + (lax.div(wanted, fine_rows * columns) ^ own_ref[0])
        block = held_ref[piece, pl.ds(pl.multiple_of(inside * block_size, block_size), block_size)]
        restricted = restricted_ref[near, pl.ds(pl.multiple_of(place * block_size, block_size), block_size)]
        product = transposed_product(block, restricted)
        for m in range(entries):
            column = own_ref[2 + index_ref[half + entries * piece + m, inside]]
            total[m % len(total)][column] += product[m * block_size : (m + 1) * block_size]

    def step(i, carry):
        add_product(2 * i, sums[:2])
        add_product(2 * i + 1, sums[2:])
        return carry

    lax.fori_loop(0, half * slot_count, step, 0, unroll=8)
    out_ref[...] = (sums[0][...] + sums[1][...]) + (sums[2][...] + sums[3][...])


def combine(own, restricted, pieces, coarse_all, slot_count, fine_rows, block_size):
    half, _, wide = restricted.shape
    width = pieces[0].shape[1]
    entries = width // block_size
    table_rows = -(-(half + entries * len(pieces)) // 8) * 8
    return pl.pallas_call(
        functools.partial(combine_kernel, slot_count=slot_count, fine_rows=fine_rows, entries=entries),
        out_shape=jax.ShapeDtypeStruct((coarse_all, block_size, wide), jnp.float32),
        in_specs=[pl.BlockSpec(memory_space=pltpu.SMEM)]
        + [pl.BlockSpec(memory_space=pltpu.VMEM)] * (1 + len(pieces)),
        out_specs=pl.BlockSpec(memory_space=pltpu.VMEM),
        scratch_shapes=[
            pltpu.VMEM((len(pieces), fine_rows * block_size, width), jnp.float32),
            pltpu.VMEM((table_rows, LANES), jnp.int32),
            pltpu.SMEM((table_rows, LANES), jnp.int32),
            pltpu.SemaphoreType.DMA,
        ]
        + [pltpu.VMEM((coarse_all, block_size, wide), jnp.float32)] * 4,
        compiler_params=pltpu.CompilerParams(vmem_limit_bytes=VMEM_LIMIT),
        cost_estimate=pl.CostEstimate(flops=1 << 28, bytes_accessed=4 << 20, transcendentals=0),
        name="combine",
    )(own, restricted, *pieces)


def row_swap(x, bit):
    return lax.ppermute(x, "row", [(r, r ^ bit) for r in range(lax.axis_size("row"))])


def half_swap(x):
    return lax.ppermute(x, "half", [(0, 1), (1, 0)])


def spread_over_rows(blocks, rows):
    pieces = {0: blocks}
    bit = rows // 2
    while bit:
        for mask in list(pieces):
            pieces[mask ^ bit] = row_swap(pieces[mask], bit)
        bit //= 2
    return [pieces[mask] for mask in range(rows)]


def place_of_columns(half):
    own = lax.axis_index("half") * half + lax.axis_index("near")
    ahead = jnp.arange(2 * half, dtype=jnp.int32) ^ own
    return ahead % half * 2 + ahead // half


def add_over_columns(sums, half):
    total = sums[:2]
    for near in range(1, half):
        total = total + lax.ppermute(sums[2 * near : 2 * near + 2], "near", [(n, n ^ near) for n in range(half)])
    return total[0] + half_swap(total[1])


def local(
    operator_blocks,
    operator_count,
    operator_slot,
    fetch_lists,
    prolong_blocks,
    prolong_cols,
    restrict_blocks,
    restrict_rows,
):
    rows, half = lax.axis_size("row"), lax.axis_size("near")
    slot_count = fetch_lists.shape[3]
    fine_rows, block_size, width = prolong_blocks.shape
    fetch = fetch_lists.reshape(2 * half, slot_count).T
    own = jnp.stack([lax.axis_index("row"), lax.axis_index("half")])
    own = jnp.concatenate([own, place_of_columns(half)])

    near_blocks = prolong_blocks.reshape(fine_rows * block_size, width)
    far_blocks = half_swap(near_blocks)
    restricted, own_columns, near_blocks = restrict_operator(
        operator_count,
        operator_slot,
        restrict_rows.T,
        fetch,
        operator_blocks,
        restrict_blocks,
        prolong_cols.T,
        near_blocks,
    )
    restricted = lax.all_to_all(restricted, "near", split_axis=0, concat_axis=0, tiled=True)
    far_columns = half_swap(own_columns)
    near_pieces = spread_over_rows(near_blocks, rows)
    far_blocks = append_columns(near_pieces[rows // 2], far_columns, own_columns, far_blocks)
    pieces = near_pieces + spread_over_rows(far_blocks, rows)
    sums = combine(own, restricted, pieces, NCR * rows, slot_count, fine_rows, block_size)
    return add_over_columns(sums, half).T


def solution(mesh):
    rows, columns = mesh.shape["row"], mesh.shape["col"]
    split = Mesh(mesh.devices.reshape(rows, 2, columns // 2), ("row", "half", "near"))
    flat = ("row", "half", "near")
    return jax.shard_map(
        local,
        mesh=split,
        in_specs=(
            P(flat, None, None),
            P(flat),
            P(flat, None),
            P("row", ("half", "near"), None, None),
            P(flat, None, None),
            P(flat, None),
            P(flat, None, None),
            P(flat, None),
        ),
        out_specs=P("row", ("half", "near")),
        check_vma=False,
    )
```

```python
import functools

import jax
import jax.numpy as jnp
from jax import lax
from jax.experimental import pallas as pl
from jax.experimental.pallas import tpu as pltpu
from jax.sharding import Mesh
from jax.sharding import PartitionSpec as P

NCR = 2
LANES = 128
EXTRA = 8
HOLD_FLOPS = 16 << 30
VMEM_LIMIT = 48 * 1024 * 1024


def halves(x):
    high = x.astype(jnp.bfloat16)
    return high, (x - high.astype(jnp.float32)).astype(jnp.bfloat16)


def transposed_product(left, right):
    tall = jnp.concatenate(halves(left), axis=0)
    wide = jnp.concatenate(halves(right), axis=1)
    wide = jnp.concatenate([wide, wide], axis=0)
    both = lax.dot_general(tall, wide, (((0,), (0,)), ((), ())), preferred_element_type=jnp.float32)
    width = right.shape[1]
    return both[:, :width] + both[:, width:]


def append_kernel(next_ref, far_columns_ref, own_columns_ref, blocks_ref, out_ref):
    used = blocks_ref.shape[0]
    entries, fine_rows = own_columns_ref.shape
    out_ref[:used] = blocks_ref[...]
    out_ref[used:] = jnp.zeros((EXTRA, out_ref.shape[1]), jnp.float32)
    out_ref[used : used + entries, :fine_rows] = far_columns_ref[...].astype(jnp.float32)
    out_ref[used + entries : used + 2 * entries, :fine_rows] = own_columns_ref[...].astype(jnp.float32)


def append_columns(next_blocks, far_columns, own_columns, blocks):
    used, width = blocks.shape
    return pl.pallas_call(
        append_kernel,
        out_shape=jax.ShapeDtypeStruct((used + EXTRA, width), blocks.dtype),
        in_specs=[pl.BlockSpec(memory_space=pltpu.VMEM)] * 4,
        out_specs=pl.BlockSpec(memory_space=pltpu.VMEM),
        compiler_params=pltpu.CompilerParams(vmem_limit_bytes=VMEM_LIMIT),
        cost_estimate=pl.CostEstimate(flops=HOLD_FLOPS, bytes_accessed=HOLD_FLOPS >> 8, transcendentals=0),
        name="append_columns",
    )(next_blocks, far_columns, own_columns, blocks)


def restrict_kernel(own_ref, *refs):
    count_any, slot_any, rows_any, fetch_any, restrict_any, operator_any, columns_any, blocks_any = refs[:8]
    own_columns_ref, own_blocks_any = refs[8:10]
    count_ref, slot_ref, rows_ref, fetch_ref, restrict_ref, operator_ref, blocks_ref, sums_ref = refs[-12:-4]
    sems, operator_sems, blocks_sem, out_sems = refs[-4:]
    outs = refs[10:-12]
    fine_rows, block_size, _ = operator_ref.shape
    entries = slot_ref.shape[1]
    slot_count, columns = fetch_ref.shape
    half = columns // 2
    used = 2 * slot_count * block_size
    wide = NCR * block_size
    own_near = own_ref[2]

    pairs = [
        (count_any, count_ref), (slot_any, slot_ref), (rows_any, rows_ref),
        (fetch_any, fetch_ref), (restrict_any, restrict_ref),
        (columns_any, own_columns_ref), (blocks_any, blocks_ref),
    ]
    copies = [pltpu.make_async_copy(a, b, sems.at[i]) for i, (a, b) in enumerate(pairs)]
    operators = [
        pltpu.make_async_copy(operator_any.at[i], operator_ref.at[i], operator_sems.at[i]) for i in range(fine_rows)
    ]
    for copy in copies + operators:
        copy.start()

    lane = lax.broadcasted_iota(jnp.int32, (block_size, wide), 1)
    second = (lane >= block_size).astype(jnp.int32)
    short_lane = lax.broadcasted_iota(jnp.int32, (EXTRA, wide), 1)
    for ahead in range(half):
        sums_ref[ahead, :used] = jnp.zeros((used, wide), jnp.float32)
    for copy in copies:
        copy.wait()
    pass_on = pltpu.make_async_copy(blocks_ref, own_blocks_any, blocks_sem)
    pass_on.start()

    for near in range(half):
        value = jnp.zeros((EXTRA, wide), jnp.int32)
        for side in range(2):
            for s in range(slot_count):
                wanted = fetch_ref[s, side * half + near]
                value = jnp.where(short_lane == side * slot_count + s, wanted, value)
        sums_ref[near ^ own_near, used:] = value.astype(jnp.float32)
    for copy in operators:
        copy.wait()

    for i in range(fine_rows):
        value = restrict_ref[i]
        swapped = pltpu.roll(value, block_size, 1)
        own_row = jnp.where(second == 0, rows_ref[0, i], rows_ref[1, i])
        other_row = jnp.where(second == 0, rows_ref[1, i], rows_ref[0, i])
        dense = jnp.where(own_row == second, value, 0.0) + jnp.where(other_row == second, swapped, 0.0)
        product = transposed_product(operator_ref[i], dense)
        for k in range(entries):
            part = jnp.where(k < count_ref[i], product[k * block_size : (k + 1) * block_size], 0.0)
            peer = lax.div(slot_ref[i, k], slot_count)
            place = lax.div(peer, half) * slot_count + lax.rem(slot_ref[i, k], slot_count)
            start = pl.multiple_of(place * block_size, block_size)
            sums_ref[lax.rem(peer, half) ^ own_near, pl.ds(start, block_size)] += part

    writes = [pltpu.make_async_copy(sums_ref.at[ahead], out, out_sems.at[ahead]) for ahead, out in enumerate(outs)]
    for copy in writes:
        copy.start()
    for copy in writes:
        copy.wait()
    pass_on.wait()


def restrict_operator(
    own, operator_count, operator_slot, restrict_rows, fetch, operator_blocks, restrict_blocks, own_columns, own_blocks
):
    fine_rows, block_size, width = operator_blocks.shape
    slot_count, columns = fetch.shape
    wide = NCR * block_size
    rows = 2 * slot_count * block_size + EXTRA
    small = (operator_count, operator_slot, restrict_rows, fetch)
    hbm = pl.BlockSpec(memory_space=pltpu.HBM)
    results = pl.pallas_call(
        restrict_kernel,
        out_shape=(
            jax.ShapeDtypeStruct(own_columns.shape, own_columns.dtype),
            jax.ShapeDtypeStruct(own_blocks.shape, own_blocks.dtype),
        )
        + (jax.ShapeDtypeStruct((rows, wide), jnp.float32),) * (columns // 2),
        in_specs=[pl.BlockSpec(memory_space=pltpu.SMEM)] + [hbm] * 8,
        out_specs=[pl.BlockSpec(memory_space=pltpu.VMEM)] + [hbm] * (1 + columns // 2),
        scratch_shapes=[pltpu.SMEM(x.shape, x.dtype) for x in small]
        + [pltpu.VMEM(x.shape, x.dtype) for x in (restrict_blocks, operator_blocks, own_blocks)]
        + [pltpu.VMEM((columns // 2, rows, wide), jnp.float32)]
        + [pltpu.SemaphoreType.DMA((7,)), pltpu.SemaphoreType.DMA((fine_rows,))]
        + [pltpu.SemaphoreType.DMA, pltpu.SemaphoreType.DMA((columns // 2,))],
        cost_estimate=pl.CostEstimate(
            flops=6 * fine_rows * block_size * width * wide, bytes_accessed=4 << 20, transcendentals=0
        ),
        name="restrict_operator",
    )(own, *small, restrict_blocks, operator_blocks, own_columns, own_blocks)
    return results[0], results[1], results[2:]


def index_kernel(*refs):
    out_ref = refs[-1]
    out_ref[...] = jnp.zeros_like(out_ref)
    for i, part in enumerate(refs[:-1]):
        out_ref[i : i + 1] = part[part.shape[0] - EXTRA : part.shape[0] - EXTRA + 1].astype(jnp.int32)


def index_table(parts):
    rows = -(-len(parts) // 8) * 8
    return pl.pallas_call(
        index_kernel,
        out_shape=jax.ShapeDtypeStruct((rows, LANES), jnp.int32),
        in_specs=[pl.BlockSpec(memory_space=pltpu.VMEM)] * len(parts),
        out_specs=pl.BlockSpec(memory_space=pltpu.VMEM),
        compiler_params=pltpu.CompilerParams(vmem_limit_bytes=VMEM_LIMIT),
        cost_estimate=pl.CostEstimate(flops=HOLD_FLOPS, bytes_accessed=HOLD_FLOPS >> 8, transcendentals=0),
        name="index_table",
    )(*parts)


def combine_kernel(own_ref, wanted_ref, *rest, half, split, slot_count, fine_rows, entries):
    parts, chunks = rest[:half], list(rest[half:-5])
    out_ref, held_ref, table_ref, index_ref, sem = rest[-5:]
    rows = len(split) // 2
    block_size = out_ref.shape[1]
    columns = 2 * half
    held = fine_rows * block_size
    pieces = [[chunks.pop(0) for _ in range(count)] for count in split]

    table_ref[:half] = wanted_ref[:half]
    for i, piece in enumerate(pieces[rows:]):
        last = piece[-1]
        for far in range(2):
            first = half + entries * (far * rows + i)
            row = last.shape[0] - EXTRA + entries * (1 - far)
            table_ref[first : first + entries] = last[row : row + entries].astype(jnp.int32)
    copy = pltpu.make_async_copy(table_ref, index_ref, sem)
    copy.start()
    for i, piece in enumerate(pieces):
        start = 0
        for chunk in piece:
            size = min(chunk.shape[0], held - start)
            held_ref[i, start : start + size] = chunk[:size]
            start += size
    out_ref[...] = jnp.zeros_like(out_ref)
    copy.wait()

    for ahead, part in enumerate(parts):

        def step(place, carry, ahead=ahead, part=part):
            wanted = index_ref[ahead, place]
            inside = lax.rem(wanted, fine_rows)
            far = lax.div(place, slot_count) ^ own_ref[1]
            piece = far * rows + (lax.div(wanted, fine_rows * columns) ^ own_ref[0])
            block = held_ref[piece, pl.ds(pl.multiple_of(inside * block_size, block_size), block_size)]
            restricted = part[pl.ds(pl.multiple_of(place * block_size, block_size), block_size)]
            product = transposed_product(block, restricted)
            for m in range(entries):
                column = own_ref[3 + index_ref[half + entries * piece + m, inside]]
                out_ref[column] += product[m * block_size : (m + 1) * block_size]
            return carry

        lax.fori_loop(0, 2 * slot_count, step, 0, unroll=half <= 4)


def combine(own, wanted, parts, pieces, coarse_all, slot_count, fine_rows, block_size):
    half = len(parts)
    wide = parts[0].shape[1]
    width = pieces[0][0].shape[1]
    entries = width // block_size
    split = tuple(len(piece) for piece in pieces)
    chunks = [chunk for piece in pieces for chunk in piece]
    table_rows = -(-(half + entries * len(pieces)) // 8) * 8
    return pl.pallas_call(
        functools.partial(
            combine_kernel, half=half, split=split, slot_count=slot_count, fine_rows=fine_rows, entries=entries
        ),
        out_shape=jax.ShapeDtypeStruct((coarse_all, block_size, wide), jnp.float32),
        in_specs=[pl.BlockSpec(memory_space=pltpu.SMEM)]
        + [pl.BlockSpec(memory_space=pltpu.VMEM)] * (1 + half + len(chunks)),
        out_specs=pl.BlockSpec(memory_space=pltpu.VMEM),
        scratch_shapes=[
            pltpu.VMEM((len(pieces), fine_rows * block_size, width), jnp.float32),
            pltpu.VMEM((table_rows, LANES), jnp.int32),
            pltpu.SMEM((table_rows, LANES), jnp.int32),
            pltpu.SemaphoreType.DMA,
        ],
        compiler_params=pltpu.CompilerParams(vmem_limit_bytes=VMEM_LIMIT),
        cost_estimate=pl.CostEstimate(flops=1 << 28, bytes_accessed=4 << 20, transcendentals=0),
        name="combine",
    )(own, wanted, *parts, *chunks)


def row_swap(x, bit):
    return lax.ppermute(x, "row", [(r, r ^ bit) for r in range(lax.axis_size("row"))])


def half_swap(x):
    return lax.ppermute(x, "half", [(0, 1), (1, 0)])


def spread_over_rows(blocks, rows, cut):
    pieces = {0: [blocks]}
    bit = rows // 2
    while bit:
        for mask in list(pieces):
            chunks = pieces[mask]
            if cut and bit == rows // 2:
                chunks = [blocks[:cut], blocks[cut:]]
            pieces[mask ^ bit] = [row_swap(chunk, bit) for chunk in chunks]
        bit //= 2
    return [pieces[mask] for mask in range(rows)]


def place_of_columns(half):
    own = lax.axis_index("half") * half + lax.axis_index("near")
    ahead = jnp.arange(2 * half, dtype=jnp.int32) ^ own
    return ahead % half * 2 + ahead // half


def add_over_columns(sums, half):
    total = sums[:2]
    for near in range(1, half):
        total = total + lax.ppermute(sums[2 * near : 2 * near + 2], "near", [(n, n ^ near) for n in range(half)])
    return total[0] + half_swap(total[1])


def local(
    operator_blocks,
    operator_count,
    operator_slot,
    fetch_lists,
    prolong_blocks,
    prolong_cols,
    restrict_blocks,
    restrict_rows,
):
    rows, half = lax.axis_size("row"), lax.axis_size("near")
    slot_count = fetch_lists.shape[3]
    fine_rows, block_size, width = prolong_blocks.shape
    fetch = fetch_lists.reshape(2 * half, slot_count).T
    own = jnp.stack([lax.axis_index("row"), lax.axis_index("half"), lax.axis_index("near")])
    own = jnp.concatenate([own, place_of_columns(half)])

    near_blocks = prolong_blocks.reshape(fine_rows * block_size, width)
    far_blocks = half_swap(near_blocks)
    own_columns, near_blocks, parts = restrict_operator(
        own,
        operator_count,
        operator_slot,
        restrict_rows.T,
        fetch,
        operator_blocks,
        restrict_blocks,
        prolong_cols.T,
        near_blocks,
    )
    parts = [parts[0]] + [
        lax.ppermute(parts[ahead], "near", [(n, n ^ ahead) for n in range(half)]) for ahead in range(1, half)
    ]
    wanted = index_table(parts)
    far_columns = half_swap(own_columns)
    near_pieces = spread_over_rows(near_blocks, rows, 0)
    far_blocks = append_columns(near_pieces[rows // 2][0], far_columns, own_columns, far_blocks)
    pieces = near_pieces + spread_over_rows(far_blocks, rows, fine_rows * block_size // 2)
    sums = combine(own, wanted, parts, pieces, NCR * rows, slot_count, fine_rows, block_size)
    return add_over_columns(sums, half).T


def solution(mesh):
    rows, columns = mesh.shape["row"], mesh.shape["col"]
    split = Mesh(mesh.devices.reshape(rows, 2, columns // 2), ("row", "half", "near"))
    flat = ("row", "half", "near")
    return jax.shard_map(
        local,
        mesh=split,
        in_specs=(
            P(flat, None, None),
            P(flat),
            P(flat, None),
            P("row", ("half", "near"), None, None),
            P(flat, None, None),
            P(flat, None),
            P(flat, None, None),
            P(flat, None),
        ),
        out_specs=P("row", ("half", "near")),
        check_vma=False,
    )
```

```python
import functools

import jax
import jax.numpy as jnp
from jax import lax
from jax.experimental import pallas as pl
from jax.experimental.pallas import tpu as pltpu
from jax.sharding import Mesh
from jax.sharding import PartitionSpec as P

NCR = 2
LANES = 128
EXTRA = 8
HOLD_FLOPS = 16 << 30
VMEM_LIMIT = 48 * 1024 * 1024


def halves(x):
    high = x.astype(jnp.bfloat16)
    return high, (x - high.astype(jnp.float32)).astype(jnp.bfloat16)


def transposed_product(left, right):
    tall = jnp.concatenate(halves(left), axis=0)
    wide = jnp.concatenate(halves(right), axis=1)
    wide = jnp.concatenate([wide, wide], axis=0)
    both = lax.dot_general(tall, wide, (((0,), (0,)), ((), ())), preferred_element_type=jnp.float32)
    width = right.shape[1]
    return both[:, :width] + both[:, width:]


def hold_kernel(mark_ref, blocks_ref, out_ref):
    out_ref[...] = blocks_ref[...]


def hold_until(mark, blocks):
    return pl.pallas_call(
        hold_kernel,
        out_shape=jax.ShapeDtypeStruct(blocks.shape, blocks.dtype),
        in_specs=[pl.BlockSpec(memory_space=pltpu.VMEM)] * 2,
        out_specs=pl.BlockSpec(memory_space=pltpu.VMEM),
        compiler_params=pltpu.CompilerParams(vmem_limit_bytes=VMEM_LIMIT),
        cost_estimate=pl.CostEstimate(flops=HOLD_FLOPS, bytes_accessed=HOLD_FLOPS >> 8, transcendentals=0),
        name="hold_until",
    )(mark, blocks)


def append_kernel(far_columns_ref, own_columns_ref, next_ref, blocks_ref, out_ref):
    used = blocks_ref.shape[0]
    entries, fine_rows = own_columns_ref.shape
    out_ref[:used] = blocks_ref[...]
    out_ref[used:] = jnp.zeros((EXTRA, out_ref.shape[1]), jnp.float32)
    out_ref[used : used + entries, :fine_rows] = far_columns_ref[...].astype(jnp.float32)
    out_ref[used + entries : used + 2 * entries, :fine_rows] = own_columns_ref[...].astype(jnp.float32)


def append_columns(far_columns, own_columns, next_blocks, blocks):
    used, width = blocks.shape
    return pl.pallas_call(
        append_kernel,
        out_shape=jax.ShapeDtypeStruct((used + EXTRA, width), blocks.dtype),
        in_specs=[pl.BlockSpec(memory_space=pltpu.VMEM)] * 4,
        out_specs=pl.BlockSpec(memory_space=pltpu.VMEM),
        compiler_params=pltpu.CompilerParams(vmem_limit_bytes=VMEM_LIMIT),
        cost_estimate=pl.CostEstimate(flops=0, bytes_accessed=1 << 19, transcendentals=0),
        name="append_columns",
    )(far_columns, own_columns, next_blocks, blocks)


def restrict_kernel(
    count_any, slot_any, rows_any, fetch_any, restrict_any, operator_any, columns_any,
    out_ref, own_columns_ref,
    count_ref, slot_ref, rows_ref, fetch_ref, restrict_ref, operator_ref, sems, operator_sems,
):
    fine_rows, block_size, _ = operator_ref.shape
    entries = slot_ref.shape[1]
    slot_count, columns = fetch_ref.shape
    half = columns // 2
    used = 2 * slot_count * block_size
    wide = NCR * block_size

    pairs = [
        (count_any, count_ref), (slot_any, slot_ref), (rows_any, rows_ref),
        (fetch_any, fetch_ref), (restrict_any, restrict_ref),
        (columns_any, own_columns_ref),
    ]
    copies = [pltpu.make_async_copy(a, b, sems.at[i]) for i, (a, b) in enumerate(pairs)]
    operators = [
        pltpu.make_async_copy(operator_any.at[i], operator_ref.at[i], operator_sems.at[i]) for i in range(fine_rows)
    ]
    for copy in copies + operators:
        copy.start()

    lane = lax.broadcasted_iota(jnp.int32, (block_size, wide), 1)
    second = (lane >= block_size).astype(jnp.int32)
    short_lane = lax.broadcasted_iota(jnp.int32, (EXTRA, wide), 1)
    for near in range(half):
        out_ref[near, :used] = jnp.zeros((used, wide), jnp.float32)
    for copy in copies + operators:
        copy.wait()

    for near in range(half):
        value = jnp.zeros((EXTRA, wide), jnp.int32)
        for side in range(2):
            for s in range(slot_count):
                wanted = fetch_ref[s, side * half + near]
                value = jnp.where(short_lane == side * slot_count + s, wanted, value)
        out_ref[near, used:] = value.astype(jnp.float32)

    for i in range(fine_rows):
        value = restrict_ref[i]
        swapped = pltpu.roll(value, block_size, 1)
        own_row = jnp.where(second == 0, rows_ref[0, i], rows_ref[1, i])
        other_row = jnp.where(second == 0, rows_ref[1, i], rows_ref[0, i])
        dense = jnp.where(own_row == second, value, 0.0) + jnp.where(other_row == second, swapped, 0.0)
        product = transposed_product(operator_ref[i], dense)
        for k in range(entries):
            part = jnp.where(k < count_ref[i], product[k * block_size : (k + 1) * block_size], 0.0)
            peer = lax.div(slot_ref[i, k], slot_count)
            place = lax.div(peer, half) * slot_count + lax.rem(slot_ref[i, k], slot_count)
            start = pl.multiple_of(place * block_size, block_size)
            out_ref[lax.rem(peer, half), pl.ds(start, block_size)] += part


def restrict_operator(
    operator_count, operator_slot, restrict_rows, fetch, operator_blocks, restrict_blocks, own_columns
):
    fine_rows, block_size, width = operator_blocks.shape
    slot_count, columns = fetch.shape
    wide = NCR * block_size
    rows = 2 * slot_count * block_size + EXTRA
    small = (operator_count, operator_slot, restrict_rows, fetch)
    return pl.pallas_call(
        restrict_kernel,
        out_shape=(
            jax.ShapeDtypeStruct((columns // 2, rows, wide), jnp.float32),
            jax.ShapeDtypeStruct(own_columns.shape, own_columns.dtype),
        ),
        in_specs=[pl.BlockSpec(memory_space=pltpu.HBM)] * 7,
        out_specs=[pl.BlockSpec(memory_space=pltpu.VMEM)] * 2,
        scratch_shapes=[pltpu.SMEM(x.shape, x.dtype) for x in small]
        + [pltpu.VMEM(x.shape, x.dtype) for x in (restrict_blocks, operator_blocks)]
        + [pltpu.SemaphoreType.DMA((6,)), pltpu.SemaphoreType.DMA((fine_rows,))],
        cost_estimate=pl.CostEstimate(
            flops=6 * fine_rows * block_size * width * wide, bytes_accessed=4 << 20, transcendentals=0
        ),
        name="restrict_operator",
    )(*small, restrict_blocks, operator_blocks, own_columns)


def combine_kernel(own_ref, restricted_ref, *rest, slot_count, fine_rows, entries):
    pieces, (out_ref, held_ref, table_ref, index_ref, sem) = rest[:-5], rest[-5:]
    half = restricted_ref.shape[0]
    rows = len(pieces) // 2
    block_size = out_ref.shape[1]
    columns = 2 * half
    used = 2 * slot_count * block_size
    held = fine_rows * block_size

    for near in range(half):
        table_ref[near : near + 1] = restricted_ref[near, used : used + 1].astype(jnp.int32)
    for i, piece in enumerate(pieces[rows:]):
        for far in range(2):
            first = half + entries * (far * rows + i)
            row = held + entries * (1 - far)
            table_ref[first : first + entries] = piece[row : row + entries].astype(jnp.int32)
    copy = pltpu.make_async_copy(table_ref, index_ref, sem)
    copy.start()
    for i, piece in enumerate(pieces):
        held_ref[i] = piece[...] if i < rows else piece[:held]
    out_ref[...] = jnp.zeros_like(out_ref)
    copy.wait()

    def step(i, carry):
        near = lax.div(i, 2 * slot_count)
        place = lax.rem(i, 2 * slot_count)
        wanted = index_ref[near, place]
        inside = lax.rem(wanted, fine_rows)
        far = lax.div(place, slot_count) ^ own_ref[1]
        piece = far * rows + (lax.div(wanted, fine_rows * columns) ^ own_ref[0])
        block = held_ref[piece, pl.ds(pl.multiple_of(inside * block_size, block_size), block_size)]
        restricted = restricted_ref[near, pl.ds(pl.multiple_of(place * block_size, block_size), block_size)]
        product = transposed_product(block, restricted)
        for m in range(entries):
            column = own_ref[2 + index_ref[half + entries * piece + m, inside]]
            out_ref[column] += product[m * block_size : (m + 1) * block_size]
        return carry

    lax.fori_loop(0, half * 2 * slot_count, step, 0, unroll=16)


def combine(own, restricted, pieces, coarse_all, slot_count, fine_rows, block_size):
    half, _, wide = restricted.shape
    width = pieces[0].shape[1]
    entries = width // block_size
    table_rows = -(-(half + entries * len(pieces)) // 8) * 8
    return pl.pallas_call(
        functools.partial(combine_kernel, slot_count=slot_count, fine_rows=fine_rows, entries=entries),
        out_shape=jax.ShapeDtypeStruct((coarse_all, block_size, wide), jnp.float32),
        in_specs=[pl.BlockSpec(memory_space=pltpu.SMEM)]
        + [pl.BlockSpec(memory_space=pltpu.VMEM)] * (1 + len(pieces)),
        out_specs=pl.BlockSpec(memory_space=pltpu.VMEM),
        scratch_shapes=[
            pltpu.VMEM((len(pieces), fine_rows * block_size, width), jnp.float32),
            pltpu.VMEM((table_rows, LANES), jnp.int32),
            pltpu.SMEM((table_rows, LANES), jnp.int32),
            pltpu.SemaphoreType.DMA,
        ],
        compiler_params=pltpu.CompilerParams(vmem_limit_bytes=VMEM_LIMIT),
        cost_estimate=pl.CostEstimate(flops=1 << 28, bytes_accessed=4 << 20, transcendentals=0),
        name="combine",
    )(own, restricted, *pieces)


def row_swap(x, bit):
    return lax.ppermute(x, "row", [(r, r ^ bit) for r in range(lax.axis_size("row"))])


def half_swap(x):
    return lax.ppermute(x, "half", [(0, 1), (1, 0)])


def spread_over_rows(blocks, rows):
    pieces = {0: blocks}
    bit = rows // 2
    while bit:
        for mask in list(pieces):
            pieces[mask ^ bit] = row_swap(pieces[mask], bit)
        bit //= 2
    return [pieces[mask] for mask in range(rows)]


def place_of_columns(half):
    own = lax.axis_index("half") * half + lax.axis_index("near")
    ahead = jnp.arange(2 * half, dtype=jnp.int32) ^ own
    return ahead % half * 2 + ahead // half


def add_over_columns(sums, half):
    total = sums[:2]
    for near in range(1, half):
        total = total + lax.ppermute(sums[2 * near : 2 * near + 2], "near", [(n, n ^ near) for n in range(half)])
    return total[0] + half_swap(total[1])


def local(
    operator_blocks,
    operator_count,
    operator_slot,
    fetch_lists,
    prolong_blocks,
    prolong_cols,
    restrict_blocks,
    restrict_rows,
):
    rows, half = lax.axis_size("row"), lax.axis_size("near")
    slot_count = fetch_lists.shape[3]
    fine_rows, block_size, width = prolong_blocks.shape
    fetch = fetch_lists.reshape(2 * half, slot_count).T
    own = jnp.stack([lax.axis_index("row"), lax.axis_index("half")])
    own = jnp.concatenate([own, place_of_columns(half)])

    near_blocks = prolong_blocks.reshape(fine_rows * block_size, width)
    far_blocks = half_swap(near_blocks)
    restricted, own_columns = restrict_operator(
        operator_count,
        operator_slot,
        restrict_rows.T,
        fetch,
        operator_blocks,
        restrict_blocks,
        prolong_cols.T,
    )
    restricted = lax.all_to_all(restricted, "near", split_axis=0, concat_axis=0, tiled=True)
    far_columns = half_swap(own_columns)
    near_pieces = spread_over_rows(near_blocks, rows)
    far_blocks = hold_until(far_columns, far_blocks)
    far_blocks = append_columns(far_columns, own_columns, near_pieces[rows // 2], far_blocks)
    pieces = near_pieces + spread_over_rows(far_blocks, rows)
    sums = combine(own, restricted, pieces, NCR * rows, slot_count, fine_rows, block_size)
    return add_over_columns(sums, half).T


def solution(mesh):
    rows, columns = mesh.shape["row"], mesh.shape["col"]
    split = Mesh(mesh.devices.reshape(rows, 2, columns // 2), ("row", "half", "near"))
    flat = ("row", "half", "near")
    return jax.shard_map(
        local,
        mesh=split,
        in_specs=(
            P(flat, None, None),
            P(flat),
            P(flat, None),
            P("row", ("half", "near"), None, None),
            P(flat, None, None),
            P(flat, None),
            P(flat, None, None),
            P(flat, None),
        ),
        out_specs=P("row", ("half", "near")),
        check_vma=False,
    )
```

```python
import functools

import jax
import jax.numpy as jnp
from jax import lax
from jax.experimental import pallas as pl
from jax.experimental.pallas import tpu as pltpu
from jax.sharding import Mesh
from jax.sharding import PartitionSpec as P

NCR = 2
LANES = 128
EXTRA = 8
HOLD_FLOPS = 16 << 30
VMEM_LIMIT = 48 * 1024 * 1024


def halves(x):
    high = x.astype(jnp.bfloat16)
    return high, (x - high.astype(jnp.float32)).astype(jnp.bfloat16)


def transposed_product(left, right):
    tall = jnp.concatenate(halves(left), axis=0)
    wide = jnp.concatenate(halves(right), axis=1)
    wide = jnp.concatenate([wide, wide], axis=0)
    both = lax.dot_general(tall, wide, (((0,), (0,)), ((), ())), preferred_element_type=jnp.float32)
    width = right.shape[1]
    return both[:, :width] + both[:, width:]


def append_kernel(next_ref, far_columns_ref, own_columns_ref, blocks_ref, out_ref):
    used = blocks_ref.shape[0]
    entries, fine_rows = own_columns_ref.shape
    out_ref[:used] = blocks_ref[...]
    out_ref[used:] = jnp.zeros((EXTRA, out_ref.shape[1]), jnp.float32)
    out_ref[used : used + entries, :fine_rows] = far_columns_ref[...].astype(jnp.float32)
    out_ref[used + entries : used + 2 * entries, :fine_rows] = own_columns_ref[...].astype(jnp.float32)


def append_columns(next_blocks, far_columns, own_columns, blocks):
    used, width = blocks.shape
    return pl.pallas_call(
        append_kernel,
        out_shape=jax.ShapeDtypeStruct((used + EXTRA, width), blocks.dtype),
        in_specs=[pl.BlockSpec(memory_space=pltpu.VMEM)] * 4,
        out_specs=pl.BlockSpec(memory_space=pltpu.VMEM),
        compiler_params=pltpu.CompilerParams(vmem_limit_bytes=VMEM_LIMIT),
        cost_estimate=pl.CostEstimate(flops=HOLD_FLOPS, bytes_accessed=HOLD_FLOPS >> 8, transcendentals=0),
        name="append_columns",
    )(next_blocks, far_columns, own_columns, blocks)


def restrict_kernel(
    count_any, slot_any, rows_any, fetch_any, restrict_any, operator_any, columns_any, blocks_any, side_any,
    out_ref, own_columns_ref, own_blocks_ref,
    count_ref, slot_ref, rows_ref, fetch_ref, side_ref, restrict_ref, operator_ref, sems, operator_sems,
):
    fine_rows, block_size, _ = operator_ref.shape
    entries = slot_ref.shape[1]
    slot_count, columns = fetch_ref.shape
    half = columns // 2
    used = 2 * slot_count * block_size
    wide = NCR * block_size

    pairs = [
        (count_any, count_ref), (slot_any, slot_ref), (rows_any, rows_ref),
        (fetch_any, fetch_ref), (restrict_any, restrict_ref),
        (columns_any, own_columns_ref), (blocks_any, own_blocks_ref), (side_any, side_ref),
    ]
    copies = [pltpu.make_async_copy(a, b, sems.at[i]) for i, (a, b) in enumerate(pairs)]
    operators = [
        pltpu.make_async_copy(operator_any.at[i], operator_ref.at[i], operator_sems.at[i]) for i in range(fine_rows)
    ]
    for copy in copies + operators:
        copy.start()

    lane = lax.broadcasted_iota(jnp.int32, (block_size, wide), 1)
    second = (lane >= block_size).astype(jnp.int32)
    short_lane = lax.broadcasted_iota(jnp.int32, (EXTRA, wide), 1)
    for near in range(half):
        out_ref[near, :used] = jnp.zeros((used, wide), jnp.float32)
    for copy in copies + operators:
        copy.wait()

    for near in range(half):
        value = jnp.zeros((EXTRA, wide), jnp.int32)
        for side in range(2):
            for s in range(slot_count):
                turned = near ^ jnp.where(side_ref[0] == side, 0, half // 2)
                wanted = fetch_ref[s, side * half + turned]
                value = jnp.where(short_lane == side * slot_count + s, wanted, value)
        out_ref[near, used:] = value.astype(jnp.float32)

    for i in range(fine_rows):
        value = restrict_ref[i]
        swapped = pltpu.roll(value, block_size, 1)
        own_row = jnp.where(second == 0, rows_ref[0, i], rows_ref[1, i])
        other_row = jnp.where(second == 0, rows_ref[1, i], rows_ref[0, i])
        dense = jnp.where(own_row == second, value, 0.0) + jnp.where(other_row == second, swapped, 0.0)
        product = transposed_product(operator_ref[i], dense)
        for k in range(entries):
            part = jnp.where(k < count_ref[i], product[k * block_size : (k + 1) * block_size], 0.0)
            peer = lax.div(slot_ref[i, k], slot_count)
            side = lax.div(peer, half)
            place = side * slot_count + lax.rem(slot_ref[i, k], slot_count)
            near = lax.rem(peer, half) ^ jnp.where(side_ref[0] == side, 0, half // 2)
            start = pl.multiple_of(place * block_size, block_size)
            out_ref[near, pl.ds(start, block_size)] += part


def restrict_operator(
    operator_count, operator_slot, restrict_rows, fetch, operator_blocks, restrict_blocks, own_columns, own_blocks, side
):
    fine_rows, block_size, width = operator_blocks.shape
    slot_count, columns = fetch.shape
    wide = NCR * block_size
    rows = 2 * slot_count * block_size + EXTRA
    small = (operator_count, operator_slot, restrict_rows, fetch)
    kept = small + (side,)
    return pl.pallas_call(
        restrict_kernel,
        out_shape=(
            jax.ShapeDtypeStruct((columns // 2, rows, wide), jnp.float32),
            jax.ShapeDtypeStruct(own_columns.shape, own_columns.dtype),
            jax.ShapeDtypeStruct(own_blocks.shape, own_blocks.dtype),
        ),
        in_specs=[pl.BlockSpec(memory_space=pltpu.HBM)] * 9,
        out_specs=[pl.BlockSpec(memory_space=pltpu.VMEM)] * 3,
        scratch_shapes=[pltpu.SMEM(x.shape, x.dtype) for x in kept]
        + [pltpu.VMEM(x.shape, x.dtype) for x in (restrict_blocks, operator_blocks)]
        + [pltpu.SemaphoreType.DMA((8,)), pltpu.SemaphoreType.DMA((fine_rows,))],
        cost_estimate=pl.CostEstimate(
            flops=6 * fine_rows * block_size * width * wide, bytes_accessed=4 << 20, transcendentals=0
        ),
        name="restrict_operator",
    )(*small, restrict_blocks, operator_blocks, own_columns, own_blocks, side)


def combine_kernel(own_ref, restricted_ref, *rest, slot_count, fine_rows, entries):
    pieces, (out_ref, held_ref, table_ref, index_ref, sem) = rest[:-5], rest[-5:]
    half = restricted_ref.shape[0]
    rows = len(pieces) // 2
    block_size = out_ref.shape[1]
    columns = 2 * half
    used = 2 * slot_count * block_size
    held = fine_rows * block_size

    table_ref[:1, : own_ref.shape[1]] = own_ref[...]
    for near in range(half):
        table_ref[1 + near : 2 + near] = restricted_ref[near, used : used + 1].astype(jnp.int32)
    for i, piece in enumerate(pieces[rows:]):
        for far in range(2):
            first = 1 + half + entries * (far * rows + i)
            row = held + entries * (1 - far)
            table_ref[first : first + entries] = piece[row : row + entries].astype(jnp.int32)
    copy = pltpu.make_async_copy(table_ref, index_ref, sem)
    copy.start()
    for i, piece in enumerate(pieces):
        held_ref[i] = piece[...] if i < rows else piece[:held]
    out_ref[...] = jnp.zeros_like(out_ref)
    copy.wait()

    def step(i, carry):
        near = lax.div(i, 2 * slot_count)
        place = lax.rem(i, 2 * slot_count)
        wanted = index_ref[1 + near, place]
        inside = lax.rem(wanted, fine_rows)
        far = lax.div(place, slot_count) ^ index_ref[0, 1]
        piece = far * rows + (lax.div(wanted, fine_rows * columns) ^ index_ref[0, 0])
        block = held_ref[piece, pl.ds(pl.multiple_of(inside * block_size, block_size), block_size)]
        restricted = restricted_ref[near, pl.ds(pl.multiple_of(place * block_size, block_size), block_size)]
        product = transposed_product(block, restricted)
        for m in range(entries):
            column = index_ref[0, 2 + index_ref[1 + half + entries * piece + m, inside]]
            out_ref[column] += product[m * block_size : (m + 1) * block_size]
        return carry

    lax.fori_loop(0, half * 2 * slot_count, step, 0, unroll=16)


def combine(own, restricted, pieces, coarse_all, slot_count, fine_rows, block_size):
    half, _, wide = restricted.shape
    width = pieces[0].shape[1]
    entries = width // block_size
    table_rows = -(-(1 + half + entries * len(pieces)) // 8) * 8
    return pl.pallas_call(
        functools.partial(combine_kernel, slot_count=slot_count, fine_rows=fine_rows, entries=entries),
        out_shape=jax.ShapeDtypeStruct((coarse_all, block_size, wide), jnp.float32),
        in_specs=[pl.BlockSpec(memory_space=pltpu.VMEM)] * (2 + len(pieces)),
        out_specs=pl.BlockSpec(memory_space=pltpu.VMEM),
        scratch_shapes=[
            pltpu.VMEM((len(pieces), fine_rows * block_size, width), jnp.float32),
            pltpu.VMEM((table_rows, LANES), jnp.int32),
            pltpu.SMEM((table_rows, LANES), jnp.int32),
            pltpu.SemaphoreType.DMA,
        ],
        compiler_params=pltpu.CompilerParams(vmem_limit_bytes=VMEM_LIMIT),
        cost_estimate=pl.CostEstimate(flops=1 << 28, bytes_accessed=4 << 20, transcendentals=0),
        name="combine",
    )(own, restricted, *pieces)


def row_swap(x, bit):
    return lax.ppermute(x, "row", [(r, r ^ bit) for r in range(lax.axis_size("row"))])


def half_swap(x):
    return lax.ppermute(x, "half", [(0, 1), (1, 0)])


def far_swap(x):
    half = lax.axis_size("near")
    pairs = [(h * half + n, (1 - h) * half + (n ^ half // 2)) for h in range(2) for n in range(half)]
    return lax.ppermute(x, ("half", "near"), pairs)


def spread_over_rows(blocks, rows):
    pieces = {0: blocks}
    bit = rows // 2
    while bit:
        for mask in list(pieces):
            pieces[mask ^ bit] = row_swap(pieces[mask], bit)
        bit //= 2
    return [pieces[mask] for mask in range(rows)]


def place_of_columns(half):
    own = lax.axis_index("half") * half + lax.axis_index("near")
    ahead = jnp.arange(2 * half, dtype=jnp.int32) ^ own
    return ahead % half * 2 + ahead // half


def add_over_columns(sums, half):
    total = sums[:2]
    for near in range(1, half):
        total = total + lax.ppermute(sums[2 * near : 2 * near + 2], "near", [(n, n ^ near) for n in range(half)])
    return total[0] + half_swap(total[1])


def local(
    operator_blocks,
    operator_count,
    operator_slot,
    fetch_lists,
    prolong_blocks,
    prolong_cols,
    restrict_blocks,
    restrict_rows,
):
    rows, half = lax.axis_size("row"), lax.axis_size("near")
    slot_count = fetch_lists.shape[3]
    fine_rows, block_size, width = prolong_blocks.shape
    fetch = fetch_lists.reshape(2 * half, slot_count).T
    own = jnp.stack([lax.axis_index("row"), lax.axis_index("half")])
    own = jnp.concatenate([own, place_of_columns(half)])[None]

    near_blocks = prolong_blocks.reshape(fine_rows * block_size, width)
    far_blocks = far_swap(near_blocks)
    restricted, own_columns, near_blocks = restrict_operator(
        operator_count,
        operator_slot,
        restrict_rows.T,
        fetch,
        operator_blocks,
        restrict_blocks,
        prolong_cols.T,
        near_blocks,
        lax.axis_index("half").reshape(1),
    )
    restricted = lax.all_to_all(restricted, "near", split_axis=0, concat_axis=0, tiled=True)
    far_columns = far_swap(own_columns)
    near_pieces = spread_over_rows(near_blocks, rows)
    far_blocks = append_columns(near_pieces[rows // 2], far_columns, own_columns, far_blocks)
    pieces = near_pieces + spread_over_rows(far_blocks, rows)
    sums = combine(own, restricted, pieces, NCR * rows, slot_count, fine_rows, block_size)
    return add_over_columns(sums, half).T


def solution(mesh):
    rows, columns = mesh.shape["row"], mesh.shape["col"]
    split = Mesh(mesh.devices.reshape(rows, 2, columns // 2), ("row", "half", "near"))
    flat = ("row", "half", "near")
    return jax.shard_map(
        local,
        mesh=split,
        in_specs=(
            P(flat, None, None),
            P(flat),
            P(flat, None),
            P("row", ("half", "near"), None, None),
            P(flat, None, None),
            P(flat, None),
            P(flat, None, None),
            P(flat, None),
        ),
        out_specs=P("row", ("half", "near")),
        check_vma=False,
    )
```

```python
import functools

import jax
import jax.numpy as jnp
from jax import lax
from jax.experimental import pallas as pl
from jax.experimental.pallas import tpu as pltpu
from jax.sharding import Mesh
from jax.sharding import PartitionSpec as P

NCR = 2
LANES = 128
EXTRA = 8
HOLD_FLOPS = 16 << 30
COLUMN_FLOPS = 3 << 30
VMEM_LIMIT = 48 * 1024 * 1024


def halves(x):
    high = x.astype(jnp.bfloat16)
    return high, (x - high.astype(jnp.float32)).astype(jnp.bfloat16)


def transposed_product(left, right):
    tall = jnp.concatenate(halves(left), axis=0)
    wide = jnp.concatenate(halves(right), axis=1)
    wide = jnp.concatenate([wide, wide], axis=0)
    both = lax.dot_general(tall, wide, (((0,), (0,)), ((), ())), preferred_element_type=jnp.float32)
    width = right.shape[1]
    return both[:, :width] + both[:, width:]


def column_kernel(far_columns_ref, own_columns_ref, out_ref):
    entries, fine_rows = own_columns_ref.shape
    out_ref[...] = jnp.zeros_like(out_ref)
    out_ref[:entries, :fine_rows] = far_columns_ref[...].astype(jnp.float32)
    out_ref[entries : 2 * entries, :fine_rows] = own_columns_ref[...].astype(jnp.float32)


def column_rows(far_columns, own_columns):
    return pl.pallas_call(
        column_kernel,
        out_shape=jax.ShapeDtypeStruct((EXTRA, LANES), jnp.float32),
        in_specs=[pl.BlockSpec(memory_space=pltpu.VMEM)] * 2,
        out_specs=pl.BlockSpec(memory_space=pltpu.VMEM),
        compiler_params=pltpu.CompilerParams(vmem_limit_bytes=VMEM_LIMIT),
        cost_estimate=pl.CostEstimate(flops=COLUMN_FLOPS, bytes_accessed=COLUMN_FLOPS >> 8, transcendentals=0),
        name="column_rows",
    )(far_columns, own_columns)


def append_kernel(next_ref, extra_ref, blocks_ref, out_ref):
    used = blocks_ref.shape[0]
    out_ref[:used] = blocks_ref[...]
    out_ref[used:] = extra_ref[...]


def append_columns(next_blocks, extra, blocks):
    used, width = blocks.shape
    return pl.pallas_call(
        append_kernel,
        out_shape=jax.ShapeDtypeStruct((used + EXTRA, width), blocks.dtype),
        in_specs=[pl.BlockSpec(memory_space=pltpu.VMEM)] * 3,
        out_specs=pl.BlockSpec(memory_space=pltpu.VMEM),
        compiler_params=pltpu.CompilerParams(vmem_limit_bytes=VMEM_LIMIT),
        cost_estimate=pl.CostEstimate(flops=HOLD_FLOPS, bytes_accessed=HOLD_FLOPS >> 8, transcendentals=0),
        name="append_columns",
    )(next_blocks, extra, blocks)


def restrict_kernel(
    count_any, slot_any, rows_any, fetch_any, restrict_any, operator_any, columns_any, blocks_any, side_any,
    out_ref, own_columns_ref, own_blocks_ref,
    count_ref, slot_ref, rows_ref, fetch_ref, side_ref, restrict_ref, operator_ref, sems, operator_sems,
):
    fine_rows, block_size, _ = operator_ref.shape
    entries = slot_ref.shape[1]
    slot_count, columns = fetch_ref.shape
    half = columns // 2
    used = 2 * slot_count * block_size
    wide = NCR * block_size

    pairs = [
        (count_any, count_ref), (slot_any, slot_ref), (rows_any, rows_ref),
        (fetch_any, fetch_ref), (restrict_any, restrict_ref),
        (columns_any, own_columns_ref), (blocks_any, own_blocks_ref), (side_any, side_ref),
    ]
    copies = [pltpu.make_async_copy(a, b, sems.at[i]) for i, (a, b) in enumerate(pairs)]
    operators = [
        pltpu.make_async_copy(operator_any.at[i], operator_ref.at[i], operator_sems.at[i]) for i in range(fine_rows)
    ]
    for copy in copies + operators:
        copy.start()

    lane = lax.broadcasted_iota(jnp.int32, (block_size, wide), 1)
    second = (lane >= block_size).astype(jnp.int32)
    short_lane = lax.broadcasted_iota(jnp.int32, (EXTRA, wide), 1)
    for near in range(half):
        out_ref[near, :used] = jnp.zeros((used, wide), jnp.float32)
    for copy in copies + operators:
        copy.wait()

    for near in range(half):
        value = jnp.zeros((EXTRA, wide), jnp.int32)
        for side in range(2):
            for s in range(slot_count):
                turned = near ^ jnp.where(side_ref[0] == side, 0, half // 2)
                wanted = fetch_ref[s, side * half + turned]
                value = jnp.where(short_lane == side * slot_count + s, wanted, value)
        out_ref[near, used:] = value.astype(jnp.float32)

    for i in range(fine_rows):
        value = restrict_ref[i]
        swapped = pltpu.roll(value, block_size, 1)
        own_row = jnp.where(second == 0, rows_ref[0, i], rows_ref[1, i])
        other_row = jnp.where(second == 0, rows_ref[1, i], rows_ref[0, i])
        dense = jnp.where(own_row == second, value, 0.0) + jnp.where(other_row == second, swapped, 0.0)
        product = transposed_product(operator_ref[i], dense)
        for k in range(entries):
            part = jnp.where(k < count_ref[i], product[k * block_size : (k + 1) * block_size], 0.0)
            peer = lax.div(slot_ref[i, k], slot_count)
            side = lax.div(peer, half)
            place = side * slot_count + lax.rem(slot_ref[i, k], slot_count)
            near = lax.rem(peer, half) ^ jnp.where(side_ref[0] == side, 0, half // 2)
            start = pl.multiple_of(place * block_size, block_size)
            out_ref[near, pl.ds(start, block_size)] += part


def restrict_operator(
    operator_count, operator_slot, restrict_rows, fetch, operator_blocks, restrict_blocks, own_columns, own_blocks, side
):
    fine_rows, block_size, width = operator_blocks.shape
    slot_count, columns = fetch.shape
    wide = NCR * block_size
    rows = 2 * slot_count * block_size + EXTRA
    small = (operator_count, operator_slot, restrict_rows, fetch)
    kept = small + (side,)
    return pl.pallas_call(
        restrict_kernel,
        out_shape=(
            jax.ShapeDtypeStruct((columns // 2, rows, wide), jnp.float32),
            jax.ShapeDtypeStruct(own_columns.shape, own_columns.dtype),
            jax.ShapeDtypeStruct(own_blocks.shape, own_blocks.dtype),
        ),
        in_specs=[pl.BlockSpec(memory_space=pltpu.HBM)] * 9,
        out_specs=[pl.BlockSpec(memory_space=pltpu.VMEM)] * 3,
        scratch_shapes=[pltpu.SMEM(x.shape, x.dtype) for x in kept]
        + [pltpu.VMEM(x.shape, x.dtype) for x in (restrict_blocks, operator_blocks)]
        + [pltpu.SemaphoreType.DMA((8,)), pltpu.SemaphoreType.DMA((fine_rows,))],
        cost_estimate=pl.CostEstimate(
            flops=6 * fine_rows * block_size * width * wide, bytes_accessed=4 << 20, transcendentals=0
        ),
        name="restrict_operator",
    )(*small, restrict_blocks, operator_blocks, own_columns, own_blocks, side)


def combine_kernel(own_ref, restricted_ref, *rest, slot_count, fine_rows, entries):
    pieces, (out_ref, held_ref, table_ref, index_ref, sem) = rest[:-5], rest[-5:]
    half = restricted_ref.shape[0]
    rows = len(pieces) // 2
    block_size = out_ref.shape[1]
    columns = 2 * half
    used = 2 * slot_count * block_size
    held = fine_rows * block_size

    table_ref[:1, : own_ref.shape[1]] = own_ref[...]
    for near in range(half):
        table_ref[1 + near : 2 + near] = restricted_ref[near, used : used + 1].astype(jnp.int32)
    for i, piece in enumerate(pieces[rows:]):
        for far in range(2):
            first = 1 + half + entries * (far * rows + i)
            row = held + entries * (1 - far)
            table_ref[first : first + entries] = piece[row : row + entries].astype(jnp.int32)
    copy = pltpu.make_async_copy(table_ref, index_ref, sem)
    copy.start()
    for i, piece in enumerate(pieces):
        held_ref[i] = piece[...] if i < rows else piece[:held]
    out_ref[...] = jnp.zeros_like(out_ref)
    copy.wait()

    def step(i, carry):
        near = lax.div(i, 2 * slot_count)
        place = lax.rem(i, 2 * slot_count)
        wanted = index_ref[1 + near, place]
        inside = lax.rem(wanted, fine_rows)
        far = lax.div(place, slot_count) ^ index_ref[0, 1]
        piece = far * rows + (lax.div(wanted, fine_rows * columns) ^ index_ref[0, 0])
        block = held_ref[piece, pl.ds(pl.multiple_of(inside * block_size, block_size), block_size)]
        restricted = restricted_ref[near, pl.ds(pl.multiple_of(place * block_size, block_size), block_size)]
        product = transposed_product(block, restricted)
        for m in range(entries):
            column = index_ref[0, 2 + index_ref[1 + half + entries * piece + m, inside]]
            out_ref[column] += product[m * block_size : (m + 1) * block_size]
        return carry

    lax.fori_loop(0, half * 2 * slot_count, step, 0, unroll=16)


def combine(own, restricted, pieces, coarse_all, slot_count, fine_rows, block_size):
    half, _, wide = restricted.shape
    width = pieces[0].shape[1]
    entries = width // block_size
    table_rows = -(-(1 + half + entries * len(pieces)) // 8) * 8
    return pl.pallas_call(
        functools.partial(combine_kernel, slot_count=slot_count, fine_rows=fine_rows, entries=entries),
        out_shape=jax.ShapeDtypeStruct((coarse_all, block_size, wide), jnp.float32),
        in_specs=[pl.BlockSpec(memory_space=pltpu.VMEM)] * (2 + len(pieces)),
        out_specs=pl.BlockSpec(memory_space=pltpu.VMEM),
        scratch_shapes=[
            pltpu.VMEM((len(pieces), fine_rows * block_size, width), jnp.float32),
            pltpu.VMEM((table_rows, LANES), jnp.int32),
            pltpu.SMEM((table_rows, LANES), jnp.int32),
            pltpu.SemaphoreType.DMA,
        ],
        compiler_params=pltpu.CompilerParams(vmem_limit_bytes=VMEM_LIMIT),
        cost_estimate=pl.CostEstimate(flops=1 << 28, bytes_accessed=4 << 20, transcendentals=0),
        name="combine",
    )(own, restricted, *pieces)


def row_swap(x, bit):
    return lax.ppermute(x, "row", [(r, r ^ bit) for r in range(lax.axis_size("row"))])


def half_swap(x):
    return lax.ppermute(x, "half", [(0, 1), (1, 0)])


def far_swap(x):
    half = lax.axis_size("near")
    pairs = [(h * half + n, (1 - h) * half + (n ^ half // 2)) for h in range(2) for n in range(half)]
    return lax.ppermute(x, ("half", "near"), pairs)


def spread_over_rows(blocks, rows):
    pieces = {0: blocks}
    bit = rows // 2
    while bit:
        for mask in list(pieces):
            pieces[mask ^ bit] = row_swap(pieces[mask], bit)
        bit //= 2
    return [pieces[mask] for mask in range(rows)]


def place_of_columns(half):
    own = lax.axis_index("half") * half + lax.axis_index("near")
    ahead = jnp.arange(2 * half, dtype=jnp.int32) ^ own
    return ahead % half * 2 + ahead // half


def add_over_columns(sums, half):
    total = sums[:2]
    for near in range(1, half):
        total = total + lax.ppermute(sums[2 * near : 2 * near + 2], "near", [(n, n ^ near) for n in range(half)])
    return total[0] + half_swap(total[1])


def local(
    operator_blocks,
    operator_count,
    operator_slot,
    fetch_lists,
    prolong_blocks,
    prolong_cols,
    restrict_blocks,
    restrict_rows,
):
    rows, half = lax.axis_size("row"), lax.axis_size("near")
    slot_count = fetch_lists.shape[3]
    fine_rows, block_size, width = prolong_blocks.shape
    fetch = fetch_lists.reshape(2 * half, slot_count).T
    own = jnp.stack([lax.axis_index("row"), lax.axis_index("half")])
    own = jnp.concatenate([own, place_of_columns(half)])[None]

    near_blocks = prolong_blocks.reshape(fine_rows * block_size, width)
    far_blocks = far_swap(near_blocks)
    restricted, own_columns, near_blocks = restrict_operator(
        operator_count,
        operator_slot,
        restrict_rows.T,
        fetch,
        operator_blocks,
        restrict_blocks,
        prolong_cols.T,
        near_blocks,
        lax.axis_index("half").reshape(1),
    )
    restricted = lax.all_to_all(restricted, "near", split_axis=0, concat_axis=0, tiled=True)
    far_columns = far_swap(own_columns)
    near_pieces = spread_over_rows(near_blocks, rows)
    far_blocks = append_columns(near_pieces[rows // 2], column_rows(far_columns, own_columns), far_blocks)
    pieces = near_pieces + spread_over_rows(far_blocks, rows)
    sums = combine(own, restricted, pieces, NCR * rows, slot_count, fine_rows, block_size)
    return add_over_columns(sums, half).T


def solution(mesh):
    rows, columns = mesh.shape["row"], mesh.shape["col"]
    split = Mesh(mesh.devices.reshape(rows, 2, columns // 2), ("row", "half", "near"))
    flat = ("row", "half", "near")
    return jax.shard_map(
        local,
        mesh=split,
        in_specs=(
            P(flat, None, None),
            P(flat),
            P(flat, None),
            P("row", ("half", "near"), None, None),
            P(flat, None, None),
            P(flat, None),
            P(flat, None, None),
            P(flat, None),
        ),
        out_specs=P("row", ("half", "near")),
        check_vma=False,
    )
```

```python
import functools

import jax
import jax.numpy as jnp
from jax import lax
from jax.experimental import pallas as pl
from jax.experimental.pallas import tpu as pltpu
from jax.sharding import Mesh
from jax.sharding import PartitionSpec as P

NCR = 2
LANES = 128
EXTRA = 8
HOLD_FLOPS = 16 << 30
COLUMN_FLOPS = 3 << 29
VMEM_LIMIT = 48 * 1024 * 1024


def halves(x):
    high = x.astype(jnp.bfloat16)
    return high, (x - high.astype(jnp.float32)).astype(jnp.bfloat16)


def transposed_product(left, right):
    tall = jnp.concatenate(halves(left), axis=0)
    wide = jnp.concatenate(halves(right), axis=1)
    wide = jnp.concatenate([wide, wide], axis=0)
    both = lax.dot_general(tall, wide, (((0,), (0,)), ((), ())), preferred_element_type=jnp.float32)
    width = right.shape[1]
    return both[:, :width] + both[:, width:]


def column_kernel(far_columns_ref, own_columns_ref, out_ref):
    entries, fine_rows = own_columns_ref.shape
    out_ref[...] = jnp.zeros_like(out_ref)
    out_ref[:entries, :fine_rows] = far_columns_ref[...].astype(jnp.float32)
    out_ref[entries : 2 * entries, :fine_rows] = own_columns_ref[...].astype(jnp.float32)


def column_rows(far_columns, own_columns):
    return pl.pallas_call(
        column_kernel,
        out_shape=jax.ShapeDtypeStruct((EXTRA, LANES), jnp.float32),
        in_specs=[pl.BlockSpec(memory_space=pltpu.VMEM)] * 2,
        out_specs=pl.BlockSpec(memory_space=pltpu.VMEM),
        compiler_params=pltpu.CompilerParams(vmem_limit_bytes=VMEM_LIMIT),
        cost_estimate=pl.CostEstimate(flops=COLUMN_FLOPS, bytes_accessed=COLUMN_FLOPS >> 8, transcendentals=0),
        name="column_rows",
    )(far_columns, own_columns)


def append_kernel(next_ref, extra_ref, blocks_ref, out_ref):
    used = blocks_ref.shape[0]
    out_ref[:used] = blocks_ref[...]
    out_ref[used:] = extra_ref[...]


def append_columns(next_blocks, extra, blocks):
    used, width = blocks.shape
    return pl.pallas_call(
        append_kernel,
        out_shape=jax.ShapeDtypeStruct((used + EXTRA, width), blocks.dtype),
        in_specs=[pl.BlockSpec(memory_space=pltpu.VMEM)] * 3,
        out_specs=pl.BlockSpec(memory_space=pltpu.VMEM),
        compiler_params=pltpu.CompilerParams(vmem_limit_bytes=VMEM_LIMIT),
        cost_estimate=pl.CostEstimate(flops=HOLD_FLOPS, bytes_accessed=HOLD_FLOPS >> 8, transcendentals=0),
        name="append_columns",
    )(next_blocks, extra, blocks)


def restrict_kernel(
    count_any, slot_any, rows_any, fetch_any, restrict_any, operator_any, columns_any, blocks_any, side_any,
    out_ref, own_columns_ref, own_blocks_ref,
    count_ref, slot_ref, rows_ref, fetch_ref, side_ref, restrict_ref, operator_ref, sems, operator_sems,
):
    fine_rows, block_size, _ = operator_ref.shape
    entries = slot_ref.shape[1]
    slot_count, columns = fetch_ref.shape
    half = columns // 2
    used = 2 * slot_count * block_size
    wide = NCR * block_size

    pairs = [
        (count_any, count_ref), (slot_any, slot_ref), (rows_any, rows_ref),
        (fetch_any, fetch_ref), (restrict_any, restrict_ref),
        (columns_any, own_columns_ref), (blocks_any, own_blocks_ref), (side_any, side_ref),
    ]
    copies = [pltpu.make_async_copy(a, b, sems.at[i]) for i, (a, b) in enumerate(pairs)]
    operators = [
        pltpu.make_async_copy(operator_any.at[i], operator_ref.at[i], operator_sems.at[i]) for i in range(fine_rows)
    ]
    for copy in copies + operators:
        copy.start()

    lane = lax.broadcasted_iota(jnp.int32, (block_size, wide), 1)
    second = (lane >= block_size).astype(jnp.int32)
    short_lane = lax.broadcasted_iota(jnp.int32, (EXTRA, wide), 1)
    for near in range(half):
        out_ref[near, :used] = jnp.zeros((used, wide), jnp.float32)
    for copy in copies + operators:
        copy.wait()

    for near in range(half):
        value = jnp.zeros((EXTRA, wide), jnp.int32)
        for side in range(2):
            for s in range(slot_count):
                turned = near ^ jnp.where(side_ref[0] == side, 0, half // 2)
                wanted = fetch_ref[s, side * half + turned]
                value = jnp.where(short_lane == side * slot_count + s, wanted, value)
        out_ref[near, used:] = value.astype(jnp.float32)

    for i in range(fine_rows):
        value = restrict_ref[i]
        swapped = pltpu.roll(value, block_size, 1)
        own_row = jnp.where(second == 0, rows_ref[0, i], rows_ref[1, i])
        other_row = jnp.where(second == 0, rows_ref[1, i], rows_ref[0, i])
        dense = jnp.where(own_row == second, value, 0.0) + jnp.where(other_row == second, swapped, 0.0)
        product = transposed_product(operator_ref[i], dense)
        for k in range(entries):
            part = jnp.where(k < count_ref[i], product[k * block_size : (k + 1) * block_size], 0.0)
            peer = lax.div(slot_ref[i, k], slot_count)
            side = lax.div(peer, half)
            place = side * slot_count + lax.rem(slot_ref[i, k], slot_count)
            near = lax.rem(peer, half) ^ jnp.where(side_ref[0] == side, 0, half // 2)
            start = pl.multiple_of(place * block_size, block_size)
            out_ref[near, pl.ds(start, block_size)] += part


def restrict_operator(
    operator_count, operator_slot, restrict_rows, fetch, operator_blocks, restrict_blocks, own_columns, own_blocks, side
):
    fine_rows, block_size, width = operator_blocks.shape
    slot_count, columns = fetch.shape
    wide = NCR * block_size
    rows = 2 * slot_count * block_size + EXTRA
    small = (operator_count, operator_slot, restrict_rows, fetch)
    kept = small + (side,)
    return pl.pallas_call(
        restrict_kernel,
        out_shape=(
            jax.ShapeDtypeStruct((columns // 2, rows, wide), jnp.float32),
            jax.ShapeDtypeStruct(own_columns.shape, own_columns.dtype),
            jax.ShapeDtypeStruct(own_blocks.shape, own_blocks.dtype),
        ),
        in_specs=[pl.BlockSpec(memory_space=pltpu.HBM)] * 9,
        out_specs=[pl.BlockSpec(memory_space=pltpu.VMEM)] * 3,
        scratch_shapes=[pltpu.SMEM(x.shape, x.dtype) for x in kept]
        + [pltpu.VMEM(x.shape, x.dtype) for x in (restrict_blocks, operator_blocks)]
        + [pltpu.SemaphoreType.DMA((8,)), pltpu.SemaphoreType.DMA((fine_rows,))],
        cost_estimate=pl.CostEstimate(
            flops=6 * fine_rows * block_size * width * wide, bytes_accessed=4 << 20, transcendentals=0
        ),
        name="restrict_operator",
    )(*small, restrict_blocks, operator_blocks, own_columns, own_blocks, side)


def combine_kernel(own_ref, restricted_ref, *rest, slot_count, fine_rows, entries):
    pieces, (out_ref, held_ref, table_ref, index_ref, sem) = rest[:-5], rest[-5:]
    half = restricted_ref.shape[0]
    rows = len(pieces) // 2
    block_size = out_ref.shape[1]
    columns = 2 * half
    used = 2 * slot_count * block_size
    held = fine_rows * block_size

    table_ref[:1, : own_ref.shape[1]] = own_ref[...]
    for near in range(half):
        table_ref[1 + near : 2 + near] = restricted_ref[near, used : used + 1].astype(jnp.int32)
    for i, piece in enumerate(pieces[rows:]):
        for far in range(2):
            first = 1 + half + entries * (far * rows + i)
            row = held + entries * (1 - far)
            table_ref[first : first + entries] = piece[row : row + entries].astype(jnp.int32)
    copy = pltpu.make_async_copy(table_ref, index_ref, sem)
    copy.start()
    for i, piece in enumerate(pieces):
        held_ref[i] = piece[...] if i < rows else piece[:held]
    out_ref[...] = jnp.zeros_like(out_ref)
    copy.wait()

    def step(i, carry):
        near = lax.div(i, 2 * slot_count)
        place = lax.rem(i, 2 * slot_count)
        wanted = index_ref[1 + near, place]
        inside = lax.rem(wanted, fine_rows)
        far = lax.div(place, slot_count) ^ index_ref[0, 1]
        piece = far * rows + (lax.div(wanted, fine_rows * columns) ^ index_ref[0, 0])
        block = held_ref[piece, pl.ds(pl.multiple_of(inside * block_size, block_size), block_size)]
        restricted = restricted_ref[near, pl.ds(pl.multiple_of(place * block_size, block_size), block_size)]
        product = transposed_product(block, restricted)
        for m in range(entries):
            column = index_ref[0, 2 + index_ref[1 + half + entries * piece + m, inside]]
            out_ref[column] += product[m * block_size : (m + 1) * block_size]
        return carry

    lax.fori_loop(0, half * 2 * slot_count, step, 0, unroll=16)


def combine(own, restricted, pieces, coarse_all, slot_count, fine_rows, block_size):
    half, _, wide = restricted.shape
    width = pieces[0].shape[1]
    entries = width // block_size
    table_rows = -(-(1 + half + entries * len(pieces)) // 8) * 8
    return pl.pallas_call(
        functools.partial(combine_kernel, slot_count=slot_count, fine_rows=fine_rows, entries=entries),
        out_shape=jax.ShapeDtypeStruct((coarse_all, block_size, wide), jnp.float32),
        in_specs=[pl.BlockSpec(memory_space=pltpu.VMEM)] * (2 + len(pieces)),
        out_specs=pl.BlockSpec(memory_space=pltpu.VMEM),
        scratch_shapes=[
            pltpu.VMEM((len(pieces), fine_rows * block_size, width), jnp.float32),
            pltpu.VMEM((table_rows, LANES), jnp.int32),
            pltpu.SMEM((table_rows, LANES), jnp.int32),
            pltpu.SemaphoreType.DMA,
        ],
        compiler_params=pltpu.CompilerParams(vmem_limit_bytes=VMEM_LIMIT),
        cost_estimate=pl.CostEstimate(flops=1 << 28, bytes_accessed=4 << 20, transcendentals=0),
        name="combine",
    )(own, restricted, *pieces)


def row_swap(x, bit):
    return lax.ppermute(x, "row", [(r, r ^ bit) for r in range(lax.axis_size("row"))])


def half_swap(x):
    return lax.ppermute(x, "half", [(0, 1), (1, 0)])


def far_swap(x):
    half = lax.axis_size("near")
    pairs = [(h * half + n, (1 - h) * half + (n ^ half // 2)) for h in range(2) for n in range(half)]
    return lax.ppermute(x, ("half", "near"), pairs)


def spread_over_rows(blocks, rows):
    pieces = {0: blocks}
    bit = rows // 2
    while bit:
        for mask in list(pieces):
            pieces[mask ^ bit] = row_swap(pieces[mask], bit)
        bit //= 2
    return [pieces[mask] for mask in range(rows)]


def place_of_columns(half):
    own = lax.axis_index("half") * half + lax.axis_index("near")
    ahead = jnp.arange(2 * half, dtype=jnp.int32) ^ own
    return ahead % half * 2 + ahead // half


def add_over_columns(sums, half):
    total = sums[:2]
    for near in range(1, half):
        total = total + lax.ppermute(sums[2 * near : 2 * near + 2], "near", [(n, n ^ near) for n in range(half)])
    return total[0] + half_swap(total[1])


def local(
    operator_blocks,
    operator_count,
    operator_slot,
    fetch_lists,
    prolong_blocks,
    prolong_cols,
    restrict_blocks,
    restrict_rows,
):
    rows, half = lax.axis_size("row"), lax.axis_size("near")
    slot_count = fetch_lists.shape[3]
    fine_rows, block_size, width = prolong_blocks.shape
    fetch = fetch_lists.reshape(2 * half, slot_count).T
    own = jnp.stack([lax.axis_index("row"), lax.axis_index("half")])
    own = jnp.concatenate([own, place_of_columns(half)])[None]

    near_blocks = prolong_blocks.reshape(fine_rows * block_size, width)
    far_blocks = far_swap(near_blocks)
    restricted, own_columns, near_blocks = restrict_operator(
        operator_count,
        operator_slot,
        restrict_rows.T,
        fetch,
        operator_blocks,
        restrict_blocks,
        prolong_cols.T,
        near_blocks,
        lax.axis_index("half").reshape(1),
    )
    restricted = lax.all_to_all(restricted, "near", split_axis=0, concat_axis=0, tiled=True)
    far_columns = far_swap(own_columns)
    near_pieces = spread_over_rows(near_blocks, rows)
    far_blocks = append_columns(near_pieces[rows // 2], column_rows(far_columns, own_columns), far_blocks)
    pieces = near_pieces + spread_over_rows(far_blocks, rows)
    sums = combine(own, restricted, pieces, NCR * rows, slot_count, fine_rows, block_size)
    return add_over_columns(sums, half).T


def solution(mesh):
    rows, columns = mesh.shape["row"], mesh.shape["col"]
    split = Mesh(mesh.devices.reshape(rows, 2, columns // 2), ("row", "half", "near"))
    flat = ("row", "half", "near")
    return jax.shard_map(
        local,
        mesh=split,
        in_specs=(
            P(flat, None, None),
            P(flat),
            P(flat, None),
            P("row", ("half", "near"), None, None),
            P(flat, None, None),
            P(flat, None),
            P(flat, None, None),
            P(flat, None),
        ),
        out_specs=P("row", ("half", "near")),
        check_vma=False,
    )
```

```python
import functools

import jax
import jax.numpy as jnp
from jax import lax
from jax.experimental import pallas as pl
from jax.experimental.pallas import tpu as pltpu
from jax.sharding import Mesh
from jax.sharding import PartitionSpec as P

NCR = 2
LANES = 128
EXTRA = 8
HOLD_FLOPS = 16 << 30
COLUMN_FLOPS = 9 << 28
VMEM_LIMIT = 48 * 1024 * 1024


def halves(x):
    high = x.astype(jnp.bfloat16)
    return high, (x - high.astype(jnp.float32)).astype(jnp.bfloat16)


def transposed_product(left, right):
    tall = jnp.concatenate(halves(left), axis=0)
    wide = jnp.concatenate(halves(right), axis=1)
    wide = jnp.concatenate([wide, wide], axis=0)
    both = lax.dot_general(tall, wide, (((0,), (0,)), ((), ())), preferred_element_type=jnp.float32)
    width = right.shape[1]
    return both[:, :width] + both[:, width:]


def column_kernel(far_columns_ref, own_columns_ref, out_ref):
    entries, fine_rows = own_columns_ref.shape
    out_ref[...] = jnp.zeros_like(out_ref)
    out_ref[:entries, :fine_rows] = far_columns_ref[...].astype(jnp.float32)
    out_ref[entries : 2 * entries, :fine_rows] = own_columns_ref[...].astype(jnp.float32)


def column_rows(far_columns, own_columns):
    return pl.pallas_call(
        column_kernel,
        out_shape=jax.ShapeDtypeStruct((EXTRA, LANES), jnp.float32),
        in_specs=[pl.BlockSpec(memory_space=pltpu.VMEM)] * 2,
        out_specs=pl.BlockSpec(memory_space=pltpu.VMEM),
        compiler_params=pltpu.CompilerParams(vmem_limit_bytes=VMEM_LIMIT),
        cost_estimate=pl.CostEstimate(flops=COLUMN_FLOPS, bytes_accessed=COLUMN_FLOPS >> 8, transcendentals=0),
        name="column_rows",
    )(far_columns, own_columns)


def append_kernel(next_ref, extra_ref, blocks_ref, out_ref):
    used = blocks_ref.shape[0]
    out_ref[:used] = blocks_ref[...]
    out_ref[used:] = extra_ref[...]


def append_columns(next_blocks, extra, blocks):
    used, width = blocks.shape
    return pl.pallas_call(
        append_kernel,
        out_shape=jax.ShapeDtypeStruct((used + EXTRA, width), blocks.dtype),
        in_specs=[pl.BlockSpec(memory_space=pltpu.VMEM)] * 3,
        out_specs=pl.BlockSpec(memory_space=pltpu.VMEM),
        compiler_params=pltpu.CompilerParams(vmem_limit_bytes=VMEM_LIMIT),
        cost_estimate=pl.CostEstimate(flops=HOLD_FLOPS, bytes_accessed=HOLD_FLOPS >> 8, transcendentals=0),
        name="append_columns",
    )(next_blocks, extra, blocks)


def restrict_kernel(
    count_any, slot_any, rows_any, fetch_any, restrict_any, operator_any, columns_any, blocks_any, side_any,
    out_ref, own_columns_ref, own_blocks_ref,
    count_ref, slot_ref, rows_ref, fetch_ref, side_ref, restrict_ref, operator_ref, sems, operator_sems,
):
    fine_rows, block_size, _ = operator_ref.shape
    entries = slot_ref.shape[1]
    slot_count, columns = fetch_ref.shape
    half = columns // 2
    used = 2 * slot_count * block_size
    wide = NCR * block_size

    pairs = [
        (count_any, count_ref), (slot_any, slot_ref), (rows_any, rows_ref),
        (fetch_any, fetch_ref), (restrict_any, restrict_ref),
        (columns_any, own_columns_ref), (blocks_any, own_blocks_ref), (side_any, side_ref),
    ]
    copies = [pltpu.make_async_copy(a, b, sems.at[i]) for i, (a, b) in enumerate(pairs)]
    operators = [
        pltpu.make_async_copy(operator_any.at[i], operator_ref.at[i], operator_sems.at[i]) for i in range(fine_rows)
    ]
    for copy in copies + operators:
        copy.start()

    lane = lax.broadcasted_iota(jnp.int32, (block_size, wide), 1)
    second = (lane >= block_size).astype(jnp.int32)
    short_lane = lax.broadcasted_iota(jnp.int32, (EXTRA, wide), 1)
    for near in range(half):
        out_ref[near, :used] = jnp.zeros((used, wide), jnp.float32)
    for copy in copies + operators:
        copy.wait()

    for near in range(half):
        value = jnp.zeros((EXTRA, wide), jnp.int32)
        for side in range(2):
            for s in range(slot_count):
                turned = near ^ jnp.where(side_ref[0] == side, 0, half // 2)
                wanted = fetch_ref[s, side * half + turned]
                value = jnp.where(short_lane == side * slot_count + s, wanted, value)
        out_ref[near, used:] = value.astype(jnp.float32)

    for i in range(fine_rows):
        value = restrict_ref[i]
        swapped = pltpu.roll(value, block_size, 1)
        own_row = jnp.where(second == 0, rows_ref[0, i], rows_ref[1, i])
        other_row = jnp.where(second == 0, rows_ref[1, i], rows_ref[0, i])
        dense = jnp.where(own_row == second, value, 0.0) + jnp.where(other_row == second, swapped, 0.0)
        product = transposed_product(operator_ref[i], dense)
        for k in range(entries):
            part = jnp.where(k < count_ref[i], product[k * block_size : (k + 1) * block_size], 0.0)
            peer = lax.div(slot_ref[i, k], slot_count)
            side = lax.div(peer, half)
            place = side * slot_count + lax.rem(slot_ref[i, k], slot_count)
            near = lax.rem(peer, half) ^ jnp.where(side_ref[0] == side, 0, half // 2)
            start = pl.multiple_of(place * block_size, block_size)
            out_ref[near, pl.ds(start, block_size)] += part


def restrict_operator(
    operator_count, operator_slot, restrict_rows, fetch, operator_blocks, restrict_blocks, own_columns, own_blocks, side
):
    fine_rows, block_size, width = operator_blocks.shape
    slot_count, columns = fetch.shape
    wide = NCR * block_size
    rows = 2 * slot_count * block_size + EXTRA
    small = (operator_count, operator_slot, restrict_rows, fetch)
    kept = small + (side,)
    return pl.pallas_call(
        restrict_kernel,
        out_shape=(
            jax.ShapeDtypeStruct((columns // 2, rows, wide), jnp.float32),
            jax.ShapeDtypeStruct(own_columns.shape, own_columns.dtype),
            jax.ShapeDtypeStruct(own_blocks.shape, own_blocks.dtype),
        ),
        in_specs=[pl.BlockSpec(memory_space=pltpu.HBM)] * 9,
        out_specs=[pl.BlockSpec(memory_space=pltpu.VMEM)] * 3,
        scratch_shapes=[pltpu.SMEM(x.shape, x.dtype) for x in kept]
        + [pltpu.VMEM(x.shape, x.dtype) for x in (restrict_blocks, operator_blocks)]
        + [pltpu.SemaphoreType.DMA((8,)), pltpu.SemaphoreType.DMA((fine_rows,))],
        cost_estimate=pl.CostEstimate(
            flops=6 * fine_rows * block_size * width * wide, bytes_accessed=4 << 20, transcendentals=0
        ),
        name="restrict_operator",
    )(*small, restrict_blocks, operator_blocks, own_columns, own_blocks, side)


def combine_kernel(own_ref, restricted_ref, *rest, slot_count, fine_rows, entries):
    pieces, (out_ref, held_ref, table_ref, index_ref, sem) = rest[:-5], rest[-5:]
    half = restricted_ref.shape[0]
    rows = len(pieces) // 2
    block_size = out_ref.shape[1]
    columns = 2 * half
    used = 2 * slot_count * block_size
    held = fine_rows * block_size

    table_ref[:1, : own_ref.shape[1]] = own_ref[...]
    for near in range(half):
        table_ref[1 + near : 2 + near] = restricted_ref[near, used : used + 1].astype(jnp.int32)
    for i, piece in enumerate(pieces[rows:]):
        for far in range(2):
            first = 1 + half + entries * (far * rows + i)
            row = held + entries * (1 - far)
            table_ref[first : first + entries] = piece[row : row + entries].astype(jnp.int32)
    copy = pltpu.make_async_copy(table_ref, index_ref, sem)
    copy.start()
    for i, piece in enumerate(pieces):
        held_ref[i] = piece[...] if i < rows else piece[:held]
    out_ref[...] = jnp.zeros_like(out_ref)
    copy.wait()

    def step(i, carry):
        near = lax.div(i, 2 * slot_count)
        place = lax.rem(i, 2 * slot_count)
        wanted = index_ref[1 + near, place]
        inside = lax.rem(wanted, fine_rows)
        far = lax.div(place, slot_count) ^ index_ref[0, 1]
        piece = far * rows + (lax.div(wanted, fine_rows * columns) ^ index_ref[0, 0])
        block = held_ref[piece, pl.ds(pl.multiple_of(inside * block_size, block_size), block_size)]
        restricted = restricted_ref[near, pl.ds(pl.multiple_of(place * block_size, block_size), block_size)]
        product = transposed_product(block, restricted)
        for m in range(entries):
            column = index_ref[0, 2 + index_ref[1 + half + entries * piece + m, inside]]
            out_ref[column] += product[m * block_size : (m + 1) * block_size]
        return carry

    lax.fori_loop(0, half * 2 * slot_count, step, 0, unroll=16)


def combine(own, restricted, pieces, coarse_all, slot_count, fine_rows, block_size):
    half, _, wide = restricted.shape
    width = pieces[0].shape[1]
    entries = width // block_size
    table_rows = -(-(1 + half + entries * len(pieces)) // 8) * 8
    return pl.pallas_call(
        functools.partial(combine_kernel, slot_count=slot_count, fine_rows=fine_rows, entries=entries),
        out_shape=jax.ShapeDtypeStruct((coarse_all, block_size, wide), jnp.float32),
        in_specs=[pl.BlockSpec(memory_space=pltpu.VMEM)] * (2 + len(pieces)),
        out_specs=pl.BlockSpec(memory_space=pltpu.VMEM),
        scratch_shapes=[
            pltpu.VMEM((len(pieces), fine_rows * block_size, width), jnp.float32),
            pltpu.VMEM((table_rows, LANES), jnp.int32),
            pltpu.SMEM((table_rows, LANES), jnp.int32),
            pltpu.SemaphoreType.DMA,
        ],
        compiler_params=pltpu.CompilerParams(vmem_limit_bytes=VMEM_LIMIT),
        cost_estimate=pl.CostEstimate(flops=1 << 28, bytes_accessed=4 << 20, transcendentals=0),
        name="combine",
    )(own, restricted, *pieces)


def row_swap(x, bit):
    return lax.ppermute(x, "row", [(r, r ^ bit) for r in range(lax.axis_size("row"))])


def half_swap(x):
    return lax.ppermute(x, "half", [(0, 1), (1, 0)])


def far_swap(x):
    half = lax.axis_size("near")
    pairs = [(h * half + n, (1 - h) * half + (n ^ half // 2)) for h in range(2) for n in range(half)]
    return lax.ppermute(x, ("half", "near"), pairs)


def spread_over_rows(blocks, rows):
    pieces = {0: blocks}
    bit = rows // 2
    while bit:
        for mask in list(pieces):
            pieces[mask ^ bit] = row_swap(pieces[mask], bit)
        bit //= 2
    return [pieces[mask] for mask in range(rows)]


def place_of_columns(half):
    own = lax.axis_index("half") * half + lax.axis_index("near")
    ahead = jnp.arange(2 * half, dtype=jnp.int32) ^ own
    return ahead % half * 2 + ahead // half


def add_over_columns(sums, half):
    total = sums[:2]
    for near in range(1, half):
        total = total + lax.ppermute(sums[2 * near : 2 * near + 2], "near", [(n, n ^ near) for n in range(half)])
    return total[0] + half_swap(total[1])


def local(
    operator_blocks,
    operator_count,
    operator_slot,
    fetch_lists,
    prolong_blocks,
    prolong_cols,
    restrict_blocks,
    restrict_rows,
):
    rows, half = lax.axis_size("row"), lax.axis_size("near")
    slot_count = fetch_lists.shape[3]
    fine_rows, block_size, width = prolong_blocks.shape
    fetch = fetch_lists.reshape(2 * half, slot_count).T
    own = jnp.stack([lax.axis_index("row"), lax.axis_index("half")])
    own = jnp.concatenate([own, place_of_columns(half)])[None]

    near_blocks = prolong_blocks.reshape(fine_rows * block_size, width)
    far_blocks = far_swap(near_blocks)
    restricted, own_columns, near_blocks = restrict_operator(
        operator_count,
        operator_slot,
        restrict_rows.T,
        fetch,
        operator_blocks,
        restrict_blocks,
        prolong_cols.T,
        near_blocks,
        lax.axis_index("half").reshape(1),
    )
    restricted = lax.all_to_all(restricted, "near", split_axis=0, concat_axis=0, tiled=True)
    far_columns = far_swap(own_columns)
    near_pieces = spread_over_rows(near_blocks, rows)
    far_blocks = append_columns(near_pieces[rows // 2], column_rows(far_columns, own_columns), far_blocks)
    pieces = near_pieces + spread_over_rows(far_blocks, rows)
    sums = combine(own, restricted, pieces, NCR * rows, slot_count, fine_rows, block_size)
    return add_over_columns(sums, half).T


def solution(mesh):
    rows, columns = mesh.shape["row"], mesh.shape["col"]
    split = Mesh(mesh.devices.reshape(rows, 2, columns // 2), ("row", "half", "near"))
    flat = ("row", "half", "near")
    return jax.shard_map(
        local,
        mesh=split,
        in_specs=(
            P(flat, None, None),
            P(flat),
            P(flat, None),
            P("row", ("half", "near"), None, None),
            P(flat, None, None),
            P(flat, None),
            P(flat, None, None),
            P(flat, None),
        ),
        out_specs=P("row", ("half", "near")),
        check_vma=False,
    )
```

```python
import functools

import jax
import jax.numpy as jnp
from jax import lax
from jax.experimental import pallas as pl
from jax.experimental.pallas import tpu as pltpu
from jax.sharding import Mesh
from jax.sharding import PartitionSpec as P

NCR = 2
LANES = 128
EXTRA = 8
HOLD_FLOPS = 16 << 30
VMEM_LIMIT = 48 * 1024 * 1024


def halves(x):
    high = x.astype(jnp.bfloat16)
    return high, (x - high.astype(jnp.float32)).astype(jnp.bfloat16)


def transposed_product(left, right):
    tall = jnp.concatenate(halves(left), axis=0)
    wide = jnp.concatenate(halves(right), axis=1)
    wide = jnp.concatenate([wide, wide], axis=0)
    both = lax.dot_general(tall, wide, (((0,), (0,)), ((), ())), preferred_element_type=jnp.float32)
    width = right.shape[1]
    return both[:, :width] + both[:, width:]


def append_kernel(next_ref, far_columns_ref, own_columns_ref, blocks_ref, out_ref):
    used = blocks_ref.shape[0]
    entries, fine_rows = own_columns_ref.shape
    out_ref[:used] = blocks_ref[...]
    out_ref[used:] = jnp.zeros((EXTRA, out_ref.shape[1]), jnp.float32)
    out_ref[used : used + entries, :fine_rows] = far_columns_ref[...].astype(jnp.float32)
    out_ref[used + entries : used + 2 * entries, :fine_rows] = own_columns_ref[...].astype(jnp.float32)


def append_columns(next_blocks, far_columns, own_columns, blocks):
    used, width = blocks.shape
    return pl.pallas_call(
        append_kernel,
        out_shape=jax.ShapeDtypeStruct((used + EXTRA, width), blocks.dtype),
        in_specs=[pl.BlockSpec(memory_space=pltpu.VMEM)] * 4,
        out_specs=pl.BlockSpec(memory_space=pltpu.VMEM),
        compiler_params=pltpu.CompilerParams(vmem_limit_bytes=VMEM_LIMIT),
        cost_estimate=pl.CostEstimate(flops=HOLD_FLOPS, bytes_accessed=HOLD_FLOPS >> 8, transcendentals=0),
        name="append_columns",
    )(next_blocks, far_columns, own_columns, blocks)


def restrict_kernel(
    count_any, slot_any, rows_any, fetch_any, restrict_any, operator_any, columns_any, blocks_any, side_any,
    out_ref, own_columns_ref, own_blocks_ref,
    count_ref, slot_ref, rows_ref, fetch_ref, side_ref, restrict_ref, operator_ref, sems, operator_sems,
):
    fine_rows, block_size, _ = operator_ref.shape
    entries = slot_ref.shape[1]
    slot_count, columns = fetch_ref.shape
    half = columns // 2
    used = 2 * slot_count * block_size
    wide = NCR * block_size

    pairs = [
        (count_any, count_ref), (slot_any, slot_ref), (rows_any, rows_ref),
        (fetch_any, fetch_ref), (restrict_any, restrict_ref),
        (columns_any, own_columns_ref), (blocks_any, own_blocks_ref), (side_any, side_ref),
    ]
    copies = [pltpu.make_async_copy(a, b, sems.at[i]) for i, (a, b) in enumerate(pairs)]
    operators = [
        pltpu.make_async_copy(operator_any.at[i], operator_ref.at[i], operator_sems.at[i]) for i in range(fine_rows)
    ]
    for copy in copies + operators:
        copy.start()

    lane = lax.broadcasted_iota(jnp.int32, (block_size, wide), 1)
    second = (lane >= block_size).astype(jnp.int32)
    short_lane = lax.broadcasted_iota(jnp.int32, (EXTRA, wide), 1)
    for near in range(half):
        out_ref[near, :used] = jnp.zeros((used, wide), jnp.float32)
    for copy in copies + operators:
        copy.wait()

    for near in range(half):
        value = jnp.zeros((EXTRA, wide), jnp.int32)
        for side in range(2):
            for s in range(slot_count):
                turned = near ^ jnp.where(side_ref[0] == side, 0, half // 2)
                wanted = fetch_ref[s, side * half + turned]
                value = jnp.where(short_lane == side * slot_count + s, wanted, value)
        out_ref[near, used:] = value.astype(jnp.float32)

    for i in range(fine_rows):
        value = restrict_ref[i]
        swapped = pltpu.roll(value, block_size, 1)
        own_row = jnp.where(second == 0, rows_ref[0, i], rows_ref[1, i])
        other_row = jnp.where(second == 0, rows_ref[1, i], rows_ref[0, i])
        dense = jnp.where(own_row == second, value, 0.0) + jnp.where(other_row == second, swapped, 0.0)
        product = transposed_product(operator_ref[i], dense)
        for k in range(entries):
            part = jnp.where(k < count_ref[i], product[k * block_size : (k + 1) * block_size], 0.0)
            peer = lax.div(slot_ref[i, k], slot_count)
            side = lax.div(peer, half)
            place = side * slot_count + lax.rem(slot_ref[i, k], slot_count)
            near = lax.rem(peer, half) ^ jnp.where(side_ref[0] == side, 0, half // 2)
            start = pl.multiple_of(place * block_size, block_size)
            out_ref[near, pl.ds(start, block_size)] += part


def restrict_operator(
    operator_count, operator_slot, restrict_rows, fetch, operator_blocks, restrict_blocks, own_columns, own_blocks, side
):
    fine_rows, block_size, width = operator_blocks.shape
    slot_count, columns = fetch.shape
    wide = NCR * block_size
    rows = 2 * slot_count * block_size + EXTRA
    small = (operator_count, operator_slot, restrict_rows, fetch)
    kept = small + (side,)
    return pl.pallas_call(
        restrict_kernel,
        out_shape=(
            jax.ShapeDtypeStruct((columns // 2, rows, wide), jnp.float32),
            jax.ShapeDtypeStruct(own_columns.shape, own_columns.dtype),
            jax.ShapeDtypeStruct(own_blocks.shape, own_blocks.dtype),
        ),
        in_specs=[pl.BlockSpec(memory_space=pltpu.HBM)] * 9,
        out_specs=[pl.BlockSpec(memory_space=pltpu.VMEM)] * 3,
        scratch_shapes=[pltpu.SMEM(x.shape, x.dtype) for x in kept]
        + [pltpu.VMEM(x.shape, x.dtype) for x in (restrict_blocks, operator_blocks)]
        + [pltpu.SemaphoreType.DMA((8,)), pltpu.SemaphoreType.DMA((fine_rows,))],
        cost_estimate=pl.CostEstimate(
            flops=6 * fine_rows * block_size * width * wide, bytes_accessed=4 << 20, transcendentals=0
        ),
        name="restrict_operator",
    )(*small, restrict_blocks, operator_blocks, own_columns, own_blocks, side)


def combine_kernel(own_ref, restricted_ref, *rest, slot_count, fine_rows, entries):
    pieces, (out_ref, held_ref, table_ref, index_ref, sem) = rest[:-5], rest[-5:]
    half = restricted_ref.shape[0]
    rows = len(pieces) // 2
    block_size = out_ref.shape[1]
    columns = 2 * half
    used = 2 * slot_count * block_size
    held = fine_rows * block_size

    table_ref[:1, : own_ref.shape[1]] = own_ref[...]
    for near in range(half):
        table_ref[1 + near : 2 + near] = restricted_ref[near, used : used + 1].astype(jnp.int32)
    for i, piece in enumerate(pieces[rows:]):
        for far in range(2):
            first = 1 + half + entries * (far * rows + i)
            row = held + entries * (1 - far)
            table_ref[first : first + entries] = piece[row : row + entries].astype(jnp.int32)
    copy = pltpu.make_async_copy(table_ref, index_ref, sem)
    copy.start()
    for i, piece in enumerate(pieces):
        held_ref[i] = piece[...] if i < rows else piece[:held]
    out_ref[...] = jnp.zeros_like(out_ref)
    copy.wait()

    def step(i, carry):
        near = lax.div(i, 2 * slot_count)
        place = lax.rem(i, 2 * slot_count)
        wanted = index_ref[1 + near, place]
        inside = lax.rem(wanted, fine_rows)
        far = lax.div(place, slot_count) ^ index_ref[0, 1]
        piece = far * rows + (lax.div(wanted, fine_rows * columns) ^ index_ref[0, 0])
        block = held_ref[piece, pl.ds(pl.multiple_of(inside * block_size, block_size), block_size)]
        restricted = restricted_ref[near, pl.ds(pl.multiple_of(place * block_size, block_size), block_size)]
        product = transposed_product(block, restricted)
        for m in range(entries):
            column = index_ref[0, 2 + index_ref[1 + half + entries * piece + m, inside]]
            out_ref[column] += product[m * block_size : (m + 1) * block_size]
        return carry

    lax.fori_loop(0, half * 2 * slot_count, step, 0, unroll=16)


def combine(own, restricted, pieces, coarse_all, slot_count, fine_rows, block_size):
    half, _, wide = restricted.shape
    width = pieces[0].shape[1]
    entries = width // block_size
    table_rows = -(-(1 + half + entries * len(pieces)) // 8) * 8
    return pl.pallas_call(
        functools.partial(combine_kernel, slot_count=slot_count, fine_rows=fine_rows, entries=entries),
        out_shape=jax.ShapeDtypeStruct((coarse_all, block_size, wide), jnp.float32),
        in_specs=[pl.BlockSpec(memory_space=pltpu.VMEM)] * (2 + len(pieces)),
        out_specs=pl.BlockSpec(memory_space=pltpu.VMEM),
        scratch_shapes=[
            pltpu.VMEM((len(pieces), fine_rows * block_size, width), jnp.float32),
            pltpu.VMEM((table_rows, LANES), jnp.int32),
            pltpu.SMEM((table_rows, LANES), jnp.int32),
            pltpu.SemaphoreType.DMA,
        ],
        compiler_params=pltpu.CompilerParams(vmem_limit_bytes=VMEM_LIMIT),
        cost_estimate=pl.CostEstimate(flops=1 << 28, bytes_accessed=4 << 20, transcendentals=0),
        name="combine",
    )(own, restricted, *pieces)


def row_swap(x, bit):
    return lax.ppermute(x, "row", [(r, r ^ bit) for r in range(lax.axis_size("row"))])


def half_swap(x):
    return lax.ppermute(x, "half", [(0, 1), (1, 0)])


def far_swap(x):
    half = lax.axis_size("near")
    pairs = [(h * half + n, (1 - h) * half + (n ^ half // 2)) for h in range(2) for n in range(half)]
    return lax.ppermute(x, ("half", "near"), pairs)


def spread_over_rows(blocks, rows):
    pieces = {0: blocks}
    bit = rows // 2
    while bit:
        for mask in list(pieces):
            pieces[mask ^ bit] = row_swap(pieces[mask], bit)
        bit //= 2
    return [pieces[mask] for mask in range(rows)]


def place_of_columns(half):
    own = lax.axis_index("half") * half + lax.axis_index("near")
    return jnp.arange(2 * half, dtype=jnp.int32) ^ own


def add_over_near(sums, half):
    total = sums[0]
    for near in range(1, half):
        total = total + lax.ppermute(sums[near], "near", [(n, n ^ near) for n in range(half)])
    return total


def add_over_columns(sums, half):
    crossing = half_swap(add_over_near(sums[half:], half))
    return add_over_near(sums[:half], half) + crossing


def local(
    operator_blocks,
    operator_count,
    operator_slot,
    fetch_lists,
    prolong_blocks,
    prolong_cols,
    restrict_blocks,
    restrict_rows,
):
    rows, half = lax.axis_size("row"), lax.axis_size("near")
    slot_count = fetch_lists.shape[3]
    fine_rows, block_size, width = prolong_blocks.shape
    fetch = fetch_lists.reshape(2 * half, slot_count).T
    own = jnp.stack([lax.axis_index("row"), lax.axis_index("half")])
    own = jnp.concatenate([own, place_of_columns(half)])[None]

    near_blocks = prolong_blocks.reshape(fine_rows * block_size, width)
    far_blocks = far_swap(near_blocks)
    restricted, own_columns, near_blocks = restrict_operator(
        operator_count,
        operator_slot,
        restrict_rows.T,
        fetch,
        operator_blocks,
        restrict_blocks,
        prolong_cols.T,
        near_blocks,
        lax.axis_index("half").reshape(1),
    )
    restricted = lax.all_to_all(restricted, "near", split_axis=0, concat_axis=0, tiled=True)
    far_columns = far_swap(own_columns)
    near_pieces = spread_over_rows(near_blocks, rows)
    far_blocks = append_columns(near_pieces[rows // 2], far_columns, own_columns, far_blocks)
    pieces = near_pieces + spread_over_rows(far_blocks, rows)
    sums = combine(own, restricted, pieces, NCR * rows, slot_count, fine_rows, block_size)
    return add_over_columns(sums, half).T


def solution(mesh):
    rows, columns = mesh.shape["row"], mesh.shape["col"]
    split = Mesh(mesh.devices.reshape(rows, 2, columns // 2), ("row", "half", "near"))
    flat = ("row", "half", "near")
    return jax.shard_map(
        local,
        mesh=split,
        in_specs=(
            P(flat, None, None),
            P(flat),
            P(flat, None),
            P("row", ("half", "near"), None, None),
            P(flat, None, None),
            P(flat, None),
            P(flat, None, None),
            P(flat, None),
        ),
        out_specs=P("row", ("half", "near")),
        check_vma=False,
    )
```

```python
import functools

import jax
import jax.numpy as jnp
from jax import lax
from jax.experimental import pallas as pl
from jax.experimental.pallas import tpu as pltpu
from jax.sharding import Mesh
from jax.sharding import PartitionSpec as P

NCR = 2
LANES = 128
EXTRA = 8
HOLD_FLOPS = 16 << 30
VMEM_LIMIT = 48 * 1024 * 1024


def halves(x):
    high = x.astype(jnp.bfloat16)
    return high, (x - high.astype(jnp.float32)).astype(jnp.bfloat16)


def transposed_product(left, right):
    tall = jnp.concatenate(halves(left), axis=0)
    wide = jnp.concatenate(halves(right), axis=1)
    wide = jnp.concatenate([wide, wide], axis=0)
    both = lax.dot_general(tall, wide, (((0,), (0,)), ((), ())), preferred_element_type=jnp.float32)
    width = right.shape[1]
    return both[:, :width] + both[:, width:]


def hold_kernel(mark_ref, blocks_ref, out_ref):
    out_ref[...] = blocks_ref[...]


def hold_until(mark, blocks):
    return pl.pallas_call(
        hold_kernel,
        out_shape=jax.ShapeDtypeStruct(blocks.shape, blocks.dtype),
        in_specs=[pl.BlockSpec(memory_space=pltpu.VMEM)] * 2,
        out_specs=pl.BlockSpec(memory_space=pltpu.VMEM),
        compiler_params=pltpu.CompilerParams(vmem_limit_bytes=VMEM_LIMIT),
        cost_estimate=pl.CostEstimate(flops=HOLD_FLOPS, bytes_accessed=HOLD_FLOPS >> 8, transcendentals=0),
        name="hold_until",
    )(mark, blocks)


def append_kernel(far_columns_ref, own_columns_ref, next_ref, blocks_ref, out_ref):
    used = blocks_ref.shape[0]
    entries, fine_rows = own_columns_ref.shape
    out_ref[:used] = blocks_ref[...]
    out_ref[used:] = jnp.zeros((EXTRA, out_ref.shape[1]), jnp.float32)
    out_ref[used : used + entries, :fine_rows] = far_columns_ref[...].astype(jnp.float32)
    out_ref[used + entries : used + 2 * entries, :fine_rows] = own_columns_ref[...].astype(jnp.float32)


def append_columns(far_columns, own_columns, next_blocks, blocks):
    used, width = blocks.shape
    return pl.pallas_call(
        append_kernel,
        out_shape=jax.ShapeDtypeStruct((used + EXTRA, width), blocks.dtype),
        in_specs=[pl.BlockSpec(memory_space=pltpu.VMEM)] * 4,
        out_specs=pl.BlockSpec(memory_space=pltpu.VMEM),
        compiler_params=pltpu.CompilerParams(vmem_limit_bytes=VMEM_LIMIT),
        cost_estimate=pl.CostEstimate(flops=0, bytes_accessed=1 << 19, transcendentals=0),
        name="append_columns",
    )(far_columns, own_columns, next_blocks, blocks)


def restrict_kernel(
    count_any, slot_any, rows_any, fetch_any, restrict_any, operator_any, columns_any, side_any,
    out_ref, own_columns_ref,
    count_ref, slot_ref, rows_ref, fetch_ref, side_ref, restrict_ref, operator_ref, sems, operator_sems,
):
    fine_rows, block_size, _ = operator_ref.shape
    entries = slot_ref.shape[1]
    slot_count, columns = fetch_ref.shape
    half = columns // 2
    used = 2 * slot_count * block_size
    wide = NCR * block_size

    pairs = [
        (count_any, count_ref), (slot_any, slot_ref), (rows_any, rows_ref),
        (fetch_any, fetch_ref), (restrict_any, restrict_ref),
        (columns_any, own_columns_ref), (side_any, side_ref),
    ]
    copies = [pltpu.make_async_copy(a, b, sems.at[i]) for i, (a, b) in enumerate(pairs)]
    operators = [
        pltpu.make_async_copy(operator_any.at[i], operator_ref.at[i], operator_sems.at[i]) for i in range(fine_rows)
    ]
    for copy in copies + operators:
        copy.start()

    lane = lax.broadcasted_iota(jnp.int32, (block_size, wide), 1)
    second = (lane >= block_size).astype(jnp.int32)
    short_lane = lax.broadcasted_iota(jnp.int32, (EXTRA, wide), 1)
    for near in range(half):
        out_ref[near, :used] = jnp.zeros((used, wide), jnp.float32)
    for copy in copies + operators:
        copy.wait()

    for near in range(half):
        value = jnp.zeros((EXTRA, wide), jnp.int32)
        for side in range(2):
            for s in range(slot_count):
                turned = near ^ jnp.where(side_ref[0] == side, 0, half // 2)
                wanted = fetch_ref[s, side * half + turned]
                value = jnp.where(short_lane == side * slot_count + s, wanted, value)
        out_ref[near, used:] = value.astype(jnp.float32)

    for i in range(fine_rows):
        value = restrict_ref[i]
        swapped = pltpu.roll(value, block_size, 1)
        own_row = jnp.where(second == 0, rows_ref[0, i], rows_ref[1, i])
        other_row = jnp.where(second == 0, rows_ref[1, i], rows_ref[0, i])
        dense = jnp.where(own_row == second, value, 0.0) + jnp.where(other_row == second, swapped, 0.0)
        product = transposed_product(operator_ref[i], dense)
        for k in range(entries):
            part = jnp.where(k < count_ref[i], product[k * block_size : (k + 1) * block_size], 0.0)
            peer = lax.div(slot_ref[i, k], slot_count)
            side = lax.div(peer, half)
            place = side * slot_count + lax.rem(slot_ref[i, k], slot_count)
            near = lax.rem(peer, half) ^ jnp.where(side_ref[0] == side, 0, half // 2)
            start = pl.multiple_of(place * block_size, block_size)
            out_ref[near, pl.ds(start, block_size)] += part


def restrict_operator(
    operator_count, operator_slot, restrict_rows, fetch, operator_blocks, restrict_blocks, own_columns, side
):
    fine_rows, block_size, width = operator_blocks.shape
    slot_count, columns = fetch.shape
    wide = NCR * block_size
    rows = 2 * slot_count * block_size + EXTRA
    small = (operator_count, operator_slot, restrict_rows, fetch)
    kept = small + (side,)
    return pl.pallas_call(
        restrict_kernel,
        out_shape=(
            jax.ShapeDtypeStruct((columns // 2, rows, wide), jnp.float32),
            jax.ShapeDtypeStruct(own_columns.shape, own_columns.dtype),
        ),
        in_specs=[pl.BlockSpec(memory_space=pltpu.HBM)] * 8,
        out_specs=[pl.BlockSpec(memory_space=pltpu.VMEM)] * 2,
        scratch_shapes=[pltpu.SMEM(x.shape, x.dtype) for x in kept]
        + [pltpu.VMEM(x.shape, x.dtype) for x in (restrict_blocks, operator_blocks)]
        + [pltpu.SemaphoreType.DMA((7,)), pltpu.SemaphoreType.DMA((fine_rows,))],
        cost_estimate=pl.CostEstimate(
            flops=6 * fine_rows * block_size * width * wide, bytes_accessed=4 << 20, transcendentals=0
        ),
        name="restrict_operator",
    )(*small, restrict_blocks, operator_blocks, own_columns, side)


def combine_kernel(own_ref, restricted_ref, *rest, slot_count, fine_rows, entries):
    pieces, (out_ref, held_ref, table_ref, index_ref, sem) = rest[:-5], rest[-5:]
    half = restricted_ref.shape[0]
    rows = len(pieces) // 2
    block_size = out_ref.shape[1]
    columns = 2 * half
    used = 2 * slot_count * block_size
    held = fine_rows * block_size

    table_ref[:1, : own_ref.shape[1]] = own_ref[...]
    for near in range(half):
        table_ref[1 + near : 2 + near] = restricted_ref[near, used : used + 1].astype(jnp.int32)
    for i, piece in enumerate(pieces[rows:]):
        for far in range(2):
            first = 1 + half + entries * (far * rows + (i ^ (far * rows // 2)))
            row = held + entries * (1 - far)
            table_ref[first : first + entries] = piece[row : row + entries].astype(jnp.int32)
    copy = pltpu.make_async_copy(table_ref, index_ref, sem)
    copy.start()
    for i, piece in enumerate(pieces):
        held_ref[i] = piece[...] if i < rows else piece[:held]
    out_ref[...] = jnp.zeros_like(out_ref)
    copy.wait()

    def step(i, carry):
        near = lax.div(i, 2 * slot_count)
        place = lax.rem(i, 2 * slot_count)
        wanted = index_ref[1 + near, place]
        inside = lax.rem(wanted, fine_rows)
        far = lax.div(place, slot_count) ^ index_ref[0, 1]
        piece = far * rows + (lax.div(wanted, fine_rows * columns) ^ index_ref[0, 0])
        block = held_ref[piece, pl.ds(pl.multiple_of(inside * block_size, block_size), block_size)]
        restricted = restricted_ref[near, pl.ds(pl.multiple_of(place * block_size, block_size), block_size)]
        product = transposed_product(block, restricted)
        for m in range(entries):
            column = index_ref[0, 2 + index_ref[1 + half + entries * piece + m, inside]]
            out_ref[column] += product[m * block_size : (m + 1) * block_size]
        return carry

    lax.fori_loop(0, half * 2 * slot_count, step, 0, unroll=16)


def combine(own, restricted, pieces, coarse_all, slot_count, fine_rows, block_size):
    half, _, wide = restricted.shape
    width = pieces[0].shape[1]
    entries = width // block_size
    table_rows = -(-(1 + half + entries * len(pieces)) // 8) * 8
    return pl.pallas_call(
        functools.partial(combine_kernel, slot_count=slot_count, fine_rows=fine_rows, entries=entries),
        out_shape=jax.ShapeDtypeStruct((coarse_all, block_size, wide), jnp.float32),
        in_specs=[pl.BlockSpec(memory_space=pltpu.VMEM)] * (2 + len(pieces)),
        out_specs=pl.BlockSpec(memory_space=pltpu.VMEM),
        scratch_shapes=[
            pltpu.VMEM((len(pieces), fine_rows * block_size, width), jnp.float32),
            pltpu.VMEM((table_rows, LANES), jnp.int32),
            pltpu.SMEM((table_rows, LANES), jnp.int32),
            pltpu.SemaphoreType.DMA,
        ],
        compiler_params=pltpu.CompilerParams(vmem_limit_bytes=VMEM_LIMIT),
        cost_estimate=pl.CostEstimate(flops=1 << 28, bytes_accessed=4 << 20, transcendentals=0),
        name="combine",
    )(own, restricted, *pieces)


def row_swap(x, bit):
    return lax.ppermute(x, "row", [(r, r ^ bit) for r in range(lax.axis_size("row"))])


def half_swap(x):
    return lax.ppermute(x, "half", [(0, 1), (1, 0)])


def far_swap(x):
    half = lax.axis_size("near")
    pairs = [(h * half + n, (1 - h) * half + (n ^ half // 2)) for h in range(2) for n in range(half)]
    return lax.ppermute(x, ("half", "near"), pairs)


def far_turn(x):
    rows, half = lax.axis_size("row"), lax.axis_size("near")
    pairs = [
        ((r * 2 + h) * half + n, ((r ^ rows // 2) * 2 + 1 - h) * half + (n ^ half // 2))
        for r in range(rows)
        for h in range(2)
        for n in range(half)
    ]
    return lax.ppermute(x, ("row", "half", "near"), pairs)


def spread_over_rows(blocks, rows):
    pieces = {0: blocks}
    bit = rows // 2
    while bit:
        for mask in list(pieces):
            pieces[mask ^ bit] = row_swap(pieces[mask], bit)
        bit //= 2
    return [pieces[mask] for mask in range(rows)]


def place_of_columns(half):
    own = lax.axis_index("half") * half + lax.axis_index("near")
    return jnp.arange(2 * half, dtype=jnp.int32) ^ own


def add_over_near(sums, half):
    total = sums[0]
    for near in range(1, half):
        total = total + lax.ppermute(sums[near], "near", [(n, n ^ near) for n in range(half)])
    return total


def add_over_columns(sums, half):
    crossing = half_swap(add_over_near(sums[half:], half))
    return add_over_near(sums[:half], half) + crossing


def local(
    operator_blocks,
    operator_count,
    operator_slot,
    fetch_lists,
    prolong_blocks,
    prolong_cols,
    restrict_blocks,
    restrict_rows,
):
    rows, half = lax.axis_size("row"), lax.axis_size("near")
    slot_count = fetch_lists.shape[3]
    fine_rows, block_size, width = prolong_blocks.shape
    fetch = fetch_lists.reshape(2 * half, slot_count).T
    own = jnp.stack([lax.axis_index("row"), lax.axis_index("half")])
    own = jnp.concatenate([own, place_of_columns(half)])[None]

    near_blocks = prolong_blocks.reshape(fine_rows * block_size, width)
    far_blocks = far_swap(near_blocks)
    restricted, own_columns = restrict_operator(
        operator_count,
        operator_slot,
        restrict_rows.T,
        fetch,
        operator_blocks,
        restrict_blocks,
        prolong_cols.T,
        lax.axis_index("half").reshape(1),
    )
    restricted = lax.all_to_all(restricted, "near", split_axis=0, concat_axis=0, tiled=True)
    far_columns = far_turn(own_columns)
    near_pieces = spread_over_rows(near_blocks, rows)
    far_blocks = hold_until(own_columns, far_blocks)
    far_blocks = append_columns(far_columns, own_columns, near_pieces[rows // 2], far_blocks)
    pieces = near_pieces + spread_over_rows(far_blocks, rows)
    sums = combine(own, restricted, pieces, NCR * rows, slot_count, fine_rows, block_size)
    return add_over_columns(sums, half).T


def solution(mesh):
    rows, columns = mesh.shape["row"], mesh.shape["col"]
    split = Mesh(mesh.devices.reshape(rows, 2, columns // 2), ("row", "half", "near"))
    flat = ("row", "half", "near")
    return jax.shard_map(
        local,
        mesh=split,
        in_specs=(
            P(flat, None, None),
            P(flat),
            P(flat, None),
            P("row", ("half", "near"), None, None),
            P(flat, None, None),
            P(flat, None),
            P(flat, None, None),
            P(flat, None),
        ),
        out_specs=P("row", ("half", "near")),
        check_vma=False,
    )
```

```python
import functools

import jax
import jax.numpy as jnp
from jax import lax
from jax.experimental import pallas as pl
from jax.experimental.pallas import tpu as pltpu
from jax.sharding import Mesh
from jax.sharding import PartitionSpec as P

NCR = 2
LANES = 128
EXTRA = 8
HOLD_FLOPS = 16 << 30
VMEM_LIMIT = 48 * 1024 * 1024


def halves(x):
    high = x.astype(jnp.bfloat16)
    return high, (x - high.astype(jnp.float32)).astype(jnp.bfloat16)


def transposed_product(left, right):
    tall = jnp.concatenate(halves(left), axis=0)
    wide = jnp.concatenate(halves(right), axis=1)
    wide = jnp.concatenate([wide, wide], axis=0)
    both = lax.dot_general(tall, wide, (((0,), (0,)), ((), ())), preferred_element_type=jnp.float32)
    width = right.shape[1]
    return both[:, :width] + both[:, width:]


def append_kernel(next_ref, far_columns_ref, own_columns_ref, blocks_ref, out_ref):
    used = blocks_ref.shape[0]
    entries, fine_rows = own_columns_ref.shape
    out_ref[:used] = blocks_ref[...]
    out_ref[used:] = jnp.zeros((EXTRA, out_ref.shape[1]), jnp.float32)
    out_ref[used : used + entries, :fine_rows] = far_columns_ref[...].astype(jnp.float32)
    out_ref[used + entries : used + 2 * entries, :fine_rows] = own_columns_ref[...].astype(jnp.float32)


def append_columns(next_blocks, far_columns, own_columns, blocks):
    used, width = blocks.shape
    return pl.pallas_call(
        append_kernel,
        out_shape=jax.ShapeDtypeStruct((used + EXTRA, width), blocks.dtype),
        in_specs=[pl.BlockSpec(memory_space=pltpu.VMEM)] * 4,
        out_specs=pl.BlockSpec(memory_space=pltpu.VMEM),
        compiler_params=pltpu.CompilerParams(vmem_limit_bytes=VMEM_LIMIT),
        cost_estimate=pl.CostEstimate(flops=HOLD_FLOPS, bytes_accessed=HOLD_FLOPS >> 8, transcendentals=0),
        name="append_columns",
    )(next_blocks, far_columns, own_columns, blocks)


def restrict_kernel(
    count_any, slot_any, rows_any, fetch_any, restrict_any, operator_any, columns_any, blocks_any, side_any,
    out_ref, own_columns_ref, own_blocks_any,
    count_ref, slot_ref, rows_ref, fetch_ref, side_ref, restrict_ref, operator_ref, blocks_ref,
    sems, operator_sems, blocks_sems,
):
    fine_rows, block_size, _ = operator_ref.shape
    entries = slot_ref.shape[1]
    slot_count, columns = fetch_ref.shape
    half = columns // 2
    used = 2 * slot_count * block_size
    wide = NCR * block_size

    pairs = [
        (count_any, count_ref), (slot_any, slot_ref), (rows_any, rows_ref),
        (fetch_any, fetch_ref), (restrict_any, restrict_ref),
        (columns_any, own_columns_ref), (side_any, side_ref),
    ]
    copies = [pltpu.make_async_copy(a, b, sems.at[i]) for i, (a, b) in enumerate(pairs)]
    operators = [
        pltpu.make_async_copy(operator_any.at[i], operator_ref.at[i], operator_sems.at[i]) for i in range(fine_rows)
    ]
    blocks_in = pltpu.make_async_copy(blocks_any, blocks_ref, blocks_sems.at[0])
    blocks_out = pltpu.make_async_copy(blocks_ref, own_blocks_any, blocks_sems.at[1])
    for copy in copies + operators + [blocks_in]:
        copy.start()

    lane = lax.broadcasted_iota(jnp.int32, (block_size, wide), 1)
    second = (lane >= block_size).astype(jnp.int32)
    short_lane = lax.broadcasted_iota(jnp.int32, (EXTRA, wide), 1)
    for near in range(half):
        out_ref[near, :used] = jnp.zeros((used, wide), jnp.float32)
    for copy in copies:
        copy.wait()

    for near in range(half):
        value = jnp.zeros((EXTRA, wide), jnp.int32)
        for side in range(2):
            for s in range(slot_count):
                turned = near ^ jnp.where(side_ref[0] == side, 0, half // 2)
                wanted = fetch_ref[s, side * half + turned]
                value = jnp.where(short_lane == side * slot_count + s, wanted, value)
        out_ref[near, used:] = value.astype(jnp.float32)

    for i in range(fine_rows):
        if i % (fine_rows // 2) == 0:
            for copy in operators[i : i + fine_rows // 2]:
                copy.wait()
        if i == fine_rows // 2:
            blocks_in.wait()
            blocks_out.start()
        value = restrict_ref[i]
        swapped = pltpu.roll(value, block_size, 1)
        own_row = jnp.where(second == 0, rows_ref[0, i], rows_ref[1, i])
        other_row = jnp.where(second == 0, rows_ref[1, i], rows_ref[0, i])
        dense = jnp.where(own_row == second, value, 0.0) + jnp.where(other_row == second, swapped, 0.0)
        product = transposed_product(operator_ref[i], dense)
        for k in range(entries):
            part = jnp.where(k < count_ref[i], product[k * block_size : (k + 1) * block_size], 0.0)
            peer = lax.div(slot_ref[i, k], slot_count)
            side = lax.div(peer, half)
            place = side * slot_count + lax.rem(slot_ref[i, k], slot_count)
            near = lax.rem(peer, half) ^ jnp.where(side_ref[0] == side, 0, half // 2)
            start = pl.multiple_of(place * block_size, block_size)
            out_ref[near, pl.ds(start, block_size)] += part
    blocks_out.wait()


def restrict_operator(
    operator_count, operator_slot, restrict_rows, fetch, operator_blocks, restrict_blocks, own_columns, own_blocks, side
):
    fine_rows, block_size, width = operator_blocks.shape
    slot_count, columns = fetch.shape
    wide = NCR * block_size
    rows = 2 * slot_count * block_size + EXTRA
    small = (operator_count, operator_slot, restrict_rows, fetch)
    kept = small + (side,)
    return pl.pallas_call(
        restrict_kernel,
        out_shape=(
            jax.ShapeDtypeStruct((columns // 2, rows, wide), jnp.float32),
            jax.ShapeDtypeStruct(own_columns.shape, own_columns.dtype),
            jax.ShapeDtypeStruct(own_blocks.shape, own_blocks.dtype),
        ),
        in_specs=[pl.BlockSpec(memory_space=pltpu.HBM)] * 9,
        out_specs=[pl.BlockSpec(memory_space=pltpu.VMEM)] * 2 + [pl.BlockSpec(memory_space=pltpu.HBM)],
        scratch_shapes=[pltpu.SMEM(x.shape, x.dtype) for x in kept]
        + [pltpu.VMEM(x.shape, x.dtype) for x in (restrict_blocks, operator_blocks, own_blocks)]
        + [pltpu.SemaphoreType.DMA((7,)), pltpu.SemaphoreType.DMA((fine_rows,)), pltpu.SemaphoreType.DMA((2,))],
        cost_estimate=pl.CostEstimate(
            flops=6 * fine_rows * block_size * width * wide, bytes_accessed=4 << 20, transcendentals=0
        ),
        name="restrict_operator",
    )(*small, restrict_blocks, operator_blocks, own_columns, own_blocks, side)


def combine_kernel(own_ref, restricted_ref, *rest, slot_count, fine_rows, entries):
    pieces, (out_ref, held_ref, table_ref, index_ref, sem) = rest[:-5], rest[-5:]
    half = restricted_ref.shape[0]
    rows = len(pieces) // 2
    block_size = out_ref.shape[1]
    columns = 2 * half
    used = 2 * slot_count * block_size
    held = fine_rows * block_size

    table_ref[:1, : own_ref.shape[1]] = own_ref[...]
    for near in range(half):
        table_ref[1 + near : 2 + near] = restricted_ref[near, used : used + 1].astype(jnp.int32)
    for i, piece in enumerate(pieces[rows:]):
        for far in range(2):
            first = 1 + half + entries * (far * rows + i)
            row = held + entries * (1 - far)
            table_ref[first : first + entries] = piece[row : row + entries].astype(jnp.int32)
    copy = pltpu.make_async_copy(table_ref, index_ref, sem)
    copy.start()
    for i, piece in enumerate(pieces):
        held_ref[i] = piece[...] if i < rows else piece[:held]
    out_ref[...] = jnp.zeros_like(out_ref)
    copy.wait()

    def step(i, carry):
        near = lax.div(i, 2 * slot_count)
        place = lax.rem(i, 2 * slot_count)
        wanted = index_ref[1 + near, place]
        inside = lax.rem(wanted, fine_rows)
        far = lax.div(place, slot_count) ^ index_ref[0, 1]
        piece = far * rows + (lax.div(wanted, fine_rows * columns) ^ index_ref[0, 0])
        block = held_ref[piece, pl.ds(pl.multiple_of(inside * block_size, block_size), block_size)]
        restricted = restricted_ref[near, pl.ds(pl.multiple_of(place * block_size, block_size), block_size)]
        product = transposed_product(block, restricted)
        for m in range(entries):
            column = index_ref[0, 2 + index_ref[1 + half + entries * piece + m, inside]]
            out_ref[column] += product[m * block_size : (m + 1) * block_size]
        return carry

    lax.fori_loop(0, half * 2 * slot_count, step, 0, unroll=16)


def combine(own, restricted, pieces, coarse_all, slot_count, fine_rows, block_size):
    half, _, wide = restricted.shape
    width = pieces[0].shape[1]
    entries = width // block_size
    table_rows = -(-(1 + half + entries * len(pieces)) // 8) * 8
    return pl.pallas_call(
        functools.partial(combine_kernel, slot_count=slot_count, fine_rows=fine_rows, entries=entries),
        out_shape=jax.ShapeDtypeStruct((coarse_all, block_size, wide), jnp.float32),
        in_specs=[pl.BlockSpec(memory_space=pltpu.VMEM)] * (2 + len(pieces)),
        out_specs=pl.BlockSpec(memory_space=pltpu.VMEM),
        scratch_shapes=[
            pltpu.VMEM((len(pieces), fine_rows * block_size, width), jnp.float32),
            pltpu.VMEM((table_rows, LANES), jnp.int32),
            pltpu.SMEM((table_rows, LANES), jnp.int32),
            pltpu.SemaphoreType.DMA,
        ],
        compiler_params=pltpu.CompilerParams(vmem_limit_bytes=VMEM_LIMIT),
        cost_estimate=pl.CostEstimate(flops=1 << 28, bytes_accessed=4 << 20, transcendentals=0),
        name="combine",
    )(own, restricted, *pieces)


def row_swap(x, bit):
    return lax.ppermute(x, "row", [(r, r ^ bit) for r in range(lax.axis_size("row"))])


def half_swap(x):
    return lax.ppermute(x, "half", [(0, 1), (1, 0)])


def far_swap(x):
    half = lax.axis_size("near")
    pairs = [(h * half + n, (1 - h) * half + (n ^ half // 2)) for h in range(2) for n in range(half)]
    return lax.ppermute(x, ("half", "near"), pairs)


def spread_over_rows(blocks, rows):
    pieces = {0: blocks}
    bit = rows // 2
    while bit:
        for mask in list(pieces):
            pieces[mask ^ bit] = row_swap(pieces[mask], bit)
        bit //= 2
    return [pieces[mask] for mask in range(rows)]


def place_of_columns(half):
    own = lax.axis_index("half") * half + lax.axis_index("near")
    return jnp.arange(2 * half, dtype=jnp.int32) ^ own


def add_over_near(sums, half):
    total = sums[0]
    for near in range(1, half):
        total = total + lax.ppermute(sums[near], "near", [(n, n ^ near) for n in range(half)])
    return total


def add_over_columns(sums, half):
    crossing = half_swap(add_over_near(sums[half:], half))
    return add_over_near(sums[:half], half) + crossing


def local(
    operator_blocks,
    operator_count,
    operator_slot,
    fetch_lists,
    prolong_blocks,
    prolong_cols,
    restrict_blocks,
    restrict_rows,
):
    rows, half = lax.axis_size("row"), lax.axis_size("near")
    slot_count = fetch_lists.shape[3]
    fine_rows, block_size, width = prolong_blocks.shape
    fetch = fetch_lists.reshape(2 * half, slot_count).T
    own = jnp.stack([lax.axis_index("row"), lax.axis_index("half")])
    own = jnp.concatenate([own, place_of_columns(half)])[None]

    near_blocks = prolong_blocks.reshape(fine_rows * block_size, width)
    far_blocks = far_swap(near_blocks)
    restricted, own_columns, near_blocks = restrict_operator(
        operator_count,
        operator_slot,
        restrict_rows.T,
        fetch,
        operator_blocks,
        restrict_blocks,
        prolong_cols.T,
        near_blocks,
        lax.axis_index("half").reshape(1),
    )
    restricted = lax.all_to_all(restricted, "near", split_axis=0, concat_axis=0, tiled=True)
    far_columns = far_swap(own_columns)
    near_pieces = spread_over_rows(near_blocks, rows)
    far_blocks = append_columns(near_pieces[rows // 2], far_columns, own_columns, far_blocks)
    pieces = near_pieces + spread_over_rows(far_blocks, rows)
    sums = combine(own, restricted, pieces, NCR * rows, slot_count, fine_rows, block_size)
    return add_over_columns(sums, half).T


def solution(mesh):
    rows, columns = mesh.shape["row"], mesh.shape["col"]
    split = Mesh(mesh.devices.reshape(rows, 2, columns // 2), ("row", "half", "near"))
    flat = ("row", "half", "near")
    return jax.shard_map(
        local,
        mesh=split,
        in_specs=(
            P(flat, None, None),
            P(flat),
            P(flat, None),
            P("row", ("half", "near"), None, None),
            P(flat, None, None),
            P(flat, None),
            P(flat, None, None),
            P(flat, None),
        ),
        out_specs=P("row", ("half", "near")),
        check_vma=False,
    )
```

```python
import functools

import jax
import jax.numpy as jnp
from jax import lax
from jax.experimental import pallas as pl
from jax.experimental.pallas import tpu as pltpu
from jax.sharding import Mesh
from jax.sharding import PartitionSpec as P

NCR = 2
LANES = 128
EXTRA = 8
HOLD_FLOPS = 16 << 30
VMEM_LIMIT = 48 * 1024 * 1024


def halves(x):
    high = x.astype(jnp.bfloat16)
    return high, (x - high.astype(jnp.float32)).astype(jnp.bfloat16)


def tall_halves(left):
    return jnp.concatenate(halves(left), axis=0)


def transposed_product(tall, right):
    wide = jnp.concatenate(halves(right), axis=1)
    wide = jnp.concatenate([wide, wide], axis=0)
    both = lax.dot_general(tall, wide, (((0,), (0,)), ((), ())), preferred_element_type=jnp.float32)
    width = right.shape[1]
    return both[:, :width] + both[:, width:]


def append_kernel(next_ref, far_columns_ref, own_columns_ref, blocks_ref, out_ref):
    used = blocks_ref.shape[0]
    entries, fine_rows = own_columns_ref.shape
    out_ref[:used] = blocks_ref[...]
    out_ref[used:] = jnp.zeros((EXTRA, out_ref.shape[1]), jnp.float32)
    out_ref[used : used + entries, :fine_rows] = far_columns_ref[...].astype(jnp.float32)
    out_ref[used + entries : used + 2 * entries, :fine_rows] = own_columns_ref[...].astype(jnp.float32)


def append_columns(next_blocks, far_columns, own_columns, blocks):
    used, width = blocks.shape
    return pl.pallas_call(
        append_kernel,
        out_shape=jax.ShapeDtypeStruct((used + EXTRA, width), blocks.dtype),
        in_specs=[pl.BlockSpec(memory_space=pltpu.VMEM)] * 4,
        out_specs=pl.BlockSpec(memory_space=pltpu.VMEM),
        compiler_params=pltpu.CompilerParams(vmem_limit_bytes=VMEM_LIMIT),
        cost_estimate=pl.CostEstimate(flops=HOLD_FLOPS, bytes_accessed=HOLD_FLOPS >> 8, transcendentals=0),
        name="append_columns",
    )(next_blocks, far_columns, own_columns, blocks)


def restrict_kernel(
    count_any, slot_any, rows_any, fetch_any, restrict_any, operator_any, columns_any, blocks_any, side_any,
    out_ref, own_columns_ref, own_blocks_ref,
    count_ref, slot_ref, rows_ref, fetch_ref, side_ref, restrict_ref, operator_ref, sems, operator_sems,
):
    fine_rows, block_size, _ = operator_ref.shape
    entries = slot_ref.shape[1]
    slot_count, columns = fetch_ref.shape
    half = columns // 2
    used = 2 * slot_count * block_size
    wide = NCR * block_size

    pairs = [
        (count_any, count_ref), (slot_any, slot_ref), (rows_any, rows_ref),
        (fetch_any, fetch_ref), (restrict_any, restrict_ref),
        (columns_any, own_columns_ref), (blocks_any, own_blocks_ref), (side_any, side_ref),
    ]
    copies = [pltpu.make_async_copy(a, b, sems.at[i]) for i, (a, b) in enumerate(pairs)]
    operators = [
        pltpu.make_async_copy(operator_any.at[i], operator_ref.at[i], operator_sems.at[i]) for i in range(fine_rows)
    ]
    for copy in copies + operators:
        copy.start()

    lane = lax.broadcasted_iota(jnp.int32, (block_size, wide), 1)
    second = (lane >= block_size).astype(jnp.int32)
    short_lane = lax.broadcasted_iota(jnp.int32, (EXTRA, wide), 1)
    for near in range(half):
        out_ref[near, :used] = jnp.zeros((used, wide), jnp.float32)
    for copy in copies + operators:
        copy.wait()

    for near in range(half):
        value = jnp.zeros((EXTRA, wide), jnp.int32)
        for side in range(2):
            for s in range(slot_count):
                turned = near ^ jnp.where(side_ref[0] == side, 0, half // 2)
                wanted = fetch_ref[s, side * half + turned]
                value = jnp.where(short_lane == side * slot_count + s, wanted, value)
        out_ref[near, used:] = value.astype(jnp.float32)

    for i in range(fine_rows):
        value = restrict_ref[i]
        swapped = pltpu.roll(value, block_size, 1)
        own_row = jnp.where(second == 0, rows_ref[0, i], rows_ref[1, i])
        other_row = jnp.where(second == 0, rows_ref[1, i], rows_ref[0, i])
        dense = jnp.where(own_row == second, value, 0.0) + jnp.where(other_row == second, swapped, 0.0)
        product = transposed_product(tall_halves(operator_ref[i]), dense)
        for k in range(entries):
            part = jnp.where(k < count_ref[i], product[k * block_size : (k + 1) * block_size], 0.0)
            peer = lax.div(slot_ref[i, k], slot_count)
            side = lax.div(peer, half)
            place = side * slot_count + lax.rem(slot_ref[i, k], slot_count)
            near = lax.rem(peer, half) ^ jnp.where(side_ref[0] == side, 0, half // 2)
            start = pl.multiple_of(place * block_size, block_size)
            out_ref[near, pl.ds(start, block_size)] += part


def restrict_operator(
    operator_count, operator_slot, restrict_rows, fetch, operator_blocks, restrict_blocks, own_columns, own_blocks, side
):
    fine_rows, block_size, width = operator_blocks.shape
    slot_count, columns = fetch.shape
    wide = NCR * block_size
    rows = 2 * slot_count * block_size + EXTRA
    small = (operator_count, operator_slot, restrict_rows, fetch)
    kept = small + (side,)
    return pl.pallas_call(
        restrict_kernel,
        out_shape=(
            jax.ShapeDtypeStruct((columns // 2, rows, wide), jnp.float32),
            jax.ShapeDtypeStruct(own_columns.shape, own_columns.dtype),
            jax.ShapeDtypeStruct(own_blocks.shape, own_blocks.dtype),
        ),
        in_specs=[pl.BlockSpec(memory_space=pltpu.HBM)] * 9,
        out_specs=[pl.BlockSpec(memory_space=pltpu.VMEM)] * 3,
        scratch_shapes=[pltpu.SMEM(x.shape, x.dtype) for x in kept]
        + [pltpu.VMEM(x.shape, x.dtype) for x in (restrict_blocks, operator_blocks)]
        + [pltpu.SemaphoreType.DMA((8,)), pltpu.SemaphoreType.DMA((fine_rows,))],
        cost_estimate=pl.CostEstimate(
            flops=6 * fine_rows * block_size * width * wide, bytes_accessed=4 << 20, transcendentals=0
        ),
        name="restrict_operator",
    )(*small, restrict_blocks, operator_blocks, own_columns, own_blocks, side)


def prepare_kernel(*refs, fine_rows, entries):
    pieces, (held_ref, columns_ref) = refs[:-2], refs[-2:]
    rows = len(pieces) // 2
    block_size = held_ref.shape[2] // 2
    held = fine_rows * block_size
    for i, piece in enumerate(pieces):
        for inside in range(fine_rows):
            held_ref[i, inside] = tall_halves(piece[inside * block_size : (inside + 1) * block_size])
    for i, piece in enumerate(pieces[rows:]):
        for far in range(2):
            first = entries * (far * rows + i)
            row = held + entries * (1 - far)
            columns_ref[first : first + entries] = piece[row : row + entries].astype(jnp.int32)


def prepare(pieces, fine_rows, block_size):
    width = pieces[0].shape[1]
    entries = width // block_size
    return pl.pallas_call(
        functools.partial(prepare_kernel, fine_rows=fine_rows, entries=entries),
        out_shape=(
            jax.ShapeDtypeStruct((len(pieces), fine_rows, 2 * block_size, width), jnp.bfloat16),
            jax.ShapeDtypeStruct((entries * len(pieces), LANES), jnp.int32),
        ),
        in_specs=[pl.BlockSpec(memory_space=pltpu.VMEM)] * len(pieces),
        out_specs=[pl.BlockSpec(memory_space=pltpu.VMEM)] * 2,
        compiler_params=pltpu.CompilerParams(vmem_limit_bytes=VMEM_LIMIT),
        cost_estimate=pl.CostEstimate(flops=1 << 20, bytes_accessed=4 << 20, transcendentals=0),
        name="prepare",
    )(*pieces)


def combine_kernel(
    own_ref, columns_ref, restricted_ref, held_ref, out_ref, table_ref, index_ref, sem, *, slot_count, entries
):
    half = restricted_ref.shape[0]
    rows = held_ref.shape[0] // 2
    fine_rows = held_ref.shape[1]
    block_size = out_ref.shape[1]
    columns = 2 * half
    used = 2 * slot_count * block_size

    table_ref[:1, : own_ref.shape[1]] = own_ref[...]
    for near in range(half):
        table_ref[1 + near : 2 + near] = restricted_ref[near, used : used + 1].astype(jnp.int32)
    table_ref[1 + half : 1 + half + columns_ref.shape[0]] = columns_ref[...]
    copy = pltpu.make_async_copy(table_ref, index_ref, sem)
    copy.start()
    out_ref[...] = jnp.zeros_like(out_ref)
    copy.wait()

    def step(i, carry):
        near = lax.div(i, 2 * slot_count)
        place = lax.rem(i, 2 * slot_count)
        wanted = index_ref[1 + near, place]
        inside = lax.rem(wanted, fine_rows)
        far = lax.div(place, slot_count) ^ index_ref[0, 1]
        piece = far * rows + (lax.div(wanted, fine_rows * columns) ^ index_ref[0, 0])
        restricted = restricted_ref[near, pl.ds(pl.multiple_of(place * block_size, block_size), block_size)]
        product = transposed_product(held_ref[piece, inside], restricted)
        for m in range(entries):
            column = index_ref[0, 2 + index_ref[1 + half + entries * piece + m, inside]]
            out_ref[column] += product[m * block_size : (m + 1) * block_size]
        return carry

    lax.fori_loop(0, half * 2 * slot_count, step, 0, unroll=16)


def combine(own, columns, restricted, held, coarse_all, slot_count, block_size):
    half, _, wide = restricted.shape
    entries = held.shape[3] // block_size
    table_rows = -(-(1 + half + columns.shape[0]) // 8) * 8
    return pl.pallas_call(
        functools.partial(combine_kernel, slot_count=slot_count, entries=entries),
        out_shape=jax.ShapeDtypeStruct((coarse_all, block_size, wide), jnp.float32),
        in_specs=[pl.BlockSpec(memory_space=pltpu.VMEM)] * 4,
        out_specs=pl.BlockSpec(memory_space=pltpu.VMEM),
        scratch_shapes=[
            pltpu.VMEM((table_rows, LANES), jnp.int32),
            pltpu.SMEM((table_rows, LANES), jnp.int32),
            pltpu.SemaphoreType.DMA,
        ],
        compiler_params=pltpu.CompilerParams(vmem_limit_bytes=VMEM_LIMIT),
        cost_estimate=pl.CostEstimate(flops=1 << 28, bytes_accessed=4 << 20, transcendentals=0),
        name="combine",
    )(own, columns, restricted, held)


def row_swap(x, bit):
    return lax.ppermute(x, "row", [(r, r ^ bit) for r in range(lax.axis_size("row"))])


def half_swap(x):
    return lax.ppermute(x, "half", [(0, 1), (1, 0)])


def far_swap(x):
    half = lax.axis_size("near")
    pairs = [(h * half + n, (1 - h) * half + (n ^ half // 2)) for h in range(2) for n in range(half)]
    return lax.ppermute(x, ("half", "near"), pairs)


def spread_over_rows(blocks, rows):
    pieces = {0: blocks}
    bit = rows // 2
    while bit:
        for mask in list(pieces):
            pieces[mask ^ bit] = row_swap(pieces[mask], bit)
        bit //= 2
    return [pieces[mask] for mask in range(rows)]


def place_of_columns(half):
    own = lax.axis_index("half") * half + lax.axis_index("near")
    return jnp.arange(2 * half, dtype=jnp.int32) ^ own


def add_over_near(sums, half):
    total = sums[0]
    for near in range(1, half):
        total = total + lax.ppermute(sums[near], "near", [(n, n ^ near) for n in range(half)])
    return total


def add_over_columns(sums, half):
    crossing = half_swap(add_over_near(sums[half:], half))
    return add_over_near(sums[:half], half) + crossing


def local(
    operator_blocks,
    operator_count,
    operator_slot,
    fetch_lists,
    prolong_blocks,
    prolong_cols,
    restrict_blocks,
    restrict_rows,
):
    rows, half = lax.axis_size("row"), lax.axis_size("near")
    slot_count = fetch_lists.shape[3]
    fine_rows, block_size, width = prolong_blocks.shape
    fetch = fetch_lists.reshape(2 * half, slot_count).T
    own = jnp.stack([lax.axis_index("row"), lax.axis_index("half")])
    own = jnp.concatenate([own, place_of_columns(half)])[None]

    near_blocks = prolong_blocks.reshape(fine_rows * block_size, width)
    far_blocks = far_swap(near_blocks)
    restricted, own_columns, near_blocks = restrict_operator(
        operator_count,
        operator_slot,
        restrict_rows.T,
        fetch,
        operator_blocks,
        restrict_blocks,
        prolong_cols.T,
        near_blocks,
        lax.axis_index("half").reshape(1),
    )
    restricted = lax.all_to_all(restricted, "near", split_axis=0, concat_axis=0, tiled=True)
    far_columns = far_swap(own_columns)
    near_pieces = spread_over_rows(near_blocks, rows)
    far_blocks = append_columns(near_pieces[rows // 2], far_columns, own_columns, far_blocks)
    pieces = near_pieces + spread_over_rows(far_blocks, rows)
    held, columns = prepare(pieces, fine_rows, block_size)
    sums = combine(own, columns, restricted, held, NCR * rows, slot_count, block_size)
    return add_over_columns(sums, half).T


def solution(mesh):
    rows, columns = mesh.shape["row"], mesh.shape["col"]
    split = Mesh(mesh.devices.reshape(rows, 2, columns // 2), ("row", "half", "near"))
    flat = ("row", "half", "near")
    return jax.shard_map(
        local,
        mesh=split,
        in_specs=(
            P(flat, None, None),
            P(flat),
            P(flat, None),
            P("row", ("half", "near"), None, None),
            P(flat, None, None),
            P(flat, None),
            P(flat, None, None),
            P(flat, None),
        ),
        out_specs=P("row", ("half", "near")),
        check_vma=False,
    )
```

```python
import functools

import jax
import jax.numpy as jnp
from jax import lax
from jax.experimental import pallas as pl
from jax.experimental.pallas import tpu as pltpu
from jax.sharding import Mesh
from jax.sharding import PartitionSpec as P

NCR = 2
LANES = 128
EXTRA = 8
HOLD_FLOPS = 16 << 30
VMEM_LIMIT = 48 * 1024 * 1024


def halves(x):
    high = x.astype(jnp.bfloat16)
    return high, (x - high.astype(jnp.float32)).astype(jnp.bfloat16)


def transposed_product(left, right):
    tall = jnp.concatenate(halves(left), axis=0)
    wide = jnp.concatenate(halves(right), axis=1)
    wide = jnp.concatenate([wide, wide], axis=0)
    both = lax.dot_general(tall, wide, (((0,), (0,)), ((), ())), preferred_element_type=jnp.float32)
    width = right.shape[1]
    return both[:, :width] + both[:, width:]


def append_kernel(next_ref, far_columns_ref, own_columns_ref, blocks_ref, out_ref):
    used = blocks_ref.shape[0]
    entries, fine_rows = own_columns_ref.shape
    out_ref[:used] = blocks_ref[...]
    out_ref[used:] = jnp.zeros((EXTRA, out_ref.shape[1]), jnp.float32)
    out_ref[used : used + entries, :fine_rows] = far_columns_ref[...].astype(jnp.float32)
    out_ref[used + entries : used + 2 * entries, :fine_rows] = own_columns_ref[...].astype(jnp.float32)


def append_columns(next_blocks, far_columns, own_columns, blocks):
    used, width = blocks.shape
    return pl.pallas_call(
        append_kernel,
        out_shape=jax.ShapeDtypeStruct((used + EXTRA, width), blocks.dtype),
        in_specs=[pl.BlockSpec(memory_space=pltpu.VMEM)] * 4,
        out_specs=pl.BlockSpec(memory_space=pltpu.VMEM),
        compiler_params=pltpu.CompilerParams(vmem_limit_bytes=VMEM_LIMIT),
        cost_estimate=pl.CostEstimate(flops=HOLD_FLOPS, bytes_accessed=HOLD_FLOPS >> 8, transcendentals=0),
        name="append_columns",
    )(next_blocks, far_columns, own_columns, blocks)


def restrict_kernel(
    count_any, slot_any, rows_any, fetch_any, restrict_any, operator_any, columns_any, blocks_any, side_any,
    out_ref, own_columns_ref, own_blocks_ref,
    count_ref, slot_ref, rows_ref, fetch_ref, side_ref, restrict_ref, operator_ref, sems, operator_sems,
):
    fine_rows, block_size, _ = operator_ref.shape
    entries = slot_ref.shape[1]
    slot_count, columns = fetch_ref.shape
    half = columns // 2
    used = 2 * slot_count * block_size
    wide = NCR * block_size

    pairs = [
        (count_any, count_ref), (slot_any, slot_ref), (rows_any, rows_ref),
        (fetch_any, fetch_ref), (restrict_any, restrict_ref),
        (columns_any, own_columns_ref), (blocks_any, own_blocks_ref), (side_any, side_ref),
    ]
    copies = [pltpu.make_async_copy(a, b, sems.at[i]) for i, (a, b) in enumerate(pairs)]
    operators = [
        pltpu.make_async_copy(operator_any.at[i], operator_ref.at[i], operator_sems.at[i]) for i in range(fine_rows)
    ]
    for copy in copies + operators:
        copy.start()

    lane = lax.broadcasted_iota(jnp.int32, (block_size, wide), 1)
    second = (lane >= block_size).astype(jnp.int32)
    short_lane = lax.broadcasted_iota(jnp.int32, (EXTRA, wide), 1)
    for near in range(half):
        out_ref[near, :used] = jnp.zeros((used, wide), jnp.float32)
    for copy in copies + operators:
        copy.wait()

    for near in range(half):
        value = jnp.zeros((EXTRA, wide), jnp.int32)
        for side in range(2):
            for s in range(slot_count):
                turned = near ^ jnp.where(side_ref[0] == side, 0, half // 2)
                wanted = fetch_ref[s, side * half + turned]
                value = jnp.where(short_lane == side * slot_count + s, wanted, value)
        out_ref[near, used:] = value.astype(jnp.float32)

    for i in range(fine_rows):
        value = restrict_ref[i]
        swapped = pltpu.roll(value, block_size, 1)
        own_row = jnp.where(second == 0, rows_ref[0, i], rows_ref[1, i])
        other_row = jnp.where(second == 0, rows_ref[1, i], rows_ref[0, i])
        dense = jnp.where(own_row == second, value, 0.0) + jnp.where(other_row == second, swapped, 0.0)
        product = transposed_product(operator_ref[i], dense)
        for k in range(entries):
            part = jnp.where(k < count_ref[i], product[k * block_size : (k + 1) * block_size], 0.0)
            peer = lax.div(slot_ref[i, k], slot_count)
            side = lax.div(peer, half)
            place = side * slot_count + lax.rem(slot_ref[i, k], slot_count)
            near = lax.rem(peer, half) ^ jnp.where(side_ref[0] == side, 0, half // 2)
            start = pl.multiple_of(place * block_size, block_size)
            out_ref[near, pl.ds(start, block_size)] += part


def restrict_operator(
    operator_count, operator_slot, restrict_rows, fetch, operator_blocks, restrict_blocks, own_columns, own_blocks, side
):
    fine_rows, block_size, width = operator_blocks.shape
    slot_count, columns = fetch.shape
    wide = NCR * block_size
    rows = 2 * slot_count * block_size + EXTRA
    small = (operator_count, operator_slot, restrict_rows, fetch)
    kept = small + (side,)
    return pl.pallas_call(
        restrict_kernel,
        out_shape=(
            jax.ShapeDtypeStruct((columns // 2, rows, wide), jnp.float32),
            jax.ShapeDtypeStruct(own_columns.shape, own_columns.dtype),
            jax.ShapeDtypeStruct(own_blocks.shape, own_blocks.dtype),
        ),
        in_specs=[pl.BlockSpec(memory_space=pltpu.HBM)] * 9,
        out_specs=[pl.BlockSpec(memory_space=pltpu.VMEM)] * 3,
        scratch_shapes=[pltpu.SMEM(x.shape, x.dtype) for x in kept]
        + [pltpu.VMEM(x.shape, x.dtype) for x in (restrict_blocks, operator_blocks)]
        + [pltpu.SemaphoreType.DMA((8,)), pltpu.SemaphoreType.DMA((fine_rows,))],
        cost_estimate=pl.CostEstimate(
            flops=6 * fine_rows * block_size * width * wide, bytes_accessed=4 << 20, transcendentals=0
        ),
        name="restrict_operator",
    )(*small, restrict_blocks, operator_blocks, own_columns, own_blocks, side)


def combine_kernel(own_ref, restricted_ref, *rest, slot_count, fine_rows, entries):
    pieces, (out_ref, held_ref, table_ref, index_ref, sem) = rest[:-5], rest[-5:]
    half = restricted_ref.shape[0]
    rows = len(pieces) // 2
    block_size = out_ref.shape[1]
    columns = 2 * half
    used = 2 * slot_count * block_size
    held = fine_rows * block_size

    table_ref[:1, : own_ref.shape[1]] = own_ref[...]
    for near in range(half):
        table_ref[1 + near : 2 + near] = restricted_ref[near, used : used + 1].astype(jnp.int32)
    for i, piece in enumerate(pieces[rows:]):
        for far in range(2):
            first = 1 + half + entries * (far * rows + i)
            row = held + entries * (1 - far)
            table_ref[first : first + entries] = piece[row : row + entries].astype(jnp.int32)
    copy = pltpu.make_async_copy(table_ref, index_ref, sem)
    copy.start()
    for i, piece in enumerate(pieces):
        held_ref[i] = piece[...] if i < rows else piece[:held]
    out_ref[...] = jnp.zeros_like(out_ref)
    copy.wait()

    def step(i, carry):
        near = lax.div(i, 2 * slot_count)
        place = lax.rem(i, 2 * slot_count)
        wanted = index_ref[1 + near, place]
        inside = lax.rem(wanted, fine_rows)
        far = lax.div(place, slot_count) ^ index_ref[0, 1]
        piece = far * rows + (lax.div(wanted, fine_rows * columns) ^ index_ref[0, 0])
        block = held_ref[piece, pl.ds(pl.multiple_of(inside * block_size, block_size), block_size)]
        restricted = restricted_ref[near, pl.ds(pl.multiple_of(place * block_size, block_size), block_size)]
        product = transposed_product(block, restricted)
        for m in range(entries):
            column = index_ref[0, 2 + index_ref[1 + half + entries * piece + m, inside]]
            out_ref[column] += product[m * block_size : (m + 1) * block_size]
        return carry

    lax.fori_loop(0, half * 2 * slot_count, step, 0, unroll=16)


def combine(own, restricted, pieces, coarse_all, slot_count, fine_rows, block_size):
    half, _, wide = restricted.shape
    width = pieces[0].shape[1]
    entries = width // block_size
    table_rows = -(-(1 + half + entries * len(pieces)) // 8) * 8
    return pl.pallas_call(
        functools.partial(combine_kernel, slot_count=slot_count, fine_rows=fine_rows, entries=entries),
        out_shape=jax.ShapeDtypeStruct((coarse_all, block_size, wide), jnp.float32),
        in_specs=[pl.BlockSpec(memory_space=pltpu.VMEM)] * (2 + len(pieces)),
        out_specs=pl.BlockSpec(memory_space=pltpu.VMEM),
        scratch_shapes=[
            pltpu.VMEM((len(pieces), fine_rows * block_size, width), jnp.float32),
            pltpu.VMEM((table_rows, LANES), jnp.int32),
            pltpu.SMEM((table_rows, LANES), jnp.int32),
            pltpu.SemaphoreType.DMA,
        ],
        compiler_params=pltpu.CompilerParams(vmem_limit_bytes=VMEM_LIMIT),
        cost_estimate=pl.CostEstimate(flops=1 << 28, bytes_accessed=4 << 20, transcendentals=0),
        name="combine",
    )(own, restricted, *pieces)


def row_swap(x, bit):
    return lax.ppermute(x, "row", [(r, r ^ bit) for r in range(lax.axis_size("row"))])


def half_swap(x):
    return lax.ppermute(x, "half", [(0, 1), (1, 0)])


def far_swap(x):
    half = lax.axis_size("near")
    pairs = [(h * half + n, (1 - h) * half + (n ^ half // 2)) for h in range(2) for n in range(half)]
    return lax.ppermute(x, ("half", "near"), pairs)


def spread_over_rows(blocks, rows):
    pieces = {0: blocks}
    bit = rows // 2
    while bit:
        for mask in list(pieces):
            pieces[mask ^ bit] = row_swap(pieces[mask], bit)
        bit //= 2
    return [pieces[mask] for mask in range(rows)]


def place_of_columns(half):
    column = jnp.arange(2 * half, dtype=jnp.int32)
    return column % half * 2 + (column // half ^ lax.axis_index("half"))


def add_over_columns(sums, half):
    parts = lax.all_to_all(sums.reshape((half, 2) + sums.shape[1:]), "near", split_axis=0, concat_axis=0, tiled=True)
    total = parts[0]
    for near in range(1, half):
        total = total + parts[near]
    return total[0] + half_swap(total[1])


def local(
    operator_blocks,
    operator_count,
    operator_slot,
    fetch_lists,
    prolong_blocks,
    prolong_cols,
    restrict_blocks,
    restrict_rows,
):
    rows, half = lax.axis_size("row"), lax.axis_size("near")
    slot_count = fetch_lists.shape[3]
    fine_rows, block_size, width = prolong_blocks.shape
    fetch = fetch_lists.reshape(2 * half, slot_count).T
    own = jnp.stack([lax.axis_index("row"), lax.axis_index("half")])
    own = jnp.concatenate([own, place_of_columns(half)])[None]

    near_blocks = prolong_blocks.reshape(fine_rows * block_size, width)
    far_blocks = far_swap(near_blocks)
    restricted, own_columns, near_blocks = restrict_operator(
        operator_count,
        operator_slot,
        restrict_rows.T,
        fetch,
        operator_blocks,
        restrict_blocks,
        prolong_cols.T,
        near_blocks,
        lax.axis_index("half").reshape(1),
    )
    restricted = lax.all_to_all(restricted, "near", split_axis=0, concat_axis=0, tiled=True)
    far_columns = far_swap(own_columns)
    near_pieces = spread_over_rows(near_blocks, rows)
    far_blocks = append_columns(near_pieces[rows // 2], far_columns, own_columns, far_blocks)
    pieces = near_pieces + spread_over_rows(far_blocks, rows)
    sums = combine(own, restricted, pieces, NCR * rows, slot_count, fine_rows, block_size)
    return add_over_columns(sums, half).T


def solution(mesh):
    rows, columns = mesh.shape["row"], mesh.shape["col"]
    split = Mesh(mesh.devices.reshape(rows, 2, columns // 2), ("row", "half", "near"))
    flat = ("row", "half", "near")
    return jax.shard_map(
        local,
        mesh=split,
        in_specs=(
            P(flat, None, None),
            P(flat),
            P(flat, None),
            P("row", ("half", "near"), None, None),
            P(flat, None, None),
            P(flat, None),
            P(flat, None, None),
            P(flat, None),
        ),
        out_specs=P("row", ("half", "near")),
        check_vma=False,
    )
```

```python
import functools

import jax
import jax.numpy as jnp
from jax import lax
from jax.experimental import pallas as pl
from jax.experimental.pallas import tpu as pltpu
from jax.sharding import Mesh
from jax.sharding import PartitionSpec as P

NCR = 2
LANES = 128
EXTRA = 8
HOLD_FLOPS = 16 << 30
VMEM_LIMIT = 48 * 1024 * 1024


def halves(x):
    high = x.astype(jnp.bfloat16)
    return high, (x - high.astype(jnp.float32)).astype(jnp.bfloat16)


def transposed_product(left, right):
    tall = jnp.concatenate(halves(left), axis=0)
    wide = jnp.concatenate(halves(right), axis=1)
    wide = jnp.concatenate([wide, wide], axis=0)
    both = lax.dot_general(tall, wide, (((0,), (0,)), ((), ())), preferred_element_type=jnp.float32)
    width = right.shape[1]
    return both[:, :width] + both[:, width:]


def hold_kernel(mark_ref, next_ref, blocks_ref, out_ref):
    out_ref[...] = blocks_ref[...]


def hold_until(mark, next_blocks, blocks):
    return pl.pallas_call(
        hold_kernel,
        out_shape=jax.ShapeDtypeStruct(blocks.shape, blocks.dtype),
        in_specs=[pl.BlockSpec(memory_space=pltpu.VMEM)] * 3,
        out_specs=pl.BlockSpec(memory_space=pltpu.VMEM),
        compiler_params=pltpu.CompilerParams(vmem_limit_bytes=VMEM_LIMIT),
        cost_estimate=pl.CostEstimate(flops=HOLD_FLOPS, bytes_accessed=HOLD_FLOPS >> 8, transcendentals=0),
        name="hold_until",
    )(mark, next_blocks, blocks)


def restrict_kernel(
    count_any, slot_any, rows_any, fetch_any, restrict_any, operator_any, side_any, near_any,
    mark_ref, *refs,
):
    outs = refs[:-11]
    count_ref, slot_ref, rows_ref, fetch_ref, side_ref, near_ref, restrict_ref, operator_ref = refs[-11:-3]
    sems, operator_sems, out_sems = refs[-3:]
    out_ref = outs[-1]
    outs = outs[:-1]
    fine_rows, block_size, _ = operator_ref.shape
    entries = slot_ref.shape[1]
    slot_count, columns = fetch_ref.shape
    half = columns // 2
    used = 2 * slot_count * block_size
    wide = NCR * block_size

    pairs = [
        (count_any, count_ref), (slot_any, slot_ref), (rows_any, rows_ref),
        (fetch_any, fetch_ref), (restrict_any, restrict_ref),
        (side_any, side_ref), (near_any, near_ref),
    ]
    copies = [pltpu.make_async_copy(a, b, sems.at[i]) for i, (a, b) in enumerate(pairs)]
    operators = [
        pltpu.make_async_copy(operator_any.at[i], operator_ref.at[i], operator_sems.at[i]) for i in range(fine_rows)
    ]
    for copy in copies + operators:
        copy.start()

    lane = lax.broadcasted_iota(jnp.int32, (block_size, wide), 1)
    second = (lane >= block_size).astype(jnp.int32)
    short_lane = lax.broadcasted_iota(jnp.int32, (EXTRA, wide), 1)
    for near in range(half):
        out_ref[near, :used] = jnp.zeros((used, wide), jnp.float32)
    for copy in copies + operators:
        copy.wait()

    for near in range(half):
        value = jnp.zeros((EXTRA, wide), jnp.int32)
        for side in range(2):
            for s in range(slot_count):
                turned = near ^ jnp.where(side_ref[0] == side, 0, half // 2)
                wanted = fetch_ref[s, side * half + turned]
                value = jnp.where(short_lane == side * slot_count + s, wanted, value)
        out_ref[near ^ near_ref[0], used:] = value.astype(jnp.float32)
        mark_ref[...] = value.astype(jnp.float32)

    for i in range(fine_rows):
        value = restrict_ref[i]
        swapped = pltpu.roll(value, block_size, 1)
        own_row = jnp.where(second == 0, rows_ref[0, i], rows_ref[1, i])
        other_row = jnp.where(second == 0, rows_ref[1, i], rows_ref[0, i])
        dense = jnp.where(own_row == second, value, 0.0) + jnp.where(other_row == second, swapped, 0.0)
        product = transposed_product(operator_ref[i], dense)
        for k in range(entries):
            part = jnp.where(k < count_ref[i], product[k * block_size : (k + 1) * block_size], 0.0)
            peer = lax.div(slot_ref[i, k], slot_count)
            side = lax.div(peer, half)
            place = side * slot_count + lax.rem(slot_ref[i, k], slot_count)
            near = lax.rem(peer, half) ^ jnp.where(side_ref[0] == side, 0, half // 2) ^ near_ref[0]
            start = pl.multiple_of(place * block_size, block_size)
            out_ref[near, pl.ds(start, block_size)] += part

    writes = [pltpu.make_async_copy(out_ref.at[ahead], out, out_sems.at[ahead]) for ahead, out in enumerate(outs)]
    for copy in writes:
        copy.start()
    for copy in writes:
        copy.wait()


def restrict_operator(
    operator_count, operator_slot, restrict_rows, fetch, operator_blocks, restrict_blocks, side, near
):
    fine_rows, block_size, width = operator_blocks.shape
    slot_count, columns = fetch.shape
    half = columns // 2
    wide = NCR * block_size
    rows = 2 * slot_count * block_size + EXTRA
    small = (operator_count, operator_slot, restrict_rows, fetch)
    kept = small + (side, near)
    hbm = pl.BlockSpec(memory_space=pltpu.HBM)
    results = pl.pallas_call(
        restrict_kernel,
        out_shape=(jax.ShapeDtypeStruct((EXTRA, wide), jnp.float32),)
        + (jax.ShapeDtypeStruct((rows, wide), jnp.float32),) * half,
        in_specs=[hbm] * 8,
        out_specs=[pl.BlockSpec(memory_space=pltpu.VMEM)] + [hbm] * half,
        scratch_shapes=[pltpu.VMEM((half, rows, wide), jnp.float32)]
        + [pltpu.SMEM(x.shape, x.dtype) for x in kept]
        + [pltpu.VMEM(x.shape, x.dtype) for x in (restrict_blocks, operator_blocks)]
        + [pltpu.SemaphoreType.DMA((7,)), pltpu.SemaphoreType.DMA((fine_rows,)), pltpu.SemaphoreType.DMA((half,))],
        cost_estimate=pl.CostEstimate(
            flops=6 * fine_rows * block_size * width * wide, bytes_accessed=4 << 20, transcendentals=0
        ),
        name="restrict_operator",
    )(*small, restrict_blocks, operator_blocks, side, near)
    return results[0], results[1:]


def index_kernel(*refs):
    out_ref = refs[-1]
    out_ref[...] = jnp.zeros_like(out_ref)
    for i, part in enumerate(refs[:-1]):
        out_ref[i : i + 1] = part[part.shape[0] - EXTRA : part.shape[0] - EXTRA + 1].astype(jnp.int32)


def index_table(parts):
    rows = -(-len(parts) // 8) * 8
    return pl.pallas_call(
        index_kernel,
        out_shape=jax.ShapeDtypeStruct((rows, LANES), jnp.int32),
        in_specs=[pl.BlockSpec(memory_space=pltpu.VMEM)] * len(parts),
        out_specs=pl.BlockSpec(memory_space=pltpu.VMEM),
        compiler_params=pltpu.CompilerParams(vmem_limit_bytes=VMEM_LIMIT),
        cost_estimate=pl.CostEstimate(flops=HOLD_FLOPS, bytes_accessed=HOLD_FLOPS >> 8, transcendentals=0),
        name="index_table",
    )(*parts)


def combine_kernel(own_ref, wanted_ref, *rest, half, split, slot_count, fine_rows, entries):
    parts, chunks = rest[:half], list(rest[half:-5])
    out_ref, held_ref, table_ref, index_ref, sem = rest[-5:]
    rows = len(split) // 2
    block_size = out_ref.shape[1]
    columns = 2 * half
    held = fine_rows * block_size
    pieces = [[chunks.pop(0) for _ in range(count)] for count in split]

    table_ref[:1, : own_ref.shape[1]] = own_ref[...]
    table_ref[1 : 1 + half] = wanted_ref[:half]
    for i, piece in enumerate(pieces):
        first = 1 + half + entries * i
        row = piece[-1].shape[0] - EXTRA
        table_ref[first : first + entries] = piece[-1][row : row + entries].astype(jnp.int32)
    copy = pltpu.make_async_copy(table_ref, index_ref, sem)
    copy.start()
    for i, piece in enumerate(pieces):
        start = 0
        for chunk in piece:
            size = min(chunk.shape[0], held - start)
            held_ref[i, start : start + size] = chunk[:size]
            start += size
    out_ref[...] = jnp.zeros_like(out_ref)
    copy.wait()

    for ahead, part in enumerate(parts):

        def step(place, carry, ahead=ahead, part=part):
            wanted = index_ref[1 + ahead, place]
            inside = lax.rem(wanted, fine_rows)
            far = lax.div(place, slot_count) ^ index_ref[0, 1]
            piece = far * rows + (lax.div(wanted, fine_rows * columns) ^ index_ref[0, 0])
            block = held_ref[piece, pl.ds(pl.multiple_of(inside * block_size, block_size), block_size)]
            restricted = part[pl.ds(pl.multiple_of(place * block_size, block_size), block_size)]
            product = transposed_product(block, restricted)
            for m in range(entries):
                column = index_ref[0, 2 + index_ref[1 + half + entries * piece + m, inside]]
                out_ref[column] += product[m * block_size : (m + 1) * block_size]
            return carry

        lax.fori_loop(0, 2 * slot_count, step, 0, unroll=half <= 4)


def combine(own, wanted, parts, pieces, coarse_all, slot_count, fine_rows, block_size):
    half = len(parts)
    wide = parts[0].shape[1]
    width = pieces[0][0].shape[1]
    entries = width // block_size
    split = tuple(len(piece) for piece in pieces)
    chunks = [chunk for piece in pieces for chunk in piece]
    table_rows = -(-(1 + half + entries * len(pieces)) // 8) * 8
    return pl.pallas_call(
        functools.partial(
            combine_kernel, half=half, split=split, slot_count=slot_count, fine_rows=fine_rows, entries=entries
        ),
        out_shape=jax.ShapeDtypeStruct((coarse_all, block_size, wide), jnp.float32),
        in_specs=[pl.BlockSpec(memory_space=pltpu.VMEM)] * (2 + half + len(chunks)),
        out_specs=pl.BlockSpec(memory_space=pltpu.VMEM),
        scratch_shapes=[
            pltpu.VMEM((len(pieces), fine_rows * block_size, width), jnp.float32),
            pltpu.VMEM((table_rows, LANES), jnp.int32),
            pltpu.SMEM((table_rows, LANES), jnp.int32),
            pltpu.SemaphoreType.DMA,
        ],
        compiler_params=pltpu.CompilerParams(vmem_limit_bytes=VMEM_LIMIT),
        cost_estimate=pl.CostEstimate(flops=1 << 28, bytes_accessed=4 << 20, transcendentals=0),
        name="combine",
    )(own, wanted, *parts, *chunks)


def row_swap(x, bit):
    return lax.ppermute(x, "row", [(r, r ^ bit) for r in range(lax.axis_size("row"))])


def half_swap(x):
    return lax.ppermute(x, "half", [(0, 1), (1, 0)])


def far_swap(x):
    half = lax.axis_size("near")
    pairs = [(h * half + n, (1 - h) * half + (n ^ half // 2)) for h in range(2) for n in range(half)]
    return lax.ppermute(x, ("half", "near"), pairs)


def spread_over_rows(blocks, rows, cut):
    pieces = {0: [blocks]}
    bit = rows // 2
    while bit:
        for mask in list(pieces):
            chunks = pieces[mask]
            if cut and bit == rows // 2:
                chunks = [blocks[:cut], blocks[cut:]]
            pieces[mask ^ bit] = [row_swap(chunk, bit) for chunk in chunks]
        bit //= 2
    return [pieces[mask] for mask in range(rows)]


def place_of_columns(half):
    own = lax.axis_index("half") * half + lax.axis_index("near")
    return jnp.arange(2 * half, dtype=jnp.int32) ^ own


def add_over_near(sums, half):
    total = sums[0]
    for near in range(1, half):
        total = total + lax.ppermute(sums[near], "near", [(n, n ^ near) for n in range(half)])
    return total


def add_over_columns(sums, half):
    crossing = half_swap(add_over_near(sums[half:], half))
    return add_over_near(sums[:half], half) + crossing


def with_columns(columns, blocks):
    entries, fine_rows = columns.shape
    used, width = blocks.shape
    rows = jnp.pad(columns.astype(blocks.dtype), ((0, EXTRA - entries), (0, width - fine_rows)))
    return jnp.concatenate([blocks, rows], axis=0)


def local(
    operator_blocks,
    operator_count,
    operator_slot,
    fetch_lists,
    prolong_blocks,
    prolong_cols,
    restrict_blocks,
    restrict_rows,
):
    rows, half = lax.axis_size("row"), lax.axis_size("near")
    slot_count = fetch_lists.shape[3]
    fine_rows, block_size, width = prolong_blocks.shape
    fetch = fetch_lists.reshape(2 * half, slot_count).T
    own = jnp.stack([lax.axis_index("row"), lax.axis_index("half")])
    own = jnp.concatenate([own, place_of_columns(half)])[None]

    near_blocks = with_columns(prolong_cols.T, prolong_blocks.reshape(fine_rows * block_size, width))
    far_blocks = far_swap(near_blocks)
    mark, parts = restrict_operator(
        operator_count,
        operator_slot,
        restrict_rows.T,
        fetch,
        operator_blocks,
        restrict_blocks,
        lax.axis_index("half").reshape(1),
        lax.axis_index("near").reshape(1),
    )
    parts = [parts[0]] + [
        lax.ppermute(parts[ahead], "near", [(n, n ^ ahead) for n in range(half)]) for ahead in range(1, half)
    ]
    wanted = index_table(parts)
    near_pieces = spread_over_rows(near_blocks, rows, 0)
    far_blocks = hold_until(mark, near_pieces[rows // 2][0], far_blocks)
    pieces = near_pieces + spread_over_rows(far_blocks, rows, fine_rows * block_size // 2)
    sums = combine(own, wanted, parts, pieces, NCR * rows, slot_count, fine_rows, block_size)
    return add_over_columns(sums, half).T


def solution(mesh):
    rows, columns = mesh.shape["row"], mesh.shape["col"]
    split = Mesh(mesh.devices.reshape(rows, 2, columns // 2), ("row", "half", "near"))
    flat = ("row", "half", "near")
    return jax.shard_map(
        local,
        mesh=split,
        in_specs=(
            P(flat, None, None),
            P(flat),
            P(flat, None),
            P("row", ("half", "near"), None, None),
            P(flat, None, None),
            P(flat, None),
            P(flat, None, None),
            P(flat, None),
        ),
        out_specs=P("row", ("half", "near")),
        check_vma=False,
    )
```

```python
import functools

import jax
import jax.numpy as jnp
from jax import lax
from jax.experimental import pallas as pl
from jax.experimental.pallas import tpu as pltpu
from jax.sharding import Mesh
from jax.sharding import PartitionSpec as P

NCR = 2
LANES = 128
EXTRA = 8
HOLD_FLOPS = 16 << 30
INDEX_FLOPS = 1 << 30
VMEM_LIMIT = 48 * 1024 * 1024


def halves(x):
    high = x.astype(jnp.bfloat16)
    return high, (x - high.astype(jnp.float32)).astype(jnp.bfloat16)


def transposed_product(left, right):
    tall = jnp.concatenate(halves(left), axis=0)
    wide = jnp.concatenate(halves(right), axis=1)
    wide = jnp.concatenate([wide, wide], axis=0)
    both = lax.dot_general(tall, wide, (((0,), (0,)), ((), ())), preferred_element_type=jnp.float32)
    width = right.shape[1]
    return both[:, :width] + both[:, width:]


def hold_kernel(mark_ref, next_ref, blocks_ref, out_ref):
    out_ref[...] = blocks_ref[...]


def hold_until(mark, next_blocks, blocks):
    return pl.pallas_call(
        hold_kernel,
        out_shape=jax.ShapeDtypeStruct(blocks.shape, blocks.dtype),
        in_specs=[pl.BlockSpec(memory_space=pltpu.VMEM)] * 3,
        out_specs=pl.BlockSpec(memory_space=pltpu.VMEM),
        compiler_params=pltpu.CompilerParams(vmem_limit_bytes=VMEM_LIMIT),
        cost_estimate=pl.CostEstimate(flops=HOLD_FLOPS, bytes_accessed=HOLD_FLOPS >> 8, transcendentals=0),
        name="hold_until",
    )(mark, next_blocks, blocks)


def restrict_kernel(
    count_any, slot_any, rows_any, fetch_any, restrict_any, operator_any, side_any, near_any,
    mark_ref, *refs,
):
    outs = refs[:-11]
    count_ref, slot_ref, rows_ref, fetch_ref, side_ref, near_ref, restrict_ref, operator_ref = refs[-11:-3]
    sems, operator_sems, out_sems = refs[-3:]
    out_ref = outs[-1]
    outs = outs[:-1]
    fine_rows, block_size, _ = operator_ref.shape
    entries = slot_ref.shape[1]
    slot_count, columns = fetch_ref.shape
    half = columns // 2
    used = 2 * slot_count * block_size
    wide = NCR * block_size

    pairs = [
        (count_any, count_ref), (slot_any, slot_ref), (rows_any, rows_ref),
        (fetch_any, fetch_ref), (restrict_any, restrict_ref),
        (side_any, side_ref), (near_any, near_ref),
    ]
    copies = [pltpu.make_async_copy(a, b, sems.at[i]) for i, (a, b) in enumerate(pairs)]
    operators = [
        pltpu.make_async_copy(operator_any.at[i], operator_ref.at[i], operator_sems.at[i]) for i in range(fine_rows)
    ]
    for copy in copies + operators:
        copy.start()

    lane = lax.broadcasted_iota(jnp.int32, (block_size, wide), 1)
    second = (lane >= block_size).astype(jnp.int32)
    short_lane = lax.broadcasted_iota(jnp.int32, (EXTRA, wide), 1)
    for near in range(half):
        out_ref[near, :used] = jnp.zeros((used, wide), jnp.float32)
    for copy in copies + operators:
        copy.wait()

    for near in range(half):
        value = jnp.zeros((EXTRA, wide), jnp.int32)
        for side in range(2):
            for s in range(slot_count):
                turned = near ^ jnp.where(side_ref[0] == side, 0, half // 2)
                wanted = fetch_ref[s, side * half + turned]
                value = jnp.where(short_lane == side * slot_count + s, wanted, value)
        out_ref[near ^ near_ref[0], used:] = value.astype(jnp.float32)
        mark_ref[...] = value.astype(jnp.float32)

    for i in range(fine_rows):
        value = restrict_ref[i]
        swapped = pltpu.roll(value, block_size, 1)
        own_row = jnp.where(second == 0, rows_ref[0, i], rows_ref[1, i])
        other_row = jnp.where(second == 0, rows_ref[1, i], rows_ref[0, i])
        dense = jnp.where(own_row == second, value, 0.0) + jnp.where(other_row == second, swapped, 0.0)
        product = transposed_product(operator_ref[i], dense)
        for k in range(entries):
            part = jnp.where(k < count_ref[i], product[k * block_size : (k + 1) * block_size], 0.0)
            peer = lax.div(slot_ref[i, k], slot_count)
            side = lax.div(peer, half)
            place = side * slot_count + lax.rem(slot_ref[i, k], slot_count)
            near = lax.rem(peer, half) ^ jnp.where(side_ref[0] == side, 0, half // 2) ^ near_ref[0]
            start = pl.multiple_of(place * block_size, block_size)
            out_ref[near, pl.ds(start, block_size)] += part

    writes = [pltpu.make_async_copy(out_ref.at[ahead], out, out_sems.at[ahead]) for ahead, out in enumerate(outs)]
    for copy in writes:
        copy.start()
    for copy in writes:
        copy.wait()


def restrict_operator(
    operator_count, operator_slot, restrict_rows, fetch, operator_blocks, restrict_blocks, side, near
):
    fine_rows, block_size, width = operator_blocks.shape
    slot_count, columns = fetch.shape
    half = columns // 2
    wide = NCR * block_size
    rows = 2 * slot_count * block_size + EXTRA
    small = (operator_count, operator_slot, restrict_rows, fetch)
    kept = small + (side, near)
    hbm = pl.BlockSpec(memory_space=pltpu.HBM)
    results = pl.pallas_call(
        restrict_kernel,
        out_shape=(jax.ShapeDtypeStruct((EXTRA, wide), jnp.float32),)
        + (jax.ShapeDtypeStruct((rows, wide), jnp.float32),) * half,
        in_specs=[hbm] * 8,
        out_specs=[pl.BlockSpec(memory_space=pltpu.VMEM)] + [hbm] * half,
        scratch_shapes=[pltpu.VMEM((half, rows, wide), jnp.float32)]
        + [pltpu.SMEM(x.shape, x.dtype) for x in kept]
        + [pltpu.VMEM(x.shape, x.dtype) for x in (restrict_blocks, operator_blocks)]
        + [pltpu.SemaphoreType.DMA((7,)), pltpu.SemaphoreType.DMA((fine_rows,)), pltpu.SemaphoreType.DMA((half,))],
        cost_estimate=pl.CostEstimate(
            flops=6 * fine_rows * block_size * width * wide, bytes_accessed=4 << 20, transcendentals=0
        ),
        name="restrict_operator",
    )(*small, restrict_blocks, operator_blocks, side, near)
    return results[0], results[1:]


def index_kernel(*refs):
    out_ref = refs[-1]
    out_ref[...] = jnp.zeros_like(out_ref)
    for i, part in enumerate(refs[:-1]):
        out_ref[i : i + 1] = part[part.shape[0] - EXTRA : part.shape[0] - EXTRA + 1].astype(jnp.int32)


def index_table(parts):
    rows = -(-len(parts) // 8) * 8
    return pl.pallas_call(
        index_kernel,
        out_shape=jax.ShapeDtypeStruct((rows, LANES), jnp.int32),
        in_specs=[pl.BlockSpec(memory_space=pltpu.VMEM)] * len(parts),
        out_specs=pl.BlockSpec(memory_space=pltpu.VMEM),
        compiler_params=pltpu.CompilerParams(vmem_limit_bytes=VMEM_LIMIT),
        cost_estimate=pl.CostEstimate(flops=INDEX_FLOPS, bytes_accessed=INDEX_FLOPS >> 8, transcendentals=0),
        name="index_table",
    )(*parts)


def combine_kernel(own_ref, wanted_ref, *rest, half, split, slot_count, fine_rows, entries):
    parts, chunks = rest[:half], list(rest[half:-5])
    out_ref, held_ref, table_ref, index_ref, sem = rest[-5:]
    rows = len(split) // 2
    block_size = out_ref.shape[1]
    columns = 2 * half
    held = fine_rows * block_size
    pieces = [[chunks.pop(0) for _ in range(count)] for count in split]

    table_ref[:1, : own_ref.shape[1]] = own_ref[...]
    table_ref[1 : 1 + half] = wanted_ref[:half]
    for i, piece in enumerate(pieces):
        first = 1 + half + entries * i
        row = piece[-1].shape[0] - EXTRA
        table_ref[first : first + entries] = piece[-1][row : row + entries].astype(jnp.int32)
    copy = pltpu.make_async_copy(table_ref, index_ref, sem)
    copy.start()
    for i, piece in enumerate(pieces):
        start = 0
        for chunk in piece:
            size = min(chunk.shape[0], held - start)
            held_ref[i, start : start + size] = chunk[:size]
            start += size
    out_ref[...] = jnp.zeros_like(out_ref)
    copy.wait()

    for ahead, part in enumerate(parts):

        def step(place, carry, ahead=ahead, part=part):
            wanted = index_ref[1 + ahead, place]
            inside = lax.rem(wanted, fine_rows)
            far = lax.div(place, slot_count) ^ index_ref[0, 1]
            piece = far * rows + (lax.div(wanted, fine_rows * columns) ^ index_ref[0, 0])
            block = held_ref[piece, pl.ds(pl.multiple_of(inside * block_size, block_size), block_size)]
            restricted = part[pl.ds(pl.multiple_of(place * block_size, block_size), block_size)]
            product = transposed_product(block, restricted)
            for m in range(entries):
                column = index_ref[0, 2 + index_ref[1 + half + entries * piece + m, inside]]
                out_ref[column] += product[m * block_size : (m + 1) * block_size]
            return carry

        lax.fori_loop(0, 2 * slot_count, step, 0, unroll=half <= 4)


def combine(own, wanted, parts, pieces, coarse_all, slot_count, fine_rows, block_size):
    half = len(parts)
    wide = parts[0].shape[1]
    width = pieces[0][0].shape[1]
    entries = width // block_size
    split = tuple(len(piece) for piece in pieces)
    chunks = [chunk for piece in pieces for chunk in piece]
    table_rows = -(-(1 + half + entries * len(pieces)) // 8) * 8
    return pl.pallas_call(
        functools.partial(
            combine_kernel, half=half, split=split, slot_count=slot_count, fine_rows=fine_rows, entries=entries
        ),
        out_shape=jax.ShapeDtypeStruct((coarse_all, block_size, wide), jnp.float32),
        in_specs=[pl.BlockSpec(memory_space=pltpu.VMEM)] * (2 + half + len(chunks)),
        out_specs=pl.BlockSpec(memory_space=pltpu.VMEM),
        scratch_shapes=[
            pltpu.VMEM((len(pieces), fine_rows * block_size, width), jnp.float32),
            pltpu.VMEM((table_rows, LANES), jnp.int32),
            pltpu.SMEM((table_rows, LANES), jnp.int32),
            pltpu.SemaphoreType.DMA,
        ],
        compiler_params=pltpu.CompilerParams(vmem_limit_bytes=VMEM_LIMIT),
        cost_estimate=pl.CostEstimate(flops=1 << 28, bytes_accessed=4 << 20, transcendentals=0),
        name="combine",
    )(own, wanted, *parts, *chunks)


def row_swap(x, bit):
    return lax.ppermute(x, "row", [(r, r ^ bit) for r in range(lax.axis_size("row"))])


def half_swap(x):
    return lax.ppermute(x, "half", [(0, 1), (1, 0)])


def far_swap(x):
    half = lax.axis_size("near")
    pairs = [(h * half + n, (1 - h) * half + (n ^ half // 2)) for h in range(2) for n in range(half)]
    return lax.ppermute(x, ("half", "near"), pairs)


def spread_over_rows(blocks, rows, cut):
    pieces = {0: [blocks]}
    bit = rows // 2
    while bit:
        for mask in list(pieces):
            chunks = pieces[mask]
            if cut and bit == rows // 2:
                chunks = [blocks[:cut], blocks[cut:]]
            pieces[mask ^ bit] = [row_swap(chunk, bit) for chunk in chunks]
        bit //= 2
    return [pieces[mask] for mask in range(rows)]


def place_of_columns(half):
    own = lax.axis_index("half") * half + lax.axis_index("near")
    return jnp.arange(2 * half, dtype=jnp.int32) ^ own


def add_over_near(sums, half):
    total = sums[0]
    for near in range(1, half):
        total = total + lax.ppermute(sums[near], "near", [(n, n ^ near) for n in range(half)])
    return total


def add_over_columns(sums, half):
    crossing = half_swap(add_over_near(sums[half:], half))
    return add_over_near(sums[:half], half) + crossing


def with_columns(columns, blocks):
    entries, fine_rows = columns.shape
    used, width = blocks.shape
    rows = jnp.pad(columns.astype(blocks.dtype), ((0, EXTRA - entries), (0, width - fine_rows)))
    return jnp.concatenate([blocks, rows], axis=0)


def local(
    operator_blocks,
    operator_count,
    operator_slot,
    fetch_lists,
    prolong_blocks,
    prolong_cols,
    restrict_blocks,
    restrict_rows,
):
    rows, half = lax.axis_size("row"), lax.axis_size("near")
    slot_count = fetch_lists.shape[3]
    fine_rows, block_size, width = prolong_blocks.shape
    fetch = fetch_lists.reshape(2 * half, slot_count).T
    own = jnp.stack([lax.axis_index("row"), lax.axis_index("half")])
    own = jnp.concatenate([own, place_of_columns(half)])[None]

    near_blocks = with_columns(prolong_cols.T, prolong_blocks.reshape(fine_rows * block_size, width))
    far_blocks = far_swap(near_blocks)
    mark, parts = restrict_operator(
        operator_count,
        operator_slot,
        restrict_rows.T,
        fetch,
        operator_blocks,
        restrict_blocks,
        lax.axis_index("half").reshape(1),
        lax.axis_index("near").reshape(1),
    )
    parts = [parts[0]] + [
        lax.ppermute(parts[ahead], "near", [(n, n ^ ahead) for n in range(half)]) for ahead in range(1, half)
    ]
    wanted = index_table(parts)
    near_pieces = spread_over_rows(near_blocks, rows, 0)
    far_blocks = hold_until(mark, near_pieces[rows // 2][0], far_blocks)
    pieces = near_pieces + spread_over_rows(far_blocks, rows, fine_rows * block_size // 2)
    sums = combine(own, wanted, parts, pieces, NCR * rows, slot_count, fine_rows, block_size)
    return add_over_columns(sums, half).T


def solution(mesh):
    rows, columns = mesh.shape["row"], mesh.shape["col"]
    split = Mesh(mesh.devices.reshape(rows, 2, columns // 2), ("row", "half", "near"))
    flat = ("row", "half", "near")
    return jax.shard_map(
        local,
        mesh=split,
        in_specs=(
            P(flat, None, None),
            P(flat),
            P(flat, None),
            P("row", ("half", "near"), None, None),
            P(flat, None, None),
            P(flat, None),
            P(flat, None, None),
            P(flat, None),
        ),
        out_specs=P("row", ("half", "near")),
        check_vma=False,
    )
```

```python
import functools

import jax
import jax.numpy as jnp
from jax import lax
from jax.experimental import pallas as pl
from jax.experimental.pallas import tpu as pltpu
from jax.sharding import Mesh
from jax.sharding import PartitionSpec as P

NCR = 2
LANES = 128
EXTRA = 8
HOLD_FLOPS = 16 << 30
INDEX_FLOPS = 1 << 20
VMEM_LIMIT = 48 * 1024 * 1024


def halves(x):
    high = x.astype(jnp.bfloat16)
    return high, (x - high.astype(jnp.float32)).astype(jnp.bfloat16)


def transposed_product(left, right):
    tall = jnp.concatenate(halves(left), axis=0)
    wide = jnp.concatenate(halves(right), axis=1)
    wide = jnp.concatenate([wide, wide], axis=0)
    both = lax.dot_general(tall, wide, (((0,), (0,)), ((), ())), preferred_element_type=jnp.float32)
    width = right.shape[1]
    return both[:, :width] + both[:, width:]


def hold_kernel(mark_ref, next_ref, blocks_ref, out_ref):
    out_ref[...] = blocks_ref[...]


def hold_until(mark, next_blocks, blocks):
    return pl.pallas_call(
        hold_kernel,
        out_shape=jax.ShapeDtypeStruct(blocks.shape, blocks.dtype),
        in_specs=[pl.BlockSpec(memory_space=pltpu.VMEM)] * 3,
        out_specs=pl.BlockSpec(memory_space=pltpu.VMEM),
        compiler_params=pltpu.CompilerParams(vmem_limit_bytes=VMEM_LIMIT),
        cost_estimate=pl.CostEstimate(flops=HOLD_FLOPS, bytes_accessed=HOLD_FLOPS >> 8, transcendentals=0),
        name="hold_until",
    )(mark, next_blocks, blocks)


def restrict_kernel(
    count_any, slot_any, rows_any, fetch_any, restrict_any, operator_any, side_any, near_any,
    mark_ref, *refs,
):
    outs = refs[:-11]
    count_ref, slot_ref, rows_ref, fetch_ref, side_ref, near_ref, restrict_ref, operator_ref = refs[-11:-3]
    sems, operator_sems, out_sems = refs[-3:]
    out_ref = outs[-1]
    outs = outs[:-1]
    fine_rows, block_size, _ = operator_ref.shape
    entries = slot_ref.shape[1]
    slot_count, columns = fetch_ref.shape
    half = columns // 2
    used = 2 * slot_count * block_size
    wide = NCR * block_size

    pairs = [
        (count_any, count_ref), (slot_any, slot_ref), (rows_any, rows_ref),
        (fetch_any, fetch_ref), (restrict_any, restrict_ref),
        (side_any, side_ref), (near_any, near_ref),
    ]
    copies = [pltpu.make_async_copy(a, b, sems.at[i]) for i, (a, b) in enumerate(pairs)]
    operators = [
        pltpu.make_async_copy(operator_any.at[i], operator_ref.at[i], operator_sems.at[i]) for i in range(fine_rows)
    ]
    for copy in copies + operators:
        copy.start()

    lane = lax.broadcasted_iota(jnp.int32, (block_size, wide), 1)
    second = (lane >= block_size).astype(jnp.int32)
    short_lane = lax.broadcasted_iota(jnp.int32, (EXTRA, wide), 1)
    for near in range(half):
        out_ref[near, :used] = jnp.zeros((used, wide), jnp.float32)
    for copy in copies + operators:
        copy.wait()

    for near in range(half):
        value = jnp.zeros((EXTRA, wide), jnp.int32)
        for side in range(2):
            for s in range(slot_count):
                turned = near ^ jnp.where(side_ref[0] == side, 0, half // 2)
                wanted = fetch_ref[s, side * half + turned]
                value = jnp.where(short_lane == side * slot_count + s, wanted, value)
        out_ref[near ^ near_ref[0], used:] = value.astype(jnp.float32)
        mark_ref[...] = value.astype(jnp.float32)

    for i in range(fine_rows):
        value = restrict_ref[i]
        swapped = pltpu.roll(value, block_size, 1)
        own_row = jnp.where(second == 0, rows_ref[0, i], rows_ref[1, i])
        other_row = jnp.where(second == 0, rows_ref[1, i], rows_ref[0, i])
        dense = jnp.where(own_row == second, value, 0.0) + jnp.where(other_row == second, swapped, 0.0)
        product = transposed_product(operator_ref[i], dense)
        for k in range(entries):
            part = jnp.where(k < count_ref[i], product[k * block_size : (k + 1) * block_size], 0.0)
            peer = lax.div(slot_ref[i, k], slot_count)
            side = lax.div(peer, half)
            place = side * slot_count + lax.rem(slot_ref[i, k], slot_count)
            near = lax.rem(peer, half) ^ jnp.where(side_ref[0] == side, 0, half // 2) ^ near_ref[0]
            start = pl.multiple_of(place * block_size, block_size)
            out_ref[near, pl.ds(start, block_size)] += part

    writes = [pltpu.make_async_copy(out_ref.at[ahead], out, out_sems.at[ahead]) for ahead, out in enumerate(outs)]
    for copy in writes:
        copy.start()
    for copy in writes:
        copy.wait()


def restrict_operator(
    operator_count, operator_slot, restrict_rows, fetch, operator_blocks, restrict_blocks, side, near
):
    fine_rows, block_size, width = operator_blocks.shape
    slot_count, columns = fetch.shape
    half = columns // 2
    wide = NCR * block_size
    rows = 2 * slot_count * block_size + EXTRA
    small = (operator_count, operator_slot, restrict_rows, fetch)
    kept = small + (side, near)
    hbm = pl.BlockSpec(memory_space=pltpu.HBM)
    results = pl.pallas_call(
        restrict_kernel,
        out_shape=(jax.ShapeDtypeStruct((EXTRA, wide), jnp.float32),)
        + (jax.ShapeDtypeStruct((rows, wide), jnp.float32),) * half,
        in_specs=[hbm] * 8,
        out_specs=[pl.BlockSpec(memory_space=pltpu.VMEM)] + [hbm] * half,
        scratch_shapes=[pltpu.VMEM((half, rows, wide), jnp.float32)]
        + [pltpu.SMEM(x.shape, x.dtype) for x in kept]
        + [pltpu.VMEM(x.shape, x.dtype) for x in (restrict_blocks, operator_blocks)]
        + [pltpu.SemaphoreType.DMA((7,)), pltpu.SemaphoreType.DMA((fine_rows,)), pltpu.SemaphoreType.DMA((half,))],
        cost_estimate=pl.CostEstimate(
            flops=6 * fine_rows * block_size * width * wide, bytes_accessed=4 << 20, transcendentals=0
        ),
        name="restrict_operator",
    )(*small, restrict_blocks, operator_blocks, side, near)
    return results[0], results[1:]


def index_kernel(*refs):
    out_ref = refs[-1]
    out_ref[...] = jnp.zeros_like(out_ref)
    for i, part in enumerate(refs[:-1]):
        out_ref[i : i + 1] = part[part.shape[0] - EXTRA : part.shape[0] - EXTRA + 1].astype(jnp.int32)


def index_table(parts):
    rows = -(-len(parts) // 8) * 8
    return pl.pallas_call(
        index_kernel,
        out_shape=jax.ShapeDtypeStruct((rows, LANES), jnp.int32),
        in_specs=[pl.BlockSpec(memory_space=pltpu.VMEM)] * len(parts),
        out_specs=pl.BlockSpec(memory_space=pltpu.VMEM),
        compiler_params=pltpu.CompilerParams(vmem_limit_bytes=VMEM_LIMIT),
        cost_estimate=pl.CostEstimate(flops=INDEX_FLOPS, bytes_accessed=INDEX_FLOPS >> 8, transcendentals=0),
        name="index_table",
    )(*parts)


def combine_kernel(own_ref, wanted_ref, *rest, half, split, slot_count, fine_rows, entries):
    parts, chunks = rest[:half], list(rest[half:-5])
    out_ref, held_ref, table_ref, index_ref, sem = rest[-5:]
    rows = len(split) // 2
    block_size = out_ref.shape[1]
    columns = 2 * half
    held = fine_rows * block_size
    pieces = [[chunks.pop(0) for _ in range(count)] for count in split]

    table_ref[:1, : own_ref.shape[1]] = own_ref[...]
    table_ref[1 : 1 + half] = wanted_ref[:half]
    for i, piece in enumerate(pieces):
        first = 1 + half + entries * i
        row = piece[-1].shape[0] - EXTRA
        table_ref[first : first + entries] = piece[-1][row : row + entries].astype(jnp.int32)
    copy = pltpu.make_async_copy(table_ref, index_ref, sem)
    copy.start()
    for i, piece in enumerate(pieces):
        start = 0
        for chunk in piece:
            size = min(chunk.shape[0], held - start)
            held_ref[i, start : start + size] = chunk[:size]
            start += size
    out_ref[...] = jnp.zeros_like(out_ref)
    copy.wait()

    for ahead, part in enumerate(parts):

        def step(place, carry, ahead=ahead, part=part):
            wanted = index_ref[1 + ahead, place]
            inside = lax.rem(wanted, fine_rows)
            far = lax.div(place, slot_count) ^ index_ref[0, 1]
            piece = far * rows + (lax.div(wanted, fine_rows * columns) ^ index_ref[0, 0])
            block = held_ref[piece, pl.ds(pl.multiple_of(inside * block_size, block_size), block_size)]
            restricted = part[pl.ds(pl.multiple_of(place * block_size, block_size), block_size)]
            product = transposed_product(block, restricted)
            for m in range(entries):
                column = index_ref[0, 2 + index_ref[1 + half + entries * piece + m, inside]]
                out_ref[column] += product[m * block_size : (m + 1) * block_size]
            return carry

        lax.fori_loop(0, 2 * slot_count, step, 0, unroll=half <= 4)


def combine(own, wanted, parts, pieces, coarse_all, slot_count, fine_rows, block_size):
    half = len(parts)
    wide = parts[0].shape[1]
    width = pieces[0][0].shape[1]
    entries = width // block_size
    split = tuple(len(piece) for piece in pieces)
    chunks = [chunk for piece in pieces for chunk in piece]
    table_rows = -(-(1 + half + entries * len(pieces)) // 8) * 8
    return pl.pallas_call(
        functools.partial(
            combine_kernel, half=half, split=split, slot_count=slot_count, fine_rows=fine_rows, entries=entries
        ),
        out_shape=jax.ShapeDtypeStruct((coarse_all, block_size, wide), jnp.float32),
        in_specs=[pl.BlockSpec(memory_space=pltpu.VMEM)] * (2 + half + len(chunks)),
        out_specs=pl.BlockSpec(memory_space=pltpu.VMEM),
        scratch_shapes=[
            pltpu.VMEM((len(pieces), fine_rows * block_size, width), jnp.float32),
            pltpu.VMEM((table_rows, LANES), jnp.int32),
            pltpu.SMEM((table_rows, LANES), jnp.int32),
            pltpu.SemaphoreType.DMA,
        ],
        compiler_params=pltpu.CompilerParams(vmem_limit_bytes=VMEM_LIMIT),
        cost_estimate=pl.CostEstimate(flops=1 << 28, bytes_accessed=4 << 20, transcendentals=0),
        name="combine",
    )(own, wanted, *parts, *chunks)


def row_swap(x, bit):
    return lax.ppermute(x, "row", [(r, r ^ bit) for r in range(lax.axis_size("row"))])


def half_swap(x):
    return lax.ppermute(x, "half", [(0, 1), (1, 0)])


def far_swap(x):
    half = lax.axis_size("near")
    pairs = [(h * half + n, (1 - h) * half + (n ^ half // 2)) for h in range(2) for n in range(half)]
    return lax.ppermute(x, ("half", "near"), pairs)


def spread_over_rows(blocks, rows, cut):
    pieces = {0: [blocks[:cut], blocks[cut:]] if cut else [blocks]}
    bit = rows // 2
    while bit:
        for mask in list(pieces):
            pieces[mask ^ bit] = [row_swap(chunk, bit) for chunk in pieces[mask]]
        bit //= 2
    return [pieces[mask] for mask in range(rows)]


def place_of_columns(half):
    own = lax.axis_index("half") * half + lax.axis_index("near")
    return jnp.arange(2 * half, dtype=jnp.int32) ^ own


def add_over_near(sums, half):
    total = sums[0]
    for near in range(1, half):
        total = total + lax.ppermute(sums[near], "near", [(n, n ^ near) for n in range(half)])
    return total


def add_over_columns(sums, half):
    crossing = half_swap(add_over_near(sums[half:], half))
    return add_over_near(sums[:half], half) + crossing


def with_columns(columns, blocks):
    entries, fine_rows = columns.shape
    used, width = blocks.shape
    rows = jnp.pad(columns.astype(blocks.dtype), ((0, EXTRA - entries), (0, width - fine_rows)))
    return jnp.concatenate([blocks, rows], axis=0)


def local(
    operator_blocks,
    operator_count,
    operator_slot,
    fetch_lists,
    prolong_blocks,
    prolong_cols,
    restrict_blocks,
    restrict_rows,
):
    rows, half = lax.axis_size("row"), lax.axis_size("near")
    slot_count = fetch_lists.shape[3]
    fine_rows, block_size, width = prolong_blocks.shape
    fetch = fetch_lists.reshape(2 * half, slot_count).T
    own = jnp.stack([lax.axis_index("row"), lax.axis_index("half")])
    own = jnp.concatenate([own, place_of_columns(half)])[None]

    near_blocks = with_columns(prolong_cols.T, prolong_blocks.reshape(fine_rows * block_size, width))
    far_blocks = far_swap(near_blocks)
    mark, parts = restrict_operator(
        operator_count,
        operator_slot,
        restrict_rows.T,
        fetch,
        operator_blocks,
        restrict_blocks,
        lax.axis_index("half").reshape(1),
        lax.axis_index("near").reshape(1),
    )
    parts = [parts[0]] + [
        lax.ppermute(parts[ahead], "near", [(n, n ^ ahead) for n in range(half)]) for ahead in range(1, half)
    ]
    wanted = index_table(parts)
    near_pieces = spread_over_rows(near_blocks, rows, 0)
    far_blocks = hold_until(mark, near_pieces[rows // 2][0], far_blocks)
    pieces = near_pieces + spread_over_rows(far_blocks, rows, fine_rows * block_size // 2)
    sums = combine(own, wanted, parts, pieces, NCR * rows, slot_count, fine_rows, block_size)
    return add_over_columns(sums, half).T


def solution(mesh):
    rows, columns = mesh.shape["row"], mesh.shape["col"]
    split = Mesh(mesh.devices.reshape(rows, 2, columns // 2), ("row", "half", "near"))
    flat = ("row", "half", "near")
    return jax.shard_map(
        local,
        mesh=split,
        in_specs=(
            P(flat, None, None),
            P(flat),
            P(flat, None),
            P("row", ("half", "near"), None, None),
            P(flat, None, None),
            P(flat, None),
            P(flat, None, None),
            P(flat, None),
        ),
        out_specs=P("row", ("half", "near")),
        check_vma=False,
    )
```

```python
import functools

import jax
import jax.numpy as jnp
from jax import lax
from jax.experimental import pallas as pl
from jax.experimental.pallas import tpu as pltpu
from jax.sharding import Mesh
from jax.sharding import PartitionSpec as P

NCR = 2
LANES = 128
EXTRA = 8
HOLD_FLOPS = 16 << 30
VMEM_LIMIT = 48 * 1024 * 1024


def halves(x):
    high = x.astype(jnp.bfloat16)
    return high, (x - high.astype(jnp.float32)).astype(jnp.bfloat16)


def transposed_product(left, right):
    tall = jnp.concatenate(halves(left), axis=0)
    wide = jnp.concatenate(halves(right), axis=1)
    wide = jnp.concatenate([wide, wide], axis=0)
    both = lax.dot_general(tall, wide, (((0,), (0,)), ((), ())), preferred_element_type=jnp.float32)
    width = right.shape[1]
    return both[:, :width] + both[:, width:]


def append_kernel(far_columns_ref, own_columns_ref, blocks_ref, out_ref):
    used = blocks_ref.shape[0]
    entries, fine_rows = own_columns_ref.shape
    out_ref[:used] = blocks_ref[...]
    out_ref[used:] = jnp.zeros((EXTRA, out_ref.shape[1]), jnp.float32)
    out_ref[used : used + entries, :fine_rows] = far_columns_ref[...].astype(jnp.float32)
    out_ref[used + entries : used + 2 * entries, :fine_rows] = own_columns_ref[...].astype(jnp.float32)


def append_columns(far_columns, own_columns, blocks):
    used, width = blocks.shape
    return pl.pallas_call(
        append_kernel,
        out_shape=jax.ShapeDtypeStruct((used + EXTRA, width), blocks.dtype),
        in_specs=[pl.BlockSpec(memory_space=pltpu.VMEM)] * 3,
        out_specs=pl.BlockSpec(memory_space=pltpu.VMEM),
        compiler_params=pltpu.CompilerParams(vmem_limit_bytes=VMEM_LIMIT),
        cost_estimate=pl.CostEstimate(flops=HOLD_FLOPS, bytes_accessed=HOLD_FLOPS >> 8, transcendentals=0),
        name="append_columns",
    )(far_columns, own_columns, blocks)


def hold_kernel(next_ref, blocks_ref, out_ref):
    out_ref[...] = blocks_ref[...]


def hold_until(next_blocks, blocks):
    return pl.pallas_call(
        hold_kernel,
        out_shape=jax.ShapeDtypeStruct(blocks.shape, blocks.dtype),
        in_specs=[pl.BlockSpec(memory_space=pltpu.VMEM)] * 2,
        out_specs=pl.BlockSpec(memory_space=pltpu.VMEM),
        compiler_params=pltpu.CompilerParams(vmem_limit_bytes=VMEM_LIMIT),
        cost_estimate=pl.CostEstimate(flops=0, bytes_accessed=1 << 19, transcendentals=0),
        name="hold_until",
    )(next_blocks, blocks)


def restrict_kernel(
    count_any, slot_any, rows_any, fetch_any, restrict_any, operator_any, columns_any, blocks_any, side_any,
    out_ref, own_columns_ref, own_blocks_ref,
    count_ref, slot_ref, rows_ref, fetch_ref, side_ref, restrict_ref, operator_ref, sems, operator_sems,
):
    fine_rows, block_size, _ = operator_ref.shape
    entries = slot_ref.shape[1]
    slot_count, columns = fetch_ref.shape
    half = columns // 2
    used = 2 * slot_count * block_size
    wide = NCR * block_size

    pairs = [
        (count_any, count_ref), (slot_any, slot_ref), (rows_any, rows_ref),
        (fetch_any, fetch_ref), (restrict_any, restrict_ref),
        (columns_any, own_columns_ref), (blocks_any, own_blocks_ref), (side_any, side_ref),
    ]
    copies = [pltpu.make_async_copy(a, b, sems.at[i]) for i, (a, b) in enumerate(pairs)]
    operators = [
        pltpu.make_async_copy(operator_any.at[i], operator_ref.at[i], operator_sems.at[i]) for i in range(fine_rows)
    ]
    for copy in copies + operators:
        copy.start()

    lane = lax.broadcasted_iota(jnp.int32, (block_size, wide), 1)
    second = (lane >= block_size).astype(jnp.int32)
    short_lane = lax.broadcasted_iota(jnp.int32, (EXTRA, wide), 1)
    for near in range(half):
        out_ref[near, :used] = jnp.zeros((used, wide), jnp.float32)
    for copy in copies + operators:
        copy.wait()

    for near in range(half):
        value = jnp.zeros((EXTRA, wide), jnp.int32)
        for side in range(2):
            for s in range(slot_count):
                turned = near ^ jnp.where(side_ref[0] == side, 0, half // 2)
                wanted = fetch_ref[s, side * half + turned]
                value = jnp.where(short_lane == side * slot_count + s, wanted, value)
        out_ref[near, used:] = value.astype(jnp.float32)

    for i in range(fine_rows):
        value = restrict_ref[i]
        swapped = pltpu.roll(value, block_size, 1)
        own_row = jnp.where(second == 0, rows_ref[0, i], rows_ref[1, i])
        other_row = jnp.where(second == 0, rows_ref[1, i], rows_ref[0, i])
        dense = jnp.where(own_row == second, value, 0.0) + jnp.where(other_row == second, swapped, 0.0)
        product = transposed_product(operator_ref[i], dense)
        for k in range(entries):
            part = jnp.where(k < count_ref[i], product[k * block_size : (k + 1) * block_size], 0.0)
            peer = lax.div(slot_ref[i, k], slot_count)
            side = lax.div(peer, half)
            place = side * slot_count + lax.rem(slot_ref[i, k], slot_count)
            near = lax.rem(peer, half) ^ jnp.where(side_ref[0] == side, 0, half // 2)
            start = pl.multiple_of(place * block_size, block_size)
            out_ref[near, pl.ds(start, block_size)] += part


def restrict_operator(
    operator_count, operator_slot, restrict_rows, fetch, operator_blocks, restrict_blocks, own_columns, own_blocks, side
):
    fine_rows, block_size, width = operator_blocks.shape
    slot_count, columns = fetch.shape
    wide = NCR * block_size
    rows = 2 * slot_count * block_size + EXTRA
    small = (operator_count, operator_slot, restrict_rows, fetch)
    kept = small + (side,)
    return pl.pallas_call(
        restrict_kernel,
        out_shape=(
            jax.ShapeDtypeStruct((columns // 2, rows, wide), jnp.float32),
            jax.ShapeDtypeStruct(own_columns.shape, own_columns.dtype),
            jax.ShapeDtypeStruct(own_blocks.shape, own_blocks.dtype),
        ),
        in_specs=[pl.BlockSpec(memory_space=pltpu.HBM)] * 9,
        out_specs=[pl.BlockSpec(memory_space=pltpu.VMEM)] * 3,
        scratch_shapes=[pltpu.SMEM(x.shape, x.dtype) for x in kept]
        + [pltpu.VMEM(x.shape, x.dtype) for x in (restrict_blocks, operator_blocks)]
        + [pltpu.SemaphoreType.DMA((8,)), pltpu.SemaphoreType.DMA((fine_rows,))],
        cost_estimate=pl.CostEstimate(
            flops=6 * fine_rows * block_size * width * wide, bytes_accessed=4 << 20, transcendentals=0
        ),
        name="restrict_operator",
    )(*small, restrict_blocks, operator_blocks, own_columns, own_blocks, side)


def combine_kernel(own_ref, restricted_ref, *rest, slot_count, fine_rows, entries):
    pieces, (out_ref, held_ref, table_ref, index_ref, sem) = rest[:-5], rest[-5:]
    half = restricted_ref.shape[0]
    rows = len(pieces) // 2
    block_size = out_ref.shape[1]
    columns = 2 * half
    used = 2 * slot_count * block_size
    held = fine_rows * block_size

    table_ref[:1, : own_ref.shape[1]] = own_ref[...]
    for near in range(half):
        table_ref[1 + near : 2 + near] = restricted_ref[near, used : used + 1].astype(jnp.int32)
    for i, piece in enumerate(pieces[rows:]):
        for far in range(2):
            first = 1 + half + entries * (far * rows + i)
            row = held + entries * (1 - far)
            table_ref[first : first + entries] = piece[row : row + entries].astype(jnp.int32)
    copy = pltpu.make_async_copy(table_ref, index_ref, sem)
    copy.start()
    for i, piece in enumerate(pieces):
        held_ref[i] = piece[...] if i < rows else piece[:held]
    out_ref[...] = jnp.zeros_like(out_ref)
    copy.wait()

    def step(i, carry):
        near = lax.div(i, 2 * slot_count)
        place = lax.rem(i, 2 * slot_count)
        wanted = index_ref[1 + near, place]
        inside = lax.rem(wanted, fine_rows)
        far = lax.div(place, slot_count) ^ index_ref[0, 1]
        piece = far * rows + (lax.div(wanted, fine_rows * columns) ^ index_ref[0, 0])
        block = held_ref[piece, pl.ds(pl.multiple_of(inside * block_size, block_size), block_size)]
        restricted = restricted_ref[near, pl.ds(pl.multiple_of(place * block_size, block_size), block_size)]
        product = transposed_product(block, restricted)
        for m in range(entries):
            column = index_ref[0, 2 + index_ref[1 + half + entries * piece + m, inside]]
            out_ref[column] += product[m * block_size : (m + 1) * block_size]
        return carry

    lax.fori_loop(0, half * 2 * slot_count, step, 0, unroll=16)


def combine(own, restricted, pieces, coarse_all, slot_count, fine_rows, block_size):
    half, _, wide = restricted.shape
    width = pieces[0].shape[1]
    entries = width // block_size
    table_rows = -(-(1 + half + entries * len(pieces)) // 8) * 8
    return pl.pallas_call(
        functools.partial(combine_kernel, slot_count=slot_count, fine_rows=fine_rows, entries=entries),
        out_shape=jax.ShapeDtypeStruct((coarse_all, block_size, wide), jnp.float32),
        in_specs=[pl.BlockSpec(memory_space=pltpu.VMEM)] * (2 + len(pieces)),
        out_specs=pl.BlockSpec(memory_space=pltpu.VMEM),
        scratch_shapes=[
            pltpu.VMEM((len(pieces), fine_rows * block_size, width), jnp.float32),
            pltpu.VMEM((table_rows, LANES), jnp.int32),
            pltpu.SMEM((table_rows, LANES), jnp.int32),
            pltpu.SemaphoreType.DMA,
        ],
        compiler_params=pltpu.CompilerParams(vmem_limit_bytes=VMEM_LIMIT),
        cost_estimate=pl.CostEstimate(flops=1 << 28, bytes_accessed=4 << 20, transcendentals=0),
        name="combine",
    )(own, restricted, *pieces)


def row_swap(x, bit):
    return lax.ppermute(x, "row", [(r, r ^ bit) for r in range(lax.axis_size("row"))])


def half_swap(x):
    return lax.ppermute(x, "half", [(0, 1), (1, 0)])


def far_swap(x):
    half = lax.axis_size("near")
    pairs = [(h * half + n, (1 - h) * half + (n ^ half // 2)) for h in range(2) for n in range(half)]
    return lax.ppermute(x, ("half", "near"), pairs)


def spread_over_rows(blocks, rows):
    pieces = {0: blocks}
    bit = rows // 2
    while bit:
        for mask in list(pieces):
            pieces[mask ^ bit] = row_swap(pieces[mask], bit)
        bit //= 2
    return [pieces[mask] for mask in range(rows)]


def place_of_columns(half):
    own = lax.axis_index("half") * half + lax.axis_index("near")
    return jnp.arange(2 * half, dtype=jnp.int32) ^ own


def add_over_near(sums, half):
    total = sums[0]
    for near in range(1, half):
        total = total + lax.ppermute(sums[near], "near", [(n, n ^ near) for n in range(half)])
    return total


def add_over_columns(sums, half):
    crossing = half_swap(add_over_near(sums[half:], half))
    return add_over_near(sums[:half], half) + crossing


def local(
    operator_blocks,
    operator_count,
    operator_slot,
    fetch_lists,
    prolong_blocks,
    prolong_cols,
    restrict_blocks,
    restrict_rows,
):
    rows, half = lax.axis_size("row"), lax.axis_size("near")
    slot_count = fetch_lists.shape[3]
    fine_rows, block_size, width = prolong_blocks.shape
    fetch = fetch_lists.reshape(2 * half, slot_count).T
    own = jnp.stack([lax.axis_index("row"), lax.axis_index("half")])
    own = jnp.concatenate([own, place_of_columns(half)])[None]

    near_blocks = prolong_blocks.reshape(fine_rows * block_size, width)
    far_blocks = far_swap(near_blocks)
    restricted, own_columns, near_blocks = restrict_operator(
        operator_count,
        operator_slot,
        restrict_rows.T,
        fetch,
        operator_blocks,
        restrict_blocks,
        prolong_cols.T,
        near_blocks,
        lax.axis_index("half").reshape(1),
    )
    restricted = lax.all_to_all(restricted, "near", split_axis=0, concat_axis=0, tiled=True)
    far_columns = far_swap(own_columns)
    near_pieces = spread_over_rows(near_blocks, rows)
    far_blocks = append_columns(far_columns, own_columns, far_blocks)
    far_blocks = hold_until(near_pieces[rows // 2], far_blocks)
    pieces = near_pieces + spread_over_rows(far_blocks, rows)
    sums = combine(own, restricted, pieces, NCR * rows, slot_count, fine_rows, block_size)
    return add_over_columns(sums, half).T


def solution(mesh):
    rows, columns = mesh.shape["row"], mesh.shape["col"]
    split = Mesh(mesh.devices.reshape(rows, 2, columns // 2), ("row", "half", "near"))
    flat = ("row", "half", "near")
    return jax.shard_map(
        local,
        mesh=split,
        in_specs=(
            P(flat, None, None),
            P(flat),
            P(flat, None),
            P("row", ("half", "near"), None, None),
            P(flat, None, None),
            P(flat, None),
            P(flat, None, None),
            P(flat, None),
        ),
        out_specs=P("row", ("half", "near")),
        check_vma=False,
    )
```

```python
import functools

import jax
import jax.numpy as jnp
from jax import lax
from jax.experimental import pallas as pl
from jax.experimental.pallas import tpu as pltpu
from jax.sharding import Mesh
from jax.sharding import PartitionSpec as P

NCR = 2
LANES = 128
EXTRA = 8
HOLD_FLOPS = 16 << 30
VMEM_LIMIT = 48 * 1024 * 1024


def halves(x):
    high = x.astype(jnp.bfloat16)
    return high, (x - high.astype(jnp.float32)).astype(jnp.bfloat16)


def transposed_product(left, right):
    tall = jnp.concatenate(halves(left), axis=0)
    wide = jnp.concatenate(halves(right), axis=1)
    wide = jnp.concatenate([wide, wide], axis=0)
    both = lax.dot_general(tall, wide, (((0,), (0,)), ((), ())), preferred_element_type=jnp.float32)
    width = right.shape[1]
    return both[:, :width] + both[:, width:]


def hold_kernel(mark_ref, next_ref, blocks_ref, out_ref):
    out_ref[...] = blocks_ref[...]


def hold_until(mark, next_blocks, blocks):
    return pl.pallas_call(
        hold_kernel,
        out_shape=jax.ShapeDtypeStruct(blocks.shape, blocks.dtype),
        in_specs=[pl.BlockSpec(memory_space=pltpu.VMEM)] * 3,
        out_specs=pl.BlockSpec(memory_space=pltpu.VMEM),
        compiler_params=pltpu.CompilerParams(vmem_limit_bytes=VMEM_LIMIT),
        cost_estimate=pl.CostEstimate(flops=HOLD_FLOPS, bytes_accessed=HOLD_FLOPS >> 8, transcendentals=0),
        name="hold_until",
    )(mark, next_blocks, blocks)


def restrict_kernel(
    count_any, slot_any, rows_any, fetch_any, restrict_any, operator_any, side_any,
    out_ref, mark_ref,
    count_ref, slot_ref, rows_ref, fetch_ref, side_ref, restrict_ref, operator_ref, sems, operator_sems,
):
    fine_rows, block_size, _ = operator_ref.shape
    entries = slot_ref.shape[1]
    slot_count, columns = fetch_ref.shape
    half = columns // 2
    used = 2 * slot_count * block_size
    wide = NCR * block_size

    pairs = [
        (count_any, count_ref), (slot_any, slot_ref), (rows_any, rows_ref),
        (fetch_any, fetch_ref), (restrict_any, restrict_ref),
        (side_any, side_ref),
    ]
    copies = [pltpu.make_async_copy(a, b, sems.at[i]) for i, (a, b) in enumerate(pairs)]
    operators = [
        pltpu.make_async_copy(operator_any.at[i], operator_ref.at[i], operator_sems.at[i]) for i in range(fine_rows)
    ]
    for copy in copies + operators:
        copy.start()

    lane = lax.broadcasted_iota(jnp.int32, (block_size, wide), 1)
    second = (lane >= block_size).astype(jnp.int32)
    short_lane = lax.broadcasted_iota(jnp.int32, (EXTRA, wide), 1)
    for near in range(half):
        out_ref[near, :used] = jnp.zeros((used, wide), jnp.float32)
    for copy in copies + operators:
        copy.wait()

    for near in range(half):
        value = jnp.zeros((EXTRA, wide), jnp.int32)
        for side in range(2):
            for s in range(slot_count):
                turned = near ^ jnp.where(side_ref[0] == side, 0, half // 2)
                wanted = fetch_ref[s, side * half + turned]
                value = jnp.where(short_lane == side * slot_count + s, wanted, value)
        out_ref[near, used:] = value.astype(jnp.float32)
    mark_ref[...] = out_ref[0, used:]

    for i in range(fine_rows):
        value = restrict_ref[i]
        swapped = pltpu.roll(value, block_size, 1)
        own_row = jnp.where(second == 0, rows_ref[0, i], rows_ref[1, i])
        other_row = jnp.where(second == 0, rows_ref[1, i], rows_ref[0, i])
        dense = jnp.where(own_row == second, value, 0.0) + jnp.where(other_row == second, swapped, 0.0)
        product = transposed_product(operator_ref[i], dense)
        for k in range(entries):
            part = jnp.where(k < count_ref[i], product[k * block_size : (k + 1) * block_size], 0.0)
            peer = lax.div(slot_ref[i, k], slot_count)
            side = lax.div(peer, half)
            place = side * slot_count + lax.rem(slot_ref[i, k], slot_count)
            near = lax.rem(peer, half) ^ jnp.where(side_ref[0] == side, 0, half // 2)
            start = pl.multiple_of(place * block_size, block_size)
            out_ref[near, pl.ds(start, block_size)] += part


def restrict_operator(
    operator_count, operator_slot, restrict_rows, fetch, operator_blocks, restrict_blocks, side
):
    fine_rows, block_size, width = operator_blocks.shape
    slot_count, columns = fetch.shape
    wide = NCR * block_size
    rows = 2 * slot_count * block_size + EXTRA
    small = (operator_count, operator_slot, restrict_rows, fetch)
    kept = small + (side,)
    return pl.pallas_call(
        restrict_kernel,
        out_shape=(
            jax.ShapeDtypeStruct((columns // 2, rows, wide), jnp.float32),
            jax.ShapeDtypeStruct((EXTRA, wide), jnp.float32),
        ),
        in_specs=[pl.BlockSpec(memory_space=pltpu.HBM)] * 7,
        out_specs=[pl.BlockSpec(memory_space=pltpu.VMEM)] * 2,
        scratch_shapes=[pltpu.SMEM(x.shape, x.dtype) for x in kept]
        + [pltpu.VMEM(x.shape, x.dtype) for x in (restrict_blocks, operator_blocks)]
        + [pltpu.SemaphoreType.DMA((6,)), pltpu.SemaphoreType.DMA((fine_rows,))],
        cost_estimate=pl.CostEstimate(
            flops=6 * fine_rows * block_size * width * wide, bytes_accessed=4 << 20, transcendentals=0
        ),
        name="restrict_operator",
    )(*small, restrict_blocks, operator_blocks, side)


def combine_kernel(own_ref, restricted_ref, *rest, slot_count, fine_rows, entries):
    pieces, (out_ref, held_ref, table_ref, index_ref, sem) = rest[:-5], rest[-5:]
    half = restricted_ref.shape[0]
    rows = len(pieces) // 2
    block_size = out_ref.shape[1]
    columns = 2 * half
    used = 2 * slot_count * block_size
    held = fine_rows * block_size

    table_ref[:1, : own_ref.shape[1]] = own_ref[...]
    for near in range(half):
        table_ref[1 + near : 2 + near] = restricted_ref[near, used : used + 1].astype(jnp.int32)
    for i, piece in enumerate(pieces):
        first = 1 + half + entries * i
        table_ref[first : first + entries] = piece[held : held + entries].astype(jnp.int32)
    copy = pltpu.make_async_copy(table_ref, index_ref, sem)
    copy.start()
    for i, piece in enumerate(pieces):
        held_ref[i] = piece[:held]
    out_ref[...] = jnp.zeros_like(out_ref)
    copy.wait()

    def step(i, carry):
        near = lax.div(i, 2 * slot_count)
        place = lax.rem(i, 2 * slot_count)
        wanted = index_ref[1 + near, place]
        inside = lax.rem(wanted, fine_rows)
        far = lax.div(place, slot_count) ^ index_ref[0, 1]
        piece = far * rows + (lax.div(wanted, fine_rows * columns) ^ index_ref[0, 0])
        block = held_ref[piece, pl.ds(pl.multiple_of(inside * block_size, block_size), block_size)]
        restricted = restricted_ref[near, pl.ds(pl.multiple_of(place * block_size, block_size), block_size)]
        product = transposed_product(block, restricted)
        for m in range(entries):
            column = index_ref[0, 2 + index_ref[1 + half + entries * piece + m, inside]]
            out_ref[column] += product[m * block_size : (m + 1) * block_size]
        return carry

    lax.fori_loop(0, half * 2 * slot_count, step, 0, unroll=16)


def combine(own, restricted, pieces, coarse_all, slot_count, fine_rows, block_size):
    half, _, wide = restricted.shape
    width = pieces[0].shape[1]
    entries = width // block_size
    table_rows = -(-(1 + half + entries * len(pieces)) // 8) * 8
    return pl.pallas_call(
        functools.partial(combine_kernel, slot_count=slot_count, fine_rows=fine_rows, entries=entries),
        out_shape=jax.ShapeDtypeStruct((coarse_all, block_size, wide), jnp.float32),
        in_specs=[pl.BlockSpec(memory_space=pltpu.VMEM)] * (2 + len(pieces)),
        out_specs=pl.BlockSpec(memory_space=pltpu.VMEM),
        scratch_shapes=[
            pltpu.VMEM((len(pieces), fine_rows * block_size, width), jnp.float32),
            pltpu.VMEM((table_rows, LANES), jnp.int32),
            pltpu.SMEM((table_rows, LANES), jnp.int32),
            pltpu.SemaphoreType.DMA,
        ],
        compiler_params=pltpu.CompilerParams(vmem_limit_bytes=VMEM_LIMIT),
        cost_estimate=pl.CostEstimate(flops=1 << 28, bytes_accessed=4 << 20, transcendentals=0),
        name="combine",
    )(own, restricted, *pieces)


def row_swap(x, bit):
    return lax.ppermute(x, "row", [(r, r ^ bit) for r in range(lax.axis_size("row"))])


def half_swap(x):
    return lax.ppermute(x, "half", [(0, 1), (1, 0)])


def far_swap(x):
    half = lax.axis_size("near")
    pairs = [(h * half + n, (1 - h) * half + (n ^ half // 2)) for h in range(2) for n in range(half)]
    return lax.ppermute(x, ("half", "near"), pairs)


def spread_over_rows(blocks, rows):
    pieces = {0: blocks}
    bit = rows // 2
    while bit:
        for mask in list(pieces):
            pieces[mask ^ bit] = row_swap(pieces[mask], bit)
        bit //= 2
    return [pieces[mask] for mask in range(rows)]


def place_of_columns(half):
    own = lax.axis_index("half") * half + lax.axis_index("near")
    return jnp.arange(2 * half, dtype=jnp.int32) ^ own


def add_over_near(sums, half):
    total = sums[0]
    for near in range(1, half):
        total = total + lax.ppermute(sums[near], "near", [(n, n ^ near) for n in range(half)])
    return total


def add_over_columns(sums, half):
    crossing = half_swap(add_over_near(sums[half:], half))
    return add_over_near(sums[:half], half) + crossing


def with_columns(columns, blocks):
    entries, fine_rows = columns.shape
    used, width = blocks.shape
    rows = jnp.pad(columns.astype(blocks.dtype), ((0, EXTRA - entries), (0, width - fine_rows)))
    return jnp.concatenate([blocks, rows], axis=0)


def local(
    operator_blocks,
    operator_count,
    operator_slot,
    fetch_lists,
    prolong_blocks,
    prolong_cols,
    restrict_blocks,
    restrict_rows,
):
    rows, half = lax.axis_size("row"), lax.axis_size("near")
    slot_count = fetch_lists.shape[3]
    fine_rows, block_size, width = prolong_blocks.shape
    fetch = fetch_lists.reshape(2 * half, slot_count).T
    own = jnp.stack([lax.axis_index("row"), lax.axis_index("half")])
    own = jnp.concatenate([own, place_of_columns(half)])[None]

    near_blocks = with_columns(prolong_cols.T, prolong_blocks.reshape(fine_rows * block_size, width))
    far_blocks = far_swap(near_blocks)
    restricted, mark = restrict_operator(
        operator_count,
        operator_slot,
        restrict_rows.T,
        fetch,
        operator_blocks,
        restrict_blocks,
        lax.axis_index("half").reshape(1),
    )
    restricted = lax.all_to_all(restricted, "near", split_axis=0, concat_axis=0, tiled=True)
    near_pieces = spread_over_rows(near_blocks, rows)
    far_blocks = hold_until(mark, near_pieces[rows // 2], far_blocks)
    pieces = near_pieces + spread_over_rows(far_blocks, rows)
    sums = combine(own, restricted, pieces, NCR * rows, slot_count, fine_rows, block_size)
    return add_over_columns(sums, half).T


def solution(mesh):
    rows, columns = mesh.shape["row"], mesh.shape["col"]
    split = Mesh(mesh.devices.reshape(rows, 2, columns // 2), ("row", "half", "near"))
    flat = ("row", "half", "near")
    return jax.shard_map(
        local,
        mesh=split,
        in_specs=(
            P(flat, None, None),
            P(flat),
            P(flat, None),
            P("row", ("half", "near"), None, None),
            P(flat, None, None),
            P(flat, None),
            P(flat, None, None),
            P(flat, None),
        ),
        out_specs=P("row", ("half", "near")),
        check_vma=False,
    )
```

```python
import functools

import jax
import jax.numpy as jnp
from jax import lax
from jax.experimental import pallas as pl
from jax.experimental.pallas import tpu as pltpu
from jax.sharding import Mesh
from jax.sharding import PartitionSpec as P

NCR = 2
LANES = 128
EXTRA = 8
HOLD_FLOPS = 16 << 30
VMEM_LIMIT = 48 * 1024 * 1024


def halves(x):
    high = x.astype(jnp.bfloat16)
    return high, (x - high.astype(jnp.float32)).astype(jnp.bfloat16)


def transposed_product(left, right):
    tall = jnp.concatenate(halves(left), axis=0)
    wide = jnp.concatenate(halves(right), axis=1)
    wide = jnp.concatenate([wide, wide], axis=0)
    both = lax.dot_general(tall, wide, (((0,), (0,)), ((), ())), preferred_element_type=jnp.float32)
    width = right.shape[1]
    return both[:, :width] + both[:, width:]


def append_kernel(next_ref, far_columns_ref, own_columns_ref, blocks_ref, out_ref):
    used = blocks_ref.shape[0]
    entries, fine_rows = own_columns_ref.shape
    out_ref[:used] = blocks_ref[...]
    out_ref[used:] = jnp.zeros((EXTRA, out_ref.shape[1]), jnp.float32)
    out_ref[used : used + entries, :fine_rows] = far_columns_ref[...].astype(jnp.float32)
    out_ref[used + entries : used + 2 * entries, :fine_rows] = own_columns_ref[...].astype(jnp.float32)


def append_columns(next_blocks, far_columns, own_columns, blocks):
    used, width = blocks.shape
    return pl.pallas_call(
        append_kernel,
        out_shape=jax.ShapeDtypeStruct((used + EXTRA, width), blocks.dtype),
        in_specs=[pl.BlockSpec(memory_space=pltpu.VMEM)] * 4,
        out_specs=pl.BlockSpec(memory_space=pltpu.VMEM),
        compiler_params=pltpu.CompilerParams(vmem_limit_bytes=VMEM_LIMIT),
        cost_estimate=pl.CostEstimate(flops=HOLD_FLOPS, bytes_accessed=HOLD_FLOPS >> 8, transcendentals=0),
        name="append_columns",
    )(next_blocks, far_columns, own_columns, blocks)


def restrict_kernel(
    count_any, slot_any, rows_any, fetch_any, restrict_any, operator_any, columns_any, blocks_any, side_any,
    out_ref, own_columns_ref, own_blocks_ref,
    count_ref, slot_ref, rows_ref, fetch_ref, side_ref, restrict_ref, operator_ref, sems, operator_sems,
):
    fine_rows, block_size, _ = operator_ref.shape
    entries = slot_ref.shape[1]
    slot_count, columns = fetch_ref.shape
    half = columns // 2
    used = 2 * slot_count * block_size
    wide = NCR * block_size

    pairs = [
        (count_any, count_ref), (slot_any, slot_ref), (rows_any, rows_ref),
        (fetch_any, fetch_ref), (restrict_any, restrict_ref),
        (columns_any, own_columns_ref), (blocks_any, own_blocks_ref), (side_any, side_ref),
    ]
    copies = [pltpu.make_async_copy(a, b, sems.at[i]) for i, (a, b) in enumerate(pairs)]
    operators = [
        pltpu.make_async_copy(operator_any.at[i], operator_ref.at[i], operator_sems.at[i]) for i in range(fine_rows)
    ]
    for copy in copies + operators:
        copy.start()

    lane = lax.broadcasted_iota(jnp.int32, (block_size, wide), 1)
    second = (lane >= block_size).astype(jnp.int32)
    short_lane = lax.broadcasted_iota(jnp.int32, (EXTRA, wide), 1)
    for near in range(half):
        out_ref[near, :used] = jnp.zeros((used, wide), jnp.float32)
    for copy in copies + operators:
        copy.wait()

    for near in range(half):
        value = jnp.zeros((EXTRA, wide), jnp.int32)
        for side in range(2):
            for s in range(slot_count):
                turned = near ^ jnp.where(side_ref[0] == side, 0, half // 2)
                wanted = fetch_ref[s, side * half + turned]
                value = jnp.where(short_lane == side * slot_count + s, wanted, value)
        out_ref[near, used:] = value.astype(jnp.float32)

    for i in range(fine_rows):
        value = restrict_ref[i]
        swapped = pltpu.roll(value, block_size, 1)
        own_row = jnp.where(second == 0, rows_ref[0, i], rows_ref[1, i])
        other_row = jnp.where(second == 0, rows_ref[1, i], rows_ref[0, i])
        dense = jnp.where(own_row == second, value, 0.0) + jnp.where(other_row == second, swapped, 0.0)
        for k in range(entries):
            first = k % 2 * block_size
            if first == 0:
                product = transposed_product(operator_ref[i, :, k * block_size : (k + 2) * block_size], dense)
            part = jnp.where(k < count_ref[i], product[first : first + block_size], 0.0)
            peer = lax.div(slot_ref[i, k], slot_count)
            side = lax.div(peer, half)
            place = side * slot_count + lax.rem(slot_ref[i, k], slot_count)
            near = lax.rem(peer, half) ^ jnp.where(side_ref[0] == side, 0, half // 2)
            start = pl.multiple_of(place * block_size, block_size)
            out_ref[near, pl.ds(start, block_size)] += part


def restrict_operator(
    operator_count, operator_slot, restrict_rows, fetch, operator_blocks, restrict_blocks, own_columns, own_blocks, side
):
    fine_rows, block_size, width = operator_blocks.shape
    slot_count, columns = fetch.shape
    wide = NCR * block_size
    rows = 2 * slot_count * block_size + EXTRA
    small = (operator_count, operator_slot, restrict_rows, fetch)
    kept = small + (side,)
    return pl.pallas_call(
        restrict_kernel,
        out_shape=(
            jax.ShapeDtypeStruct((columns // 2, rows, wide), jnp.float32),
            jax.ShapeDtypeStruct(own_columns.shape, own_columns.dtype),
            jax.ShapeDtypeStruct(own_blocks.shape, own_blocks.dtype),
        ),
        in_specs=[pl.BlockSpec(memory_space=pltpu.HBM)] * 9,
        out_specs=[pl.BlockSpec(memory_space=pltpu.VMEM)] * 3,
        scratch_shapes=[pltpu.SMEM(x.shape, x.dtype) for x in kept]
        + [pltpu.VMEM(x.shape, x.dtype) for x in (restrict_blocks, operator_blocks)]
        + [pltpu.SemaphoreType.DMA((8,)), pltpu.SemaphoreType.DMA((fine_rows,))],
        cost_estimate=pl.CostEstimate(
            flops=6 * fine_rows * block_size * width * wide, bytes_accessed=4 << 20, transcendentals=0
        ),
        name="restrict_operator",
    )(*small, restrict_blocks, operator_blocks, own_columns, own_blocks, side)


def combine_kernel(own_ref, restricted_ref, *rest, slot_count, fine_rows, entries):
    pieces, (out_ref, held_ref, table_ref, index_ref, sem) = rest[:-5], rest[-5:]
    half = restricted_ref.shape[0]
    rows = len(pieces) // 2
    block_size = out_ref.shape[1]
    columns = 2 * half
    used = 2 * slot_count * block_size
    held = fine_rows * block_size

    table_ref[:1, : own_ref.shape[1]] = own_ref[...]
    for near in range(half):
        table_ref[1 + near : 2 + near] = restricted_ref[near, used : used + 1].astype(jnp.int32)
    for i, piece in enumerate(pieces[rows:]):
        for far in range(2):
            first = 1 + half + entries * (far * rows + i)
            row = held + entries * (1 - far)
            table_ref[first : first + entries] = piece[row : row + entries].astype(jnp.int32)
    copy = pltpu.make_async_copy(table_ref, index_ref, sem)
    copy.start()
    for i, piece in enumerate(pieces):
        held_ref[i] = piece[...] if i < rows else piece[:held]
    out_ref[...] = jnp.zeros_like(out_ref)
    copy.wait()

    def step(i, carry):
        near = lax.div(i, 2 * slot_count)
        place = lax.rem(i, 2 * slot_count)
        wanted = index_ref[1 + near, place]
        inside = lax.rem(wanted, fine_rows)
        far = lax.div(place, slot_count) ^ index_ref[0, 1]
        piece = far * rows + (lax.div(wanted, fine_rows * columns) ^ index_ref[0, 0])
        block = held_ref[piece, pl.ds(pl.multiple_of(inside * block_size, block_size), block_size)]
        restricted = restricted_ref[near, pl.ds(pl.multiple_of(place * block_size, block_size), block_size)]
        product = transposed_product(block, restricted)
        for m in range(entries):
            column = index_ref[0, 2 + index_ref[1 + half + entries * piece + m, inside]]
            out_ref[column] += product[m * block_size : (m + 1) * block_size]
        return carry

    lax.fori_loop(0, half * 2 * slot_count, step, 0, unroll=16)


def combine(own, restricted, pieces, coarse_all, slot_count, fine_rows, block_size):
    half, _, wide = restricted.shape
    width = pieces[0].shape[1]
    entries = width // block_size
    table_rows = -(-(1 + half + entries * len(pieces)) // 8) * 8
    return pl.pallas_call(
        functools.partial(combine_kernel, slot_count=slot_count, fine_rows=fine_rows, entries=entries),
        out_shape=jax.ShapeDtypeStruct((coarse_all, block_size, wide), jnp.float32),
        in_specs=[pl.BlockSpec(memory_space=pltpu.VMEM)] * (2 + len(pieces)),
        out_specs=pl.BlockSpec(memory_space=pltpu.VMEM),
        scratch_shapes=[
            pltpu.VMEM((len(pieces), fine_rows * block_size, width), jnp.float32),
            pltpu.VMEM((table_rows, LANES), jnp.int32),
            pltpu.SMEM((table_rows, LANES), jnp.int32),
            pltpu.SemaphoreType.DMA,
        ],
        compiler_params=pltpu.CompilerParams(vmem_limit_bytes=VMEM_LIMIT),
        cost_estimate=pl.CostEstimate(flops=1 << 28, bytes_accessed=4 << 20, transcendentals=0),
        name="combine",
    )(own, restricted, *pieces)


def row_swap(x, bit):
    return lax.ppermute(x, "row", [(r, r ^ bit) for r in range(lax.axis_size("row"))])


def half_swap(x):
    return lax.ppermute(x, "half", [(0, 1), (1, 0)])


def far_swap(x):
    half = lax.axis_size("near")
    pairs = [(h * half + n, (1 - h) * half + (n ^ half // 2)) for h in range(2) for n in range(half)]
    return lax.ppermute(x, ("half", "near"), pairs)


def spread_over_rows(blocks, rows):
    pieces = {0: blocks}
    bit = rows // 2
    while bit:
        for mask in list(pieces):
            pieces[mask ^ bit] = row_swap(pieces[mask], bit)
        bit //= 2
    return [pieces[mask] for mask in range(rows)]


def place_of_columns(half):
    own = lax.axis_index("half") * half + lax.axis_index("near")
    return jnp.arange(2 * half, dtype=jnp.int32) ^ own


def add_over_near(sums, half):
    total = sums[0]
    for near in range(1, half):
        total = total + lax.ppermute(sums[near], "near", [(n, n ^ near) for n in range(half)])
    return total


def add_over_columns(sums, half):
    crossing = half_swap(add_over_near(sums[half:], half))
    return add_over_near(sums[:half], half) + crossing


def local(
    operator_blocks,
    operator_count,
    operator_slot,
    fetch_lists,
    prolong_blocks,
    prolong_cols,
    restrict_blocks,
    restrict_rows,
):
    rows, half = lax.axis_size("row"), lax.axis_size("near")
    slot_count = fetch_lists.shape[3]
    fine_rows, block_size, width = prolong_blocks.shape
    fetch = fetch_lists.reshape(2 * half, slot_count).T
    own = jnp.stack([lax.axis_index("row"), lax.axis_index("half")])
    own = jnp.concatenate([own, place_of_columns(half)])[None]

    near_blocks = prolong_blocks.reshape(fine_rows * block_size, width)
    far_blocks = far_swap(near_blocks)
    restricted, own_columns, near_blocks = restrict_operator(
        operator_count,
        operator_slot,
        restrict_rows.T,
        fetch,
        operator_blocks,
        restrict_blocks,
        prolong_cols.T,
        near_blocks,
        lax.axis_index("half").reshape(1),
    )
    restricted = lax.all_to_all(restricted, "near", split_axis=0, concat_axis=0, tiled=True)
    far_columns = far_swap(own_columns)
    near_pieces = spread_over_rows(near_blocks, rows)
    far_blocks = append_columns(near_pieces[rows // 2], far_columns, own_columns, far_blocks)
    pieces = near_pieces + spread_over_rows(far_blocks, rows)
    sums = combine(own, restricted, pieces, NCR * rows, slot_count, fine_rows, block_size)
    return add_over_columns(sums, half).T


def solution(mesh):
    rows, columns = mesh.shape["row"], mesh.shape["col"]
    split = Mesh(mesh.devices.reshape(rows, 2, columns // 2), ("row", "half", "near"))
    flat = ("row", "half", "near")
    return jax.shard_map(
        local,
        mesh=split,
        in_specs=(
            P(flat, None, None),
            P(flat),
            P(flat, None),
            P("row", ("half", "near"), None, None),
            P(flat, None, None),
            P(flat, None),
            P(flat, None, None),
            P(flat, None),
        ),
        out_specs=P("row", ("half", "near")),
        check_vma=False,
    )
```

```python
import functools

import jax
import jax.numpy as jnp
from jax import lax
from jax.experimental import pallas as pl
from jax.experimental.pallas import tpu as pltpu
from jax.sharding import Mesh
from jax.sharding import PartitionSpec as P

NCR = 2
LANES = 128
EXTRA = 8
HOLD_FLOPS = 16 << 30
VMEM_LIMIT = 48 * 1024 * 1024


def halves(x):
    high = x.astype(jnp.bfloat16)
    return high, (x - high.astype(jnp.float32)).astype(jnp.bfloat16)


def transposed_product(left, right):
    tall = jnp.concatenate(halves(left), axis=0)
    wide = jnp.concatenate(halves(right), axis=1)
    wide = jnp.concatenate([wide, wide], axis=0)
    both = lax.dot_general(tall, wide, (((0,), (0,)), ((), ())), preferred_element_type=jnp.float32)
    width = right.shape[1]
    return both[:, :width] + both[:, width:]


def append_kernel(next_ref, far_columns_ref, own_columns_ref, blocks_ref, out_ref):
    used = blocks_ref.shape[0]
    entries, fine_rows = own_columns_ref.shape
    out_ref[:used] = blocks_ref[...]
    out_ref[used:] = jnp.zeros((EXTRA, out_ref.shape[1]), jnp.float32)
    out_ref[used : used + entries, :fine_rows] = far_columns_ref[...].astype(jnp.float32)
    out_ref[used + entries : used + 2 * entries, :fine_rows] = own_columns_ref[...].astype(jnp.float32)


def append_columns(next_blocks, far_columns, own_columns, blocks):
    used, width = blocks.shape
    return pl.pallas_call(
        append_kernel,
        out_shape=jax.ShapeDtypeStruct((used + EXTRA, width), blocks.dtype),
        in_specs=[pl.BlockSpec(memory_space=pltpu.VMEM)] * 4,
        out_specs=pl.BlockSpec(memory_space=pltpu.VMEM),
        compiler_params=pltpu.CompilerParams(vmem_limit_bytes=VMEM_LIMIT),
        cost_estimate=pl.CostEstimate(flops=HOLD_FLOPS, bytes_accessed=HOLD_FLOPS >> 8, transcendentals=0),
        name="append_columns",
    )(next_blocks, far_columns, own_columns, blocks)


def restrict_kernel(
    count_any, slot_any, rows_any, fetch_any, restrict_any, operator_any, columns_any, blocks_any, side_any,
    out_ref, own_columns_ref, own_blocks_ref,
    count_ref, slot_ref, rows_ref, fetch_ref, side_ref, restrict_ref, operator_ref, sems, operator_sems,
):
    fine_rows, block_size, _ = operator_ref.shape
    entries = slot_ref.shape[1]
    slot_count, columns = fetch_ref.shape
    half = columns // 2
    used = 2 * slot_count * block_size
    wide = NCR * block_size

    pairs = [
        (count_any, count_ref), (slot_any, slot_ref), (rows_any, rows_ref),
        (fetch_any, fetch_ref), (restrict_any, restrict_ref),
        (columns_any, own_columns_ref), (blocks_any, own_blocks_ref), (side_any, side_ref),
    ]
    copies = [pltpu.make_async_copy(a, b, sems.at[i]) for i, (a, b) in enumerate(pairs)]
    operators = [
        pltpu.make_async_copy(operator_any.at[i], operator_ref.at[i], operator_sems.at[i]) for i in range(fine_rows)
    ]
    for copy in copies + operators:
        copy.start()

    lane = lax.broadcasted_iota(jnp.int32, (block_size, wide), 1)
    second = (lane >= block_size).astype(jnp.int32)
    short_lane = lax.broadcasted_iota(jnp.int32, (EXTRA, wide), 1)
    for near in range(half):
        out_ref[near, :used] = jnp.zeros((used, wide), jnp.float32)
    for copy in copies + operators:
        copy.wait()

    for near in range(half):
        value = jnp.zeros((EXTRA, wide), jnp.int32)
        for side in range(2):
            for s in range(slot_count):
                wanted = fetch_ref[s, side * half + near]
                value = jnp.where(short_lane == side * slot_count + s, wanted, value)
        out_ref[near, used:] = value.astype(jnp.float32)

    for i in range(fine_rows):
        value = restrict_ref[i]
        swapped = pltpu.roll(value, block_size, 1)
        own_row = jnp.where(second == 0, rows_ref[0, i], rows_ref[1, i])
        other_row = jnp.where(second == 0, rows_ref[1, i], rows_ref[0, i])
        dense = jnp.where(own_row == second, value, 0.0) + jnp.where(other_row == second, swapped, 0.0)
        product = transposed_product(operator_ref[i], dense)
        for k in range(entries):
            part = jnp.where(k < count_ref[i], product[k * block_size : (k + 1) * block_size], 0.0)
            peer = lax.div(slot_ref[i, k], slot_count)
            side = lax.div(peer, half)
            place = side * slot_count + lax.rem(slot_ref[i, k], slot_count)
            near = lax.rem(peer, half)
            start = pl.multiple_of(place * block_size, block_size)
            out_ref[near, pl.ds(start, block_size)] += part


def restrict_operator(
    operator_count, operator_slot, restrict_rows, fetch, operator_blocks, restrict_blocks, own_columns, own_blocks, side
):
    fine_rows, block_size, width = operator_blocks.shape
    slot_count, columns = fetch.shape
    wide = NCR * block_size
    rows = 2 * slot_count * block_size + EXTRA
    small = (operator_count, operator_slot, restrict_rows, fetch)
    kept = small + (side,)
    return pl.pallas_call(
        restrict_kernel,
        out_shape=(
            jax.ShapeDtypeStruct((columns // 2, rows, wide), jnp.float32),
            jax.ShapeDtypeStruct(own_columns.shape, own_columns.dtype),
            jax.ShapeDtypeStruct(own_blocks.shape, own_blocks.dtype),
        ),
        in_specs=[pl.BlockSpec(memory_space=pltpu.HBM)] * 9,
        out_specs=[pl.BlockSpec(memory_space=pltpu.VMEM)] * 3,
        scratch_shapes=[pltpu.SMEM(x.shape, x.dtype) for x in kept]
        + [pltpu.VMEM(x.shape, x.dtype) for x in (restrict_blocks, operator_blocks)]
        + [pltpu.SemaphoreType.DMA((8,)), pltpu.SemaphoreType.DMA((fine_rows,))],
        cost_estimate=pl.CostEstimate(
            flops=6 * fine_rows * block_size * width * wide, bytes_accessed=4 << 20, transcendentals=0
        ),
        name="restrict_operator",
    )(*small, restrict_blocks, operator_blocks, own_columns, own_blocks, side)


def combine_kernel(own_ref, restricted_ref, *rest, slot_count, fine_rows, entries):
    pieces, (out_ref, held_ref, table_ref, index_ref, sem) = rest[:-5], rest[-5:]
    half = restricted_ref.shape[0]
    rows = len(pieces) // 2
    block_size = out_ref.shape[1]
    columns = 2 * half
    used = 2 * slot_count * block_size
    held = fine_rows * block_size

    table_ref[:1, : own_ref.shape[1]] = own_ref[...]
    for near in range(half):
        table_ref[1 + near : 2 + near] = restricted_ref[near, used : used + 1].astype(jnp.int32)
    for i, piece in enumerate(pieces[rows:]):
        for far in range(2):
            first = 1 + half + entries * (far * rows + i)
            row = held + entries * (1 - far)
            table_ref[first : first + entries] = piece[row : row + entries].astype(jnp.int32)
    copy = pltpu.make_async_copy(table_ref, index_ref, sem)
    copy.start()
    for i, piece in enumerate(pieces):
        held_ref[i] = piece[...] if i < rows else piece[:held]
    out_ref[...] = jnp.zeros_like(out_ref)
    copy.wait()

    def step(i, carry):
        near = lax.div(i, 2 * slot_count)
        place = lax.rem(i, 2 * slot_count)
        wanted = index_ref[1 + near, place]
        inside = lax.rem(wanted, fine_rows)
        far = lax.div(place, slot_count) ^ index_ref[0, 1]
        piece = far * rows + (lax.div(wanted, fine_rows * columns) ^ index_ref[0, 0])
        block = held_ref[piece, pl.ds(pl.multiple_of(inside * block_size, block_size), block_size)]
        restricted = restricted_ref[near, pl.ds(pl.multiple_of(place * block_size, block_size), block_size)]
        product = transposed_product(block, restricted)
        for m in range(entries):
            column = index_ref[0, 2 + index_ref[1 + half + entries * piece + m, inside]]
            out_ref[column] += product[m * block_size : (m + 1) * block_size]
        return carry

    lax.fori_loop(0, half * 2 * slot_count, step, 0, unroll=16)


def combine(own, restricted, pieces, coarse_all, slot_count, fine_rows, block_size):
    half, _, wide = restricted.shape
    width = pieces[0].shape[1]
    entries = width // block_size
    table_rows = -(-(1 + half + entries * len(pieces)) // 8) * 8
    return pl.pallas_call(
        functools.partial(combine_kernel, slot_count=slot_count, fine_rows=fine_rows, entries=entries),
        out_shape=jax.ShapeDtypeStruct((coarse_all, block_size, wide), jnp.float32),
        in_specs=[pl.BlockSpec(memory_space=pltpu.VMEM)] * (2 + len(pieces)),
        out_specs=pl.BlockSpec(memory_space=pltpu.VMEM),
        scratch_shapes=[
            pltpu.VMEM((len(pieces), fine_rows * block_size, width), jnp.float32),
            pltpu.VMEM((table_rows, LANES), jnp.int32),
            pltpu.SMEM((table_rows, LANES), jnp.int32),
            pltpu.SemaphoreType.DMA,
        ],
        compiler_params=pltpu.CompilerParams(vmem_limit_bytes=VMEM_LIMIT),
        cost_estimate=pl.CostEstimate(flops=1 << 28, bytes_accessed=4 << 20, transcendentals=0),
        name="combine",
    )(own, restricted, *pieces)


def row_swap(x, bit):
    return lax.ppermute(x, "row", [(r, r ^ bit) for r in range(lax.axis_size("row"))])


def half_swap(x):
    return lax.ppermute(x, "half", [(0, 1), (1, 0)])


def spread_over_rows(blocks, rows):
    pieces = {0: blocks}
    bit = rows // 2
    while bit:
        for mask in list(pieces):
            pieces[mask ^ bit] = row_swap(pieces[mask], bit)
        bit //= 2
    return [pieces[mask] for mask in range(rows)]


def place_of_columns(half):
    own = lax.axis_index("half") * half + lax.axis_index("near")
    return jnp.arange(2 * half, dtype=jnp.int32) ^ own


def add_over_near(sums, half):
    total = sums[0]
    for near in range(1, half):
        total = total + lax.ppermute(sums[near], "near", [(n, n ^ near) for n in range(half)])
    return total


def add_over_columns(sums, half):
    crossing = half_swap(add_over_near(sums[half:], half))
    return add_over_near(sums[:half], half) + crossing


def local(
    operator_blocks,
    operator_count,
    operator_slot,
    fetch_lists,
    prolong_blocks,
    prolong_cols,
    restrict_blocks,
    restrict_rows,
):
    rows, half = lax.axis_size("row"), lax.axis_size("near")
    slot_count = fetch_lists.shape[3]
    fine_rows, block_size, width = prolong_blocks.shape
    fetch = fetch_lists.reshape(2 * half, slot_count).T
    own = jnp.stack([lax.axis_index("row"), lax.axis_index("half")])
    own = jnp.concatenate([own, place_of_columns(half)])[None]

    near_blocks = prolong_blocks.reshape(fine_rows * block_size, width)
    far_blocks = half_swap(near_blocks)
    restricted, own_columns, near_blocks = restrict_operator(
        operator_count,
        operator_slot,
        restrict_rows.T,
        fetch,
        operator_blocks,
        restrict_blocks,
        prolong_cols.T,
        near_blocks,
        lax.axis_index("half").reshape(1),
    )
    restricted = lax.all_to_all(restricted, "near", split_axis=0, concat_axis=0, tiled=True)
    far_columns = half_swap(own_columns)
    near_pieces = spread_over_rows(near_blocks, rows)
    far_blocks = append_columns(near_pieces[rows // 2], far_columns, own_columns, far_blocks)
    pieces = near_pieces + spread_over_rows(far_blocks, rows)
    sums = combine(own, restricted, pieces, NCR * rows, slot_count, fine_rows, block_size)
    return add_over_columns(sums, half).T


def solution(mesh):
    rows, columns = mesh.shape["row"], mesh.shape["col"]
    split = Mesh(mesh.devices.reshape(rows, 2, columns // 2), ("row", "half", "near"))
    flat = ("row", "half", "near")
    return jax.shard_map(
        local,
        mesh=split,
        in_specs=(
            P(flat, None, None),
            P(flat),
            P(flat, None),
            P("row", ("half", "near"), None, None),
            P(flat, None, None),
            P(flat, None),
            P(flat, None, None),
            P(flat, None),
        ),
        out_specs=P("row", ("half", "near")),
        check_vma=False,
    )
```

```python
import functools

import jax
import jax.numpy as jnp
from jax import lax
from jax.experimental import pallas as pl
from jax.experimental.pallas import tpu as pltpu
from jax.sharding import Mesh
from jax.sharding import PartitionSpec as P

NCR = 2
LANES = 128
EXTRA = 8
HOLD_FLOPS = 16 << 30
VMEM_LIMIT = 48 * 1024 * 1024


def halves(x):
    high = x.astype(jnp.bfloat16)
    return high, (x - high.astype(jnp.float32)).astype(jnp.bfloat16)


def transposed_product(left, right):
    tall = jnp.concatenate(halves(left), axis=0)
    wide = jnp.concatenate(halves(right), axis=1)
    wide = jnp.concatenate([wide, wide], axis=0)
    both = lax.dot_general(tall, wide, (((0,), (0,)), ((), ())), preferred_element_type=jnp.float32)
    width = right.shape[1]
    return both[:, :width] + both[:, width:]


def append_kernel(next_ref, far_columns_ref, own_columns_ref, blocks_ref, out_ref):
    used = blocks_ref.shape[0]
    entries, fine_rows = own_columns_ref.shape
    out_ref[:used] = blocks_ref[...]
    out_ref[used:] = jnp.zeros((EXTRA, out_ref.shape[1]), jnp.float32)
    out_ref[used : used + entries, :fine_rows] = far_columns_ref[...].astype(jnp.float32)
    out_ref[used + entries : used + 2 * entries, :fine_rows] = own_columns_ref[...].astype(jnp.float32)


def append_columns(next_blocks, far_columns, own_columns, blocks):
    used, width = blocks.shape
    return pl.pallas_call(
        append_kernel,
        out_shape=jax.ShapeDtypeStruct((used + EXTRA, width), blocks.dtype),
        in_specs=[pl.BlockSpec(memory_space=pltpu.VMEM)] * 4,
        out_specs=pl.BlockSpec(memory_space=pltpu.VMEM),
        compiler_params=pltpu.CompilerParams(vmem_limit_bytes=VMEM_LIMIT),
        cost_estimate=pl.CostEstimate(flops=HOLD_FLOPS, bytes_accessed=HOLD_FLOPS >> 8, transcendentals=0),
        name="append_columns",
    )(next_blocks, far_columns, own_columns, blocks)


def restrict_kernel(
    count_any, slot_any, rows_any, fetch_any, restrict_any, operator_any, columns_any, blocks_any, side_any,
    out_ref, own_columns_ref, own_blocks_ref,
    count_ref, slot_ref, rows_ref, fetch_ref, side_ref, restrict_ref, operator_ref, sems, operator_sems,
):
    fine_rows, block_size, _ = operator_ref.shape
    entries = slot_ref.shape[1]
    slot_count, columns = fetch_ref.shape
    half = columns // 2
    used = 2 * slot_count * block_size
    wide = NCR * block_size

    pairs = [
        (count_any, count_ref), (slot_any, slot_ref), (rows_any, rows_ref),
        (fetch_any, fetch_ref), (restrict_any, restrict_ref),
        (columns_any, own_columns_ref), (blocks_any, own_blocks_ref), (side_any, side_ref),
    ]
    copies = [pltpu.make_async_copy(a, b, sems.at[i]) for i, (a, b) in enumerate(pairs)]
    operators = [
        pltpu.make_async_copy(operator_any.at[i], operator_ref.at[i], operator_sems.at[i]) for i in range(fine_rows)
    ]
    for copy in copies + operators:
        copy.start()

    lane = lax.broadcasted_iota(jnp.int32, (block_size, wide), 1)
    second = (lane >= block_size).astype(jnp.int32)
    short_lane = lax.broadcasted_iota(jnp.int32, (EXTRA, wide), 1)
    for near in range(half):
        out_ref[near, :used] = jnp.zeros((used, wide), jnp.float32)
    for copy in copies + operators:
        copy.wait()

    for near in range(half):
        value = jnp.zeros((EXTRA, wide), jnp.int32)
        for side in range(2):
            for s in range(slot_count):
                turned = near ^ jnp.where(side_ref[0] == side, 0, half // 2)
                wanted = fetch_ref[s, side * half + turned]
                value = jnp.where(short_lane == side * slot_count + s, wanted, value)
        out_ref[near, used:] = value.astype(jnp.float32)

    for i in range(fine_rows):
        value = restrict_ref[i]
        swapped = pltpu.roll(value, block_size, 1)
        own_row = jnp.where(second == 0, rows_ref[0, i], rows_ref[1, i])
        other_row = jnp.where(second == 0, rows_ref[1, i], rows_ref[0, i])
        dense = jnp.where(own_row == second, value, 0.0) + jnp.where(other_row == second, swapped, 0.0)
        product = transposed_product(operator_ref[i], dense)
        for k in range(entries):
            part = jnp.where(k < count_ref[i], product[k * block_size : (k + 1) * block_size], 0.0)
            peer = lax.div(slot_ref[i, k], slot_count)
            side = lax.div(peer, half)
            place = side * slot_count + lax.rem(slot_ref[i, k], slot_count)
            near = lax.rem(peer, half) ^ jnp.where(side_ref[0] == side, 0, half // 2)
            start = pl.multiple_of(place * block_size, block_size)
            out_ref[near, pl.ds(start, block_size)] += part


def restrict_operator(
    operator_count, operator_slot, restrict_rows, fetch, operator_blocks, restrict_blocks, own_columns, own_blocks, side
):
    fine_rows, block_size, width = operator_blocks.shape
    slot_count, columns = fetch.shape
    wide = NCR * block_size
    rows = 2 * slot_count * block_size + EXTRA
    small = (operator_count, operator_slot, restrict_rows, fetch)
    kept = small + (side,)
    return pl.pallas_call(
        restrict_kernel,
        out_shape=(
            jax.ShapeDtypeStruct((columns // 2, rows, wide), jnp.float32),
            jax.ShapeDtypeStruct(own_columns.shape, own_columns.dtype),
            jax.ShapeDtypeStruct(own_blocks.shape, own_blocks.dtype),
        ),
        in_specs=[pl.BlockSpec(memory_space=pltpu.HBM)] * 9,
        out_specs=[pl.BlockSpec(memory_space=pltpu.VMEM)] * 3,
        scratch_shapes=[pltpu.SMEM(x.shape, x.dtype) for x in kept]
        + [pltpu.VMEM(x.shape, x.dtype) for x in (restrict_blocks, operator_blocks)]
        + [pltpu.SemaphoreType.DMA((8,)), pltpu.SemaphoreType.DMA((fine_rows,))],
        cost_estimate=pl.CostEstimate(
            flops=6 * fine_rows * block_size * width * wide, bytes_accessed=4 << 20, transcendentals=0
        ),
        name="restrict_operator",
    )(*small, restrict_blocks, operator_blocks, own_columns, own_blocks, side)


def combine_kernel(own_ref, restricted_ref, *rest, slot_count, fine_rows, entries):
    pieces, (out_ref, held_ref, table_ref, index_ref, sem) = rest[:-5], rest[-5:]
    half = restricted_ref.shape[0]
    rows = len(pieces) // 2
    block_size = out_ref.shape[1]
    columns = 2 * half
    used = 2 * slot_count * block_size
    held = fine_rows * block_size

    table_ref[:1, : own_ref.shape[1]] = own_ref[...]
    for near in range(half):
        table_ref[1 + near : 2 + near] = restricted_ref[near, used : used + 1].astype(jnp.int32)
    for i, piece in enumerate(pieces[rows:]):
        for far in range(2):
            first = 1 + half + entries * (far * rows + i)
            row = held + entries * (1 - far)
            table_ref[first : first + entries] = piece[row : row + entries].astype(jnp.int32)
    copy = pltpu.make_async_copy(table_ref, index_ref, sem)
    copy.start()
    for i, piece in enumerate(pieces):
        held_ref[i] = piece[...] if i < rows else piece[:held]
    out_ref[...] = jnp.zeros_like(out_ref)
    copy.wait()

    def step(i, carry):
        near = lax.div(i, 2 * slot_count)
        place = lax.rem(i, 2 * slot_count)
        wanted = index_ref[1 + near, place]
        inside = lax.rem(wanted, fine_rows)
        far = lax.div(place, slot_count) ^ index_ref[0, 1]
        piece = far * rows + (lax.div(wanted, fine_rows * columns) ^ index_ref[0, 0])
        block = held_ref[piece, pl.ds(pl.multiple_of(inside * block_size, block_size), block_size)]
        restricted = restricted_ref[near, pl.ds(pl.multiple_of(place * block_size, block_size), block_size)]
        product = transposed_product(block, restricted)
        for m in range(entries):
            column = index_ref[0, 2 + index_ref[1 + half + entries * piece + m, inside]]
            out_ref[column] += product[m * block_size : (m + 1) * block_size]
        return carry

    lax.fori_loop(0, half * 2 * slot_count, step, 0, unroll=16)


def combine(own, restricted, pieces, coarse_all, slot_count, fine_rows, block_size):
    half, _, wide = restricted.shape
    width = pieces[0].shape[1]
    entries = width // block_size
    table_rows = -(-(1 + half + entries * len(pieces)) // 8) * 8
    return pl.pallas_call(
        functools.partial(combine_kernel, slot_count=slot_count, fine_rows=fine_rows, entries=entries),
        out_shape=jax.ShapeDtypeStruct((coarse_all, block_size, wide), jnp.float32),
        in_specs=[pl.BlockSpec(memory_space=pltpu.VMEM)] * (2 + len(pieces)),
        out_specs=pl.BlockSpec(memory_space=pltpu.VMEM),
        scratch_shapes=[
            pltpu.VMEM((len(pieces), fine_rows * block_size, width), jnp.float32),
            pltpu.VMEM((table_rows, LANES), jnp.int32),
            pltpu.SMEM((table_rows, LANES), jnp.int32),
            pltpu.SemaphoreType.DMA,
        ],
        compiler_params=pltpu.CompilerParams(vmem_limit_bytes=VMEM_LIMIT),
        cost_estimate=pl.CostEstimate(flops=1 << 28, bytes_accessed=4 << 20, transcendentals=0),
        name="combine",
    )(own, restricted, *pieces)


def row_swap(x, bit):
    return lax.ppermute(x, "row", [(r, r ^ bit) for r in range(lax.axis_size("row"))])


def half_swap(x):
    return lax.ppermute(x, "half", [(0, 1), (1, 0)])


def far_swap(x):
    half = lax.axis_size("near")
    pairs = [(h * half + n, (1 - h) * half + (n ^ half // 2)) for h in range(2) for n in range(half)]
    return lax.ppermute(x, ("half", "near"), pairs)


def spread_over_rows(blocks, rows):
    pieces = {0: blocks}
    bit = rows // 2
    while bit:
        for mask in list(pieces):
            pieces[mask ^ bit] = row_swap(pieces[mask], bit)
        bit //= 2
    return [pieces[mask] for mask in range(rows)]


def place_of_columns(half):
    own = lax.axis_index("half") * half + lax.axis_index("near")
    return jnp.arange(2 * half, dtype=jnp.int32) ^ own


def add_over_near(sums, first, half):
    total = sums[0] + first
    for near in range(2, half):
        total = total + lax.ppermute(sums[near], "near", [(n, n ^ near) for n in range(half)])
    return total


def add_over_columns(sums, half):
    pair = jnp.stack([sums[1], sums[half + 1]])
    pair = lax.ppermute(pair, "near", [(n, n ^ 1) for n in range(half)])
    crossing = half_swap(add_over_near(sums[half:], pair[1], half))
    return add_over_near(sums[:half], pair[0], half) + crossing


def local(
    operator_blocks,
    operator_count,
    operator_slot,
    fetch_lists,
    prolong_blocks,
    prolong_cols,
    restrict_blocks,
    restrict_rows,
):
    rows, half = lax.axis_size("row"), lax.axis_size("near")
    slot_count = fetch_lists.shape[3]
    fine_rows, block_size, width = prolong_blocks.shape
    fetch = fetch_lists.reshape(2 * half, slot_count).T
    own = jnp.stack([lax.axis_index("row"), lax.axis_index("half")])
    own = jnp.concatenate([own, place_of_columns(half)])[None]

    near_blocks = prolong_blocks.reshape(fine_rows * block_size, width)
    far_blocks = far_swap(near_blocks)
    restricted, own_columns, near_blocks = restrict_operator(
        operator_count,
        operator_slot,
        restrict_rows.T,
        fetch,
        operator_blocks,
        restrict_blocks,
        prolong_cols.T,
        near_blocks,
        lax.axis_index("half").reshape(1),
    )
    restricted = lax.all_to_all(restricted, "near", split_axis=0, concat_axis=0, tiled=True)
    far_columns = far_swap(own_columns)
    near_pieces = spread_over_rows(near_blocks, rows)
    far_blocks = append_columns(near_pieces[rows // 2], far_columns, own_columns, far_blocks)
    pieces = near_pieces + spread_over_rows(far_blocks, rows)
    sums = combine(own, restricted, pieces, NCR * rows, slot_count, fine_rows, block_size)
    return add_over_columns(sums, half).T


def solution(mesh):
    rows, columns = mesh.shape["row"], mesh.shape["col"]
    split = Mesh(mesh.devices.reshape(rows, 2, columns // 2), ("row", "half", "near"))
    flat = ("row", "half", "near")
    return jax.shard_map(
        local,
        mesh=split,
        in_specs=(
            P(flat, None, None),
            P(flat),
            P(flat, None),
            P("row", ("half", "near"), None, None),
            P(flat, None, None),
            P(flat, None),
            P(flat, None, None),
            P(flat, None),
        ),
        out_specs=P("row", ("half", "near")),
        check_vma=False,
    )
```
